32 devices in a mesh: rep: 4 (over z), ep: 8 (over y, x, core).
Axes of the slice: x: 2, y: 2, z: 4, core: 2. Of those that a mesh axis runs over, the one named last changes fastest.
Arguments:
- tokens: bfloat16 [8192, 2048], P(('rep', 'ep')), may hold values from -6 to 6
- cotangent: bfloat16 [8192, 2048], P(('rep', 'ep')), may hold values from -6 to 6
- w_qkv: bfloat16 [2048, 6144], P(('rep', 'ep')), may hold values from -0.125 to 0.125
- w_o: bfloat16 [2048, 2048], P(('rep', 'ep')), may hold values from -1 to 1
- w_router: bfloat16 [2048, 16], P(('rep', 'ep')), may hold values from -0.06591797 to 0.06591797
- norm_gains: bfloat16 [4096], P(('rep', 'ep')), may hold values from 0.5 to 1.5
- qk_gain: bfloat16 [256], replicated, may hold values from 1 to 2
- w_in: bfloat16 [16, 2048, 2048], P('ep', 'rep'), may hold values from -0.125 to 0.125
- w_out: bfloat16 [16, 1024, 2048], P('ep', 'rep'), may hold values from -0.5 to 0.5
- segments: int32 [4, 2, 1024], P('rep'), may hold values from 0 to 3, never falling along the last dimension, each value on 1 to 512 neighbouring positions
- routes: int32 [8192, 8], P(('rep', 'ep')), may hold values from 0 to 15, all different within a row; in each aligned block of 128 rows (0 to 127, 128 to 255, ...) at most 68 rows name the same one
Outputs:
- output: bfloat16 [8192, 2048], P(('rep', 'ep'))
- grad_tokens: float32 [8192, 2048], P(('rep', 'ep'))
- grad_w_qkv: float32 [2048, 6144], P(('rep', 'ep'))
- grad_w_o: float32 [2048, 2048], P(('rep', 'ep'))
- grad_w_router: float32 [2048, 16], P(('rep', 'ep'))
- grad_norm_gains: float32 [4096], P(('rep', 'ep'))
- grad_qk_gain: float32 [256], replicated
- grad_w_in: float32 [16, 2048, 2048], P('ep', 'rep')
- grad_w_out: float32 [16, 1024, 2048], P('ep', 'rep')
The draws below stay inside these ranges and needn't reach their ends.
Inputs may be any that keep to these rules, and one draw needn't show every extreme that they name: `routes`: in each aligned block of 128 rows (one micro-batch of one device on this slice) no expert is named by more than 68 rows, a bound that some block reaches; a row names 8 different experts. `segments`: never falls along a sequence.
All inputs are finite; a program needn't handle non-finite values.
Results may differ from the reference program's by a relative error of at most 0.018.
The reference program's roundings to bfloat16 on the way count: a program that leaves them out, or rounds other values in their place, can miss the bound.
Values may be sent and summed in bfloat16 or wider, within the bound.
No kernel may reach another device: no remote copies, remote signals or barrier semaphores. Data moves between devices by JAX's collectives and lax.ppermute only.
A program may use at most 384 MiB of HBM per device.

```python
import math
import jax
import jax.numpy as jnp
import numpy as np
from jax import lax

D = 2048
HEADS = 16
HD = 128
FF = 1024
TOP = 8
HALF = 512
MICRO = 2
MB_TOK = 128
EXPERTS = 16
CAP = 68
SEQ = 1024
TOK_DEV = 256
TOKENS = 8192
N_REP = 4
N_EP = 8


def levels(own_key, shape, pieces, smallest, top_value):
    factor_of, own = 1.0, jax.random.fold_in(own_key, 6)
    for dim, shards_of in pieces:
        steps = jnp.exp(jax.random.uniform(jax.random.fold_in(own, dim), (shards_of,), jnp.float32, smallest / len(pieces), top_value / len(pieces)))
        factor_of = factor_of * jnp.repeat(steps, shape[dim] // shards_of).reshape([-1 if axis == dim else 1 for axis in range(len(shape))])
    return factor_of


def length_profile(count, total, limit, slope):
    portions = [(1 << 20) // math.isqrt(standing ** slope) + 1 for standing in range(2, count + 1)]
    spare, given = total - limit - (count - 1), [1] * (count - 1)
    while spare > 0:
        movable = [i for i in range(count - 1) if given[i] < limit]
        whole, left = sum([portions[i] for i in movable]), spare
        for i in movable:
            addition = min(limit - given[i], max(1, left * portions[i] // whole), spare)
            given[i] = given[i] + addition
            spare = spare - addition
    return np.array([limit] + given)


def ragged(rng, number_of, total, limit, skew):
    if number_of == 2:
        one = jax.random.randint(rng, (), max(1, total - limit), min(limit, total - 1) + 1)
        return jnp.stack([one, total - one])
    tallies = jnp.asarray(length_profile(number_of, total, limit, skew), jnp.int32)
    twos = (number_of - 1) // 2
    giver, sink = tallies[1:1 + 2 * twos:2], tallies[2:2 + 2 * twos:2]
    slack = jnp.minimum(giver - 1, limit - sink)
    passed = jax.random.randint(jax.random.fold_in(rng, 1), (twos,), 0, 1 << 20) % (slack + 1)
    tallies = tallies.at[1:1 + 2 * twos:2].set(giver - passed).at[2:2 + 2 * twos:2].set(sink + passed)
    return tallies[jax.random.permutation(jax.random.fold_in(rng, 2), number_of)]


def assign_block(own_key, own, number, rows, amount, top, bound, skew):
    sequence = jax.random.permutation(own_key, amount)
    heavy_load, common = portions_of(amount, rows * top, bound, skew, True), portions_of(amount, rows * top, bound, skew, False)
    places = jnp.arange(amount)

    def named(tallies, offset_by):
        used = int((tallies > 0).sum())
        fixed = max(1, used // 4)
        passed = fixed + (places - fixed + offset_by * (used - fixed)) % max(1, amount - fixed)
        return jnp.zeros((amount,), jnp.int32).at[sequence[jnp.where(places < fixed, places, passed)]].set(jnp.asarray(tallies, jnp.int32))

    tallies = jnp.where(number % 4 == 0, named(heavy_load, number // 4), named(common, number - number // 4 - 1))
    mixed = jax.random.permutation(jax.random.fold_in(own, 3), amount)
    giver, taker = mixed[0:amount // 2 * 2:2], mixed[1:amount // 2 * 2:2]
    room = jnp.minimum(tallies[giver] - 1, bound - tallies[taker]) // 2
    room = jnp.where((giver == sequence[0]) | (taker == sequence[0]) | (tallies[taker] == 0), 0, jnp.maximum(room, 0))
    passed = jax.random.randint(jax.random.fold_in(own, 4), (amount // 2,), 0, 1 << 20) % (room + 1)
    tallies = tallies.at[giver].add(-passed).at[taker].add(passed)
    items = jnp.searchsorted(jnp.cumsum(tallies), jnp.arange(rows * top), side="right").astype(jnp.int32)
    grid = items.reshape(top, rows).T
    grid = grid[jax.random.permutation(jax.random.fold_in(own, 1), rows)]
    offset_by = jax.random.randint(jax.random.fold_in(own, 2), (rows, 1), 0, top)
    return jnp.take_along_axis(grid, (jnp.arange(top)[None, :] + offset_by) % top, axis=1)


def portions_of(number_of, total, reach, skew, full):
    weights = [(1 << 20) // math.isqrt(rank ** skew) + 1 for rank in range(1, number_of + 1)]
    largest = reach if full else min(reach, max(-(-total // number_of), total * weights[0] // sum(weights)))
    least = 1 if total - largest >= number_of - 1 else 0
    holding, rest = [largest] + [least] * (number_of - 1), total - largest - least * (number_of - 1)
    while rest > 0:
        candidates = [i for i in range(1, number_of) if holding[i] < largest] or [i for i in range(1, number_of) if holding[i] < reach]
        whole, remaining = sum([weights[i] for i in candidates]), rest
        for i in candidates:
            addition = min(reach - holding[i], max(1, remaining * weights[i] // whole), rest)
            holding[i] = holding[i] + addition
            rest = rest - addition
    return np.array(holding)


def normal_values(key, extent, deviation, limit, split=(), kind=jnp.bfloat16):
    level = levels(key, extent, split, -0.22, 0.18) if split else 1.0
    drawn = jax.random.normal(key, extent, jnp.float32) * deviation * level
    return jnp.minimum(jnp.maximum(drawn, -limit), limit).astype(kind)


def setup_inputs(seed: int = 0) -> dict:
    streams_of = jax.random.split(jax.random.key(seed), 12)
    tokens = normal_values(streams_of[0], (TOKENS, D), 1.0, 6.0, ((0, 32),))
    cotangent = normal_values(streams_of[1], (TOKENS, D), 1.0, 6.0, ((0, 32),))
    w_qkv = normal_values(streams_of[2], (D, 3 * D), D ** -0.5, 0.125, ((0, 32),))
    w_o = normal_values(streams_of[3], (D, D), (D // 64) ** -0.5, 1.0, ((0, 32),))
    w_router = normal_values(streams_of[4], (D, EXPERTS), (0.5 / D ** 0.5), 0.06591797, ((0, 32),))
    norm_gains = jnp.clip(1.0 + 0.1 * jax.random.normal(streams_of[5], (2 * D,), jnp.float32), 0.5, 1.5).astype(jnp.bfloat16)
    qk_gain = jnp.clip(jax.random.uniform(streams_of[6], (2 * HD,), jnp.float32, 1.0, 2.0), 1.0, 2.0).astype(jnp.bfloat16)
    w_in = normal_values(streams_of[7], (EXPERTS, D, 2 * FF), D ** -0.5, 0.125, ((0, 8), (1, 4)))
    w_out = normal_values(streams_of[8], (EXPERTS, FF, D), (FF // 8) ** -0.5, 0.5, ((0, 8), (1, 4)))
    segments = jax.vmap(lambda own: jnp.searchsorted(jnp.cumsum(ragged(own, 4, SEQ, SEQ // 2, 0)), jnp.arange(SEQ), side="right"))(jax.random.split(streams_of[9], N_REP * MICRO)).reshape((N_REP, MICRO, SEQ)).astype(jnp.int32)
    routes_keys = jax.random.split(jax.random.fold_in(streams_of[10], 1), TOKENS // MB_TOK)
    routes_turns = jax.random.permutation(jax.random.fold_in(streams_of[10], 3), TOKENS // MB_TOK)
    routes = jax.vmap(lambda own, number: assign_block(jax.random.fold_in(streams_of[10], 2), own, number, MB_TOK, EXPERTS, TOP, CAP, 1))(routes_keys, routes_turns).reshape((TOKENS, TOP))
    return {"tokens": tokens, "cotangent": cotangent, "w_qkv": w_qkv, "w_o": w_o, "w_router": w_router, "norm_gains": norm_gains, "qk_gain": qk_gain, "w_in": w_in, "w_out": w_out, "segments": segments, "routes": routes}


@jax.custom_vjp
def low(v):
    return lax.optimization_barrier(v.astype(jnp.bfloat16)).astype(jnp.float32)

@jax.custom_vjp
def low_back(v):
    return v

def low_keep(v):
    return (low(v), None)

def low_pass(kept, grad):
    return (grad,)

def back_keep(v):
    return (v, None)

def back_low(kept, grad):
    return (low(grad),)
low.defvjp(low_keep, low_pass)
low_back.defvjp(back_keep, back_low)
highest = lax.Precision.HIGHEST
epsilon = 1e-06
rope_base = 50000.0

def rms_scale(value, gain):
    return value * lax.rsqrt(lax.optimization_barrier(jnp.mean(value * value, axis=-1, keepdims=True)) + epsilon) * gain

def rotate(value, cosine, sine):
    half = value.shape[-1] // 2
    turned = jnp.concatenate([-value[..., half:], value[..., :half]], axis=-1)
    return value * cosine + turned * sine

def doc_positions(segment):
    index = jnp.arange(segment.shape[0], dtype=jnp.int32)
    change = jnp.concatenate([jnp.ones((1,), dtype=jnp.bool_), segment[1:] != segment[:-1]])
    start = lax.cummax(jnp.where(change, index, 0), axis=0)
    return index - start

def rope_tables(position, width):
    steps = jnp.arange(width // 2, dtype=jnp.float32) * (2.0 / width)
    rates = jnp.exp(-steps * math.log(rope_base))
    angle = position.astype(jnp.float32)[:, None] * rates[None, :]
    angle = jnp.concatenate([angle, angle], axis=-1)
    return (jnp.cos(angle), jnp.sin(angle))

def block_slots(route_block, experts):
    flat = route_block.reshape(-1)
    one_hot = (flat[:, None] == jnp.arange(experts, dtype=jnp.int32)[None, :]).astype(jnp.int32)
    before = jnp.cumsum(one_hot, axis=0) - one_hot
    return lax.optimization_barrier(jnp.sum(before * one_hot, axis=1)).reshape(route_block.shape)

def attend_one(item):
    query, keys, values, segment = item
    scale = 1.0 / math.sqrt(query.shape[-1])
    scores = low_back(jnp.dot(query, keys.T, precision=highest) * scale)
    index = jnp.arange(segment.shape[0], dtype=jnp.int32)
    keep = (jnp.abs(index[:, None] - index[None, :]) <= HALF) & (segment[:, None] == segment[None, :])
    scores = jnp.where(keep, scores, -1e+30)
    top = lax.optimization_barrier(jnp.max(scores, axis=1, keepdims=True))
    weights = jnp.exp(scores - top)
    weights = weights / lax.optimization_barrier(jnp.sum(weights, axis=1, keepdims=True))
    return low_back(low(jnp.dot(low(weights), values, precision=highest)))

def route_gates(route_rows, logits):
    chosen = jnp.take_along_axis(logits, route_rows, axis=1)
    chosen = jnp.exp(chosen - lax.optimization_barrier(jnp.max(chosen, axis=1, keepdims=True)))
    return chosen / lax.optimization_barrier(jnp.sum(chosen, axis=1, keepdims=True))

def reference(tokens, cotangent, w_qkv, w_o, w_router, norm_gains, qk_gain, w_in, w_out, segments, routes):
    seq_count = N_REP * MICRO
    seg_flat = segments.reshape(seq_count, SEQ)
    pos_seq = jax.vmap(doc_positions)(seg_flat)
    pos_tok = pos_seq.reshape(N_REP, MICRO, N_EP, MB_TOK).transpose(0, 2, 1, 3).reshape(TOKENS)
    cosine, sine = rope_tables(pos_tok, HD)
    cosine = cosine[:, None, :]
    sine = sine[:, None, :]
    seg_items = jnp.repeat(seg_flat, HEADS, axis=0)
    slot_of = jax.vmap(partial_slots)(routes.reshape(-1, MB_TOK, TOP)).reshape(TOKENS, TOP)
    token_index = jnp.arange(TOKENS, dtype=jnp.int32)
    group = token_index // (N_EP * TOK_DEV)
    member = token_index // TOK_DEV % N_EP
    micro_index = token_index % TOK_DEV // MB_TOK
    capacity_rows = N_REP * MICRO * N_EP * CAP
    base = ((group * MICRO + micro_index) * N_EP + member) * CAP
    place = routes * capacity_rows + base[:, None] + slot_of
    assign = token_index[:, None] * TOP + jnp.arange(TOP, dtype=jnp.int32)[None, :]
    table = jnp.full((EXPERTS * capacity_rows,), -1, dtype=jnp.int32)
    table = table.at[place.reshape(-1)].set(assign.reshape(-1)).reshape(EXPERTS, capacity_rows)

    def to_seq(value):
        shaped = value.reshape(N_REP, N_EP, MICRO, MB_TOK, HEADS, HD).transpose(0, 2, 4, 1, 3, 5)
        return shaped.reshape(seq_count * HEADS, SEQ, HD)

    def forward(stream, qkv_weight, out_weight, router_weight, gains, qk_gains, expert_in, expert_out):
        normed = low(rms_scale(stream, gains[:D]))
        projected = low_back(jnp.dot(normed, qkv_weight, precision=highest))
        query = projected[:, :D].reshape(TOKENS, HEADS, HD)
        keys = projected[:, D:2 * D].reshape(TOKENS, HEADS, HD)
        values = projected[:, 2 * D:].reshape(TOKENS, HEADS, HD)
        query = low_back(low(rotate(rms_scale(query, qk_gains[:HD]), cosine, sine)))
        keys = low_back(low(rotate(rms_scale(keys, qk_gains[HD:]), cosine, sine)))
        values = low_back(low(values))
        mixed = lax.map(jax.checkpoint(attend_one), (to_seq(query), to_seq(keys), to_seq(values), seg_items))
        mixed = mixed.reshape(N_REP, MICRO, HEADS, N_EP, MB_TOK, HD).transpose(0, 3, 1, 4, 2, 5).reshape(TOKENS, D)
        hidden_state = stream + low_back(jnp.dot(mixed, out_weight, precision=highest))
        normed_two = low(rms_scale(hidden_state, gains[D:]))
        logits = low_back(jnp.dot(normed_two, router_weight, precision=highest))
        gates = route_gates(routes, logits)

        def expert_one(item):
            weight_in, weight_out, owner = item
            valid = owner >= 0
            picked = jnp.where(valid, owner // TOP, 0)
            rows_in = low_back(normed_two[picked] * valid[:, None].astype(jnp.float32))
            both = low_back(jnp.dot(rows_in, weight_in, precision=highest))
            gate_part = both[:, :FF]
            up_part = both[:, FF:]
            active = low_back(low(gate_part / (1.0 + jnp.exp(-gate_part)) * up_part))
            return low_back(low(jnp.dot(active, weight_out, precision=highest)))
        results = lax.map(jax.checkpoint(expert_one), (expert_in, expert_out, table)).reshape(EXPERTS * capacity_rows, D)
        mixture = jnp.zeros_like(stream)
        for slot in range(TOP):
            mixture = mixture + gates[:, slot:slot + 1] * results[place[:, slot]]
        return hidden_state + mixture
    primals = (tokens.astype(jnp.float32), w_qkv.astype(jnp.float32), w_o.astype(jnp.float32), w_router.astype(jnp.float32), norm_gains.astype(jnp.float32), qk_gain.astype(jnp.float32), w_in.astype(jnp.float32), w_out.astype(jnp.float32))
    result, pullback = jax.vjp(forward, *primals)
    grads = pullback(cotangent.astype(jnp.float32))
    return (result.astype(jnp.bfloat16), grads[0], grads[1], grads[2], grads[3], grads[4], grads[5], grads[6], grads[7])

def partial_slots(route_block):
    return block_slots(route_block, EXPERTS)
```

```python
import math

import jax
import jax.numpy as jnp
from jax import lax
from jax.experimental import pallas as pl
from jax.experimental.pallas import tpu as pltpu
from jax.sharding import PartitionSpec as P

D = 2048
HEADS = 16
HD = 128
FF = 1024
TOP = 8
HALF = 512
PAD = 128

epsilon = 1e-06
rope_base = 50000.0
bf16 = jnp.bfloat16
f32 = jnp.float32


def dot(a, b, dims=((1,), (0,))):
    return lax.dot_general(a, b, (dims, ((), ())), preferred_element_type=f32)


def inverse_rms(value):
    return lax.rsqrt(jnp.mean(value * value, axis=-1, keepdims=True) + epsilon)


def rms_backward(value, inverse, gain, grad):
    scaled = grad * gain
    inner = jnp.mean(scaled * value, axis=-1, keepdims=True)
    return inverse * (scaled - value * (inverse * inverse * inner))


def doc_positions(segment):
    index = jnp.arange(segment.shape[0], dtype=jnp.int32)
    change = jnp.concatenate([jnp.ones((1,), dtype=jnp.bool_), segment[1:] != segment[:-1]])
    start = lax.cummax(jnp.where(change, index, 0), axis=0)
    return index - start


def rope_tables(position, width):
    steps = jnp.arange(width // 2, dtype=f32) * (2.0 / width)
    rates = jnp.exp(-steps * math.log(rope_base))
    angle = position.astype(f32)[:, None] * rates[None, :]
    angle = jnp.concatenate([angle, angle], axis=-1)
    return (jnp.cos(angle), jnp.sin(angle))


def norm_rope(value, gain, cosine, sine):
    inverse = lax.rsqrt(jnp.mean(value * value, axis=1, keepdims=True) + epsilon)
    value = value * inverse * gain
    return value * cosine + pltpu.roll(value, HD // 2, 1) * sine


def norm_rope_back(value, gain, cosine, sine, grad):
    inverse = lax.rsqrt(jnp.mean(value * value, axis=1, keepdims=True) + epsilon)
    grad = grad * cosine + pltpu.roll(grad * sine, HD // 2, 1)
    normal = value * inverse
    scaled = grad * gain
    inner = jnp.mean(scaled * normal, axis=1, keepdims=True)
    return inverse * (scaled - normal * inner), jnp.sum(grad * normal, axis=0, keepdims=True)


def kept_scores(query, keys, q_seg, k_seg, start):
    scores = dot(query, keys, ((1,), (1,))) * (1.0 / math.sqrt(HD))
    q_index = start + lax.broadcasted_iota(jnp.int32, scores.shape, 0)
    k_index = lax.broadcasted_iota(jnp.int32, scores.shape, 1)
    keep = (jnp.abs(q_index - k_index) <= HALF) & (q_seg == k_seg)
    return jnp.where(keep, scores, -1e30)


Q_BLOCK = 256


def forward_kernel(
    heads, proj, cosine, sine, seg_column, seg_row, gains, mixed, query, keys, values, lses
):
    length = proj.shape[1]
    k_seg = seg_row[0]
    for head in range(heads):
        at = slice(head * HD, (head + 1) * HD)
        raw_q = proj[0, :, head * HD : (head + 1) * HD]
        raw_k = proj[0, :, (heads + head) * HD : (heads + head + 1) * HD]
        raw_v = proj[0, :, (2 * heads + head) * HD : (2 * heads + head + 1) * HD]
        query[0, :, at] = norm_rope(raw_q, gains[0:1], cosine[0], sine[0]).astype(bf16)
        keys[0, :, at] = norm_rope(raw_k, gains[1:2], cosine[0], sine[0]).astype(bf16)
        values[0, :, at] = raw_v.astype(bf16)

        @pl.loop(0, length // Q_BLOCK)
        def one_block(number, head=head, at=at):
            start = pl.multiple_of(number * Q_BLOCK, Q_BLOCK)
            rows = pl.ds(start, Q_BLOCK)
            scores = kept_scores(
                query[0, rows, at], keys[0, :, at], seg_column[0, rows], k_seg, start
            )
            top = jnp.max(scores, axis=1, keepdims=True)
            weights = jnp.exp(scores - top)
            total = jnp.sum(weights, axis=1, keepdims=True)
            lses[0, head, rows] = top + jnp.log(total)
            weights = (weights * (1.0 / total)).astype(bf16)
            mixed[0, rows, at] = dot(weights, values[0, :, at]).astype(bf16)


def backward_kernel(
    heads, proj, cosine, sine, seg_column, seg_row, gains, query, keys, values, lses, grad_mixed,
    grad_proj, grad_gains, grad_q, grad_k, grad_v,
):
    length = proj.shape[1]
    k_seg = seg_row[0]
    scale = 1.0 / math.sqrt(HD)
    sum_q = jnp.zeros((1, HD), f32)
    sum_k = jnp.zeros((1, HD), f32)
    for head in range(heads):
        at = slice(head * HD, (head + 1) * HD)
        grad_k[...] = jnp.zeros_like(grad_k)
        grad_v[...] = jnp.zeros_like(grad_v)

        @pl.loop(0, length // Q_BLOCK)
        def one_block(number, head=head, at=at):
            start = pl.multiple_of(number * Q_BLOCK, Q_BLOCK)
            rows = pl.ds(start, Q_BLOCK)
            q_rows = query[0, rows, at]
            g_rows = grad_mixed[0, rows, at]
            k_all = keys[0, :, at]
            scores = kept_scores(q_rows, k_all, seg_column[0, rows], k_seg, start)
            weights = jnp.exp(scores - lses[0, head, rows])
            grad_weights = dot(g_rows, values[0, :, at], ((1,), (1,)))
            delta = jnp.sum(weights * grad_weights, axis=1, keepdims=True)
            grad_scores = (weights * (grad_weights - delta)).astype(bf16)
            grad_q[rows] = dot(grad_scores, k_all) * scale
            grad_k[...] += dot(grad_scores, q_rows, ((0,), (0,)))
            grad_v[...] += dot(weights.astype(bf16), g_rows, ((0,), (0,)))

        def rounded(value):
            return value.astype(bf16).astype(f32)

        raw_q = proj[0, :, head * HD : (head + 1) * HD]
        raw_k = proj[0, :, (heads + head) * HD : (heads + head + 1) * HD]
        back_q, gain_q = norm_rope_back(
            raw_q, gains[0:1], cosine[0], sine[0], rounded(grad_q[...])
        )
        back_k, gain_k = norm_rope_back(
            raw_k, gains[1:2], cosine[0], sine[0], rounded(grad_k[...] * scale)
        )
        sum_q, sum_k = sum_q + gain_q, sum_k + gain_k
        grad_proj[0, :, at] = back_q.astype(bf16)
        grad_proj[0, :, (heads + head) * HD : (heads + head + 1) * HD] = back_k.astype(bf16)
        grad_proj[0, :, (2 * heads + head) * HD : (2 * heads + head + 1) * HD] = grad_v[
            ...
        ].astype(bf16)
    grad_gains[0, 0:1] = sum_q
    grad_gains[0, 1:2] = sum_k


def whole_spec(shape):
    return pl.BlockSpec((1,) + shape[1:], lambda i: (i,) + (0,) * (len(shape) - 1))


def batch_call(kernel, out_shape, scratch, args, shared):
    specs = [
        pl.BlockSpec(value.shape, lambda i, n=value.ndim: (0,) * n)
        if place in shared
        else whole_spec(value.shape)
        for place, value in enumerate(args)
    ]
    return pl.pallas_call(
        kernel,
        grid=(args[0].shape[0],),
        in_specs=specs,
        out_specs=[whole_spec(out.shape) for out in out_shape],
        out_shape=out_shape,
        scratch_shapes=scratch,
        compiler_params=pltpu.CompilerParams(vmem_limit_bytes=48 * 1024 * 1024),
    )(*args)


def attention_forward(proj, cosine, sine, seg_column, seg_row, gains):
    count, length, width = proj.shape
    width = width // 3
    heads = width // HD
    part = jax.ShapeDtypeStruct((count, length, width), bf16)
    lses = jax.ShapeDtypeStruct((count, heads, length, 1), f32)
    return batch_call(
        lambda *refs: forward_kernel(heads, *refs),
        [part, part, part, part, lses],
        [],
        (proj, cosine, sine, seg_column, seg_row, gains),
        (5,),
    )


def attention_backward(
    proj, cosine, sine, seg_column, seg_row, gains, query, keys, values, lses, grad_mixed
):
    count, length, width = proj.shape
    heads = width // 3 // HD
    return batch_call(
        lambda *refs: backward_kernel(heads, *refs),
        [
            jax.ShapeDtypeStruct((count, length, width), bf16),
            jax.ShapeDtypeStruct((count, 2, HD), f32),
        ],
        [pltpu.VMEM((length, HD), f32)] * 3,
        (proj, cosine, sine, seg_column, seg_row, gains, query, keys, values, lses, grad_mixed),
        (5,),
    )


def shift_rep(value, step):
    count = lax.axis_size("rep")
    return lax.ppermute(value, "rep", [(i, (i + step) % count) for i in range(count)])


def after(value, *others):
    return lax.optimization_barrier((value,) + others)[0]


def two_parts(value):
    high = lax.reduce_precision(value, 8, 7)
    return high.astype(bf16), (value - high).astype(bf16)


def shift_order(count):
    return sorted(range(1, count), key=lambda step: (-min(step, count - step), step))


def place_rep(pieces):
    count = len(pieces)
    rank = lax.axis_index("rep")
    rows = pieces[0].shape[0]
    full = jnp.zeros((count * rows,) + pieces[0].shape[1:], pieces[0].dtype)
    for step, piece in enumerate(pieces):
        full = lax.dynamic_update_slice_in_dim(full, piece, (rank - step) % count * rows, 0)
    return full


class Chain:
    def __init__(self, depth):
        self.depth = depth
        self.done = []

    def send(self, value, step):
        if len(self.done) >= self.depth:
            value = after(value, self.done[-self.depth])
        value = shift_rep(value, step)
        self.done.append(value)
        return value


def on_device(
    tokens, cotangent, w_qkv, w_o, w_router, norm_gains, qk_gain, w_in, w_out, segments, routes
):
    planes = lax.axis_size("rep")
    ranks = lax.axis_size("ep")
    plane = lax.axis_index("rep")
    rank = lax.axis_index("ep")
    share = w_in.shape[0]
    own = plane % share
    experts = share * ranks
    expert = rank * share + own
    micro = segments.shape[1]
    mine = tokens.shape[0]
    rows = mine // micro
    length = rows * ranks
    capacity = rows * TOP * 17 // (16 * experts)
    block = share * mine
    slots = -(-share * micro * capacity // 16) * 16
    width = HEADS // ranks * HD
    qk_gains = qk_gain.astype(f32).reshape(2, HD)
    dense_rows = w_qkv.shape[0]

    def exchange(value, step):
        pairs = [(i, i // share * share + (i % share + step) % share) for i in range(planes)]
        return lax.ppermute(value, "rep", pairs)

    def with_group(value):
        return jnp.stack([value] + [exchange(value, step) for step in range(1, share)])

    def gather_ranks(value):
        return lax.all_gather(value, "ep", axis=0)

    stream_all = gather_ranks(tokens)
    out_pieces = [w_o] + [shift_rep(w_o, step) for step in range(1, planes)]
    upstream_group = with_group(cotangent)
    slab = jnp.concatenate(
        [
            w_qkv.reshape(dense_rows, 3, ranks, width)
            .transpose(2, 0, 1, 3)
            .reshape(ranks, dense_rows, 3 * width),
            jnp.broadcast_to(
                jnp.concatenate(
                    [
                        w_router,
                        norm_gains.reshape(dense_rows, 2),
                        jnp.zeros((dense_rows, PAD - experts - 2), bf16),
                    ],
                    axis=1,
                )[None],
                (ranks, dense_rows, PAD),
            ),
        ],
        axis=2,
    )
    slab = lax.all_to_all(slab, "ep", split_axis=0, concat_axis=0, tiled=True)
    slab = slab.reshape(ranks * dense_rows, 3 * width + PAD)
    slab_pieces = [slab] + [shift_rep(slab, step) for step in range(1, planes)]
    slab = place_rep(slab_pieces)
    qkv_weight = slab[:, : 3 * width]
    router_weight = slab[:, 3 * width : 3 * width + experts]
    gain_pair = slab[:, 3 * width + experts : 3 * width + experts + 2].reshape(-1).astype(f32)
    first_gain = gain_pair[:D]
    second_gain = gain_pair[D:]
    out_weight = gather_ranks(after(place_rep(out_pieces), stream_all))
    out_weight = (
        out_weight.reshape(ranks, planes, -1, D).transpose(1, 0, 2, 3).reshape(D, D)
    )

    chain = Chain(2)
    gate = slab_pieces[-1]

    def collect(weight):
        pieces = [lax.dynamic_index_in_dim(weight, own, 0, keepdims=False)] + [None] * (planes - 1)
        for step in shift_order(planes):
            part = lax.dynamic_index_in_dim(weight, (own + step) % share, 0, keepdims=False)
            pieces[step] = chain.send(after(part, gate), step)
        return place_rep(pieces)

    in_weight = collect(w_in)
    out_expert = collect(w_out)

    def by_sequence(value):
        return value.reshape(ranks, micro, rows, -1).transpose(1, 0, 2, 3).reshape(
            micro, length, -1
        )

    stream = by_sequence(stream_all).astype(f32)
    inverse = inverse_rms(stream)
    normed = (stream * inverse * first_gain).astype(bf16)
    proj = dot(normed.reshape(micro * length, D), qkv_weight).reshape(micro, length, 3 * width)
    segment = segments[0]
    cosine, sine = jax.vmap(lambda one: rope_tables(doc_positions(one), HD))(segment)
    sine = jnp.where(jnp.arange(HD) < HD // 2, -sine, sine)
    seg_column = segment[:, :, None]
    seg_row = segment[:, None, :]
    tables = (cosine, sine, seg_column, seg_row, qk_gains)
    mixed_h, query, keys, values, lses = attention_forward(proj, *tables)
    mixed = lax.all_to_all(
        mixed_h.reshape(micro, ranks, rows, width), "ep", split_axis=1, concat_axis=3, tiled=True
    ).reshape(mine, D)
    own_stream = tokens.astype(f32)
    hidden = own_stream + dot(mixed, out_weight)
    second_inverse = inverse_rms(hidden)
    normed_two = (hidden * second_inverse * second_gain).astype(bf16)
    logits = dot(normed_two, router_weight)
    routed = jnp.any(routes[:, :, None] == jnp.arange(experts, dtype=jnp.int32), axis=1)
    logits = jnp.where(routed, logits, -1e30)
    gates = jnp.where(routed, jnp.exp(logits - jnp.max(logits, axis=1, keepdims=True)), 0.0)
    gates = gates / jnp.sum(gates, axis=1, keepdims=True)
    high, low = two_parts(gates)
    payload = jnp.concatenate(
        [normed_two, high, low, jnp.zeros((mine, PAD - 2 * experts), bf16)], axis=1
    )
    payload = gather_ranks(with_group(payload)).reshape(ranks, block, D + PAD)
    upstream_all = gather_ranks(after(upstream_group, payload)).reshape(ranks, block, D)

    order = jnp.arange(block, dtype=jnp.int32)
    earlier = (order[:, None] < order[None, :]).astype(bf16)
    taken = lax.dynamic_index_in_dim(payload, D + expert, 2, keepdims=False) > 0
    slot = dot(taken.astype(bf16), earlier).astype(jnp.int32)
    slot = jnp.where(taken, slot, -1)
    select = (slot[:, None, :] == jnp.arange(slots, dtype=jnp.int32)[None, :, None]).astype(bf16)

    def pick(value):
        value = jnp.einsum("bst,btd->bsd", select, value, preferred_element_type=f32)
        return value.astype(bf16).reshape(ranks * slots, -1)

    rows_all = pick(payload)
    upstream_rows = pick(upstream_all).astype(f32)
    rows_in = rows_all[:, :D]
    gate_rows = lax.dynamic_slice_in_dim(rows_all, D + expert, 1, 1).astype(
        f32
    ) + lax.dynamic_slice_in_dim(rows_all, D + experts + expert, 1, 1).astype(f32)
    both = dot(rows_in, in_weight)
    gate_part = both[:, :FF]
    up_part = both[:, FF:]
    sigma = 1.0 / (1.0 + jnp.exp(-gate_part))
    silu_part = gate_part / (1.0 + jnp.exp(-gate_part))
    active = (silu_part * up_part).astype(bf16)
    grad_produced = (gate_rows * upstream_rows).astype(bf16)
    grad_out_expert = dot(active, grad_produced, ((0,), (0,)))
    produced = dot(active, out_expert).astype(bf16).astype(f32)
    grad_gate_rows = jnp.sum(upstream_rows * produced, axis=1, keepdims=True)
    weighted = (gate_rows * produced).astype(bf16)
    grad_active = dot(grad_produced, out_expert, ((1,), (1,))).astype(bf16)
    grad_gate = grad_active * up_part * (sigma + gate_part * sigma * (1.0 - sigma))
    grad_up = grad_active * silu_part
    grad_both = jnp.concatenate([grad_gate, grad_up], axis=1).astype(bf16)
    grad_rows_in = dot(grad_both, in_weight, ((1,), (1,))).astype(bf16)
    grad_in_expert = dot(rows_in, grad_both, ((0,), (0,)))
    high, low = two_parts(grad_gate_rows)
    columns = jnp.arange(PAD, dtype=jnp.int32)[None, :]
    zero = jnp.zeros((), bf16)
    extra = jnp.where(columns == expert, high, jnp.where(columns == experts + expert, low, zero))
    grad_rows_in = jnp.concatenate([grad_rows_in, extra], axis=1)

    select_parts = select.reshape(ranks, slots, share, micro, rows)

    def spread(step, value):
        value = jnp.einsum(
            "bskt,bsd->bktd",
            select_parts[:, :, :, step],
            value.reshape(ranks, slots, -1),
            preferred_element_type=f32,
        ).astype(bf16)
        return lax.psum_scatter(value, "ep", scatter_dimension=0)

    def join(parts):
        total = parts[0].astype(f32)
        for step in range(1, share):
            total = total + exchange(parts[step], share - step).astype(f32)
        return total

    chain = Chain(2)

    def scatter_rep(value):
        count = value.shape[0] // planes
        sums = [None] * share
        for step in [0] + shift_order(planes):
            part = lax.dynamic_slice_in_dim(value, (plane + step) % planes * count, count, 0)
            if step:
                part = chain.send(part.astype(bf16), step).astype(f32)
            sums[step % share] = part if sums[step % share] is None else sums[step % share] + part
        return jnp.stack(
            [
                sum(jnp.where((own - step) % share == j, sums[step], 0.0) for step in range(share))
                for j in range(share)
            ]
        )

    grad_w_out = scatter_rep(grad_out_expert)
    grad_w_in = scatter_rep(grad_in_expert)

    spread_back = [spread(step, grad_rows_in) for step in range(micro)]
    grad_inputs, branches = [], []
    router_sum = gain_two_sum = gain_one_sum = qk_sum = qkv_sum = 0.0
    for step in range(micro):
        at = slice(step * rows, (step + 1) * rows)
        upstream = cotangent[at].astype(f32)
        returned = join(spread_back[step])
        grad_gates = returned[:, D : D + experts] + returned[:, D + experts : D + 2 * experts]
        grad_logits = gates[at] * (
            grad_gates - jnp.sum(gates[at] * grad_gates, axis=1, keepdims=True)
        )
        grad_logits = grad_logits.astype(bf16)
        grad_normed_two = returned[:, :D] + dot(grad_logits, router_weight, ((1,), (1,)))
        router_sum = router_sum + dot(normed_two[at], grad_logits, ((0,), (0,)))
        gain_two_sum = gain_two_sum + jnp.sum(
            grad_normed_two * hidden[at] * second_inverse[at], axis=0
        )
        grad_hidden = upstream + rms_backward(
            hidden[at], second_inverse[at], second_gain, grad_normed_two
        )
        grad_branch = grad_hidden.astype(bf16)
        branches.append(grad_branch)
        grad_mixed = dot(grad_branch, out_weight, ((1,), (1,))).astype(bf16)
        grad_mixed_h = lax.all_to_all(grad_mixed, "ep", split_axis=1, concat_axis=0, tiled=True)
        one = slice(step, step + 1)
        grad_proj, grad_qk = attention_backward(
            proj[one],
            *(table[one] for table in tables[:4]),
            qk_gains,
            query[one], keys[one], values[one], lses[one], grad_mixed_h[None],
        )
        grad_proj = grad_proj[0]
        qk_sum = qk_sum + grad_qk.reshape(-1)
        qkv_sum = qkv_sum + dot(normed[step], grad_proj, ((0,), (0,)))
        grad_normed = dot(grad_proj, qkv_weight, ((1,), (1,)))
        gain_one_sum = gain_one_sum + jnp.sum(grad_normed * stream[step] * inverse[step], axis=0)
        grad_normed = lax.psum_scatter(
            grad_normed.astype(bf16), "ep", scatter_dimension=0, tiled=True
        ).astype(f32)
        own_inverse = inverse_rms(own_stream[at])
        grad_inputs.append(
            grad_hidden + rms_backward(own_stream[at], own_inverse, first_gain, grad_normed)
        )
    mixture = [join(spread(step, weighted)) for step in range(micro)]
    output = (hidden + jnp.concatenate(mixture, axis=0)).astype(bf16)
    out_sum = dot(mixed, jnp.concatenate(branches, axis=0), ((0,), (0,))).astype(bf16)
    out_sum = out_sum.reshape(planes, ranks, dense_rows, D).transpose(1, 0, 2, 3)
    out_sum = lax.psum_scatter(out_sum, "ep", scatter_dimension=0)
    grad_w_o = lax.dynamic_index_in_dim(out_sum, plane, 0, keepdims=False).astype(f32)
    for step in range(1, planes):
        part = lax.dynamic_index_in_dim(out_sum, (plane + step) % planes, 0, keepdims=False)
        grad_w_o = grad_w_o + shift_rep(part, step).astype(f32)

    qk_columns = qk_sum.shape[0] // dense_rows
    small = jnp.concatenate(
        [
            router_sum,
            jnp.concatenate([gain_one_sum, gain_two_sum]).reshape(D, 2),
            jnp.tile(qk_sum.reshape(dense_rows, qk_columns), (planes * ranks, 1)),
        ],
        axis=1,
    )
    count = small.shape[1]

    def pack(main, small):
        high, low = two_parts(small)
        blank = jnp.zeros((small.shape[0], PAD - 2 * count), bf16)
        return jnp.concatenate([main.astype(bf16), high, low, blank], axis=1)

    def unpack(packed):
        packed = packed.astype(f32)
        split = packed.shape[-1] - PAD
        tail = packed[..., split:]
        return packed[..., :split], tail[..., :count] + tail[..., count : 2 * count]

    packed = pack(qkv_sum, small)
    part_rows = D // planes
    main = lax.dynamic_slice_in_dim(qkv_sum, plane * part_rows, part_rows, 0)
    small = lax.dynamic_slice_in_dim(small, plane * part_rows, part_rows, 0)
    for step in range(1, planes):
        part = lax.dynamic_slice_in_dim(
            packed, (plane + step) % planes * part_rows, part_rows, 0
        )
        part_main, part_small = unpack(shift_rep(part, step))
        main, small = main + part_main, small + part_small
    packed = pack(main, small).reshape(ranks, dense_rows, -1)
    packed = lax.all_to_all(packed, "ep", split_axis=0, concat_axis=0, tiled=True)
    main, small = unpack(packed)
    grad_w_qkv = (
        main.reshape(ranks, dense_rows, 3, width).transpose(1, 2, 0, 3).reshape(dense_rows, 3 * D)
    )
    small = jnp.sum(small, axis=0)
    return (
        output,
        jnp.concatenate(grad_inputs, axis=0),
        grad_w_qkv,
        grad_w_o,
        small[:, :experts],
        small[:, experts : experts + 2].reshape(-1),
        small[:, experts + 2 :].reshape(-1),
        grad_w_in,
        grad_w_out,
    )


def solution(mesh):
    placed = (
        P(("rep", "ep"), None),
        P(("rep", "ep"), None),
        P(("rep", "ep"), None),
        P(("rep", "ep"), None),
        P(("rep", "ep"), None),
        P(("rep", "ep")),
        P(),
        P("ep", "rep", None),
        P("ep", "rep", None),
        P("rep", None, None),
        P(("rep", "ep"), None),
    )
    return jax.shard_map(
        on_device,
        mesh=mesh,
        in_specs=placed,
        out_specs=(
            P(("rep", "ep"), None),
            P(("rep", "ep"), None),
            P(("rep", "ep"), None),
            P(("rep", "ep"), None),
            P(("rep", "ep"), None),
            P(("rep", "ep")),
            P(),
            P("ep", "rep", None),
            P("ep", "rep", None),
        ),
        check_vma=False,
    )
```

```python
import math

import jax
import jax.numpy as jnp
from jax import lax
from jax.experimental import pallas as pl
from jax.experimental.pallas import tpu as pltpu
from jax.sharding import PartitionSpec as P

D = 2048
HEADS = 16
HD = 128
FF = 1024
TOP = 8
HALF = 512
PAD = 128

epsilon = 1e-06
rope_base = 50000.0
bf16 = jnp.bfloat16
f32 = jnp.float32


def dot(a, b, dims=((1,), (0,))):
    return lax.dot_general(a, b, (dims, ((), ())), preferred_element_type=f32)


def inverse_rms(value):
    return lax.rsqrt(jnp.mean(value * value, axis=-1, keepdims=True) + epsilon)


def rms_backward(value, inverse, gain, grad):
    scaled = grad * gain
    inner = jnp.mean(scaled * value, axis=-1, keepdims=True)
    return inverse * (scaled - value * (inverse * inverse * inner))


def doc_positions(segment):
    index = jnp.arange(segment.shape[0], dtype=jnp.int32)
    change = jnp.concatenate([jnp.ones((1,), dtype=jnp.bool_), segment[1:] != segment[:-1]])
    start = lax.cummax(jnp.where(change, index, 0), axis=0)
    return index - start


def rope_tables(position, width):
    steps = jnp.arange(width // 2, dtype=f32) * (2.0 / width)
    rates = jnp.exp(-steps * math.log(rope_base))
    angle = position.astype(f32)[:, None] * rates[None, :]
    angle = jnp.concatenate([angle, angle], axis=-1)
    return (jnp.cos(angle), jnp.sin(angle))


def norm_rope(value, gain, cosine, sine):
    inverse = lax.rsqrt(jnp.mean(value * value, axis=1, keepdims=True) + epsilon)
    value = value * inverse * gain
    return value * cosine + pltpu.roll(value, HD // 2, 1) * sine


def norm_rope_back(value, gain, cosine, sine, grad):
    inverse = lax.rsqrt(jnp.mean(value * value, axis=1, keepdims=True) + epsilon)
    grad = grad * cosine + pltpu.roll(grad * sine, HD // 2, 1)
    normal = value * inverse
    scaled = grad * gain
    inner = jnp.mean(scaled * normal, axis=1, keepdims=True)
    return inverse * (scaled - normal * inner), jnp.sum(grad * normal, axis=0, keepdims=True)


def kept_scores(query, keys, q_seg, k_seg, start):
    scores = dot(query, keys, ((1,), (1,))) * (1.0 / math.sqrt(HD))
    q_index = start + lax.broadcasted_iota(jnp.int32, scores.shape, 0)
    k_index = lax.broadcasted_iota(jnp.int32, scores.shape, 1)
    keep = (jnp.abs(q_index - k_index) <= HALF) & (q_seg == k_seg)
    return jnp.where(keep, scores, -1e30)


BIG = 100 * 1024 * 1024 // 2


def forward_kernel(
    heads, proj, cosine, sine, seg_column, seg_row, gains, mixed, query, keys, values, lses
):
    ranks, _, rows, _ = proj.shape
    length = ranks * rows
    q_block = 2 * rows
    k_seg = seg_row[0]
    for head in range(heads):
        at = slice(head * HD, (head + 1) * HD)

        def raw(part):
            first = (part * heads + head) * HD
            return proj[:, 0, :, first : first + HD].reshape(length, HD)

        query[0, :, at] = norm_rope(raw(0), gains[0:1], cosine[0], sine[0]).astype(bf16)
        keys[0, :, at] = norm_rope(raw(1), gains[1:2], cosine[0], sine[0]).astype(bf16)
        values[0, :, at] = raw(2).astype(bf16)

        @pl.loop(0, length // q_block)
        def one_block(number, head=head, at=at):
            start = pl.multiple_of(number * q_block, q_block)
            here = pl.ds(start, q_block)
            scores = kept_scores(
                query[0, here, at], keys[0, :, at], seg_column[0, here], k_seg, start
            )
            top = jnp.max(scores, axis=1, keepdims=True)
            weights = jnp.exp(scores - top)
            total = jnp.sum(weights, axis=1, keepdims=True)
            lses[0, head, here] = top + jnp.log(total)
            weights = (weights * (1.0 / total)).astype(bf16)
            result = dot(weights, values[0, :, at]).astype(bf16)
            mixed[pl.ds(number * 2, 2), 0, :, at] = result.reshape(2, rows, HD)


def backward_kernel(
    heads, proj, cosine, sine, seg_column, seg_row, gains, query, keys, values, lses, grad_mixed,
    grad_proj, grad_gains, grad_q, grad_k, grad_v,
):
    ranks, _, rows, _ = proj.shape
    length = ranks * rows
    q_block = 2 * rows
    k_seg = seg_row[0]
    scale = 1.0 / math.sqrt(HD)
    sum_q = jnp.zeros((1, HD), f32)
    sum_k = jnp.zeros((1, HD), f32)
    for head in range(heads):
        at = slice(head * HD, (head + 1) * HD)
        grad_k[...] = jnp.zeros_like(grad_k)
        grad_v[...] = jnp.zeros_like(grad_v)

        @pl.loop(0, length // q_block)
        def one_block(number, head=head, at=at):
            start = pl.multiple_of(number * q_block, q_block)
            here = pl.ds(start, q_block)
            q_rows = query[0, here, at]
            g_rows = grad_mixed[here, at]
            k_all = keys[0, :, at]
            scores = kept_scores(q_rows, k_all, seg_column[0, here], k_seg, start)
            weights = jnp.exp(scores - lses[0, head, here])
            grad_weights = dot(g_rows, values[0, :, at], ((1,), (1,)))
            delta = jnp.sum(weights * grad_weights, axis=1, keepdims=True)
            grad_scores = (weights * (grad_weights - delta)).astype(bf16)
            grad_q[here] = dot(grad_scores, k_all) * scale
            grad_k[...] += dot(grad_scores, q_rows, ((0,), (0,)))
            grad_v[...] += dot(weights.astype(bf16), g_rows, ((0,), (0,)))

        def rounded(value):
            return value.astype(bf16).astype(f32)

        def raw(part):
            first = (part * heads + head) * HD
            return proj[:, 0, :, first : first + HD].reshape(length, HD)

        def put(part, value):
            first = (part * heads + head) * HD
            grad_proj[:, :, first : first + HD] = value.astype(bf16).reshape(ranks, rows, HD)

        back_q, gain_q = norm_rope_back(
            raw(0), gains[0:1], cosine[0], sine[0], rounded(grad_q[...])
        )
        back_k, gain_k = norm_rope_back(
            raw(1), gains[1:2], cosine[0], sine[0], rounded(grad_k[...] * scale)
        )
        sum_q, sum_k = sum_q + gain_q, sum_k + gain_k
        put(0, back_q)
        put(1, back_k)
        put(2, grad_v[...])
    grad_gains[0:1] = sum_q
    grad_gains[1:2] = sum_k


def fixed(shape):
    return pl.BlockSpec(shape, lambda *_: (0,) * len(shape), pipeline_mode=pl.Buffered(1))


def leading(shape):
    return pl.BlockSpec((1,) + shape[1:], lambda i: (i,) + (0,) * (len(shape) - 1))


def params():
    return pltpu.CompilerParams(vmem_limit_bytes=BIG)


def out(shape, dtype=bf16):
    return jax.ShapeDtypeStruct(shape, dtype)


def attention_forward(proj, cosine, sine, seg_column, seg_row, gains):
    ranks, micro, rows, width = proj.shape
    length = ranks * rows
    width = width // 3
    heads = width // HD
    part = out((micro, length, width))
    by_rank = lambda n: pl.BlockSpec((ranks, 1, rows, n), lambda i: (0, i, 0, 0))
    lses = out((micro, heads, length, 1), f32)
    return pl.pallas_call(
        lambda *refs: forward_kernel(heads, *refs),
        grid=(micro,),
        in_specs=[by_rank(3 * width)]
        + [leading(v.shape) for v in (cosine, sine, seg_column, seg_row)]
        + [fixed(gains.shape)],
        out_specs=[by_rank(width)] + [leading(part.shape)] * 3 + [leading(lses.shape)],
        out_shape=[out((ranks, micro, rows, width)), part, part, part, lses],
        compiler_params=params(),
    )(proj, cosine, sine, seg_column, seg_row, gains)


def attention_backward(
    step, proj, cosine, sine, seg_column, seg_row, gains, query, keys, values, lses, grad_mixed
):
    ranks, micro, rows, width = proj.shape
    length = ranks * rows
    heads = width // 3 // HD

    def part(value):
        return pl.BlockSpec((1,) + value.shape[1:], lambda i: (step,) + (0,) * (value.ndim - 1))

    return pl.pallas_call(
        lambda *refs: backward_kernel(heads, *refs),
        grid=(1,),
        in_specs=[pl.BlockSpec((ranks, 1, rows, width), lambda i: (0, step, 0, 0))]
        + [part(v) for v in (cosine, sine, seg_column, seg_row)]
        + [fixed(gains.shape)]
        + [part(v) for v in (query, keys, values, lses)]
        + [fixed(grad_mixed.shape)],
        out_specs=[fixed((ranks, rows, width)), fixed((2, HD))],
        out_shape=[out((ranks, rows, width)), out((2, HD), f32)],
        scratch_shapes=[pltpu.VMEM((length, HD), f32)] * 3,
        compiler_params=params(),
    )(
        proj, cosine, sine, seg_column, seg_row, gains, query, keys, values, lses, grad_mixed
    )


def project(tokens, gain, slab):
    ranks, count, _ = tokens.shape
    width = slab.shape[1] - PAD

    def kernel(value, gain, weight, normed, proj):
        value = value[0].astype(f32)
        result = (value * inverse_rms(value) * gain[...]).astype(bf16)
        normed[0] = result
        proj[0] = dot(result, weight[:, :width])

    return pl.pallas_call(
        kernel,
        grid=(ranks,),
        in_specs=[leading(tokens.shape), fixed((1, D)), fixed(slab.shape)],
        out_specs=[leading((ranks, count, D)), leading((ranks, count, width))],
        out_shape=[out((ranks, count, D)), out((ranks, count, width), f32)],
        compiler_params=params(),
    )(tokens, gain, slab)


TILE = 256


def tiles(count):
    return pl.loop(0, count // TILE)


def tile(number):
    return pl.ds(pl.multiple_of(number * TILE, TILE), TILE)


def route(mixed, tokens, out_weight, gain, router, routes, experts):
    count = tokens.shape[0]

    def kernel(mixed, tokens, out_weight, gain, router, routes, hidden, payload, gates):
        @tiles(D)
        def _(number):
            at = tile(number)
            hidden[:, at] = tokens[:, at].astype(f32) + dot(mixed[...], out_weight[:, at])

        value = hidden[...]
        normed = (value * inverse_rms(value) * gain[...]).astype(bf16)
        payload[:, :D] = normed
        logits = dot(normed, router[...])
        column = lax.broadcasted_iota(jnp.int32, logits.shape, 1)
        routed = column == routes[:, 0:1]
        for choice in range(1, TOP):
            routed = routed | (column == routes[:, choice : choice + 1])
        logits = jnp.where(routed, logits, -1e30)
        weights = jnp.exp(logits - jnp.max(logits, axis=1, keepdims=True))
        weights = jnp.where(routed, weights, 0.0)
        weights = weights / jnp.sum(weights, axis=1, keepdims=True)
        gates[...] = weights
        high = weights.astype(bf16).astype(f32)
        payload[:, D:] = (high + pltpu.roll(weights - high, experts, 1)).astype(bf16)

    return pl.pallas_call(
        kernel,
        out_shape=[out((count, D), f32), out((count, D + PAD)), out((count, PAD), f32)],
        compiler_params=params(),
    )(mixed, tokens, out_weight, gain, router, routes)


def lane(value, number):
    column = lax.broadcasted_iota(jnp.int32, value.shape, 1)
    return jnp.sum(jnp.where(column == number, value.astype(f32), 0.0), axis=1, keepdims=True)


def expert_forward(expert, payload, upstream, in_weight, slots, experts):
    ranks, share, micro, rows, _ = payload.shape
    block = 2 * share * rows

    def kernel(
        expert, payload, upstream, in_weight, rows_in, tail, both, active, grad_produced,
        up_rows, places,
    ):
        number = expert[0]
        value = payload[...].reshape(block, D + PAD)
        marks = value[:, D:]
        first = lax.broadcasted_iota(jnp.int32, (8, PAD), 1) == number
        taken = dot(first.astype(bf16), marks, ((1,), (1,))) > 0.0
        before = lax.broadcasted_iota(jnp.int32, (block, block), 0)
        behind = lax.broadcasted_iota(jnp.int32, (block, block), 1)
        slot = dot(taken.astype(bf16), (before < behind).astype(bf16))
        slot = jnp.where(taken, slot, -1.0)[0:1]
        place = lax.broadcasted_iota(jnp.int32, (slots, block), 0).astype(f32)
        select = (place == slot).astype(bf16)
        taken = lane(marks, number) > 0.0
        wide = jnp.broadcast_to(taken, (block, PAD))
        slot = dot((before > behind).astype(bf16), wide.astype(bf16))
        places[0, 0] = jnp.where(wide, slot, -1.0)
        rows_in[0, 0] = dot(select, value[:, :D]).astype(bf16)
        marks = dot(select, marks)
        tail[0, 0] = marks
        gate = lane(marks, number) + lane(marks, experts + number)

        @tiles(D)
        def _(number):
            at = tile(number)
            picked = dot(select, upstream[:, :, 0, :, at].reshape(block, TILE))
            up_rows[0, 0, :, at] = picked.astype(bf16)
            grad_produced[0, 0, :, at] = (gate * picked).astype(bf16)

        @tiles(FF)
        def _(number):
            at = tile(number)
            more = pl.ds(pl.multiple_of(FF + number * TILE, TILE), TILE)
            gate_part = dot(rows_in[0, 0], in_weight[:, at])
            up_part = dot(rows_in[0, 0], in_weight[:, more])
            both[0, 0, :, at] = gate_part
            both[0, 0, :, more] = up_part
            active[0, 0, :, at] = (
                gate_part / (1.0 + jnp.exp(-gate_part)) * up_part
            ).astype(bf16)

    def tokens_spec(width):
        return pl.BlockSpec((2, share, 1, rows, width), lambda m, b, _: (b, 0, m, 0, 0))

    shapes = [
        out((micro, ranks // 2, slots, D)),
        out((micro, ranks // 2, slots, PAD), f32),
        out((micro, ranks // 2, slots, 2 * FF), f32),
        out((micro, ranks // 2, slots, FF)),
        out((micro, ranks // 2, slots, D)),
        out((micro, ranks // 2, slots, D)),
        out((micro, ranks // 2, block, PAD), f32),
    ]
    return pl.pallas_call(
        kernel,
        grid_spec=pltpu.PrefetchScalarGridSpec(
            num_scalar_prefetch=1,
            grid=(micro, ranks // 2),
            in_specs=[tokens_spec(D + PAD), tokens_spec(D), fixed(in_weight.shape)],
            out_specs=[
                pl.BlockSpec((1, 1) + s.shape[2:], lambda m, b, _: (m, b, 0, 0)) for s in shapes
            ],
        ),
        out_shape=shapes,
        compiler_params=params(),
    )(expert, payload, upstream, in_weight)


def expert_backward(
    step, expert, tail, both, active, grad_produced, up_rows, places, in_weight, out_weight,
    share, rows, experts,
):
    pairs, slots = tail.shape[1:3]
    block = places.shape[2]

    def kernel(
        expert, tail, both, active, grad_produced, up_rows, places, in_weight, out_weight,
        mixture, grad_tokens, grad_both,
    ):
        number = expert[0]
        gate = lane(tail[0, 0], number) + lane(tail[0, 0], experts + number)
        place = lax.broadcasted_iota(jnp.int32, (block, slots), 1).astype(f32)
        select = (places[0, 0][:, 0:1] == place).astype(bf16)
        shape = (2, share, rows)

        def produce(number, grad_gate):
            at = tile(number)
            produced = dot(active[0, 0], out_weight[:, at]).astype(bf16).astype(f32)
            weighted = (gate * produced).astype(bf16)
            mixture[:, :, :, at] = dot(select, weighted).astype(bf16).reshape(shape + (TILE,))
            return grad_gate + jnp.sum(
                up_rows[0, 0, :, at].astype(f32) * produced, axis=1, keepdims=True
            )

        grad_gate = lax.fori_loop(0, D // TILE, produce, jnp.zeros((slots, 1), f32))

        @tiles(FF)
        def _(number):
            at = tile(number)
            more = pl.ds(pl.multiple_of(FF + number * TILE, TILE), TILE)
            grad_active = dot(grad_produced[0, 0], out_weight[at, :], ((1,), (1,)))
            grad_active = grad_active.astype(bf16).astype(f32)
            gate_part = both[0, 0, :, at]
            up_part = both[0, 0, :, more]
            sigma = 1.0 / (1.0 + jnp.exp(-gate_part))
            grad_both[0, :, at] = (
                grad_active * up_part * (sigma * (1.0 + gate_part * (1.0 - sigma)))
            ).astype(bf16)
            grad_both[0, :, more] = (grad_active * (gate_part * sigma)).astype(bf16)

        @tiles(D)
        def _(number):
            at = tile(number)
            grad_rows = dot(grad_both[0], in_weight[at, :], ((1,), (1,))).astype(bf16)
            grad_tokens[:, :, :, at] = dot(select, grad_rows).astype(bf16).reshape(shape + (TILE,))

        high = grad_gate.astype(bf16).astype(f32)
        column = lax.broadcasted_iota(jnp.int32, (slots, PAD), 1)
        extra = jnp.where(column == number, high, 0.0)
        extra = jnp.where(column == experts + number, grad_gate - high, extra)
        grad_tokens[:, :, :, D:] = (
            dot(select, extra.astype(bf16)).astype(bf16).reshape(shape + (PAD,))
        )

    def part(value):
        return pl.BlockSpec((1, 1) + value.shape[2:], lambda b, _: (step, b, 0, 0))

    def tokens_spec(width):
        return pl.BlockSpec((2, share, rows, width), lambda b, _: (b, 0, 0, 0))

    return pl.pallas_call(
        kernel,
        grid_spec=pltpu.PrefetchScalarGridSpec(
            num_scalar_prefetch=1,
            grid=(pairs,),
            in_specs=[part(v) for v in (tail, both, active, grad_produced, up_rows, places)]
            + [fixed(in_weight.shape), fixed(out_weight.shape)],
            out_specs=[
                tokens_spec(D),
                tokens_spec(D + PAD),
                pl.BlockSpec((1, slots, 2 * FF), lambda b, _: (b, 0, 0)),
            ],
        ),
        out_shape=[
            out((2 * pairs, share, rows, D)),
            out((2 * pairs, share, rows, D + PAD)),
            out((pairs, slots, 2 * FF)),
        ],
        compiler_params=params(),
    )(
        expert, tail, both, active, grad_produced, up_rows, places, in_weight, out_weight
    )


def hidden_backward(parts, hidden, gates, upstream, gain, router, out_weight, experts):
    count = hidden.shape[0]
    terms = len(parts)

    def kernel(*refs):
        parts = refs[:terms]
        hidden, gates, upstream, gain, router, out_weight = refs[terms : terms + 6]
        grad_hidden, grad_branch, grad_mixed, grad_logits, grad_gain = refs[terms + 6 :]
        returned = sum(part[...].astype(f32) for part in parts)
        tail = returned[:, D:]
        grad_gates = gates[...] * (tail + pltpu.roll(tail, PAD - experts, 1))
        logits = grad_gates - gates[...] * jnp.sum(grad_gates, axis=1, keepdims=True)
        logits = logits.astype(bf16)
        grad_logits[...] = logits
        grad_normed = returned[:, :D] + dot(logits, router[...], ((1,), (1,)))
        value = hidden[...]
        inverse = inverse_rms(value)
        grad_gain[...] = jnp.sum(grad_normed * value * inverse, axis=0, keepdims=True)
        grad = upstream[...].astype(f32) + rms_backward(value, inverse, gain[...], grad_normed)
        grad_hidden[...] = grad
        grad_branch[...] = grad.astype(bf16)

        @tiles(D)
        def _(number):
            at = tile(number)
            grad_mixed[:, at] = dot(grad_branch[...], out_weight[at, :], ((1,), (1,))).astype(bf16)

    return pl.pallas_call(
        kernel,
        out_shape=[
            out((count, D), f32), out((count, D)), out((count, D)), out((count, PAD)),
            out((1, D), f32),
        ],
        compiler_params=params(),
    )(*parts, hidden, gates, upstream, gain, router, out_weight)


def project_backward(step, grad_proj, tokens, slab):
    ranks, micro, rows, _ = tokens.shape
    width = slab.shape[1] - PAD

    def kernel(grad_proj, tokens, weight, grad_normed, grad_gain):
        value = tokens[0, 0].astype(f32)
        inverse = inverse_rms(value)
        grad = dot(grad_proj[0], weight[:, :width], ((1,), (1,)))
        grad_normed[...] = grad.astype(bf16)

        @pl.when(pl.program_id(0) == 0)
        def _():
            grad_gain[...] = jnp.zeros_like(grad_gain)

        grad_gain[...] += jnp.sum(grad * value * inverse, axis=0, keepdims=True)

    return pl.pallas_call(
        kernel,
        grid=(ranks,),
        in_specs=[
            leading(grad_proj.shape),
            pl.BlockSpec((1, 1, rows, D), lambda i: (i, step, 0, 0)),
            fixed(slab.shape),
        ],
        out_specs=[pl.BlockSpec((rows, D), lambda i: (i, 0)), fixed((1, D))],
        out_shape=[out((ranks * rows, D)), out((1, D), f32)],
        compiler_params=params(),
    )(grad_proj, tokens, slab)


def shift_rep(value, step):
    count = lax.axis_size("rep")
    return lax.ppermute(value, "rep", [(i, (i + step) % count) for i in range(count)])


def after(value, *others):
    return lax.optimization_barrier((value,) + others)[0]


def two_parts(value):
    high = lax.reduce_precision(value, 8, 7)
    return high.astype(bf16), (value - high).astype(bf16)


def shift_order(count):
    return sorted(range(1, count), key=lambda step: (min(step, count - step), step))


def place_rep(pieces):
    count = len(pieces)
    rank = lax.axis_index("rep")
    rows = pieces[0].shape[0]
    full = jnp.zeros((count * rows,) + pieces[0].shape[1:], pieces[0].dtype)
    for step, piece in enumerate(pieces):
        full = lax.dynamic_update_slice_in_dim(full, piece, (rank - step) % count * rows, 0)
    return full


def on_device(
    tokens, cotangent, w_qkv, w_o, w_router, norm_gains, qk_gain, w_in, w_out, segments, routes
):
    planes = lax.axis_size("rep")
    ranks = lax.axis_size("ep")
    plane = lax.axis_index("rep")
    rank = lax.axis_index("ep")
    share = w_in.shape[0]
    own = plane % share
    experts = share * ranks
    expert = (rank * share + own).astype(jnp.int32).reshape(1)
    micro = segments.shape[1]
    mine = tokens.shape[0]
    rows = mine // micro
    length = rows * ranks
    capacity = rows * TOP * 17 // (16 * experts)
    slots = -(-2 * share * capacity // 16) * 16
    width = HEADS // ranks * HD
    qk_gains = qk_gain.astype(f32).reshape(2, HD)
    dense_rows = w_qkv.shape[0]

    def exchange(value, step):
        pairs = [(i, i // share * share + (i % share + step) % share) for i in range(planes)]
        return lax.ppermute(value, "rep", pairs)

    def with_group(value):
        return jnp.stack([value] + [exchange(value, step) for step in range(1, share)])

    def gather_ranks(value):
        return lax.all_gather(value, "ep", axis=0)

    stream = gather_ranks(tokens)
    slab = jnp.concatenate(
        [
            w_qkv.reshape(dense_rows, 3, ranks, width)
            .transpose(2, 0, 1, 3)
            .reshape(ranks, dense_rows, 3 * width),
            jnp.broadcast_to(
                jnp.concatenate(
                    [
                        w_router,
                        norm_gains.reshape(dense_rows, 2),
                        jnp.zeros((dense_rows, PAD - experts - 2), bf16),
                    ],
                    axis=1,
                )[None],
                (ranks, dense_rows, PAD),
            ),
        ],
        axis=2,
    )
    slab = lax.all_to_all(slab, "ep", split_axis=0, concat_axis=0, tiled=True)
    slab = slab.reshape(ranks * dense_rows, 3 * width + PAD)
    w_o, cotangent_late = after((w_o, cotangent), slab)
    out_pieces = [w_o] + [shift_rep(w_o, step) for step in range(1, planes)]
    slab_pieces = [slab] + [shift_rep(slab, step) for step in range(1, planes)]
    upstream_group = with_group(cotangent_late)
    slab = place_rep(slab_pieces)
    router = slab[:, 3 * width :]
    gain_pair = router[:, experts : experts + 2].reshape(-1).astype(f32)
    first_gain = gain_pair[None, :D]
    second_gain = gain_pair[None, D:]
    out_weight = gather_ranks(after(place_rep(out_pieces), stream))
    out_weight = (
        out_weight.reshape(ranks, planes, -1, D).transpose(1, 0, 2, 3).reshape(D, D)
    )
    upstream_all = gather_ranks(after(upstream_group, out_weight))

    def send_weight(weight, step):
        part = lax.dynamic_index_in_dim(weight, (own + step) % share, 0, keepdims=False)
        return shift_rep(part, step) if step else part

    order = shift_order(planes)
    early, late = after((w_in, (w_in, w_out)), slab)
    in_pieces = {0: send_weight(w_in, 0), order[0]: send_weight(early, order[0])}

    normed, proj = project(stream, first_gain, slab)
    proj = proj.reshape(ranks, micro, rows, 3 * width)
    segment = segments[0]
    cosine, sine = jax.vmap(lambda one: rope_tables(doc_positions(one), HD))(segment)
    sine = jnp.where(jnp.arange(HD) < HD // 2, -sine, sine)
    tables = (cosine, sine, segment[:, :, None], segment[:, None, :], qk_gains)
    mixed_h, query, keys, values, lses = attention_forward(proj, *tables)
    mixed_h, out_weight = lax.optimization_barrier((mixed_h, out_weight))
    mixed = lax.all_to_all(mixed_h, "ep", split_axis=0, concat_axis=3, tiled=True)
    mixed = mixed.reshape(mine, D)
    hidden, payload, gates = route(
        mixed, tokens, out_weight, second_gain, router, routes, experts
    )
    normed_two = payload[:, :D]
    (payload, in_pieces[order[0]]), late = after(
        ((payload, in_pieces[order[0]]), late), payload, in_pieces[order[0]]
    )
    payload = with_group(payload)
    payload, late = lax.optimization_barrier((payload, late))
    for step in order[1:]:
        in_pieces[step] = send_weight(late[0], step)
    out_parts = {step: send_weight(late[1], step) for step in [0] + order}
    in_weight = place_rep([in_pieces[step] for step in range(planes)])
    out_expert = place_rep([out_parts[step] for step in range(planes)])
    payload = gather_ranks(after(payload, upstream_all))

    shape = (ranks, share, micro, rows, -1)
    rows_in, tail, both, active, grad_produced, up_rows, places = expert_forward(
        expert, payload.reshape(shape), upstream_all.reshape(shape), in_weight, slots, experts
    )
    in_rows = micro * ranks // 2 * slots

    def flat(value):
        return value.reshape(in_rows, -1)

    grad_out_expert = dot(flat(active), flat(grad_produced), ((0,), (0,)))

    def by_expert(sums):
        return jnp.stack(
            [
                sum(jnp.where((own - step) % share == j, sums[step], 0.0) for step in range(share))
                for j in range(share)
            ]
        )

    def scatter_rep(value):
        count = value.shape[0] // planes
        sums = [None] * share
        for step in [0] + order:
            part = lax.dynamic_slice_in_dim(value, (plane + step) % planes * count, count, 0)
            if step:
                part = shift_rep(part.astype(bf16), step).astype(f32)
            sums[step % share] = part if sums[step % share] is None else sums[step % share] + part
        return by_expert(sums)

    grad_w_out = scatter_rep(grad_out_expert)
    back = [
        expert_backward(
            step, expert, tail, both, active, grad_produced, up_rows, places, in_weight,
            out_expert, share, rows, experts,
        )
        for step in range(micro)
    ]
    grad_in_expert = sum(
        dot(
            rows_in[step].reshape(in_rows // micro, D),
            back[step][2].reshape(in_rows // micro, 2 * FF),
            ((0,), (0,)),
        )
        for step in range(micro)
    )
    grad_w_in = scatter_rep(grad_in_expert)

    def scatter_ranks(value):
        value = lax.psum_scatter(value, "ep", scatter_dimension=0)
        return [value[0]] + [exchange(value[step], share - step) for step in range(1, share)]

    returned = [scatter_ranks(back[step][1]) for step in range(micro)]
    grad_inputs, branches, logit_grads = [], [], []
    gain_two_sum = gain_one_sum = qk_sum = qkv_sum = 0.0
    by_rank = stream.reshape(ranks, micro, rows, D)
    for step in range(micro):
        at = slice(step * rows, (step + 1) * rows)
        grad_hidden, grad_branch, grad_mixed, grad_logits, gain_two = hidden_backward(
            returned[step], hidden[at], gates[at], cotangent[at], second_gain, router, out_weight,
            experts,
        )
        branches.append(grad_branch)
        logit_grads.append(grad_logits)
        gain_two_sum = gain_two_sum + gain_two
        grad_mixed = lax.all_to_all(grad_mixed, "ep", split_axis=1, concat_axis=0, tiled=True)
        grad_proj, grad_qk = attention_backward(
            step, proj, *tables, query, keys, values, lses, grad_mixed
        )
        qk_sum = qk_sum + grad_qk.reshape(-1)
        grad_normed, gain_one = project_backward(step, grad_proj, by_rank, slab)
        gain_one_sum = gain_one_sum + gain_one
        qkv_sum = qkv_sum + dot(
            normed.reshape(ranks, micro, rows, D)[:, step].reshape(length, D),
            grad_proj.reshape(length, 3 * width),
            ((0,), (0,)),
        )
        grad_normed = lax.psum_scatter(
            grad_normed, "ep", scatter_dimension=0, tiled=True
        ).astype(f32)
        own_stream = tokens[at].astype(f32)
        own_inverse = inverse_rms(own_stream)
        grad_inputs.append(
            grad_hidden + rms_backward(own_stream, own_inverse, first_gain, grad_normed)
        )
    mixture = [
        sum(part.astype(f32) for part in scatter_ranks(back[step][0])) for step in range(micro)
    ]
    output = (hidden + jnp.concatenate(mixture, axis=0)).astype(bf16)
    out_sum = dot(mixed, jnp.concatenate(branches, axis=0), ((0,), (0,))).astype(bf16)
    out_sum = out_sum.reshape(planes, ranks, dense_rows, D).transpose(1, 0, 2, 3)
    out_sum = lax.psum_scatter(out_sum, "ep", scatter_dimension=0)
    grad_w_o = lax.dynamic_index_in_dim(out_sum, plane, 0, keepdims=False).astype(f32)
    for step in range(1, planes):
        part = lax.dynamic_index_in_dim(out_sum, (plane + step) % planes, 0, keepdims=False)
        grad_w_o = grad_w_o + shift_rep(part, step).astype(f32)

    router_sum = dot(normed_two, jnp.concatenate(logit_grads, axis=0), ((0,), (0,)))
    qk_columns = qk_sum.shape[0] // dense_rows
    small = jnp.concatenate(
        [
            router_sum[:, :experts],
            jnp.concatenate([gain_one_sum, gain_two_sum], axis=1).reshape(D, 2),
            jnp.tile(qk_sum.reshape(dense_rows, qk_columns), (planes * ranks, 1)),
        ],
        axis=1,
    )
    count = small.shape[1]

    def pack(main, small):
        high, low = two_parts(small)
        blank = jnp.zeros((small.shape[0], PAD - 2 * count), bf16)
        return jnp.concatenate([main.astype(bf16), high, low, blank], axis=1)

    def unpack(packed):
        packed = packed.astype(f32)
        split = packed.shape[-1] - PAD
        tail = packed[..., split:]
        return packed[..., :split], tail[..., :count] + tail[..., count : 2 * count]

    packed = pack(qkv_sum, small)
    part_rows = D // planes
    main = lax.dynamic_slice_in_dim(qkv_sum, plane * part_rows, part_rows, 0)
    small = lax.dynamic_slice_in_dim(small, plane * part_rows, part_rows, 0)
    for step in range(1, planes):
        part = lax.dynamic_slice_in_dim(
            packed, (plane + step) % planes * part_rows, part_rows, 0
        )
        part_main, part_small = unpack(shift_rep(part, step))
        main, small = main + part_main, small + part_small
    packed = pack(main, small).reshape(ranks, dense_rows, -1)
    packed = lax.all_to_all(packed, "ep", split_axis=0, concat_axis=0, tiled=True)
    main, small = unpack(packed)
    grad_w_qkv = (
        main.reshape(ranks, dense_rows, 3, width).transpose(1, 2, 0, 3).reshape(dense_rows, 3 * D)
    )
    small = jnp.sum(small, axis=0)
    return (
        output,
        jnp.concatenate(grad_inputs, axis=0),
        grad_w_qkv,
        grad_w_o,
        small[:, :experts],
        small[:, experts : experts + 2].reshape(-1),
        small[:, experts + 2 :].reshape(-1),
        grad_w_in,
        grad_w_out,
    )


def solution(mesh):
    placed = (
        P(("rep", "ep"), None),
        P(("rep", "ep"), None),
        P(("rep", "ep"), None),
        P(("rep", "ep"), None),
        P(("rep", "ep"), None),
        P(("rep", "ep")),
        P(),
        P("ep", "rep", None),
        P("ep", "rep", None),
        P("rep", None, None),
        P(("rep", "ep"), None),
    )
    return jax.shard_map(
        on_device,
        mesh=mesh,
        in_specs=placed,
        out_specs=(
            P(("rep", "ep"), None),
            P(("rep", "ep"), None),
            P(("rep", "ep"), None),
            P(("rep", "ep"), None),
            P(("rep", "ep"), None),
            P(("rep", "ep")),
            P(),
            P("ep", "rep", None),
            P("ep", "rep", None),
        ),
        check_vma=False,
    )
```

```python
import math

import jax
import jax.numpy as jnp
from jax import lax
from jax.experimental import pallas as pl
from jax.experimental.pallas import tpu as pltpu
from jax.sharding import PartitionSpec as P

D = 2048
HEADS = 16
HD = 128
FF = 1024
TOP = 8
HALF = 512
PAD = 128

epsilon = 1e-06
rope_base = 50000.0
bf16 = jnp.bfloat16
f32 = jnp.float32


def dot(a, b, dims=((1,), (0,))):
    return lax.dot_general(a, b, (dims, ((), ())), preferred_element_type=f32)


def inverse_rms(value):
    return lax.rsqrt(jnp.mean(value * value, axis=-1, keepdims=True) + epsilon)


def rms_backward(value, inverse, gain, grad):
    scaled = grad * gain
    inner = jnp.mean(scaled * value, axis=-1, keepdims=True)
    return inverse * (scaled - value * (inverse * inverse * inner))


def doc_positions(segment):
    index = jnp.arange(segment.shape[0], dtype=jnp.int32)
    change = jnp.concatenate([jnp.ones((1,), dtype=jnp.bool_), segment[1:] != segment[:-1]])
    start = lax.cummax(jnp.where(change, index, 0), axis=0)
    return index - start


def rope_tables(position, width):
    steps = jnp.arange(width // 2, dtype=f32) * (2.0 / width)
    rates = jnp.exp(-steps * math.log(rope_base))
    angle = position.astype(f32)[:, None] * rates[None, :]
    angle = jnp.concatenate([angle, angle], axis=-1)
    return (jnp.cos(angle), jnp.sin(angle))


def norm_rope(value, gain, cosine, sine):
    inverse = lax.rsqrt(jnp.mean(value * value, axis=1, keepdims=True) + epsilon)
    value = value * inverse * gain
    return value * cosine + pltpu.roll(value, HD // 2, 1) * sine


def norm_rope_back(value, gain, cosine, sine, grad):
    inverse = lax.rsqrt(jnp.mean(value * value, axis=1, keepdims=True) + epsilon)
    grad = grad * cosine + pltpu.roll(grad * sine, HD // 2, 1)
    normal = value * inverse
    scaled = grad * gain
    inner = jnp.mean(scaled * normal, axis=1, keepdims=True)
    return inverse * (scaled - normal * inner), jnp.sum(grad * normal, axis=0, keepdims=True)


def kept_scores(query, keys, q_seg, k_seg, start):
    scores = dot(query, keys, ((1,), (1,))) * (1.0 / math.sqrt(HD))
    q_index = start + lax.broadcasted_iota(jnp.int32, scores.shape, 0)
    k_index = lax.broadcasted_iota(jnp.int32, scores.shape, 1)
    keep = (jnp.abs(q_index - k_index) <= HALF) & (q_seg == k_seg)
    return jnp.where(keep, scores, -1e30)


BIG = 100 * 1024 * 1024 // 2


def forward_kernel(
    heads, proj, cosine, sine, seg_column, seg_row, gains, mixed, query, keys, values, lses
):
    ranks, _, rows, _ = proj.shape
    length = ranks * rows
    q_block = 2 * rows
    k_seg = seg_row[0]
    for head in range(heads):
        at = slice(head * HD, (head + 1) * HD)

        def raw(part):
            first = (part * heads + head) * HD
            return proj[:, 0, :, first : first + HD].reshape(length, HD)

        query[0, :, at] = norm_rope(raw(0), gains[0:1], cosine[0], sine[0]).astype(bf16)
        keys[0, :, at] = norm_rope(raw(1), gains[1:2], cosine[0], sine[0]).astype(bf16)
        values[0, :, at] = raw(2).astype(bf16)

        @pl.loop(0, length // q_block)
        def one_block(number, head=head, at=at):
            start = pl.multiple_of(number * q_block, q_block)
            here = pl.ds(start, q_block)
            scores = kept_scores(
                query[0, here, at], keys[0, :, at], seg_column[0, here], k_seg, start
            )
            top = jnp.max(scores, axis=1, keepdims=True)
            weights = jnp.exp(scores - top)
            total = jnp.sum(weights, axis=1, keepdims=True)
            lses[0, head, here] = top + jnp.log(total)
            weights = (weights * (1.0 / total)).astype(bf16)
            result = dot(weights, values[0, :, at]).astype(bf16)
            mixed[pl.ds(number * 2, 2), 0, :, at] = result.reshape(2, rows, HD)


def backward_kernel(
    heads, proj, cosine, sine, seg_column, seg_row, gains, query, keys, values, lses, grad_mixed,
    grad_proj, grad_gains, grad_q, grad_k, grad_v,
):
    ranks, _, rows, _ = proj.shape
    length = ranks * rows
    q_block = 2 * rows
    k_seg = seg_row[0]
    scale = 1.0 / math.sqrt(HD)
    sum_q = jnp.zeros((1, HD), f32)
    sum_k = jnp.zeros((1, HD), f32)
    for head in range(heads):
        at = slice(head * HD, (head + 1) * HD)
        grad_k[...] = jnp.zeros_like(grad_k)
        grad_v[...] = jnp.zeros_like(grad_v)

        @pl.loop(0, length // q_block)
        def one_block(number, head=head, at=at):
            start = pl.multiple_of(number * q_block, q_block)
            here = pl.ds(start, q_block)
            q_rows = query[0, here, at]
            g_rows = grad_mixed[here, at]
            k_all = keys[0, :, at]
            scores = kept_scores(q_rows, k_all, seg_column[0, here], k_seg, start)
            weights = jnp.exp(scores - lses[0, head, here])
            grad_weights = dot(g_rows, values[0, :, at], ((1,), (1,)))
            delta = jnp.sum(weights * grad_weights, axis=1, keepdims=True)
            grad_scores = (weights * (grad_weights - delta)).astype(bf16)
            grad_q[here] = dot(grad_scores, k_all) * scale
            grad_k[...] += dot(grad_scores, q_rows, ((0,), (0,)))
            grad_v[...] += dot(weights.astype(bf16), g_rows, ((0,), (0,)))

        def rounded(value):
            return value.astype(bf16).astype(f32)

        def raw(part):
            first = (part * heads + head) * HD
            return proj[:, 0, :, first : first + HD].reshape(length, HD)

        def put(part, value):
            first = (part * heads + head) * HD
            grad_proj[:, :, first : first + HD] = value.astype(bf16).reshape(ranks, rows, HD)

        back_q, gain_q = norm_rope_back(
            raw(0), gains[0:1], cosine[0], sine[0], rounded(grad_q[...])
        )
        back_k, gain_k = norm_rope_back(
            raw(1), gains[1:2], cosine[0], sine[0], rounded(grad_k[...] * scale)
        )
        sum_q, sum_k = sum_q + gain_q, sum_k + gain_k
        put(0, back_q)
        put(1, back_k)
        put(2, grad_v[...])
    grad_gains[0:1] = sum_q
    grad_gains[1:2] = sum_k


def fixed(shape):
    return pl.BlockSpec(shape, lambda *_: (0,) * len(shape), pipeline_mode=pl.Buffered(1))


def leading(shape):
    return pl.BlockSpec((1,) + shape[1:], lambda i: (i,) + (0,) * (len(shape) - 1))


def params():
    return pltpu.CompilerParams(vmem_limit_bytes=BIG)


def out(shape, dtype=bf16):
    return jax.ShapeDtypeStruct(shape, dtype)


def attention_forward(proj, cosine, sine, seg_column, seg_row, gains):
    ranks, micro, rows, width = proj.shape
    length = ranks * rows
    width = width // 3
    heads = width // HD
    part = out((micro, length, width))
    by_rank = lambda n: pl.BlockSpec((ranks, 1, rows, n), lambda i: (0, i, 0, 0))
    lses = out((micro, heads, length, 1), f32)
    return pl.pallas_call(
        lambda *refs: forward_kernel(heads, *refs),
        grid=(micro,),
        in_specs=[by_rank(3 * width)]
        + [leading(v.shape) for v in (cosine, sine, seg_column, seg_row)]
        + [fixed(gains.shape)],
        out_specs=[by_rank(width)] + [leading(part.shape)] * 3 + [leading(lses.shape)],
        out_shape=[out((ranks, micro, rows, width)), part, part, part, lses],
        compiler_params=params(),
    )(proj, cosine, sine, seg_column, seg_row, gains)


def attention_backward(
    step, proj, cosine, sine, seg_column, seg_row, gains, query, keys, values, lses, grad_mixed
):
    ranks, micro, rows, width = proj.shape
    length = ranks * rows
    heads = width // 3 // HD

    def part(value):
        return pl.BlockSpec((1,) + value.shape[1:], lambda i: (step,) + (0,) * (value.ndim - 1))

    return pl.pallas_call(
        lambda *refs: backward_kernel(heads, *refs),
        grid=(1,),
        in_specs=[pl.BlockSpec((ranks, 1, rows, width), lambda i: (0, step, 0, 0))]
        + [part(v) for v in (cosine, sine, seg_column, seg_row)]
        + [fixed(gains.shape)]
        + [part(v) for v in (query, keys, values, lses)]
        + [fixed(grad_mixed.shape)],
        out_specs=[fixed((ranks, rows, width)), fixed((2, HD))],
        out_shape=[out((ranks, rows, width)), out((2, HD), f32)],
        scratch_shapes=[pltpu.VMEM((length, HD), f32)] * 3,
        compiler_params=params(),
    )(
        proj, cosine, sine, seg_column, seg_row, gains, query, keys, values, lses, grad_mixed
    )


def project(tokens, gain, slab):
    ranks, count, _ = tokens.shape
    width = slab.shape[1] - PAD

    def kernel(value, gain, weight, normed, proj):
        value = value[0].astype(f32)
        result = (value * inverse_rms(value) * gain[...]).astype(bf16)
        normed[0] = result
        proj[0] = dot(result, weight[:, :width])

    return pl.pallas_call(
        kernel,
        grid=(ranks,),
        in_specs=[leading(tokens.shape), fixed((1, D)), fixed(slab.shape)],
        out_specs=[leading((ranks, count, D)), leading((ranks, count, width))],
        out_shape=[out((ranks, count, D)), out((ranks, count, width), f32)],
        compiler_params=params(),
    )(tokens, gain, slab)


TILE = 512


def tiles(count):
    return pl.loop(0, count // TILE)


def tile(number):
    return pl.ds(pl.multiple_of(number * TILE, TILE), TILE)


def route(mixed, tokens, out_weight, gain, router, routes, experts):
    count = tokens.shape[0]

    def kernel(mixed, tokens, out_weight, gain, router, routes, hidden, payload, gates):
        @tiles(D)
        def _(number):
            at = tile(number)
            hidden[:, at] = tokens[:, at].astype(f32) + dot(mixed[...], out_weight[:, at])

        value = hidden[...]
        normed = (value * inverse_rms(value) * gain[...]).astype(bf16)
        payload[:, :D] = normed
        logits = dot(normed, router[...])
        column = lax.broadcasted_iota(jnp.int32, logits.shape, 1)
        routed = column == routes[:, 0:1]
        for choice in range(1, TOP):
            routed = routed | (column == routes[:, choice : choice + 1])
        logits = jnp.where(routed, logits, -1e30)
        weights = jnp.exp(logits - jnp.max(logits, axis=1, keepdims=True))
        weights = jnp.where(routed, weights, 0.0)
        weights = weights / jnp.sum(weights, axis=1, keepdims=True)
        gates[...] = weights
        high = weights.astype(bf16).astype(f32)
        payload[:, D:] = (high + pltpu.roll(weights - high, experts, 1)).astype(bf16)

    return pl.pallas_call(
        kernel,
        out_shape=[out((count, D), f32), out((count, D + PAD)), out((count, PAD), f32)],
        compiler_params=params(),
    )(mixed, tokens, out_weight, gain, router, routes)


def lane(value, number):
    column = lax.broadcasted_iota(jnp.int32, value.shape, 1)
    return jnp.sum(jnp.where(column == number, value.astype(f32), 0.0), axis=1, keepdims=True)


def one_hot(slot, slots):
    place = lax.broadcasted_iota(jnp.int32, (slots, slot.shape[1]), 0).astype(f32)
    return (place == slot).astype(bf16)


def expert_forward(expert, payload, upstream, in_weight, slots, experts):
    ranks, share, micro, rows, _ = payload.shape
    count = share * rows
    block = 2 * slots

    def kernel(
        expert, payload, upstream, in_weight, rows_in, tail, both, active, grad_produced,
        up_rows, places,
    ):
        number = expert[0]
        for part in range(2):
            here = slice(part * slots, (part + 1) * slots)
            value = payload[part].reshape(count, D + PAD)
            marks = value[:, D:]
            first = lax.broadcasted_iota(jnp.int32, (8, PAD), 1) == number
            taken = dot(first.astype(bf16), marks, ((1,), (1,))) > 0.0
            before = lax.broadcasted_iota(jnp.int32, (count, count), 0)
            behind = lax.broadcasted_iota(jnp.int32, (count, count), 1)
            slot = dot(taken.astype(bf16), (before < behind).astype(bf16))
            select = one_hot(jnp.where(taken, slot, -1.0)[0:1], slots)
            wide = jnp.broadcast_to(lane(marks, number) > 0.0, (count, PAD))
            slot = dot((before > behind).astype(bf16), wide.astype(bf16))
            places[0, 0, part] = jnp.where(wide, slot, -1.0)
            rows_in[0, 0, here] = dot(select, value[:, :D]).astype(bf16)
            marks = dot(select, marks)
            tail[0, 0, here] = marks
            gate = lane(marks, number) + lane(marks, experts + number)
            picked = dot(select, upstream[part].reshape(count, D))
            up_rows[0, 0, here] = picked.astype(bf16)
            grad_produced[0, 0, here] = (gate * picked).astype(bf16)

        for number in range(FF // TILE):
            at = slice(number * TILE, (number + 1) * TILE)
            more = slice(FF + number * TILE, FF + (number + 1) * TILE)
            gate_part = dot(rows_in[0, 0], in_weight[:, at])
            up_part = dot(rows_in[0, 0], in_weight[:, more])
            both[0, 0, :, at] = gate_part
            both[0, 0, :, more] = up_part
            active[0, 0, :, at] = (
                gate_part / (1.0 + jnp.exp(-gate_part)) * up_part
            ).astype(bf16)

    def tokens_spec(width):
        return pl.BlockSpec((2, share, 1, rows, width), lambda m, b, _: (b, 0, m, 0, 0))

    pairs = ranks // 2
    shapes = [
        out((micro, pairs, block, D)),
        out((micro, pairs, block, PAD), f32),
        out((micro, pairs, block, 2 * FF), f32),
        out((micro, pairs, block, FF)),
        out((micro, pairs, block, D)),
        out((micro, pairs, block, D)),
        out((micro, pairs, 2, count, PAD), f32),
    ]
    return pl.pallas_call(
        kernel,
        grid_spec=pltpu.PrefetchScalarGridSpec(
            num_scalar_prefetch=1,
            grid=(micro, pairs),
            in_specs=[tokens_spec(D + PAD), tokens_spec(D), fixed(in_weight.shape)],
            out_specs=[
                pl.BlockSpec(
                    (1, 1) + s.shape[2:], lambda m, b, _, n=len(s.shape): (m, b) + (0,) * (n - 2)
                )
                for s in shapes
            ],
        ),
        out_shape=shapes,
        compiler_params=params(),
    )(expert, payload, upstream, in_weight)


def expert_backward(
    step, expert, tail, both, active, grad_produced, up_rows, places, in_weight, out_weight,
    share, rows, experts,
):
    pairs, block = tail.shape[1:3]
    slots = block // 2
    count = places.shape[3]

    def kernel(
        expert, tail, both, active, grad_produced, up_rows, places, in_weight, out_weight,
        mixture, grad_tokens, grad_both,
    ):
        number = expert[0]
        gate = lane(tail[0, 0], number) + lane(tail[0, 0], experts + number)
        place = lax.broadcasted_iota(jnp.int32, (count, slots), 1).astype(f32)
        selects = [(places[0, 0, part][:, 0:1] == place).astype(bf16) for part in range(2)]

        def spread(target, at, value):
            for part in range(2):
                result = dot(selects[part], value[part * slots : (part + 1) * slots])
                target[part, :, :, at] = result.astype(bf16).reshape(share, rows, -1)

        grad_gate = jnp.zeros((block, 1), f32)
        for tile in range(D // TILE):
            at = slice(tile * TILE, (tile + 1) * TILE)
            produced = dot(active[0, 0], out_weight[:, at]).astype(bf16).astype(f32)
            spread(mixture, at, (gate * produced).astype(bf16))
            grad_gate = grad_gate + jnp.sum(
                up_rows[0, 0, :, at].astype(f32) * produced, axis=1, keepdims=True
            )

        for tile in range(FF // TILE):
            at = slice(tile * TILE, (tile + 1) * TILE)
            more = slice(FF + tile * TILE, FF + (tile + 1) * TILE)
            grad_active = dot(grad_produced[0, 0], out_weight[at, :], ((1,), (1,)))
            grad_active = grad_active.astype(bf16).astype(f32)
            gate_part = both[0, 0, :, at]
            up_part = both[0, 0, :, more]
            sigma = 1.0 / (1.0 + jnp.exp(-gate_part))
            grad_both[0, :, at] = (
                grad_active * up_part * (sigma * (1.0 + gate_part * (1.0 - sigma)))
            ).astype(bf16)
            grad_both[0, :, more] = (grad_active * (gate_part * sigma)).astype(bf16)

        for tile in range(D // TILE):
            at = slice(tile * TILE, (tile + 1) * TILE)
            grad_rows = dot(grad_both[0], in_weight[at, :], ((1,), (1,))).astype(bf16)
            spread(grad_tokens, at, grad_rows)

        high = grad_gate.astype(bf16).astype(f32)
        column = lax.broadcasted_iota(jnp.int32, (block, PAD), 1)
        extra = jnp.where(column == number, high, 0.0)
        extra = jnp.where(column == experts + number, grad_gate - high, extra)
        spread(grad_tokens, slice(D, D + PAD), extra.astype(bf16))

    def part(value):
        return pl.BlockSpec(
            (1, 1) + value.shape[2:], lambda b, _: (step, b) + (0,) * (value.ndim - 2)
        )

    def tokens_spec(width):
        return pl.BlockSpec((2, share, rows, width), lambda b, _: (b, 0, 0, 0))

    return pl.pallas_call(
        kernel,
        grid_spec=pltpu.PrefetchScalarGridSpec(
            num_scalar_prefetch=1,
            grid=(pairs,),
            in_specs=[part(v) for v in (tail, both, active, grad_produced, up_rows, places)]
            + [fixed(in_weight.shape), fixed(out_weight.shape)],
            out_specs=[
                tokens_spec(D),
                tokens_spec(D + PAD),
                pl.BlockSpec((1, block, 2 * FF), lambda b, _: (b, 0, 0)),
            ],
        ),
        out_shape=[
            out((2 * pairs, share, rows, D)),
            out((2 * pairs, share, rows, D + PAD)),
            out((pairs, block, 2 * FF)),
        ],
        compiler_params=params(),
    )(
        expert, tail, both, active, grad_produced, up_rows, places, in_weight, out_weight
    )


def hidden_backward(parts, hidden, gates, upstream, gain, router, out_weight, experts):
    count = hidden.shape[0]
    terms = len(parts)

    def kernel(*refs):
        parts = refs[:terms]
        hidden, gates, upstream, gain, router, out_weight = refs[terms : terms + 6]
        grad_hidden, grad_branch, grad_mixed, grad_logits, grad_gain = refs[terms + 6 :]
        returned = sum(part[...].astype(f32) for part in parts)
        tail = returned[:, D:]
        grad_gates = gates[...] * (tail + pltpu.roll(tail, PAD - experts, 1))
        logits = grad_gates - gates[...] * jnp.sum(grad_gates, axis=1, keepdims=True)
        logits = logits.astype(bf16)
        grad_logits[...] = logits
        grad_normed = returned[:, :D] + dot(logits, router[...], ((1,), (1,)))
        value = hidden[...]
        inverse = inverse_rms(value)
        grad_gain[...] = jnp.sum(grad_normed * value * inverse, axis=0, keepdims=True)
        grad = upstream[...].astype(f32) + rms_backward(value, inverse, gain[...], grad_normed)
        grad_hidden[...] = grad
        grad_branch[...] = grad.astype(bf16)

        @tiles(D)
        def _(number):
            at = tile(number)
            grad_mixed[:, at] = dot(grad_branch[...], out_weight[at, :], ((1,), (1,))).astype(bf16)

    return pl.pallas_call(
        kernel,
        out_shape=[
            out((count, D), f32), out((count, D)), out((count, D)), out((count, PAD)),
            out((1, D), f32),
        ],
        compiler_params=params(),
    )(*parts, hidden, gates, upstream, gain, router, out_weight)


def project_backward(step, grad_proj, tokens, slab):
    ranks, micro, rows, _ = tokens.shape
    width = slab.shape[1] - PAD

    def kernel(grad_proj, tokens, weight, grad_normed, grad_gain):
        value = tokens[0, 0].astype(f32)
        inverse = inverse_rms(value)
        grad = dot(grad_proj[0], weight[:, :width], ((1,), (1,)))
        grad_normed[...] = grad.astype(bf16)

        @pl.when(pl.program_id(0) == 0)
        def _():
            grad_gain[...] = jnp.zeros_like(grad_gain)

        grad_gain[...] += jnp.sum(grad * value * inverse, axis=0, keepdims=True)

    return pl.pallas_call(
        kernel,
        grid=(ranks,),
        in_specs=[
            leading(grad_proj.shape),
            pl.BlockSpec((1, 1, rows, D), lambda i: (i, step, 0, 0)),
            fixed(slab.shape),
        ],
        out_specs=[pl.BlockSpec((rows, D), lambda i: (i, 0)), fixed((1, D))],
        out_shape=[out((ranks * rows, D)), out((1, D), f32)],
        compiler_params=params(),
    )(grad_proj, tokens, slab)


def shift_rep(value, step):
    count = lax.axis_size("rep")
    return lax.ppermute(value, "rep", [(i, (i + step) % count) for i in range(count)])


def after(value, *others):
    return lax.optimization_barrier((value,) + others)[0]


def two_parts(value):
    high = lax.reduce_precision(value, 8, 7)
    return high.astype(bf16), (value - high).astype(bf16)


def shift_order(count):
    return sorted(range(1, count), key=lambda step: (min(step, count - step), step))


def place_rep(pieces):
    count = len(pieces)
    rank = lax.axis_index("rep")
    rows = pieces[0].shape[0]
    full = jnp.zeros((count * rows,) + pieces[0].shape[1:], pieces[0].dtype)
    for step, piece in enumerate(pieces):
        full = lax.dynamic_update_slice_in_dim(full, piece, (rank - step) % count * rows, 0)
    return full


def on_device(
    tokens, cotangent, w_qkv, w_o, w_router, norm_gains, qk_gain, w_in, w_out, segments, routes
):
    planes = lax.axis_size("rep")
    ranks = lax.axis_size("ep")
    plane = lax.axis_index("rep")
    rank = lax.axis_index("ep")
    share = w_in.shape[0]
    own = plane % share
    experts = share * ranks
    expert = (rank * share + own).astype(jnp.int32).reshape(1)
    micro = segments.shape[1]
    mine = tokens.shape[0]
    rows = mine // micro
    length = rows * ranks
    capacity = rows * TOP * 17 // (16 * experts)
    slots = -(-share * capacity // 16) * 16
    width = HEADS // ranks * HD
    qk_gains = qk_gain.astype(f32).reshape(2, HD)
    dense_rows = w_qkv.shape[0]

    def exchange(value, step):
        pairs = [(i, i // share * share + (i % share + step) % share) for i in range(planes)]
        return lax.ppermute(value, "rep", pairs)

    def with_group(value):
        return jnp.stack([value] + [exchange(value, step) for step in range(1, share)])

    def gather_ranks(value):
        return lax.all_gather(value, "ep", axis=0)

    stream = gather_ranks(tokens)
    out_pieces = [w_o] + [shift_rep(w_o, step) for step in range(1, planes)]
    upstream_group = with_group(cotangent)
    slab = jnp.concatenate(
        [
            w_qkv.reshape(dense_rows, 3, ranks, width)
            .transpose(2, 0, 1, 3)
            .reshape(ranks, dense_rows, 3 * width),
            jnp.broadcast_to(
                jnp.concatenate(
                    [
                        w_router,
                        norm_gains.reshape(dense_rows, 2),
                        jnp.zeros((dense_rows, PAD - experts - 2), bf16),
                    ],
                    axis=1,
                )[None],
                (ranks, dense_rows, PAD),
            ),
        ],
        axis=2,
    )
    slab = lax.all_to_all(slab, "ep", split_axis=0, concat_axis=0, tiled=True)
    slab = slab.reshape(ranks * dense_rows, 3 * width + PAD)
    out_pieces, slab = lax.optimization_barrier((out_pieces, slab))
    slab_pieces = [slab] + [shift_rep(slab, step) for step in range(1, planes)]
    slab = place_rep(slab_pieces)
    router = slab[:, 3 * width :]
    gain_pair = router[:, experts : experts + 2].reshape(-1).astype(f32)
    first_gain = gain_pair[None, :D]
    second_gain = gain_pair[None, D:]
    out_weight = gather_ranks(place_rep(out_pieces))
    out_weight = (
        out_weight.reshape(ranks, planes, -1, D).transpose(1, 0, 2, 3).reshape(D, D)
    )

    def send_weight(weight, step):
        part = lax.dynamic_index_in_dim(weight, (own + step) % share, 0, keepdims=False)
        return shift_rep(part, step) if step else part

    order = shift_order(planes)
    early = after((w_in, w_out), slab)
    in_pieces = {step: send_weight(early[0], step) for step in [0] + order[:1]}
    out_parts = {step: send_weight(early[1], step) for step in [0] + order[:1]}

    normed, proj = project(stream, first_gain, slab)
    proj = proj.reshape(ranks, micro, rows, 3 * width)
    upstream_all = gather_ranks(after(upstream_group, proj))
    segment = segments[0]
    cosine, sine = jax.vmap(lambda one: rope_tables(doc_positions(one), HD))(segment)
    sine = jnp.where(jnp.arange(HD) < HD // 2, -sine, sine)
    tables = (cosine, sine, segment[:, :, None], segment[:, None, :], qk_gains)
    mixed_h, query, keys, values, lses = attention_forward(proj, *tables)
    mixed_h, out_weight = lax.optimization_barrier((mixed_h, out_weight))
    mixed = lax.all_to_all(mixed_h, "ep", split_axis=0, concat_axis=3, tiled=True)
    mixed = mixed.reshape(mine, D)
    hidden, payload, gates = route(
        mixed, tokens, out_weight, second_gain, router, routes, experts
    )
    normed_two = payload[:, :D]
    payload, in_pieces, out_parts = lax.optimization_barrier((payload, in_pieces, out_parts))
    payload = with_group(payload)
    payload, late = lax.optimization_barrier((payload, (w_in, w_out)))
    for step in order[1:]:
        in_pieces[step] = send_weight(late[0], step)
    for step in order[1:]:
        out_parts[step] = send_weight(late[1], step)
    in_weight = place_rep([in_pieces[step] for step in range(planes)])
    payload = gather_ranks(payload)

    shape = (ranks, share, micro, rows, -1)
    rows_in, tail, both, active, grad_produced, up_rows, places = expert_forward(
        expert, payload.reshape(shape), upstream_all.reshape(shape), in_weight, slots, experts
    )
    in_rows = micro * ranks * slots

    def flat(value):
        return value.reshape(in_rows, -1)

    grad_out_expert = dot(flat(active), flat(grad_produced), ((0,), (0,)))

    def cut_rep(value):
        count = value.shape[0] // planes
        parts = {}
        for step in [0] + order:
            part = lax.dynamic_slice_in_dim(value, (plane + step) % planes * count, count, 0)
            parts[step] = part.astype(bf16) if step else part
        return parts

    def sum_rep(parts):
        sums = [None] * share
        for step in [0] + order:
            part = parts[step].astype(f32)
            sums[step % share] = part if sums[step % share] is None else sums[step % share] + part
        return jnp.stack(
            [
                sum(jnp.where((own - step) % share == j, sums[step], 0.0) for step in range(share))
                for j in range(share)
            ]
        )

    def send(parts, steps):
        return {step: shift_rep(parts[step], step) for step in steps}

    out_cut = cut_rep(grad_out_expert)
    out_expert = place_rep([out_parts[step] for step in range(planes)])
    out_expert, out_cut = lax.optimization_barrier((out_expert, out_cut))
    out_sent = send(out_cut, order)
    back = []
    returned = []

    def scatter_ranks(value):
        return lax.psum_scatter(value, "ep", scatter_dimension=0)

    def exchange_back(value):
        return [value[0]] + [exchange(value[step], share - step) for step in range(1, share)]

    for step in range(micro):
        back.append(
            expert_backward(
                step, expert, tail, both, active, grad_produced, up_rows, places, in_weight,
                out_expert, share, rows, experts,
            )
        )
        returned.append(scatter_ranks(back[step][1]))
        out_expert = after(out_expert, back[step][1])
    short = {step: out_sent[step] for step in order[:2]}
    rows_in, out_expert, short = lax.optimization_barrier((rows_in, out_expert, short))
    out_sent.update(short)
    grad_in_expert = sum(
        dot(
            rows_in[step].reshape(in_rows // micro, D),
            back[step][2].reshape(in_rows // micro, 2 * FF),
            ((0,), (0,)),
        )
        for step in range(micro)
    )
    in_cut = cut_rep(grad_in_expert)
    in_sent = {}

    def swap(value, step):
        return lax.ppermute(value, "ep", [(i, i ^ step) for i in range(ranks)])

    def pair_sum(value):
        halves = value.reshape((ranks // 2, 2) + value.shape[1:])
        keep = lax.dynamic_index_in_dim(halves, rank % 2, 1, keepdims=False)
        give = lax.dynamic_index_in_dim(halves, 1 - rank % 2, 1, keepdims=False)
        return (keep.astype(f32) + swap(give, 1).astype(f32)).astype(bf16)

    def cross(value):
        parts = []
        for step in range(ranks // 2):
            part = lax.dynamic_index_in_dim(value, rank // 2 ^ step, 0, keepdims=False)
            parts.append(swap(part, 2 * step) if step else part)
        return parts

    def total(parts):
        return sum(part.astype(f32) for part in parts)

    grad_inputs, branches, logit_grads = [], [], []
    gain_two_sum = gain_one_sum = qk_sum = qkv_sum = 0.0
    by_rank = stream.reshape(ranks, micro, rows, D)
    in_cut, mixtures = lax.optimization_barrier((in_cut, [part[0] for part in back]))
    mixtures = [pair_sum(part) for part in mixtures]
    crossed = []
    releases = [order[:1]] + [[]] * (micro - 2) + [order[1:]] if micro > 1 else [order]
    for step in range(micro):
        at = slice(step * rows, (step + 1) * rows)
        parts, out_sent, in_sent, mixtures = lax.optimization_barrier(
            (returned[step], out_sent, in_sent, mixtures)
        )
        parts = exchange_back(parts)
        parts, in_cut = lax.optimization_barrier((parts, in_cut))
        in_sent.update(send(in_cut, releases[step]))
        grad_hidden, grad_branch, grad_mixed, grad_logits, gain_two = hidden_backward(
            parts, hidden[at], gates[at], cotangent[at], second_gain, router, out_weight, experts
        )
        branches.append(grad_branch)
        logit_grads.append(grad_logits)
        gain_two_sum = gain_two_sum + gain_two
        grad_mixed = lax.all_to_all(grad_mixed, "ep", split_axis=1, concat_axis=0, tiled=True)
        if step == micro - 1:
            crossed = [cross(part) for part in after(mixtures[:1], parts)]
            grad_mixed, crossed, mixtures = lax.optimization_barrier(
                (grad_mixed, crossed, mixtures)
            )
            crossed += [cross(part) for part in mixtures[1:]]
        grad_proj, grad_qk = attention_backward(
            step, proj, *tables, query, keys, values, lses, grad_mixed
        )
        qk_sum = qk_sum + grad_qk.reshape(-1)
        grad_normed, gain_one = project_backward(step, grad_proj, by_rank, slab)
        gain_one_sum = gain_one_sum + gain_one
        grad_inputs.append(
            (at, grad_hidden, lax.psum_scatter(grad_normed, "ep", scatter_dimension=0, tiled=True))
        )
        grad_proj = after(grad_proj, grad_normed)
        qkv_sum = qkv_sum + dot(
            normed.reshape(ranks, micro, rows, D)[:, step].reshape(length, D),
            grad_proj.reshape(length, 3 * width),
            ((0,), (0,)),
        )
    grad_w_out = sum_rep({0: out_cut[0], **out_sent})
    grad_w_in = sum_rep({0: in_cut[0], **in_sent})

    router_sum = dot(normed_two, jnp.concatenate(logit_grads, axis=0), ((0,), (0,)))
    qk_columns = qk_sum.shape[0] // dense_rows
    small = jnp.concatenate(
        [
            router_sum[:, :experts],
            jnp.concatenate([gain_one_sum, gain_two_sum], axis=1).reshape(D, 2),
            jnp.tile(qk_sum.reshape(dense_rows, qk_columns), (planes * ranks, 1)),
        ],
        axis=1,
    )
    count = small.shape[1]

    def pack(main, small):
        high, low = two_parts(small)
        blank = jnp.zeros((small.shape[0], PAD - 2 * count), bf16)
        return jnp.concatenate([main.astype(bf16), high, low, blank], axis=1)

    def unpack(packed):
        packed = packed.astype(f32)
        split = packed.shape[-1] - PAD
        tail = packed[..., split:]
        return packed[..., :split], tail[..., :count] + tail[..., count : 2 * count]

    packed, crossed, branches = lax.optimization_barrier(
        (pack(qkv_sum, small), crossed, branches)
    )
    part_rows = D // planes
    main = lax.dynamic_slice_in_dim(qkv_sum, plane * part_rows, part_rows, 0)
    small = lax.dynamic_slice_in_dim(small, plane * part_rows, part_rows, 0)
    packed_sent = [
        shift_rep(
            lax.dynamic_slice_in_dim(packed, (plane + step) % planes * part_rows, part_rows, 0),
            step,
        )
        for step in range(1, planes)
    ]
    out_sum = dot(mixed, jnp.concatenate(branches, axis=0), ((0,), (0,))).astype(bf16)
    out_sum = out_sum.reshape(planes, ranks, dense_rows, D).transpose(1, 0, 2, 3)
    out_crossed = cross(pair_sum(out_sum))
    mixture = []
    for parts in crossed:
        parts = total(parts)
        mixture.append(parts[0] + total(exchange_back(parts.astype(bf16))[1:]))
    output = (hidden + jnp.concatenate(mixture, axis=0)).astype(bf16)
    grad_tokens = []
    for at, grad_hidden, grad_normed in grad_inputs:
        own_stream = tokens[at].astype(f32)
        grad_tokens.append(
            grad_hidden
            + rms_backward(
                own_stream, inverse_rms(own_stream), first_gain, grad_normed.astype(f32)
            )
        )
    for part in packed_sent:
        part_main, part_small = unpack(part)
        main, small = main + part_main, small + part_small
    packed = pack(main, small).reshape(ranks, dense_rows, -1)
    packed = lax.all_to_all(packed, "ep", split_axis=0, concat_axis=0, tiled=True)
    main, small = unpack(packed)
    grad_w_qkv = (
        main.reshape(ranks, dense_rows, 3, width).transpose(1, 2, 0, 3).reshape(dense_rows, 3 * D)
    )
    small = jnp.sum(small, axis=0)
    out_sum = total(out_crossed)
    grad_w_o = lax.dynamic_index_in_dim(out_sum, plane, 0, keepdims=False)
    out_sum = out_sum.astype(bf16)
    for step in range(1, planes):
        part = lax.dynamic_index_in_dim(out_sum, (plane + step) % planes, 0, keepdims=False)
        grad_w_o = grad_w_o + shift_rep(part, step).astype(f32)
    return (
        output,
        jnp.concatenate(grad_tokens, axis=0),
        grad_w_qkv,
        grad_w_o,
        small[:, :experts],
        small[:, experts : experts + 2].reshape(-1),
        small[:, experts + 2 :].reshape(-1),
        grad_w_in,
        grad_w_out,
    )


def solution(mesh):
    placed = (
        P(("rep", "ep"), None),
        P(("rep", "ep"), None),
        P(("rep", "ep"), None),
        P(("rep", "ep"), None),
        P(("rep", "ep"), None),
        P(("rep", "ep")),
        P(),
        P("ep", "rep", None),
        P("ep", "rep", None),
        P("rep", None, None),
        P(("rep", "ep"), None),
    )
    return jax.shard_map(
        on_device,
        mesh=mesh,
        in_specs=placed,
        out_specs=(
            P(("rep", "ep"), None),
            P(("rep", "ep"), None),
            P(("rep", "ep"), None),
            P(("rep", "ep"), None),
            P(("rep", "ep"), None),
            P(("rep", "ep")),
            P(),
            P("ep", "rep", None),
            P("ep", "rep", None),
        ),
        check_vma=False,
    )
```

```python
import math

import jax
import jax.numpy as jnp
from jax import lax
from jax.experimental import pallas as pl
from jax.experimental.pallas import tpu as pltpu
from jax.sharding import PartitionSpec as P

D = 2048
HEADS = 16
HD = 128
FF = 1024
TOP = 8
HALF = 512
PAD = 128

epsilon = 1e-06
rope_base = 50000.0
bf16 = jnp.bfloat16
f32 = jnp.float32


def dot(a, b, dims=((1,), (0,))):
    return lax.dot_general(a, b, (dims, ((), ())), preferred_element_type=f32)


def inverse_rms(value):
    return lax.rsqrt(jnp.mean(value * value, axis=-1, keepdims=True) + epsilon)


def rms_backward(value, inverse, gain, grad):
    scaled = grad * gain
    inner = jnp.mean(scaled * value, axis=-1, keepdims=True)
    return inverse * (scaled - value * (inverse * inverse * inner))


def doc_positions(segment):
    index = jnp.arange(segment.shape[0], dtype=jnp.int32)
    change = jnp.concatenate([jnp.ones((1,), dtype=jnp.bool_), segment[1:] != segment[:-1]])
    start = lax.cummax(jnp.where(change, index, 0), axis=0)
    return index - start


def rope_tables(position, width):
    steps = jnp.arange(width // 2, dtype=f32) * (2.0 / width)
    rates = jnp.exp(-steps * math.log(rope_base))
    angle = position.astype(f32)[:, None] * rates[None, :]
    angle = jnp.concatenate([angle, angle], axis=-1)
    return (jnp.cos(angle), jnp.sin(angle))


def norm_rope(value, gain, cosine, sine):
    inverse = lax.rsqrt(jnp.mean(value * value, axis=1, keepdims=True) + epsilon)
    value = value * inverse * gain
    return value * cosine + pltpu.roll(value, HD // 2, 1) * sine


def norm_rope_back(value, gain, cosine, sine, grad):
    inverse = lax.rsqrt(jnp.mean(value * value, axis=1, keepdims=True) + epsilon)
    grad = grad * cosine + pltpu.roll(grad * sine, HD // 2, 1)
    normal = value * inverse
    scaled = grad * gain
    inner = jnp.mean(scaled * normal, axis=1, keepdims=True)
    return inverse * (scaled - normal * inner), jnp.sum(grad * normal, axis=0, keepdims=True)


def kept_scores(query, keys, q_seg, k_seg, start):
    scores = dot(query, keys, ((1,), (1,))) * (1.0 / math.sqrt(HD))
    q_index = start + lax.broadcasted_iota(jnp.int32, scores.shape, 0)
    k_index = lax.broadcasted_iota(jnp.int32, scores.shape, 1)
    keep = (jnp.abs(q_index - k_index) <= HALF) & (q_seg == k_seg)
    return jnp.where(keep, scores, -1e30)


BIG = 100 * 1024 * 1024 // 2


def forward_kernel(
    heads, proj, cosine, sine, seg_column, seg_row, gains, mixed, query, keys, values, lses
):
    ranks, _, rows, _ = proj.shape
    length = ranks * rows
    q_block = 2 * rows
    k_seg = seg_row[0]
    for head in range(heads):
        at = slice(head * HD, (head + 1) * HD)

        def raw(part):
            first = (part * heads + head) * HD
            return proj[:, 0, :, first : first + HD].reshape(length, HD)

        query[0, :, at] = norm_rope(raw(0), gains[0:1], cosine[0], sine[0]).astype(bf16)
        keys[0, :, at] = norm_rope(raw(1), gains[1:2], cosine[0], sine[0]).astype(bf16)
        values[0, :, at] = raw(2).astype(bf16)

        @pl.loop(0, length // q_block)
        def one_block(number, head=head, at=at):
            start = pl.multiple_of(number * q_block, q_block)
            here = pl.ds(start, q_block)
            scores = kept_scores(
                query[0, here, at], keys[0, :, at], seg_column[0, here], k_seg, start
            )
            top = jnp.max(scores, axis=1, keepdims=True)
            weights = jnp.exp(scores - top)
            total = jnp.sum(weights, axis=1, keepdims=True)
            lses[0, head, here] = top + jnp.log(total)
            weights = (weights * (1.0 / total)).astype(bf16)
            result = dot(weights, values[0, :, at]).astype(bf16)
            mixed[pl.ds(number * 2, 2), 0, :, at] = result.reshape(2, rows, HD)


def backward_kernel(
    heads, proj, cosine, sine, seg_column, seg_row, gains, query, keys, values, lses, grad_mixed,
    grad_proj, grad_gains, grad_q, grad_k, grad_v,
):
    ranks, _, rows, _ = proj.shape
    length = ranks * rows
    q_block = 2 * rows
    k_seg = seg_row[0]
    scale = 1.0 / math.sqrt(HD)
    sum_q = jnp.zeros((1, HD), f32)
    sum_k = jnp.zeros((1, HD), f32)
    for head in range(heads):
        at = slice(head * HD, (head + 1) * HD)
        grad_k[...] = jnp.zeros_like(grad_k)
        grad_v[...] = jnp.zeros_like(grad_v)

        @pl.loop(0, length // q_block)
        def one_block(number, head=head, at=at):
            start = pl.multiple_of(number * q_block, q_block)
            here = pl.ds(start, q_block)
            q_rows = query[0, here, at]
            g_rows = grad_mixed[here, at]
            k_all = keys[0, :, at]
            scores = kept_scores(q_rows, k_all, seg_column[0, here], k_seg, start)
            weights = jnp.exp(scores - lses[0, head, here])
            grad_weights = dot(g_rows, values[0, :, at], ((1,), (1,)))
            delta = jnp.sum(weights * grad_weights, axis=1, keepdims=True)
            grad_scores = (weights * (grad_weights - delta)).astype(bf16)
            grad_q[here] = dot(grad_scores, k_all) * scale
            grad_k[...] += dot(grad_scores, q_rows, ((0,), (0,)))
            grad_v[...] += dot(weights.astype(bf16), g_rows, ((0,), (0,)))

        def rounded(value):
            return value.astype(bf16).astype(f32)

        def raw(part):
            first = (part * heads + head) * HD
            return proj[:, 0, :, first : first + HD].reshape(length, HD)

        def put(part, value):
            first = (part * heads + head) * HD
            grad_proj[:, :, first : first + HD] = value.astype(bf16).reshape(ranks, rows, HD)

        back_q, gain_q = norm_rope_back(
            raw(0), gains[0:1], cosine[0], sine[0], rounded(grad_q[...])
        )
        back_k, gain_k = norm_rope_back(
            raw(1), gains[1:2], cosine[0], sine[0], rounded(grad_k[...] * scale)
        )
        sum_q, sum_k = sum_q + gain_q, sum_k + gain_k
        put(0, back_q)
        put(1, back_k)
        put(2, grad_v[...])
    grad_gains[0:1] = sum_q
    grad_gains[1:2] = sum_k


def fixed(shape):
    return pl.BlockSpec(shape, lambda *_: (0,) * len(shape), pipeline_mode=pl.Buffered(1))


def leading(shape):
    return pl.BlockSpec((1,) + shape[1:], lambda i: (i,) + (0,) * (len(shape) - 1))


def params():
    return pltpu.CompilerParams(vmem_limit_bytes=BIG)


def cost(products):
    return pl.CostEstimate(flops=2 * products, bytes_accessed=0, transcendentals=0)


def out(shape, dtype=bf16):
    return jax.ShapeDtypeStruct(shape, dtype)


def attention_forward(proj, cosine, sine, seg_column, seg_row, gains):
    ranks, micro, rows, width = proj.shape
    length = ranks * rows
    width = width // 3
    heads = width // HD
    part = out((micro, length, width))
    by_rank = lambda n: pl.BlockSpec((ranks, 1, rows, n), lambda i: (0, i, 0, 0))
    lses = out((micro, heads, length, 1), f32)
    return pl.pallas_call(
        lambda *refs: forward_kernel(heads, *refs),
        grid=(micro,),
        in_specs=[by_rank(3 * width)]
        + [leading(v.shape) for v in (cosine, sine, seg_column, seg_row)]
        + [fixed(gains.shape)],
        out_specs=[by_rank(width)] + [leading(part.shape)] * 3 + [leading(lses.shape)],
        out_shape=[out((ranks, micro, rows, width)), part, part, part, lses],
        compiler_params=params(),
    )(proj, cosine, sine, seg_column, seg_row, gains)


def attention_backward(
    step, proj, cosine, sine, seg_column, seg_row, gains, query, keys, values, lses, grad_mixed
):
    ranks, micro, rows, width = proj.shape
    length = ranks * rows
    heads = width // 3 // HD

    def part(value):
        return pl.BlockSpec((1,) + value.shape[1:], lambda i: (step,) + (0,) * (value.ndim - 1))

    return pl.pallas_call(
        lambda *refs: backward_kernel(heads, *refs),
        grid=(1,),
        in_specs=[pl.BlockSpec((ranks, 1, rows, width), lambda i: (0, step, 0, 0))]
        + [part(v) for v in (cosine, sine, seg_column, seg_row)]
        + [fixed(gains.shape)]
        + [part(v) for v in (query, keys, values, lses)]
        + [fixed(grad_mixed.shape)],
        out_specs=[fixed((ranks, rows, width)), fixed((2, HD))],
        out_shape=[out((ranks, rows, width)), out((2, HD), f32)],
        scratch_shapes=[pltpu.VMEM((length, HD), f32)] * 3,
        compiler_params=params(),
    )(
        proj, cosine, sine, seg_column, seg_row, gains, query, keys, values, lses, grad_mixed
    )


def project(count, tokens, gain, slab):
    ranks = tokens.shape[0]
    width = slab.shape[1] - PAD

    def kernel(value, gain, weight, normed, proj):
        value = value[0].astype(f32)
        result = (value * inverse_rms(value) * gain[...]).astype(bf16)
        normed[0] = result
        proj[0] = dot(result, weight[:, :width])

    return pl.pallas_call(
        kernel,
        grid=(ranks,),
        in_specs=[leading((ranks, count, D)), fixed((1, D)), fixed(slab.shape)],
        out_specs=[leading((ranks, count, D)), leading((ranks, count, width))],
        out_shape=[out((ranks, count, D)), out((ranks, count, width), f32)],
        compiler_params=params(),
    )(tokens, gain, slab)


TILE = 512


def tiles(count):
    return pl.loop(0, count // TILE)


def tile(number):
    return pl.ds(pl.multiple_of(number * TILE, TILE), TILE)


HBM = pl.BlockSpec(memory_space=pl.ANY)


def copies(pairs, sems):
    started = [
        pltpu.make_async_copy(source, target, sems.at[place])
        for place, (source, target) in enumerate(pairs)
    ]
    for copy in started:
        copy.start()

    def wait():
        for copy in started:
            copy.wait()

    return wait


def plane_pairs(plane, pieces, target):
    planes = len(pieces)
    rows = target.shape[0] // planes
    return [
        (piece, target.at[pl.ds((plane + planes - step) % planes * rows, rows)])
        for step, piece in enumerate(pieces)
    ]


def out_weight_pairs(plane, planes, count, gathered, target):
    ranks = gathered.shape[0]
    rows = D // (planes * ranks)
    return [
        (
            gathered.at[rank, pl.ds(count + step * rows, rows)],
            target.at[pl.ds(((plane + planes - step) % planes * ranks + rank) * rows, rows)],
        )
        for rank in range(ranks)
        for step in range(planes)
    ]


def route(plane, planes, mixed, tokens, gathered, gain, router, routes, experts):
    count = tokens.shape[0]
    pieces = planes * gathered.shape[0]

    def kernel(
        plane, mixed, tokens, gathered, gain, router, routes, hidden, payload, gates,
        out_weight, sems,
    ):
        copies(out_weight_pairs(plane[0], planes, count, gathered, out_weight), sems)()

        @tiles(D)
        def _(number):
            at = tile(number)
            hidden[:, at] = tokens[:, at].astype(f32) + dot(mixed[...], out_weight[:, at])

        value = hidden[...]
        normed = (value * inverse_rms(value) * gain[...]).astype(bf16)
        payload[:, :D] = normed
        logits = dot(normed, router[...])
        column = lax.broadcasted_iota(jnp.int32, logits.shape, 1)
        routed = column == routes[:, 0:1]
        for choice in range(1, TOP):
            routed = routed | (column == routes[:, choice : choice + 1])
        logits = jnp.where(routed, logits, -1e30)
        weights = jnp.exp(logits - jnp.max(logits, axis=1, keepdims=True))
        weights = jnp.where(routed, weights, 0.0)
        weights = weights / jnp.sum(weights, axis=1, keepdims=True)
        gates[...] = weights
        high = weights.astype(bf16).astype(f32)
        payload[:, D:] = (high + pltpu.roll(weights - high, experts, 1)).astype(bf16)

    shapes = [out((count, D), f32), out((count, D + PAD)), out((count, PAD), f32)]
    return pl.pallas_call(
        kernel,
        grid_spec=pltpu.PrefetchScalarGridSpec(
            num_scalar_prefetch=1,
            grid=(1,),
            in_specs=[
                HBM if value is gathered else fixed(value.shape)
                for value in (mixed, tokens, gathered, gain, router, routes)
            ],
            out_specs=[fixed(shape.shape) for shape in shapes],
            scratch_shapes=[pltpu.VMEM((D, D), bf16), pltpu.SemaphoreType.DMA((pieces,))],
        ),
        out_shape=shapes,
        compiler_params=params(),
    )(plane, mixed, tokens, gathered, gain, router, routes)


def lane(value, number):
    column = lax.broadcasted_iota(jnp.int32, value.shape, 1)
    return jnp.sum(jnp.where(column == number, value.astype(f32), 0.0), axis=1, keepdims=True)


def one_hot(slot, slots):
    place = lax.broadcasted_iota(jnp.int32, (slots, slot.shape[1]), 0).astype(f32)
    return (place == slot).astype(bf16)


def expert_forward(where, payload, upstream, in_pieces, slots, experts):
    ranks, share, micro, rows, _ = payload.shape
    count = share * rows
    block = 2 * slots

    planes = len(in_pieces)

    def kernel(where, payload, upstream, *refs):
        (
            rows_in, tail, both, active, grad_produced, up_rows, places, in_weight, sems
        ) = refs[planes:]
        number = where[0]

        @pl.when((pl.program_id(0) == 0) & (pl.program_id(1) == 0))
        def _():
            copies(plane_pairs(where[1], refs[:planes], in_weight), sems)()

        for part in range(2):
            here = slice(part * slots, (part + 1) * slots)
            value = payload[part].reshape(count, D + PAD)
            marks = value[:, D:]
            first = lax.broadcasted_iota(jnp.int32, (8, PAD), 1) == number
            taken = dot(first.astype(bf16), marks, ((1,), (1,))) > 0.0
            before = lax.broadcasted_iota(jnp.int32, (count, count), 0)
            behind = lax.broadcasted_iota(jnp.int32, (count, count), 1)
            slot = dot(taken.astype(bf16), (before < behind).astype(bf16))
            select = one_hot(jnp.where(taken, slot, -1.0)[0:1], slots)
            wide = jnp.broadcast_to(lane(marks, number) > 0.0, (count, PAD))
            slot = dot((before > behind).astype(bf16), wide.astype(bf16))
            places[0, 0, part] = jnp.where(wide, slot, -1.0)
            rows_in[0, 0, here] = dot(select, value[:, :D]).astype(bf16)
            marks = dot(select, marks)
            tail[0, 0, here] = marks
            gate = lane(marks, number) + lane(marks, experts + number)
            picked = dot(select, upstream[part].reshape(count, D))
            up_rows[0, 0, here] = picked.astype(bf16)
            grad_produced[0, 0, here] = (gate * picked).astype(bf16)

        for number in range(FF // TILE):
            at = slice(number * TILE, (number + 1) * TILE)
            more = slice(FF + number * TILE, FF + (number + 1) * TILE)
            gate_part = dot(rows_in[0, 0], in_weight[:, at])
            up_part = dot(rows_in[0, 0], in_weight[:, more])
            both[0, 0, :, at] = gate_part
            both[0, 0, :, more] = up_part
            active[0, 0, :, at] = (
                gate_part / (1.0 + jnp.exp(-gate_part)) * up_part
            ).astype(bf16)

    def tokens_spec(width):
        return pl.BlockSpec((2, share, 1, rows, width), lambda m, b, _: (b, 0, m, 0, 0))

    pairs = ranks // 2
    shapes = [
        out((micro, pairs, block, D)),
        out((micro, pairs, block, PAD), f32),
        out((micro, pairs, block, 2 * FF), f32),
        out((micro, pairs, block, FF)),
        out((micro, pairs, block, D)),
        out((micro, pairs, block, D)),
        out((micro, pairs, 2, count, PAD), f32),
    ]
    return pl.pallas_call(
        kernel,
        grid_spec=pltpu.PrefetchScalarGridSpec(
            num_scalar_prefetch=1,
            grid=(micro, pairs),
            in_specs=[tokens_spec(D + PAD), tokens_spec(D)] + [HBM] * planes,
            out_specs=[
                pl.BlockSpec(
                    (1, 1) + s.shape[2:], lambda m, b, _, n=len(s.shape): (m, b) + (0,) * (n - 2)
                )
                for s in shapes
            ],
            scratch_shapes=[pltpu.VMEM((D, 2 * FF), bf16), pltpu.SemaphoreType.DMA((planes,))],
        ),
        out_shape=shapes,
        cost_estimate=cost(micro * pairs * block * D * (2 * FF + 2 * count)),
        compiler_params=params(),
    )(where, payload, upstream, *in_pieces)


def expert_backward(
    step, where, tail, both, active, grad_produced, up_rows, places, in_pieces, out_pieces,
    share, rows, experts,
):
    pairs, block = tail.shape[1:3]
    slots = block // 2
    count = places.shape[3]

    planes = len(in_pieces)

    def kernel(where, tail, both, active, grad_produced, up_rows, places, *refs):
        keep, give, grad_tokens, grad_both, in_weight, out_weight, sems = refs[2 * planes :]
        number = where[0]
        odd = where[2] == 1

        @pl.when(pl.program_id(0) == 0)
        def _():
            copies(
                plane_pairs(where[1], refs[:planes], in_weight)
                + plane_pairs(where[1], refs[planes : 2 * planes], out_weight),
                sems,
            )()

        gate = lane(tail[0, 0], number) + lane(tail[0, 0], experts + number)
        place = lax.broadcasted_iota(jnp.int32, (count, slots), 1).astype(f32)
        selects = [(places[0, 0, part][:, 0:1] == place).astype(bf16) for part in range(2)]

        def spread(value):
            return [
                dot(selects[part], value[part * slots : (part + 1) * slots])
                .astype(bf16)
                .reshape(share, rows, -1)
                for part in range(2)
            ]

        grad_gate = jnp.zeros((block, 1), f32)
        for tile in range(D // TILE):
            at = slice(tile * TILE, (tile + 1) * TILE)
            produced = dot(active[0, 0], out_weight[:, at]).astype(bf16).astype(f32)
            even_rank, odd_rank = spread((gate * produced).astype(bf16))
            keep[0, :, :, at] = jnp.where(odd, odd_rank, even_rank)
            give[0, :, :, at] = jnp.where(odd, even_rank, odd_rank)
            grad_gate = grad_gate + jnp.sum(
                up_rows[0, 0, :, at].astype(f32) * produced, axis=1, keepdims=True
            )

        for tile in range(FF // TILE):
            at = slice(tile * TILE, (tile + 1) * TILE)
            more = slice(FF + tile * TILE, FF + (tile + 1) * TILE)
            grad_active = dot(grad_produced[0, 0], out_weight[at, :], ((1,), (1,)))
            grad_active = grad_active.astype(bf16).astype(f32)
            gate_part = both[0, 0, :, at]
            up_part = both[0, 0, :, more]
            sigma = 1.0 / (1.0 + jnp.exp(-gate_part))
            grad_both[0, :, at] = (
                grad_active * up_part * (sigma * (1.0 + gate_part * (1.0 - sigma)))
            ).astype(bf16)
            grad_both[0, :, more] = (grad_active * (gate_part * sigma)).astype(bf16)

        for tile in range(D // TILE):
            at = slice(tile * TILE, (tile + 1) * TILE)
            grad_rows = dot(grad_both[0], in_weight[at, :], ((1,), (1,))).astype(bf16)
            grad_tokens[0, :, :, at], grad_tokens[1, :, :, at] = spread(grad_rows)

        high = grad_gate.astype(bf16).astype(f32)
        column = lax.broadcasted_iota(jnp.int32, (block, PAD), 1)
        extra = jnp.where(column == number, high, 0.0)
        extra = jnp.where(column == experts + number, grad_gate - high, extra)
        grad_tokens[0, :, :, D:], grad_tokens[1, :, :, D:] = spread(extra.astype(bf16))

    def part(value):
        return pl.BlockSpec(
            (1, 1) + value.shape[2:], lambda b, _: (step, b) + (0,) * (value.ndim - 2)
        )

    def tokens_spec(count, width):
        return pl.BlockSpec((count, share, rows, width), lambda b, _: (b, 0, 0, 0))

    return pl.pallas_call(
        kernel,
        grid_spec=pltpu.PrefetchScalarGridSpec(
            num_scalar_prefetch=1,
            grid=(pairs,),
            in_specs=[part(v) for v in (tail, both, active, grad_produced, up_rows, places)]
            + [HBM] * (2 * planes),
            out_specs=[
                tokens_spec(1, D),
                tokens_spec(1, D),
                tokens_spec(2, D + PAD),
                pl.BlockSpec((1, block, 2 * FF), lambda b, _: (b, 0, 0)),
            ],
            scratch_shapes=[
                pltpu.VMEM((D, 2 * FF), bf16),
                pltpu.VMEM((FF, D), bf16),
                pltpu.SemaphoreType.DMA((2 * planes,)),
            ],
        ),
        out_shape=[
            out((pairs, share, rows, D)),
            out((pairs, share, rows, D)),
            out((2 * pairs, share, rows, D + PAD)),
            out((pairs, block, 2 * FF)),
        ],
        cost_estimate=cost(pairs * block * D * (4 * FF + 2 * count)),
        compiler_params=params(),
    )(
        where, tail, both, active, grad_produced, up_rows, places, *in_pieces, *out_pieces
    )


def weight_gradient(where, planes, left, rights):
    count, width = left.shape
    parts = len(rights)
    part_rows = count // parts
    columns = rights[0].shape[1]
    width = width // planes

    def kernel(where, left, *refs):
        rights, target = refs[:parts], refs[parts]
        for number in range(columns // TILE):
            at = slice(number * TILE, (number + 1) * TILE)
            target[0, :, at] = sum(
                dot(left[part * part_rows : (part + 1) * part_rows], right[:, at], ((0,), (0,)))
                for part, right in enumerate(rights)
            ).astype(bf16)

    return pl.pallas_call(
        kernel,
        grid_spec=pltpu.PrefetchScalarGridSpec(
            num_scalar_prefetch=1,
            grid=(planes,),
            in_specs=[
                pl.BlockSpec((count, width), lambda i, where: (0, (where[1] + i) % planes))
            ]
            + [fixed(right.shape) for right in rights],
            out_specs=pl.BlockSpec((1, width, columns), lambda i, _: (i, 0, 0)),
        ),
        out_shape=out((planes, width, columns)),
        cost_estimate=cost(count * planes * width * columns),
        compiler_params=params(),
    )(where, left, *rights)


def hidden_backward(
    plane, planes, own_rows, parts, hidden, gates, upstream, gain, router, gathered, experts
):
    count = hidden.shape[0]
    terms = len(parts)

    def kernel(plane, *refs):
        parts = refs[:terms]
        hidden, gates, upstream, gain, router, gathered = refs[terms : terms + 6]
        (
            grad_hidden, grad_branch, grad_mixed, grad_logits, grad_gain, out_weight, sems
        ) = refs[terms + 6 :]
        wait = copies(out_weight_pairs(plane[0], planes, own_rows, gathered, out_weight), sems)
        returned = sum(part[...].astype(f32) for part in parts)
        tail = returned[:, D:]
        grad_gates = gates[...] * (tail + pltpu.roll(tail, PAD - experts, 1))
        logits = grad_gates - gates[...] * jnp.sum(grad_gates, axis=1, keepdims=True)
        logits = logits.astype(bf16)
        grad_logits[...] = logits
        grad_normed = returned[:, :D] + dot(logits, router[...], ((1,), (1,)))
        value = hidden[...]
        inverse = inverse_rms(value)
        grad_gain[...] = jnp.sum(grad_normed * value * inverse, axis=0, keepdims=True)
        grad = upstream[...].astype(f32) + rms_backward(value, inverse, gain[...], grad_normed)
        grad_hidden[...] = grad
        grad_branch[...] = grad.astype(bf16)
        wait()

        @tiles(D)
        def _(number):
            at = tile(number)
            grad_mixed[:, at] = dot(grad_branch[...], out_weight[at, :], ((1,), (1,))).astype(bf16)

    shapes = [
        out((count, D), f32), out((count, D)), out((count, D)), out((count, PAD)),
        out((1, D), f32),
    ]
    args = (*parts, hidden, gates, upstream, gain, router, gathered)
    return pl.pallas_call(
        kernel,
        grid_spec=pltpu.PrefetchScalarGridSpec(
            num_scalar_prefetch=1,
            grid=(1,),
            in_specs=[HBM if value is gathered else fixed(value.shape) for value in args],
            out_specs=[fixed(shape.shape) for shape in shapes],
            scratch_shapes=[
                pltpu.VMEM((D, D), bf16),
                pltpu.SemaphoreType.DMA((planes * gathered.shape[0],)),
            ],
        ),
        out_shape=shapes,
        compiler_params=params(),
    )(plane, *args)


def project_backward(step, grad_proj, tokens, slab):
    ranks, rows, _ = grad_proj.shape
    width = slab.shape[1] - PAD

    def kernel(grad_proj, tokens, weight, grad_normed, grad_gain):
        value = tokens[0].astype(f32)
        inverse = inverse_rms(value)
        grad = dot(grad_proj[0], weight[:, :width], ((1,), (1,)))
        grad_normed[...] = grad.astype(bf16)

        @pl.when(pl.program_id(0) == 0)
        def _():
            grad_gain[...] = jnp.zeros_like(grad_gain)

        grad_gain[...] += jnp.sum(grad * value * inverse, axis=0, keepdims=True)

    return pl.pallas_call(
        kernel,
        grid=(ranks,),
        in_specs=[
            leading(grad_proj.shape),
            pl.BlockSpec((1, rows, D), lambda i: (i, step, 0)),
            fixed(slab.shape),
        ],
        out_specs=[pl.BlockSpec((rows, D), lambda i: (i, 0)), fixed((1, D))],
        out_shape=[out((ranks * rows, D)), out((1, D), f32)],
        compiler_params=params(),
    )(grad_proj, tokens, slab)


def shift_rep(value, step):
    count = lax.axis_size("rep")
    return lax.ppermute(value, "rep", [(i, (i + step) % count) for i in range(count)])


def after(value, *others):
    return lax.optimization_barrier((value,) + others)[0]


def two_parts(value):
    high = lax.reduce_precision(value, 8, 7)
    return high.astype(bf16), (value - high).astype(bf16)


def shift_order(count):
    return sorted(range(1, count), key=lambda step: (min(step, count - step), step))


def ring_rep(value):
    count = lax.axis_size("rep")
    rank = lax.axis_index("rep")
    rows = value.shape[0]
    full = jnp.zeros((count * rows,) + value.shape[1:], value.dtype)
    full = lax.dynamic_update_slice_in_dim(full, value, rank * rows, 0)
    for step in range(1, count):
        value = shift_rep(value, 1)
        full = lax.dynamic_update_slice_in_dim(full, value, (rank - step) % count * rows, 0)
    return full


def on_device(
    tokens, cotangent, w_qkv, w_o, w_router, norm_gains, qk_gain, w_in, w_out, segments, routes
):
    planes = lax.axis_size("rep")
    ranks = lax.axis_size("ep")
    plane = lax.axis_index("rep")
    rank = lax.axis_index("ep")
    share = w_in.shape[0]
    own = plane % share
    experts = share * ranks
    where = jnp.stack([rank * share + own, plane, rank % 2]).astype(jnp.int32)
    micro = segments.shape[1]
    mine = tokens.shape[0]
    rows = mine // micro
    length = rows * ranks
    capacity = rows * TOP * 17 // (16 * experts)
    slots = -(-share * capacity // 16) * 16
    width = HEADS // ranks * HD
    qk_gains = qk_gain.astype(f32).reshape(2, HD)
    dense_rows = w_qkv.shape[0]

    def exchange(value, step):
        pairs = [(i, i // share * share + (i % share + step) % share) for i in range(planes)]
        return lax.ppermute(value, "rep", pairs)

    def with_group(value):
        return jnp.stack([value] + [exchange(value, step) for step in range(1, share)])

    def gather_ranks(value):
        return lax.all_gather(value, "ep", axis=0)

    out_rows = [w_o] + [shift_rep(w_o, step) for step in range(1, planes)]
    upstream_group = with_group(cotangent)
    slab = jnp.concatenate(
        [
            w_qkv.reshape(dense_rows, 3, ranks, width)
            .transpose(2, 0, 1, 3)
            .reshape(ranks, dense_rows, 3 * width),
            jnp.broadcast_to(
                jnp.concatenate(
                    [
                        w_router,
                        norm_gains.reshape(dense_rows, 2),
                        jnp.zeros((dense_rows, PAD - experts - 2), bf16),
                    ],
                    axis=1,
                )[None],
                (ranks, dense_rows, PAD),
            ),
        ],
        axis=2,
    )
    slab = lax.all_to_all(slab, "ep", split_axis=0, concat_axis=0, tiled=True)
    slab = slab.reshape(ranks * dense_rows, 3 * width + PAD)
    out_rows, upstream_group, slab = lax.optimization_barrier((out_rows, upstream_group, slab))
    gathered = gather_ranks(jnp.concatenate([tokens, *out_rows], axis=0))
    slab = ring_rep(slab)
    router = slab[:, 3 * width :]
    gain_pair = router[:, experts : experts + 2].reshape(-1).astype(f32)
    first_gain = gain_pair[None, :D]
    second_gain = gain_pair[None, D:]

    def send_weight(weight, step):
        part = lax.dynamic_index_in_dim(weight, (own + step) % share, 0, keepdims=False)
        return shift_rep(part, step) if step else part

    order = shift_order(planes)
    early = after((w_in, w_out), slab)
    in_pieces = {step: send_weight(early[0], step) for step in [0] + order[:1]}
    out_parts = {step: send_weight(early[1], step) for step in [0] + order[:1]}

    segment = segments[0]
    cosine, sine = jax.vmap(lambda one: rope_tables(doc_positions(one), HD))(segment)
    sine = jnp.where(jnp.arange(HD) < HD // 2, -sine, sine)
    tables = (cosine, sine, segment[:, :, None], segment[:, None, :], qk_gains)
    gathered, tables = lax.optimization_barrier((gathered, tables))
    normed, proj = project(mine, gathered, first_gain, slab)
    proj = proj.reshape(ranks, micro, rows, 3 * width)
    upstream_all = gather_ranks(after(upstream_group, proj))
    mixed_h, query, keys, values, lses = attention_forward(proj, *tables)
    mixed = lax.all_to_all(mixed_h, "ep", split_axis=0, concat_axis=3, tiled=True)
    mixed = mixed.reshape(mine, D)
    hidden, payload, gates = route(
        where[1:2], planes, mixed, tokens, gathered, second_gain, router, routes, experts
    )
    normed_two = payload[:, :D]
    payload, in_pieces, out_parts = lax.optimization_barrier((payload, in_pieces, out_parts))
    payload = with_group(payload)
    payload, late = lax.optimization_barrier((payload, (w_in, w_out)))
    for step in order[1:]:
        in_pieces[step] = send_weight(late[0], step)
    in_pieces, late = lax.optimization_barrier((in_pieces, late))
    for step in order[1:]:
        out_parts[step] = send_weight(late[1], step)
    in_pieces = [in_pieces[step] for step in range(planes)]
    payload = gather_ranks(payload)

    shape = (ranks, share, micro, rows, -1)
    rows_in, tail, both, active, grad_produced, up_rows, places = expert_forward(
        where, payload.reshape(shape), upstream_all.reshape(shape), in_pieces, slots, experts
    )
    in_rows = micro * ranks * slots
    out_cut = weight_gradient(
        where, planes, active.reshape(in_rows, FF), [grad_produced.reshape(in_rows, D)]
    )

    def sum_rep(parts):
        sums = [
            sum(parts[step].astype(f32) for step in range(first, planes, share))
            for first in range(share)
        ]
        return jnp.stack(
            [
                sum(jnp.where((own - step) % share == j, sums[step], 0.0) for step in range(share))
                for j in range(share)
            ]
        )

    def send(parts, steps):
        return {step: shift_rep(parts[step], step) for step in steps}

    tail, out_cut = lax.optimization_barrier((tail, out_cut))
    out_sent = send(out_cut, order)
    out_pieces = [out_parts[step] for step in range(planes)]
    back = []
    returned = []

    def scatter_ranks(value):
        return lax.psum_scatter(value, "ep", scatter_dimension=0)

    def exchange_back(value):
        return [value[0]] + [exchange(value[step], share - step) for step in range(1, share)]

    for step in range(micro):
        back.append(
            expert_backward(
                step, where, tail, both, active, grad_produced, up_rows, places, in_pieces,
                out_pieces, share, rows, experts,
            )
        )
        returned.append(scatter_ranks(back[step][2]))
        tail, out_sent[order[step]] = after((tail, out_sent[order[step]]), back[step][2])
    rows_in = after(rows_in, tail)
    in_cut = weight_gradient(
        where,
        planes,
        rows_in.reshape(in_rows, D),
        [back[step][3].reshape(in_rows // micro, 2 * FF) for step in range(micro)],
    )
    in_sent = {}

    def swap(value, step):
        return lax.ppermute(value, "ep", [(i, i ^ step) for i in range(ranks)])

    def pair_sum(keep, give):
        return (keep.astype(f32) + swap(give, 1).astype(f32)).astype(bf16)

    def cross(value):
        parts = []
        for step in range(ranks // 2):
            part = lax.dynamic_index_in_dim(value, rank // 2 ^ step, 0, keepdims=False)
            parts.append(swap(part, 2 * step) if step else part)
        return parts

    def total(parts):
        return sum(part.astype(f32) for part in parts)

    grad_inputs, branches, logit_grads = [], [], []
    gain_two_sum = gain_one_sum = qk_sum = qkv_sum = 0.0
    in_cut, mixtures, out_sent = lax.optimization_barrier(
        (in_cut, [part[:2] for part in back], out_sent)
    )
    mixtures = [pair_sum(*part) for part in mixtures]
    crossed = []
    releases = [order[:1]] + [[]] * (micro - 2) + [order[1:-1]]
    for step in range(micro):
        at = slice(step * rows, (step + 1) * rows)
        parts, in_sent, mixtures = lax.optimization_barrier((returned[step], in_sent, mixtures))
        parts = exchange_back(parts)
        parts, in_cut = lax.optimization_barrier((parts, in_cut))
        in_sent.update(send(in_cut, releases[step]))
        grad_hidden, grad_branch, grad_mixed, grad_logits, gain_two = hidden_backward(
            where[1:2], planes, mine, parts, hidden[at], gates[at], cotangent[at], second_gain,
            router, gathered, experts,
        )
        branches.append(grad_branch)
        logit_grads.append(grad_logits)
        gain_two_sum = gain_two_sum + gain_two
        grad_mixed = lax.all_to_all(grad_mixed, "ep", split_axis=1, concat_axis=0, tiled=True)
        if step == micro - 1:
            grad_mixed, mixtures = lax.optimization_barrier((grad_mixed, mixtures))
            crossed = [cross(part) for part in mixtures]
        grad_proj, grad_qk = attention_backward(
            step, proj, *tables, query, keys, values, lses, grad_mixed
        )
        if step == micro - 1:
            last = in_cut[order[-1]]
            half = last.shape[0] // 2
            grad_proj, in_sent, last = lax.optimization_barrier((grad_proj, in_sent, last))
            last_sent = [shift_rep(last[:half], order[-1])]
        qk_sum = qk_sum + grad_qk.reshape(-1)
        grad_normed, gain_one = project_backward(step, grad_proj, gathered, slab)
        gain_one_sum = gain_one_sum + gain_one
        grad_inputs.append(
            (at, grad_hidden, lax.psum_scatter(grad_normed, "ep", scatter_dimension=0, tiled=True))
        )
        grad_proj = after(grad_proj, grad_normed)
        qkv_sum = qkv_sum + dot(
            normed.reshape(ranks, micro, rows, D)[:, step].reshape(length, D),
            grad_proj.reshape(length, 3 * width),
            ((0,), (0,)),
        )
    grad_w_out = sum_rep({0: out_cut[0], **out_sent})

    out_sum = dot(mixed, after(jnp.concatenate(branches, axis=0), grad_normed), ((0,), (0,))).astype(bf16)
    out_sum = out_sum.reshape(planes, ranks // 2, 2, dense_rows, D).transpose(2, 1, 0, 3, 4)
    out_crossed = cross(
        pair_sum(
            *(
                lax.dynamic_index_in_dim(out_sum, rank % 2 ^ other, 0, keepdims=False)
                for other in range(2)
            )
        )
    )

    router_sum = dot(normed_two, jnp.concatenate(logit_grads, axis=0), ((0,), (0,)))
    qk_columns = qk_sum.shape[0] // dense_rows
    small = jnp.concatenate(
        [
            router_sum[:, :experts],
            jnp.concatenate([gain_one_sum, gain_two_sum], axis=1).reshape(D, 2),
            jnp.tile(qk_sum.reshape(dense_rows, qk_columns), (planes * ranks, 1)),
        ],
        axis=1,
    )
    count = small.shape[1]

    def pack(main, small):
        high, low = two_parts(small)
        blank = jnp.zeros((small.shape[0], PAD - 2 * count), bf16)
        return jnp.concatenate([main.astype(bf16), high, low, blank], axis=1)

    def unpack(packed):
        packed = packed.astype(f32)
        split = packed.shape[-1] - PAD
        tail = packed[..., split:]
        return packed[..., :split], tail[..., :count] + tail[..., count : 2 * count]

    packed, crossed, last_sent, last = lax.optimization_barrier(
        (pack(qkv_sum, small), crossed, last_sent, last)
    )
    last_sent = last_sent + [shift_rep(last[half:], order[-1])]
    part_rows = D // planes
    main = lax.dynamic_slice_in_dim(qkv_sum, plane * part_rows, part_rows, 0)
    small = lax.dynamic_slice_in_dim(small, plane * part_rows, part_rows, 0)
    packed_sent = [
        shift_rep(
            lax.dynamic_slice_in_dim(packed, (plane + step) % planes * part_rows, part_rows, 0),
            step,
        )
        for step in range(1, planes)
    ]
    mixture = []
    for parts in crossed:
        parts = total(parts)
        mixture.append(parts[0] + total(exchange_back(parts.astype(bf16))[1:]))
    output = (hidden + jnp.concatenate(mixture, axis=0)).astype(bf16)
    grad_tokens = []
    for at, grad_hidden, grad_normed in grad_inputs:
        own_stream = tokens[at].astype(f32)
        grad_tokens.append(
            grad_hidden
            + rms_backward(
                own_stream, inverse_rms(own_stream), first_gain, grad_normed.astype(f32)
            )
        )
    packed_sent, last_sent = lax.optimization_barrier((packed_sent, last_sent))
    in_sent[order[-1]] = jnp.concatenate(last_sent, axis=0)
    for part in packed_sent:
        part_main, part_small = unpack(part)
        main, small = main + part_main, small + part_small
    packed = pack(main, small).reshape(ranks, dense_rows, -1)
    packed = lax.all_to_all(packed, "ep", split_axis=0, concat_axis=0, tiled=True)
    main, small = unpack(packed)
    grad_w_qkv = (
        main.reshape(ranks, dense_rows, 3, width).transpose(1, 2, 0, 3).reshape(dense_rows, 3 * D)
    )
    small = jnp.sum(small, axis=0)
    grad_w_in = sum_rep({0: in_cut[0], **in_sent})
    out_sum = total(out_crossed)
    grad_w_o = lax.dynamic_index_in_dim(out_sum, plane, 0, keepdims=False)
    out_sum = out_sum.astype(bf16)
    for step in range(1, planes):
        part = lax.dynamic_index_in_dim(out_sum, (plane + step) % planes, 0, keepdims=False)
        grad_w_o = grad_w_o + shift_rep(part, step).astype(f32)
    return (
        output,
        jnp.concatenate(grad_tokens, axis=0),
        grad_w_qkv,
        grad_w_o,
        small[:, :experts],
        small[:, experts : experts + 2].reshape(-1),
        small[:, experts + 2 :].reshape(-1),
        grad_w_in,
        grad_w_out,
    )


def solution(mesh):
    placed = (
        P(("rep", "ep"), None),
        P(("rep", "ep"), None),
        P(("rep", "ep"), None),
        P(("rep", "ep"), None),
        P(("rep", "ep"), None),
        P(("rep", "ep")),
        P(),
        P("ep", "rep", None),
        P("ep", "rep", None),
        P("rep", None, None),
        P(("rep", "ep"), None),
    )
    return jax.shard_map(
        on_device,
        mesh=mesh,
        in_specs=placed,
        out_specs=(
            P(("rep", "ep"), None),
            P(("rep", "ep"), None),
            P(("rep", "ep"), None),
            P(("rep", "ep"), None),
            P(("rep", "ep"), None),
            P(("rep", "ep")),
            P(),
            P("ep", "rep", None),
            P("ep", "rep", None),
        ),
        check_vma=False,
    )
```

```python
import math

import jax
import jax.numpy as jnp
from jax import lax
from jax.experimental import pallas as pl
from jax.experimental.pallas import tpu as pltpu
from jax.sharding import PartitionSpec as P

D = 2048
HEADS = 16
HD = 128
FF = 1024
TOP = 8
HALF = 512
PAD = 128

epsilon = 1e-06
rope_base = 50000.0
bf16 = jnp.bfloat16
f32 = jnp.float32


def dot(a, b, dims=((1,), (0,))):
    return lax.dot_general(a, b, (dims, ((), ())), preferred_element_type=f32)


def inverse_rms(value):
    return lax.rsqrt(jnp.mean(value * value, axis=-1, keepdims=True) + epsilon)


def rms_backward(value, inverse, gain, grad):
    scaled = grad * gain
    inner = jnp.mean(scaled * value, axis=-1, keepdims=True)
    return inverse * (scaled - value * (inverse * inverse * inner))


def doc_positions(segment):
    index = jnp.arange(segment.shape[0], dtype=jnp.int32)
    change = jnp.concatenate([jnp.ones((1,), dtype=jnp.bool_), segment[1:] != segment[:-1]])
    start = lax.cummax(jnp.where(change, index, 0), axis=0)
    return index - start


def rope_tables(position, width):
    steps = jnp.arange(width // 2, dtype=f32) * (2.0 / width)
    rates = jnp.exp(-steps * math.log(rope_base))
    angle = position.astype(f32)[:, None] * rates[None, :]
    angle = jnp.concatenate([angle, angle], axis=-1)
    return (jnp.cos(angle), jnp.sin(angle))


def norm_rope(value, gain, cosine, sine):
    inverse = lax.rsqrt(jnp.mean(value * value, axis=1, keepdims=True) + epsilon)
    value = value * inverse * gain
    return value * cosine + pltpu.roll(value, HD // 2, 1) * sine


def norm_rope_back(value, gain, cosine, sine, grad):
    inverse = lax.rsqrt(jnp.mean(value * value, axis=1, keepdims=True) + epsilon)
    grad = grad * cosine + pltpu.roll(grad * sine, HD // 2, 1)
    normal = value * inverse
    scaled = grad * gain
    inner = jnp.mean(scaled * normal, axis=1, keepdims=True)
    return inverse * (scaled - normal * inner), jnp.sum(grad * normal, axis=0, keepdims=True)


def kept_scores(query, keys, q_seg, k_seg, start):
    scores = dot(query, keys, ((1,), (1,))) * (1.0 / math.sqrt(HD))
    q_index = start + lax.broadcasted_iota(jnp.int32, scores.shape, 0)
    k_index = lax.broadcasted_iota(jnp.int32, scores.shape, 1)
    keep = (jnp.abs(q_index - k_index) <= HALF) & (q_seg == k_seg)
    return jnp.where(keep, scores, -1e30)


BIG = 100 * 1024 * 1024 // 2


def forward_kernel(
    heads, proj, cosine, sine, seg_column, seg_row, gains, mixed, query, keys, values, lses
):
    ranks, _, rows, _ = proj.shape
    length = ranks * rows
    q_block = 2 * rows
    k_seg = seg_row[0]
    for head in range(heads):
        at = slice(head * HD, (head + 1) * HD)

        def raw(part):
            first = (part * heads + head) * HD
            return proj[:, 0, :, first : first + HD].reshape(length, HD)

        query[0, :, at] = norm_rope(raw(0), gains[0:1], cosine[0], sine[0]).astype(bf16)
        keys[0, :, at] = norm_rope(raw(1), gains[1:2], cosine[0], sine[0]).astype(bf16)
        values[0, :, at] = raw(2).astype(bf16)

        @pl.loop(0, length // q_block)
        def one_block(number, head=head, at=at):
            start = pl.multiple_of(number * q_block, q_block)
            here = pl.ds(start, q_block)
            scores = kept_scores(
                query[0, here, at], keys[0, :, at], seg_column[0, here], k_seg, start
            )
            top = jnp.max(scores, axis=1, keepdims=True)
            weights = jnp.exp(scores - top)
            total = jnp.sum(weights, axis=1, keepdims=True)
            lses[0, head, here] = top + jnp.log(total)
            weights = (weights * (1.0 / total)).astype(bf16)
            result = dot(weights, values[0, :, at]).astype(bf16)
            mixed[pl.ds(number * 2, 2), 0, :, at] = result.reshape(2, rows, HD)


def backward_kernel(
    heads, proj, cosine, sine, seg_column, seg_row, gains, query, keys, values, lses, grad_mixed,
    grad_proj, grad_gains, grad_q, grad_k, grad_v,
):
    ranks, _, rows, _ = proj.shape
    length = ranks * rows
    q_block = 2 * rows
    k_seg = seg_row[0]
    scale = 1.0 / math.sqrt(HD)
    sum_q = jnp.zeros((1, HD), f32)
    sum_k = jnp.zeros((1, HD), f32)
    for head in range(heads):
        at = slice(head * HD, (head + 1) * HD)
        grad_k[...] = jnp.zeros_like(grad_k)
        grad_v[...] = jnp.zeros_like(grad_v)

        @pl.loop(0, length // q_block)
        def one_block(number, head=head, at=at):
            start = pl.multiple_of(number * q_block, q_block)
            here = pl.ds(start, q_block)
            q_rows = query[0, here, at]
            g_rows = grad_mixed[here, at]
            k_all = keys[0, :, at]
            scores = kept_scores(q_rows, k_all, seg_column[0, here], k_seg, start)
            weights = jnp.exp(scores - lses[0, head, here])
            grad_weights = dot(g_rows, values[0, :, at], ((1,), (1,)))
            delta = jnp.sum(weights * grad_weights, axis=1, keepdims=True)
            grad_scores = (weights * (grad_weights - delta)).astype(bf16)
            grad_q[here] = dot(grad_scores, k_all) * scale
            grad_k[...] += dot(grad_scores, q_rows, ((0,), (0,)))
            grad_v[...] += dot(weights.astype(bf16), g_rows, ((0,), (0,)))

        def rounded(value):
            return value.astype(bf16).astype(f32)

        def raw(part):
            first = (part * heads + head) * HD
            return proj[:, 0, :, first : first + HD].reshape(length, HD)

        def put(part, value):
            first = (part * heads + head) * HD
            grad_proj[:, :, first : first + HD] = value.astype(bf16).reshape(ranks, rows, HD)

        back_q, gain_q = norm_rope_back(
            raw(0), gains[0:1], cosine[0], sine[0], rounded(grad_q[...])
        )
        back_k, gain_k = norm_rope_back(
            raw(1), gains[1:2], cosine[0], sine[0], rounded(grad_k[...] * scale)
        )
        sum_q, sum_k = sum_q + gain_q, sum_k + gain_k
        put(0, back_q)
        put(1, back_k)
        put(2, grad_v[...])
    grad_gains[0:1] = sum_q
    grad_gains[1:2] = sum_k


def fixed(shape):
    return pl.BlockSpec(shape, lambda *_: (0,) * len(shape), pipeline_mode=pl.Buffered(1))


def leading(shape):
    return pl.BlockSpec((1,) + shape[1:], lambda i: (i,) + (0,) * (len(shape) - 1))


def params():
    return pltpu.CompilerParams(vmem_limit_bytes=BIG)


def cost(products):
    return pl.CostEstimate(flops=6 * products, bytes_accessed=0, transcendentals=0)


def out(shape, dtype=bf16):
    return jax.ShapeDtypeStruct(shape, dtype)


def attention_forward(proj, cosine, sine, seg_column, seg_row, gains):
    ranks, micro, rows, width = proj.shape
    length = ranks * rows
    width = width // 3
    heads = width // HD
    part = out((micro, length, width))
    by_rank = lambda n: pl.BlockSpec((ranks, 1, rows, n), lambda i: (0, i, 0, 0))
    lses = out((micro, heads, length, 1), f32)
    return pl.pallas_call(
        lambda *refs: forward_kernel(heads, *refs),
        grid=(micro,),
        in_specs=[by_rank(3 * width)]
        + [leading(v.shape) for v in (cosine, sine, seg_column, seg_row)]
        + [fixed(gains.shape)],
        out_specs=[by_rank(width)] + [leading(part.shape)] * 3 + [leading(lses.shape)],
        out_shape=[out((ranks, micro, rows, width)), part, part, part, lses],
        compiler_params=params(),
    )(proj, cosine, sine, seg_column, seg_row, gains)


def attention_backward(
    step, proj, cosine, sine, seg_column, seg_row, gains, query, keys, values, lses, grad_mixed
):
    ranks, micro, rows, width = proj.shape
    length = ranks * rows
    heads = width // 3 // HD

    def part(value):
        return pl.BlockSpec((1,) + value.shape[1:], lambda i: (step,) + (0,) * (value.ndim - 1))

    return pl.pallas_call(
        lambda *refs: backward_kernel(heads, *refs),
        grid=(1,),
        in_specs=[pl.BlockSpec((ranks, 1, rows, width), lambda i: (0, step, 0, 0))]
        + [part(v) for v in (cosine, sine, seg_column, seg_row)]
        + [fixed(gains.shape)]
        + [part(v) for v in (query, keys, values, lses)]
        + [fixed(grad_mixed.shape)],
        out_specs=[fixed((ranks, rows, width)), fixed((2, HD))],
        out_shape=[out((ranks, rows, width)), out((2, HD), f32)],
        scratch_shapes=[pltpu.VMEM((length, HD), f32)] * 3,
        compiler_params=params(),
    )(
        proj, cosine, sine, seg_column, seg_row, gains, query, keys, values, lses, grad_mixed
    )


def project(tokens, gain, slab):
    ranks, count, _ = tokens.shape
    width = slab.shape[1] - PAD

    def kernel(value, gain, weight, normed, proj):
        value = value[0].astype(f32)
        result = (value * inverse_rms(value) * gain[...]).astype(bf16)
        normed[0] = result
        proj[0] = dot(result, weight[:, :width])

    return pl.pallas_call(
        kernel,
        grid=(ranks,),
        in_specs=[leading((ranks, count, D)), fixed((1, D)), fixed(slab.shape)],
        out_specs=[leading((ranks, count, D)), leading((ranks, count, width))],
        out_shape=[out((ranks, count, D)), out((ranks, count, width), f32)],
        compiler_params=params(),
    )(tokens, gain, slab)


TILE = 512


def tiles(count):
    return pl.loop(0, count // TILE)


def tile(number):
    return pl.ds(pl.multiple_of(number * TILE, TILE), TILE)


HBM = pl.BlockSpec(memory_space=pl.ANY)


def copies(pairs, sems):
    started = [
        pltpu.make_async_copy(source, target, sems.at[place])
        for place, (source, target) in enumerate(pairs)
    ]
    for copy in started:
        copy.start()

    def wait():
        for copy in started:
            copy.wait()

    return wait


def plane_pairs(plane, pieces, target):
    planes = len(pieces)
    rows = target.shape[0] // planes
    return [
        (piece, target.at[pl.ds((plane + planes - step) % planes * rows, rows)])
        for step, piece in enumerate(pieces)
    ]


def out_weight_pairs(plane, planes, gathered, target):
    ranks = gathered.shape[0]
    rows = D // (planes * ranks)
    return [
        (
            gathered.at[rank, pl.ds(step * rows, rows)],
            target.at[pl.ds(((plane + planes - step) % planes * ranks + rank) * rows, rows)],
        )
        for rank in range(ranks)
        for step in range(planes)
    ]


def route(plane, planes, mixed, tokens, gathered, gain, router, routes, experts):
    count = tokens.shape[0]
    pieces = planes * gathered.shape[0]

    def kernel(
        plane, mixed, tokens, gathered, gain, router, routes, hidden, payload, gates,
        out_weight, sems,
    ):
        copies(out_weight_pairs(plane[0], planes, gathered, out_weight), sems)()

        @tiles(D)
        def _(number):
            at = tile(number)
            hidden[:, at] = tokens[:, at].astype(f32) + dot(mixed[...], out_weight[:, at])

        value = hidden[...]
        normed = (value * inverse_rms(value) * gain[...]).astype(bf16)
        payload[:, :D] = normed
        logits = dot(normed, router[...])
        column = lax.broadcasted_iota(jnp.int32, logits.shape, 1)
        routed = column == routes[:, 0:1]
        for choice in range(1, TOP):
            routed = routed | (column == routes[:, choice : choice + 1])
        logits = jnp.where(routed, logits, -1e30)
        weights = jnp.exp(logits - jnp.max(logits, axis=1, keepdims=True))
        weights = jnp.where(routed, weights, 0.0)
        weights = weights / jnp.sum(weights, axis=1, keepdims=True)
        gates[...] = weights
        high = weights.astype(bf16).astype(f32)
        payload[:, D:] = (high + pltpu.roll(weights - high, experts, 1)).astype(bf16)

    shapes = [out((count, D), f32), out((count, D + PAD)), out((count, PAD), f32)]
    return pl.pallas_call(
        kernel,
        grid_spec=pltpu.PrefetchScalarGridSpec(
            num_scalar_prefetch=1,
            grid=(1,),
            in_specs=[
                HBM if value is gathered else fixed(value.shape)
                for value in (mixed, tokens, gathered, gain, router, routes)
            ],
            out_specs=[fixed(shape.shape) for shape in shapes],
            scratch_shapes=[pltpu.VMEM((D, D), bf16), pltpu.SemaphoreType.DMA((pieces,))],
        ),
        out_shape=shapes,
        compiler_params=params(),
    )(plane, mixed, tokens, gathered, gain, router, routes)


def lane(value, number):
    column = lax.broadcasted_iota(jnp.int32, value.shape, 1)
    return jnp.sum(jnp.where(column == number, value.astype(f32), 0.0), axis=1, keepdims=True)


def one_hot(slot, slots):
    place = lax.broadcasted_iota(jnp.int32, (slots, slot.shape[1]), 0).astype(f32)
    return (place == slot).astype(bf16)


def expert_forward(where, payload, upstream, in_pieces, slots, experts):
    ranks, share, micro, rows, _ = payload.shape
    count = share * rows
    block = 2 * slots

    planes = len(in_pieces)

    def kernel(where, payload, upstream, *refs):
        (
            rows_in, tail, both, active, grad_produced, up_rows, places, in_weight, sems
        ) = refs[planes:]
        number = where[0]

        @pl.when((pl.program_id(0) == 0) & (pl.program_id(1) == 0))
        def _():
            copies(plane_pairs(where[1], refs[:planes], in_weight), sems)()

        for part in range(2):
            here = slice(part * slots, (part + 1) * slots)
            value = payload[part].reshape(count, D + PAD)
            marks = value[:, D:]
            first = lax.broadcasted_iota(jnp.int32, (8, PAD), 1) == number
            taken = dot(first.astype(bf16), marks, ((1,), (1,))) > 0.0
            before = lax.broadcasted_iota(jnp.int32, (count, count), 0)
            behind = lax.broadcasted_iota(jnp.int32, (count, count), 1)
            slot = dot(taken.astype(bf16), (before < behind).astype(bf16))
            select = one_hot(jnp.where(taken, slot, -1.0)[0:1], slots)
            wide = jnp.broadcast_to(lane(marks, number) > 0.0, (count, PAD))
            slot = dot((before > behind).astype(bf16), wide.astype(bf16))
            places[0, 0, part] = jnp.where(wide, slot, -1.0)
            rows_in[0, 0, here] = dot(select, value[:, :D]).astype(bf16)
            marks = dot(select, marks)
            tail[0, 0, here] = marks
            gate = lane(marks, number) + lane(marks, experts + number)
            picked = dot(select, upstream[part].reshape(count, D))
            up_rows[0, 0, here] = picked.astype(bf16)
            grad_produced[0, 0, here] = (gate * picked).astype(bf16)

        for number in range(FF // TILE):
            at = slice(number * TILE, (number + 1) * TILE)
            more = slice(FF + number * TILE, FF + (number + 1) * TILE)
            gate_part = dot(rows_in[0, 0], in_weight[:, at])
            up_part = dot(rows_in[0, 0], in_weight[:, more])
            both[0, 0, :, at] = gate_part
            both[0, 0, :, more] = up_part
            active[0, 0, :, at] = (
                gate_part / (1.0 + jnp.exp(-gate_part)) * up_part
            ).astype(bf16)

    def tokens_spec(width):
        return pl.BlockSpec((2, share, 1, rows, width), lambda m, b, _: (b, 0, m, 0, 0))

    pairs = ranks // 2
    shapes = [
        out((micro, pairs, block, D)),
        out((micro, pairs, block, PAD), f32),
        out((micro, pairs, block, 2 * FF), f32),
        out((micro, pairs, block, FF)),
        out((micro, pairs, block, D)),
        out((micro, pairs, block, D)),
        out((micro, pairs, 2, count, PAD), f32),
    ]
    return pl.pallas_call(
        kernel,
        grid_spec=pltpu.PrefetchScalarGridSpec(
            num_scalar_prefetch=1,
            grid=(micro, pairs),
            in_specs=[tokens_spec(D + PAD), tokens_spec(D)] + [HBM] * planes,
            out_specs=[
                pl.BlockSpec(
                    (1, 1) + s.shape[2:], lambda m, b, _, n=len(s.shape): (m, b) + (0,) * (n - 2)
                )
                for s in shapes
            ],
            scratch_shapes=[pltpu.VMEM((D, 2 * FF), bf16), pltpu.SemaphoreType.DMA((planes,))],
        ),
        out_shape=shapes,
        cost_estimate=cost(micro * pairs * block * D * (2 * FF + 2 * count)),
        compiler_params=params(),
    )(where, payload, upstream, *in_pieces)


def expert_backward(
    step, where, tail, both, active, grad_produced, up_rows, places, in_pieces, out_pieces,
    share, rows, experts,
):
    pairs, block = tail.shape[1:3]
    slots = block // 2
    count = places.shape[3]

    planes = len(in_pieces)

    def kernel(where, tail, both, active, grad_produced, up_rows, places, *refs):
        keep, give, grad_tokens, grad_both, in_weight, out_weight, sems = refs[2 * planes :]
        number = where[0]
        odd = where[2] == 1

        @pl.when(pl.program_id(0) == 0)
        def _():
            copies(
                plane_pairs(where[1], refs[:planes], in_weight)
                + plane_pairs(where[1], refs[planes : 2 * planes], out_weight),
                sems,
            )()

        gate = lane(tail[0, 0], number) + lane(tail[0, 0], experts + number)
        place = lax.broadcasted_iota(jnp.int32, (count, slots), 1).astype(f32)
        selects = [(places[0, 0, part][:, 0:1] == place).astype(bf16) for part in range(2)]

        def spread(value):
            return [
                dot(selects[part], value[part * slots : (part + 1) * slots])
                .astype(bf16)
                .reshape(share, rows, -1)
                for part in range(2)
            ]

        grad_gate = jnp.zeros((block, 1), f32)
        for tile in range(D // TILE):
            at = slice(tile * TILE, (tile + 1) * TILE)
            produced = dot(active[0, 0], out_weight[:, at]).astype(bf16).astype(f32)
            even_rank, odd_rank = spread((gate * produced).astype(bf16))
            keep[0, :, :, at] = jnp.where(odd, odd_rank, even_rank)
            give[0, :, :, at] = jnp.where(odd, even_rank, odd_rank)
            grad_gate = grad_gate + jnp.sum(
                up_rows[0, 0, :, at].astype(f32) * produced, axis=1, keepdims=True
            )

        for tile in range(FF // TILE):
            at = slice(tile * TILE, (tile + 1) * TILE)
            more = slice(FF + tile * TILE, FF + (tile + 1) * TILE)
            grad_active = dot(grad_produced[0, 0], out_weight[at, :], ((1,), (1,)))
            grad_active = grad_active.astype(bf16).astype(f32)
            gate_part = both[0, 0, :, at]
            up_part = both[0, 0, :, more]
            sigma = 1.0 / (1.0 + jnp.exp(-gate_part))
            grad_both[0, :, at] = (
                grad_active * up_part * (sigma * (1.0 + gate_part * (1.0 - sigma)))
            ).astype(bf16)
            grad_both[0, :, more] = (grad_active * (gate_part * sigma)).astype(bf16)

        for tile in range(D // TILE):
            at = slice(tile * TILE, (tile + 1) * TILE)
            grad_rows = dot(grad_both[0], in_weight[at, :], ((1,), (1,))).astype(bf16)
            grad_tokens[0, :, :, at], grad_tokens[1, :, :, at] = spread(grad_rows)

        high = grad_gate.astype(bf16).astype(f32)
        column = lax.broadcasted_iota(jnp.int32, (block, PAD), 1)
        extra = jnp.where(column == number, high, 0.0)
        extra = jnp.where(column == experts + number, grad_gate - high, extra)
        grad_tokens[0, :, :, D:], grad_tokens[1, :, :, D:] = spread(extra.astype(bf16))

    def part(value):
        return pl.BlockSpec(
            (1, 1) + value.shape[2:], lambda b, _: (step, b) + (0,) * (value.ndim - 2)
        )

    def tokens_spec(count, width):
        return pl.BlockSpec((count, share, rows, width), lambda b, _: (b, 0, 0, 0))

    return pl.pallas_call(
        kernel,
        grid_spec=pltpu.PrefetchScalarGridSpec(
            num_scalar_prefetch=1,
            grid=(pairs,),
            in_specs=[part(v) for v in (tail, both, active, grad_produced, up_rows, places)]
            + [HBM] * (2 * planes),
            out_specs=[
                tokens_spec(1, D),
                tokens_spec(1, D),
                tokens_spec(2, D + PAD),
                pl.BlockSpec((1, block, 2 * FF), lambda b, _: (b, 0, 0)),
            ],
            scratch_shapes=[
                pltpu.VMEM((D, 2 * FF), bf16),
                pltpu.VMEM((FF, D), bf16),
                pltpu.SemaphoreType.DMA((2 * planes,)),
            ],
        ),
        out_shape=[
            out((pairs, share, rows, D)),
            out((pairs, share, rows, D)),
            out((2 * pairs, share, rows, D + PAD)),
            out((pairs, block, 2 * FF)),
        ],
        cost_estimate=cost(pairs * block * D * (4 * FF + 2 * count)),
        compiler_params=params(),
    )(
        where, tail, both, active, grad_produced, up_rows, places, *in_pieces, *out_pieces
    )


def weight_gradient(where, planes, left, rights, tail=None):
    count, width = left.shape
    parts = len(rights)
    part_rows = count // parts
    columns = rights[0].shape[1]
    width = width // planes
    step = min(TILE, columns & -columns)
    tails = [] if tail is None else [tail]
    whole = columns + sum(value.shape[1] for value in tails)

    def of_plane(i, where):
        return (where[1] + i) % planes

    def kernel(where, left, *refs):
        rights, target = refs[:parts], refs[-1]
        for value in refs[parts:-1]:
            target[0, :, columns:] = value[...]
        for number in range(columns // step):
            at = slice(number * step, (number + 1) * step)
            target[0, :, at] = sum(
                dot(left[part * part_rows : (part + 1) * part_rows], right[:, at], ((0,), (0,)))
                for part, right in enumerate(rights)
            ).astype(bf16)

    return pl.pallas_call(
        kernel,
        grid_spec=pltpu.PrefetchScalarGridSpec(
            num_scalar_prefetch=1,
            grid=(planes,),
            in_specs=[pl.BlockSpec((count, width), lambda i, where: (0, of_plane(i, where)))]
            + [fixed(right.shape) for right in rights]
            + [
                pl.BlockSpec((width, value.shape[1]), lambda i, where: (of_plane(i, where), 0))
                for value in tails
            ],
            out_specs=pl.BlockSpec((1, width, whole), lambda i, _: (i, 0, 0)),
        ),
        out_shape=out((planes, width, whole)),
        cost_estimate=cost(count * planes * width * columns),
        compiler_params=params(),
    )(where, left, *rights, *tails)


def hidden_backward(
    plane, planes, parts, hidden, gates, upstream, gain, router, gathered, experts
):
    count = hidden.shape[0]
    terms = len(parts)

    def kernel(plane, *refs):
        parts = refs[:terms]
        hidden, gates, upstream, gain, router, gathered = refs[terms : terms + 6]
        (
            grad_hidden, grad_branch, grad_mixed, grad_logits, grad_gain, out_weight, sems
        ) = refs[terms + 6 :]
        wait = copies(out_weight_pairs(plane[0], planes, gathered, out_weight), sems)
        returned = sum(part[...].astype(f32) for part in parts)
        tail = returned[:, D:]
        grad_gates = gates[...] * (tail + pltpu.roll(tail, PAD - experts, 1))
        logits = grad_gates - gates[...] * jnp.sum(grad_gates, axis=1, keepdims=True)
        logits = logits.astype(bf16)
        grad_logits[...] = logits
        grad_normed = returned[:, :D] + dot(logits, router[...], ((1,), (1,)))
        value = hidden[...]
        inverse = inverse_rms(value)
        grad_gain[...] = jnp.sum(grad_normed * value * inverse, axis=0, keepdims=True)
        grad = upstream[...].astype(f32) + rms_backward(value, inverse, gain[...], grad_normed)
        grad_hidden[...] = grad
        grad_branch[...] = grad.astype(bf16)
        wait()

        @tiles(D)
        def _(number):
            at = tile(number)
            grad_mixed[:, at] = dot(grad_branch[...], out_weight[at, :], ((1,), (1,))).astype(bf16)

    shapes = [
        out((count, D), f32), out((count, D)), out((count, D)), out((count, PAD)),
        out((1, D), f32),
    ]
    args = (*parts, hidden, gates, upstream, gain, router, gathered)
    return pl.pallas_call(
        kernel,
        grid_spec=pltpu.PrefetchScalarGridSpec(
            num_scalar_prefetch=1,
            grid=(1,),
            in_specs=[HBM if value is gathered else fixed(value.shape) for value in args],
            out_specs=[fixed(shape.shape) for shape in shapes],
            scratch_shapes=[
                pltpu.VMEM((D, D), bf16),
                pltpu.SemaphoreType.DMA((planes * gathered.shape[0],)),
            ],
        ),
        out_shape=shapes,
        compiler_params=params(),
    )(plane, *args)


def project_backward(step, grad_proj, tokens, slab):
    ranks, rows, _ = grad_proj.shape
    width = slab.shape[1] - PAD

    def kernel(grad_proj, tokens, weight, grad_normed, grad_gain):
        value = tokens[0].astype(f32)
        inverse = inverse_rms(value)
        grad = dot(grad_proj[0], weight[:, :width], ((1,), (1,)))
        grad_normed[...] = grad.astype(bf16)

        @pl.when(pl.program_id(0) == 0)
        def _():
            grad_gain[...] = jnp.zeros_like(grad_gain)

        grad_gain[...] += jnp.sum(grad * value * inverse, axis=0, keepdims=True)

    return pl.pallas_call(
        kernel,
        grid=(ranks,),
        in_specs=[
            leading(grad_proj.shape),
            pl.BlockSpec((1, rows, D), lambda i: (i, step, 0)),
            fixed(slab.shape),
        ],
        out_specs=[pl.BlockSpec((rows, D), lambda i: (i, 0)), fixed((1, D))],
        out_shape=[out((ranks * rows, D)), out((1, D), f32)],
        compiler_params=params(),
    )(grad_proj, tokens, slab)


def shift_rep(value, step):
    count = lax.axis_size("rep")
    return lax.ppermute(value, "rep", [(i, (i + step) % count) for i in range(count)])


def after(value, *others):
    return lax.optimization_barrier((value,) + others)[0]


def two_parts(value):
    high = lax.reduce_precision(value, 8, 7)
    return high.astype(bf16), (value - high).astype(bf16)


def shift_order(count):
    return sorted(range(1, count), key=lambda step: (min(step, count - step), step))


def ring_rep(value):
    count = lax.axis_size("rep")
    rank = lax.axis_index("rep")
    rows = value.shape[0]
    full = jnp.zeros((count * rows,) + value.shape[1:], value.dtype)
    full = lax.dynamic_update_slice_in_dim(full, value, rank * rows, 0)
    for step in range(1, count):
        value = shift_rep(value, 1)
        full = lax.dynamic_update_slice_in_dim(full, value, (rank - step) % count * rows, 0)
    return full


def on_device(
    tokens, cotangent, w_qkv, w_o, w_router, norm_gains, qk_gain, w_in, w_out, segments, routes
):
    planes = lax.axis_size("rep")
    ranks = lax.axis_size("ep")
    plane = lax.axis_index("rep")
    rank = lax.axis_index("ep")
    share = w_in.shape[0]
    own = plane % share
    experts = share * ranks
    where = jnp.stack([rank * share + own, plane, rank % 2]).astype(jnp.int32)
    micro = segments.shape[1]
    mine = tokens.shape[0]
    rows = mine // micro
    length = rows * ranks
    capacity = rows * TOP * 17 // (16 * experts)
    slots = -(-share * capacity // 16) * 16
    width = HEADS // ranks * HD
    qk_gains = qk_gain.astype(f32).reshape(2, HD)
    dense_rows = w_qkv.shape[0]

    def exchange(value, step):
        pairs = [(i, i // share * share + (i % share + step) % share) for i in range(planes)]
        return lax.ppermute(value, "rep", pairs)

    def with_group(value):
        return jnp.stack([value] + [exchange(value, step) for step in range(1, share)])

    def gather_ranks(value):
        return lax.all_gather(value, "ep", axis=0)

    order = shift_order(planes)
    in_parts, out_parts = (
        {
            step: lax.dynamic_index_in_dim(weight, (own + step) % share, 0, keepdims=False)
            for step in [0] + order
        }
        for weight in (w_in, w_out)
    )

    def send(parts, steps):
        return {step: shift_rep(parts[step], step) for step in steps}

    stream = gather_ranks(tokens)
    out_rows = [w_o] + [shift_rep(w_o, step) for step in range(1, planes)]
    upstream_group = with_group(cotangent)
    out_pieces = {0: out_parts[0], **send(out_parts, order[:1])}
    slab = jnp.concatenate(
        [
            w_qkv.reshape(dense_rows, 3, ranks, width)
            .transpose(2, 0, 1, 3)
            .reshape(ranks, dense_rows, 3 * width),
            jnp.broadcast_to(
                jnp.concatenate(
                    [
                        w_router,
                        norm_gains.reshape(dense_rows, 2),
                        jnp.zeros((dense_rows, PAD - experts - 2), bf16),
                    ],
                    axis=1,
                )[None],
                (ranks, dense_rows, PAD),
            ),
        ],
        axis=2,
    )
    slab = lax.all_to_all(slab, "ep", split_axis=0, concat_axis=0, tiled=True)
    slab = slab.reshape(ranks * dense_rows, 3 * width + PAD)
    out_rows, upstream_group, out_pieces, slab = lax.optimization_barrier(
        (out_rows, upstream_group, out_pieces, slab)
    )
    gathered = gather_ranks(jnp.concatenate(out_rows, axis=0))
    slab = ring_rep(slab)
    router = slab[:, 3 * width :]
    gain_pair = router[:, experts : experts + 2].reshape(-1).astype(f32)
    first_gain = gain_pair[None, :D]
    second_gain = gain_pair[None, D:]
    in_parts, out_parts = after((in_parts, out_parts), slab)
    in_pieces = {0: in_parts[0], **send(in_parts, order[:1])}
    out_pieces.update(send(out_parts, order[1:2]))

    segment = segments[0]
    cosine, sine = jax.vmap(lambda one: rope_tables(doc_positions(one), HD))(segment)
    sine = jnp.where(jnp.arange(HD) < HD // 2, -sine, sine)
    tables = (cosine, sine, segment[:, :, None], segment[:, None, :], qk_gains)
    stream, tables = lax.optimization_barrier((stream, tables))
    normed, proj = project(stream, first_gain, slab)
    proj = proj.reshape(ranks, micro, rows, 3 * width)
    upstream_all = gather_ranks(after(upstream_group, proj))
    mixed_h, query, keys, values, lses = attention_forward(proj, *tables)
    mixed = lax.all_to_all(mixed_h, "ep", split_axis=0, concat_axis=3, tiled=True)
    mixed = mixed.reshape(mine, D)
    hidden, payload, gates = route(
        where[1:2], planes, mixed, tokens, gathered, second_gain, router, routes, experts
    )
    normed_two = payload[:, :D]
    payload, in_pieces, out_pieces = lax.optimization_barrier((payload, in_pieces, out_pieces))
    payload = with_group(payload)
    payload, in_parts, out_parts = lax.optimization_barrier((payload, in_parts, out_parts))
    in_pieces.update(send(in_parts, order[1:]))
    in_pieces, out_parts = lax.optimization_barrier((in_pieces, out_parts))
    out_pieces.update(send(out_parts, order[2:]))
    in_pieces = [in_pieces[step] for step in range(planes)]
    out_pieces = [out_pieces[step] for step in range(planes)]
    payload = gather_ranks(payload)

    shape = (ranks, share, micro, rows, -1)
    rows_in, tail, both, active, grad_produced, up_rows, places = expert_forward(
        where, payload.reshape(shape), upstream_all.reshape(shape), in_pieces, slots, experts
    )
    in_rows = micro * ranks * slots
    out_cut = weight_gradient(
        where, planes, active.reshape(in_rows, FF), [grad_produced.reshape(in_rows, D)]
    )

    def sum_rep(parts):
        sums = [
            sum(parts[step].astype(f32) for step in range(first, planes, share))
            for first in range(share)
        ]
        return jnp.stack(
            [
                sum(jnp.where((own - step) % share == j, sums[step], 0.0) for step in range(share))
                for j in range(share)
            ]
        )

    tail, out_cut = lax.optimization_barrier((tail, out_cut))
    out_sent = send(out_cut, order)
    back = []
    returned = []

    def scatter_ranks(value):
        return lax.psum_scatter(value, "ep", scatter_dimension=0)

    def exchange_back(value):
        return [value[0]] + [exchange(value[step], share - step) for step in range(1, share)]

    for step in range(micro):
        back.append(
            expert_backward(
                step, where, tail, both, active, grad_produced, up_rows, places, in_pieces,
                out_pieces, share, rows, experts,
            )
        )
        returned.append(scatter_ranks(back[step][2]))
        tail, out_sent[order[step]] = after((tail, out_sent[order[step]]), back[step][2])
    rows_in = after(rows_in, tail)
    in_cut = weight_gradient(
        where,
        planes,
        rows_in.reshape(in_rows, D),
        [back[step][3].reshape(in_rows // micro, 2 * FF) for step in range(micro)],
    )
    in_sent = {}

    def swap(value, step):
        return lax.ppermute(value, "ep", [(i, i ^ step) for i in range(ranks)])

    def pair_sum(keep, give):
        return (keep.astype(f32) + swap(give, 1).astype(f32)).astype(bf16)

    def cross(value):
        parts = []
        for step in range(ranks // 2):
            part = lax.dynamic_index_in_dim(value, rank // 2 ^ step, 0, keepdims=False)
            parts.append(swap(part, 2 * step) if step else part)
        return parts

    def total(parts):
        return sum(part.astype(f32) for part in parts)

    grad_inputs, branches, logit_grads, grad_projs = [], [], [], []
    gain_two_sum = gain_one_sum = qk_sum = 0.0
    in_cut, mixtures, out_sent = lax.optimization_barrier(
        (in_cut, [part[:2] for part in back], out_sent)
    )
    mixtures = [pair_sum(*part) for part in mixtures]
    crossed = []
    releases = [order[:1]] + [[]] * (micro - 2) + [order[1:-1]]
    for step in range(micro):
        at = slice(step * rows, (step + 1) * rows)
        parts = after(returned[step], [one[2] for one in grad_inputs])
        parts, in_sent, crossed = lax.optimization_barrier((parts, in_sent, crossed))
        parts = exchange_back(parts)
        parts, in_cut, mixtures = lax.optimization_barrier((parts, in_cut, mixtures))
        in_sent.update(send(in_cut, releases[step]))
        if step == micro - 1:
            crossed.append(cross(mixtures[step]))
        grad_hidden, grad_branch, grad_mixed, grad_logits, gain_two = hidden_backward(
            where[1:2], planes, parts, hidden[at], gates[at], cotangent[at], second_gain,
            router, gathered, experts,
        )
        branches.append(grad_branch)
        logit_grads.append(grad_logits)
        gain_two_sum = gain_two_sum + gain_two
        grad_mixed = lax.all_to_all(grad_mixed, "ep", split_axis=1, concat_axis=0, tiled=True)
        if step < micro - 1:
            grad_mixed, mixtures = lax.optimization_barrier((grad_mixed, mixtures))
            crossed.append(cross(mixtures[step]))
        grad_proj, grad_qk = attention_backward(
            step, proj, *tables, query, keys, values, lses, grad_mixed
        )
        qk_sum = qk_sum + grad_qk.reshape(-1)
        if step == micro - 1:
            last = in_cut[order[-1]]
            half = last.shape[0] // 2
            grad_proj, in_sent, last, crossed = lax.optimization_barrier(
                (grad_proj, in_sent, last, crossed)
            )
            last_sent = [shift_rep(last[:half], order[-1])]
        grad_projs.append(grad_proj)
        grad_normed, gain_one = project_backward(step, grad_proj, stream, slab)
        gain_one_sum = gain_one_sum + gain_one
        grad_inputs.append(
            (
                at,
                grad_hidden,
                grad_normed,
                lax.psum_scatter(grad_normed, "ep", scatter_dimension=0, tiled=True),
            )
        )
    branches = after(jnp.concatenate(branches, axis=0), grad_normed)
    out_sum = dot(mixed, branches, ((0,), (0,))).astype(bf16)
    out_sum = out_sum.reshape(planes, ranks // 2, 2, dense_rows, D)
    out_sum = pair_sum(
        *(
            lax.dynamic_index_in_dim(out_sum, rank % 2 ^ other, 2, keepdims=False).transpose(
                1, 0, 2, 3
            )
            for other in range(2)
        )
    )

    router_sum = dot(normed_two, jnp.concatenate(logit_grads, axis=0), ((0,), (0,)))
    qk_columns = qk_sum.shape[0] // dense_rows
    small = jnp.concatenate(
        [
            router_sum[:, :experts],
            jnp.concatenate([gain_one_sum, gain_two_sum], axis=1).reshape(D, 2),
            jnp.tile(qk_sum.reshape(dense_rows, qk_columns), (planes * ranks, 1)),
        ],
        axis=1,
    )
    count = small.shape[1]

    def halves(value):
        high, low = two_parts(value)
        blank = jnp.zeros((value.shape[0], PAD - 2 * count), bf16)
        return jnp.concatenate([high, low, blank], axis=1)

    def joined(value):
        return value[..., :count].astype(f32) + value[..., count : 2 * count].astype(f32)

    grad_projs, out_sum = lax.optimization_barrier((grad_projs, out_sum))
    out_crossed = cross(out_sum)
    packed = weight_gradient(
        where,
        planes,
        normed.reshape(ranks * mine, D),
        [jnp.stack(grad_projs, axis=1).reshape(ranks * mine, 3 * width)],
        halves(small),
    )
    packed, last_sent, last = lax.optimization_barrier((packed, last_sent, last))
    packed_sent = [packed[0]] + [shift_rep(packed[step], step) for step in range(1, planes)]
    last_sent = last_sent + [shift_rep(last[half:], order[-1])]
    packed_sent, last_sent = lax.optimization_barrier((packed_sent, last_sent))
    mixture = []
    for parts in crossed:
        parts = total(parts)
        mixture.append(parts[0] + total(exchange_back(parts.astype(bf16))[1:]))
    output = (hidden + jnp.concatenate(mixture, axis=0)).astype(bf16)
    grad_tokens = []
    for at, grad_hidden, _, grad_normed in grad_inputs:
        grad_normed = after(grad_normed, packed_sent)
        own_stream = tokens[at].astype(f32)
        grad_tokens.append(
            grad_hidden
            + rms_backward(
                own_stream, inverse_rms(own_stream), first_gain, grad_normed.astype(f32)
            )
        )
    in_sent[order[-1]] = jnp.concatenate(last_sent, axis=0)
    main = total([part[:, : 3 * width] for part in packed_sent]).astype(bf16)
    small = sum(joined(part[:, 3 * width :]) for part in packed_sent)
    packed = jnp.concatenate([main, halves(small)], axis=1).reshape(ranks, dense_rows, -1)
    packed = lax.all_to_all(packed, "ep", split_axis=0, concat_axis=0, tiled=True)
    main = packed[..., : 3 * width].astype(f32)
    small = jnp.sum(joined(packed[..., 3 * width :]), axis=0)
    grad_w_qkv = (
        main.reshape(ranks, dense_rows, 3, width).transpose(1, 2, 0, 3).reshape(dense_rows, 3 * D)
    )
    grad_w_out = sum_rep({0: out_cut[0], **out_sent})
    grad_w_in = sum_rep({0: in_cut[0], **in_sent})
    out_sum = total(out_crossed)
    grad_w_o = lax.dynamic_index_in_dim(out_sum, plane, 0, keepdims=False)
    out_sum = out_sum.astype(bf16)
    for step in range(1, planes):
        part = lax.dynamic_index_in_dim(out_sum, (plane + step) % planes, 0, keepdims=False)
        grad_w_o = grad_w_o + shift_rep(part, step).astype(f32)
    return (
        output,
        jnp.concatenate(grad_tokens, axis=0),
        grad_w_qkv,
        grad_w_o,
        small[:, :experts],
        small[:, experts : experts + 2].reshape(-1),
        small[:, experts + 2 :].reshape(-1),
        grad_w_in,
        grad_w_out,
    )


def solution(mesh):
    placed = (
        P(("rep", "ep"), None),
        P(("rep", "ep"), None),
        P(("rep", "ep"), None),
        P(("rep", "ep"), None),
        P(("rep", "ep"), None),
        P(("rep", "ep")),
        P(),
        P("ep", "rep", None),
        P("ep", "rep", None),
        P("rep", None, None),
        P(("rep", "ep"), None),
    )
    return jax.shard_map(
        on_device,
        mesh=mesh,
        in_specs=placed,
        out_specs=(
            P(("rep", "ep"), None),
            P(("rep", "ep"), None),
            P(("rep", "ep"), None),
            P(("rep", "ep"), None),
            P(("rep", "ep"), None),
            P(("rep", "ep")),
            P(),
            P("ep", "rep", None),
            P("ep", "rep", None),
        ),
        check_vma=False,
    )
```

```python
import math

import jax
import jax.numpy as jnp
from jax import lax
from jax.experimental import pallas as pl
from jax.experimental.pallas import tpu as pltpu
from jax.sharding import PartitionSpec as P

D = 2048
HEADS = 16
HD = 128
FF = 1024
TOP = 8
HALF = 512
PAD = 128

epsilon = 1e-06
rope_base = 50000.0
bf16 = jnp.bfloat16
f32 = jnp.float32


def dot(a, b, dims=((1,), (0,))):
    return lax.dot_general(a, b, (dims, ((), ())), preferred_element_type=f32)


def inverse_rms(value):
    return lax.rsqrt(jnp.mean(value * value, axis=-1, keepdims=True) + epsilon)


def rms_backward(value, inverse, gain, grad):
    scaled = grad * gain
    inner = jnp.mean(scaled * value, axis=-1, keepdims=True)
    return inverse * (scaled - value * (inverse * inverse * inner))


def doc_positions(segment):
    index = jnp.arange(segment.shape[0], dtype=jnp.int32)
    change = jnp.concatenate([jnp.ones((1,), dtype=jnp.bool_), segment[1:] != segment[:-1]])
    start = lax.cummax(jnp.where(change, index, 0), axis=0)
    return index - start


def rope_tables(position, width):
    steps = jnp.arange(width // 2, dtype=f32) * (2.0 / width)
    rates = jnp.exp(-steps * math.log(rope_base))
    angle = position.astype(f32)[:, None] * rates[None, :]
    angle = jnp.concatenate([angle, angle], axis=-1)
    return (jnp.cos(angle), jnp.sin(angle))


def norm_rope(value, gain, cosine, sine):
    inverse = lax.rsqrt(jnp.mean(value * value, axis=1, keepdims=True) + epsilon)
    value = value * inverse * gain
    return value * cosine + pltpu.roll(value, HD // 2, 1) * sine


def norm_rope_back(value, gain, cosine, sine, grad):
    inverse = lax.rsqrt(jnp.mean(value * value, axis=1, keepdims=True) + epsilon)
    grad = grad * cosine + pltpu.roll(grad * sine, HD // 2, 1)
    normal = value * inverse
    scaled = grad * gain
    inner = jnp.mean(scaled * normal, axis=1, keepdims=True)
    return inverse * (scaled - normal * inner), jnp.sum(grad * normal, axis=0, keepdims=True)


def kept_scores(query, keys, q_seg, k_seg, start):
    scores = dot(query, keys, ((1,), (1,))) * (1.0 / math.sqrt(HD))
    q_index = start + lax.broadcasted_iota(jnp.int32, scores.shape, 0)
    k_index = lax.broadcasted_iota(jnp.int32, scores.shape, 1)
    keep = (jnp.abs(q_index - k_index) <= HALF) & (q_seg == k_seg)
    return jnp.where(keep, scores, -1e30)


BIG = 100 * 1024 * 1024 // 2


def forward_kernel(
    heads, proj, cosine, sine, seg_column, seg_row, gains, mixed, query, keys, values, lses
):
    ranks, _, rows, _ = proj.shape
    length = ranks * rows
    q_block = 2 * rows
    k_seg = seg_row[0]
    for head in range(heads):
        at = slice(head * HD, (head + 1) * HD)

        def raw(part):
            first = (part * heads + head) * HD
            return proj[:, 0, :, first : first + HD].reshape(length, HD)

        query[0, :, at] = norm_rope(raw(0), gains[0:1], cosine[0], sine[0]).astype(bf16)
        keys[0, :, at] = norm_rope(raw(1), gains[1:2], cosine[0], sine[0]).astype(bf16)
        values[0, :, at] = raw(2).astype(bf16)

        @pl.loop(0, length // q_block)
        def one_block(number, head=head, at=at):
            start = pl.multiple_of(number * q_block, q_block)
            here = pl.ds(start, q_block)
            scores = kept_scores(
                query[0, here, at], keys[0, :, at], seg_column[0, here], k_seg, start
            )
            top = jnp.max(scores, axis=1, keepdims=True)
            weights = jnp.exp(scores - top)
            total = jnp.sum(weights, axis=1, keepdims=True)
            lses[0, head, here] = top + jnp.log(total)
            weights = (weights * (1.0 / total)).astype(bf16)
            result = dot(weights, values[0, :, at]).astype(bf16)
            mixed[pl.ds(number * 2, 2), 0, :, at] = result.reshape(2, rows, HD)


def backward_kernel(
    heads, proj, cosine, sine, seg_column, seg_row, gains, query, keys, values, lses, grad_mixed,
    grad_proj, grad_gains, grad_q, grad_k, grad_v,
):
    ranks, _, rows, _ = proj.shape
    length = ranks * rows
    q_block = 2 * rows
    k_seg = seg_row[0]
    scale = 1.0 / math.sqrt(HD)
    sum_q = jnp.zeros((1, HD), f32)
    sum_k = jnp.zeros((1, HD), f32)
    for head in range(heads):
        at = slice(head * HD, (head + 1) * HD)
        grad_k[...] = jnp.zeros_like(grad_k)
        grad_v[...] = jnp.zeros_like(grad_v)

        @pl.loop(0, length // q_block)
        def one_block(number, head=head, at=at):
            start = pl.multiple_of(number * q_block, q_block)
            here = pl.ds(start, q_block)
            q_rows = query[0, here, at]
            g_rows = grad_mixed[here, at]
            k_all = keys[0, :, at]
            scores = kept_scores(q_rows, k_all, seg_column[0, here], k_seg, start)
            weights = jnp.exp(scores - lses[0, head, here])
            grad_weights = dot(g_rows, values[0, :, at], ((1,), (1,)))
            delta = jnp.sum(weights * grad_weights, axis=1, keepdims=True)
            grad_scores = (weights * (grad_weights - delta)).astype(bf16)
            grad_q[here] = dot(grad_scores, k_all) * scale
            grad_k[...] += dot(grad_scores, q_rows, ((0,), (0,)))
            grad_v[...] += dot(weights.astype(bf16), g_rows, ((0,), (0,)))

        def rounded(value):
            return value.astype(bf16).astype(f32)

        def raw(part):
            first = (part * heads + head) * HD
            return proj[:, 0, :, first : first + HD].reshape(length, HD)

        def put(part, value):
            first = (part * heads + head) * HD
            grad_proj[:, :, first : first + HD] = value.astype(bf16).reshape(ranks, rows, HD)

        back_q, gain_q = norm_rope_back(
            raw(0), gains[0:1], cosine[0], sine[0], rounded(grad_q[...])
        )
        back_k, gain_k = norm_rope_back(
            raw(1), gains[1:2], cosine[0], sine[0], rounded(grad_k[...] * scale)
        )
        sum_q, sum_k = sum_q + gain_q, sum_k + gain_k
        put(0, back_q)
        put(1, back_k)
        put(2, grad_v[...])
    grad_gains[0:1] = sum_q
    grad_gains[1:2] = sum_k


def fixed(shape):
    return pl.BlockSpec(shape, lambda *_: (0,) * len(shape), pipeline_mode=pl.Buffered(1))


def leading(shape):
    return pl.BlockSpec((1,) + shape[1:], lambda i: (i,) + (0,) * (len(shape) - 1))


def params():
    return pltpu.CompilerParams(vmem_limit_bytes=BIG)


def cost(products):
    return pl.CostEstimate(flops=20 * products, bytes_accessed=0, transcendentals=0)


def out(shape, dtype=bf16):
    return jax.ShapeDtypeStruct(shape, dtype)


def attention_forward(proj, cosine, sine, seg_column, seg_row, gains):
    ranks, micro, rows, width = proj.shape
    length = ranks * rows
    width = width // 3
    heads = width // HD
    part = out((micro, length, width))
    by_rank = lambda n: pl.BlockSpec((ranks, 1, rows, n), lambda i: (0, i, 0, 0))
    lses = out((micro, heads, length, 1), f32)
    return pl.pallas_call(
        lambda *refs: forward_kernel(heads, *refs),
        grid=(micro,),
        in_specs=[by_rank(3 * width)]
        + [leading(v.shape) for v in (cosine, sine, seg_column, seg_row)]
        + [fixed(gains.shape)],
        out_specs=[by_rank(width)] + [leading(part.shape)] * 3 + [leading(lses.shape)],
        out_shape=[out((ranks, micro, rows, width)), part, part, part, lses],
        compiler_params=params(),
    )(proj, cosine, sine, seg_column, seg_row, gains)


def attention_backward(
    step, proj, cosine, sine, seg_column, seg_row, gains, query, keys, values, lses, grad_mixed
):
    ranks, micro, rows, width = proj.shape
    length = ranks * rows
    heads = width // 3 // HD

    def part(value):
        return pl.BlockSpec((1,) + value.shape[1:], lambda i: (step,) + (0,) * (value.ndim - 1))

    return pl.pallas_call(
        lambda *refs: backward_kernel(heads, *refs),
        grid=(1,),
        in_specs=[pl.BlockSpec((ranks, 1, rows, width), lambda i: (0, step, 0, 0))]
        + [part(v) for v in (cosine, sine, seg_column, seg_row)]
        + [fixed(gains.shape)]
        + [part(v) for v in (query, keys, values, lses)]
        + [fixed(grad_mixed.shape)],
        out_specs=[fixed((ranks, rows, width)), fixed((2, HD))],
        out_shape=[out((ranks, rows, width)), out((2, HD), f32)],
        scratch_shapes=[pltpu.VMEM((length, HD), f32)] * 3,
        compiler_params=params(),
    )(
        proj, cosine, sine, seg_column, seg_row, gains, query, keys, values, lses, grad_mixed
    )


def project(tokens, gain, slab):
    ranks, count, _ = tokens.shape
    width = slab.shape[1] - PAD

    def kernel(value, gain, weight, normed, proj):
        value = value[0].astype(f32)
        result = (value * inverse_rms(value) * gain[...]).astype(bf16)
        normed[0] = result
        proj[0] = dot(result, weight[:, :width])

    return pl.pallas_call(
        kernel,
        grid=(ranks,),
        in_specs=[leading((ranks, count, D)), fixed((1, D)), fixed(slab.shape)],
        out_specs=[leading((ranks, count, D)), leading((ranks, count, width))],
        out_shape=[out((ranks, count, D)), out((ranks, count, width), f32)],
        compiler_params=params(),
    )(tokens, gain, slab)


TILE = 512


def tiles(count):
    return pl.loop(0, count // TILE)


def tile(number):
    return pl.ds(pl.multiple_of(number * TILE, TILE), TILE)


HBM = pl.BlockSpec(memory_space=pl.ANY)


def copies(pairs, sems):
    started = [
        pltpu.make_async_copy(source, target, sems.at[place])
        for place, (source, target) in enumerate(pairs)
    ]
    for copy in started:
        copy.start()

    def wait():
        for copy in started:
            copy.wait()

    return wait


def plane_pairs(plane, pieces, target):
    planes = len(pieces)
    rows = target.shape[0] // planes
    return [
        (piece, target.at[pl.ds((plane + planes - step) % planes * rows, rows)])
        for step, piece in enumerate(pieces)
    ]


def out_weight_pairs(plane, planes, gathered, target):
    ranks = gathered.shape[0]
    rows = D // (planes * ranks)
    return [
        (
            gathered.at[rank, pl.ds(step * rows, rows)],
            target.at[pl.ds(((plane + planes - step) % planes * ranks + rank) * rows, rows)],
        )
        for rank in range(ranks)
        for step in range(planes)
    ]


def route(plane, planes, mixed, tokens, gathered, gain, router, routes, experts):
    count = tokens.shape[0]
    pieces = planes * gathered.shape[0]

    def kernel(
        plane, mixed, tokens, gathered, gain, router, routes, hidden, payload, gates,
        out_weight, sems,
    ):
        copies(out_weight_pairs(plane[0], planes, gathered, out_weight), sems)()

        @tiles(D)
        def _(number):
            at = tile(number)
            hidden[:, at] = tokens[:, at].astype(f32) + dot(mixed[...], out_weight[:, at])

        value = hidden[...]
        normed = (value * inverse_rms(value) * gain[...]).astype(bf16)
        payload[:, :D] = normed
        logits = dot(normed, router[...])
        column = lax.broadcasted_iota(jnp.int32, logits.shape, 1)
        routed = column == routes[:, 0:1]
        for choice in range(1, TOP):
            routed = routed | (column == routes[:, choice : choice + 1])
        logits = jnp.where(routed, logits, -1e30)
        weights = jnp.exp(logits - jnp.max(logits, axis=1, keepdims=True))
        weights = jnp.where(routed, weights, 0.0)
        weights = weights / jnp.sum(weights, axis=1, keepdims=True)
        gates[...] = weights
        high = weights.astype(bf16).astype(f32)
        payload[:, D:] = (high + pltpu.roll(weights - high, experts, 1)).astype(bf16)

    shapes = [out((count, D), f32), out((count, D + PAD)), out((count, PAD), f32)]
    return pl.pallas_call(
        kernel,
        grid_spec=pltpu.PrefetchScalarGridSpec(
            num_scalar_prefetch=1,
            grid=(1,),
            in_specs=[
                HBM if value is gathered else fixed(value.shape)
                for value in (mixed, tokens, gathered, gain, router, routes)
            ],
            out_specs=[fixed(shape.shape) for shape in shapes],
            scratch_shapes=[pltpu.VMEM((D, D), bf16), pltpu.SemaphoreType.DMA((pieces,))],
        ),
        out_shape=shapes,
        compiler_params=params(),
    )(plane, mixed, tokens, gathered, gain, router, routes)


def lane(value, number):
    column = lax.broadcasted_iota(jnp.int32, value.shape, 1)
    return jnp.sum(jnp.where(column == number, value.astype(f32), 0.0), axis=1, keepdims=True)


def one_hot(slot, slots):
    place = lax.broadcasted_iota(jnp.int32, (slots, slot.shape[1]), 0).astype(f32)
    return (place == slot).astype(bf16)


def expert_forward(where, payload, upstream, in_pieces, slots, experts):
    ranks, share, micro, rows, _ = payload.shape
    count = share * rows
    block = 2 * slots

    planes = len(in_pieces)

    def kernel(where, payload, upstream, *refs):
        (
            rows_in, tail, both, active, grad_produced, up_rows, places, in_weight, sems
        ) = refs[planes:]
        number = where[0]

        @pl.when((pl.program_id(0) == 0) & (pl.program_id(1) == 0))
        def _():
            copies(plane_pairs(where[1], refs[:planes], in_weight), sems)()

        for part in range(2):
            here = slice(part * slots, (part + 1) * slots)
            value = payload[part].reshape(count, D + PAD)
            marks = value[:, D:]
            first = lax.broadcasted_iota(jnp.int32, (8, PAD), 1) == number
            taken = dot(first.astype(bf16), marks, ((1,), (1,))) > 0.0
            before = lax.broadcasted_iota(jnp.int32, (count, count), 0)
            behind = lax.broadcasted_iota(jnp.int32, (count, count), 1)
            slot = dot(taken.astype(bf16), (before < behind).astype(bf16))
            select = one_hot(jnp.where(taken, slot, -1.0)[0:1], slots)
            wide = jnp.broadcast_to(lane(marks, number) > 0.0, (count, PAD))
            slot = dot((before > behind).astype(bf16), wide.astype(bf16))
            places[0, 0, part] = jnp.where(wide, slot, -1.0)
            rows_in[0, 0, here] = dot(select, value[:, :D]).astype(bf16)
            marks = dot(select, marks)
            tail[0, 0, here] = marks
            gate = lane(marks, number) + lane(marks, experts + number)
            picked = dot(select, upstream[part].reshape(count, D))
            up_rows[0, 0, here] = picked.astype(bf16)
            grad_produced[0, 0, here] = (gate * picked).astype(bf16)

        for number in range(FF // TILE):
            at = slice(number * TILE, (number + 1) * TILE)
            more = slice(FF + number * TILE, FF + (number + 1) * TILE)
            gate_part = dot(rows_in[0, 0], in_weight[:, at])
            up_part = dot(rows_in[0, 0], in_weight[:, more])
            both[0, 0, :, at] = gate_part
            both[0, 0, :, more] = up_part
            active[0, 0, :, at] = (
                gate_part / (1.0 + jnp.exp(-gate_part)) * up_part
            ).astype(bf16)

    def tokens_spec(width):
        return pl.BlockSpec((2, share, 1, rows, width), lambda m, b, _: (b, 0, m, 0, 0))

    pairs = ranks // 2
    shapes = [
        out((micro, pairs, block, D)),
        out((micro, pairs, block, PAD), f32),
        out((micro, pairs, block, 2 * FF), f32),
        out((micro, pairs, block, FF)),
        out((micro, pairs, block, D)),
        out((micro, pairs, block, D)),
        out((micro, pairs, 2, count, PAD), f32),
    ]
    return pl.pallas_call(
        kernel,
        grid_spec=pltpu.PrefetchScalarGridSpec(
            num_scalar_prefetch=1,
            grid=(micro, pairs),
            in_specs=[tokens_spec(D + PAD), tokens_spec(D)] + [HBM] * planes,
            out_specs=[
                pl.BlockSpec(
                    (1, 1) + s.shape[2:], lambda m, b, _, n=len(s.shape): (m, b) + (0,) * (n - 2)
                )
                for s in shapes
            ],
            scratch_shapes=[pltpu.VMEM((D, 2 * FF), bf16), pltpu.SemaphoreType.DMA((planes,))],
        ),
        out_shape=shapes,
        cost_estimate=cost(micro * pairs * block * D * (2 * FF + 2 * count)),
        compiler_params=params(),
    )(where, payload, upstream, *in_pieces)


def expert_backward(
    step, where, tail, both, active, grad_produced, up_rows, places, in_pieces, out_pieces,
    share, rows, experts,
):
    pairs, block = tail.shape[1:3]
    slots = block // 2
    count = places.shape[3]

    planes = len(in_pieces)

    def kernel(where, tail, both, active, grad_produced, up_rows, places, *refs):
        keep, give, grad_tokens, grad_both, in_weight, out_weight, sems = refs[2 * planes :]
        number = where[0]
        odd = where[2] == 1

        @pl.when(pl.program_id(0) == 0)
        def _():
            copies(
                plane_pairs(where[1], refs[:planes], in_weight)
                + plane_pairs(where[1], refs[planes : 2 * planes], out_weight),
                sems,
            )()

        gate = lane(tail[0, 0], number) + lane(tail[0, 0], experts + number)
        place = lax.broadcasted_iota(jnp.int32, (count, slots), 1).astype(f32)
        selects = [(places[0, 0, part][:, 0:1] == place).astype(bf16) for part in range(2)]

        def spread(value):
            return [
                dot(selects[part], value[part * slots : (part + 1) * slots])
                .astype(bf16)
                .reshape(share, rows, -1)
                for part in range(2)
            ]

        grad_gate = jnp.zeros((block, 1), f32)
        for tile in range(D // TILE):
            at = slice(tile * TILE, (tile + 1) * TILE)
            produced = dot(active[0, 0], out_weight[:, at]).astype(bf16).astype(f32)
            even_rank, odd_rank = spread((gate * produced).astype(bf16))
            keep[0, :, :, at] = jnp.where(odd, odd_rank, even_rank)
            give[0, :, :, at] = jnp.where(odd, even_rank, odd_rank)
            grad_gate = grad_gate + jnp.sum(
                up_rows[0, 0, :, at].astype(f32) * produced, axis=1, keepdims=True
            )

        for tile in range(FF // TILE):
            at = slice(tile * TILE, (tile + 1) * TILE)
            more = slice(FF + tile * TILE, FF + (tile + 1) * TILE)
            grad_active = dot(grad_produced[0, 0], out_weight[at, :], ((1,), (1,)))
            grad_active = grad_active.astype(bf16).astype(f32)
            gate_part = both[0, 0, :, at]
            up_part = both[0, 0, :, more]
            sigma = 1.0 / (1.0 + jnp.exp(-gate_part))
            grad_both[0, :, at] = (
                grad_active * up_part * (sigma * (1.0 + gate_part * (1.0 - sigma)))
            ).astype(bf16)
            grad_both[0, :, more] = (grad_active * (gate_part * sigma)).astype(bf16)

        for tile in range(D // TILE):
            at = slice(tile * TILE, (tile + 1) * TILE)
            grad_rows = dot(grad_both[0], in_weight[at, :], ((1,), (1,))).astype(bf16)
            grad_tokens[0, :, :, at], grad_tokens[1, :, :, at] = spread(grad_rows)

        high = grad_gate.astype(bf16).astype(f32)
        column = lax.broadcasted_iota(jnp.int32, (block, PAD), 1)
        extra = jnp.where(column == number, high, 0.0)
        extra = jnp.where(column == experts + number, grad_gate - high, extra)
        grad_tokens[0, :, :, D:], grad_tokens[1, :, :, D:] = spread(extra.astype(bf16))

    def part(value):
        return pl.BlockSpec(
            (1, 1) + value.shape[2:], lambda b, _: (step, b) + (0,) * (value.ndim - 2)
        )

    def tokens_spec(count, width):
        return pl.BlockSpec((count, share, rows, width), lambda b, _: (b, 0, 0, 0))

    return pl.pallas_call(
        kernel,
        grid_spec=pltpu.PrefetchScalarGridSpec(
            num_scalar_prefetch=1,
            grid=(pairs,),
            in_specs=[part(v) for v in (tail, both, active, grad_produced, up_rows, places)]
            + [HBM] * (2 * planes),
            out_specs=[
                tokens_spec(1, D),
                tokens_spec(1, D),
                tokens_spec(2, D + PAD),
                pl.BlockSpec((1, block, 2 * FF), lambda b, _: (b, 0, 0)),
            ],
            scratch_shapes=[
                pltpu.VMEM((D, 2 * FF), bf16),
                pltpu.VMEM((FF, D), bf16),
                pltpu.SemaphoreType.DMA((2 * planes,)),
            ],
        ),
        out_shape=[
            out((pairs, share, rows, D)),
            out((pairs, share, rows, D)),
            out((2 * pairs, share, rows, D + PAD)),
            out((pairs, block, 2 * FF)),
        ],
        cost_estimate=cost(pairs * block * D * (4 * FF + 2 * count)),
        compiler_params=params(),
    )(
        where, tail, both, active, grad_produced, up_rows, places, *in_pieces, *out_pieces
    )


def weight_gradient(where, planes, left, rights, tail=None):
    count, width = left.shape
    parts = len(rights)
    part_rows = count // parts
    columns = rights[0].shape[1]
    width = width // planes
    step = min(TILE, columns & -columns)
    tails = [] if tail is None else [tail]
    whole = columns + sum(value.shape[1] for value in tails)

    def of_plane(i, where):
        return (where[1] + i) % planes

    def kernel(where, left, *refs):
        rights, target = refs[:parts], refs[-1]
        for value in refs[parts:-1]:
            target[0, :, columns:] = value[...]
        for number in range(columns // step):
            at = slice(number * step, (number + 1) * step)
            target[0, :, at] = sum(
                dot(left[part * part_rows : (part + 1) * part_rows], right[:, at], ((0,), (0,)))
                for part, right in enumerate(rights)
            ).astype(bf16)

    return pl.pallas_call(
        kernel,
        grid_spec=pltpu.PrefetchScalarGridSpec(
            num_scalar_prefetch=1,
            grid=(planes,),
            in_specs=[pl.BlockSpec((count, width), lambda i, where: (0, of_plane(i, where)))]
            + [fixed(right.shape) for right in rights]
            + [
                pl.BlockSpec((width, value.shape[1]), lambda i, where: (of_plane(i, where), 0))
                for value in tails
            ],
            out_specs=pl.BlockSpec((1, width, whole), lambda i, _: (i, 0, 0)),
        ),
        out_shape=out((planes, width, whole)),
        cost_estimate=cost(count * planes * width * columns),
        compiler_params=params(),
    )(where, left, *rights, *tails)


def hidden_backward(
    plane, planes, parts, hidden, gates, upstream, gain, router, gathered, experts
):
    count = hidden.shape[0]
    terms = len(parts)

    def kernel(plane, *refs):
        parts = refs[:terms]
        hidden, gates, upstream, gain, router, gathered = refs[terms : terms + 6]
        (
            grad_hidden, grad_branch, grad_mixed, grad_logits, grad_gain, out_weight, sems
        ) = refs[terms + 6 :]
        wait = copies(out_weight_pairs(plane[0], planes, gathered, out_weight), sems)
        returned = sum(part[...].astype(f32) for part in parts)
        tail = returned[:, D:]
        grad_gates = gates[...] * (tail + pltpu.roll(tail, PAD - experts, 1))
        logits = grad_gates - gates[...] * jnp.sum(grad_gates, axis=1, keepdims=True)
        logits = logits.astype(bf16)
        grad_logits[...] = logits
        grad_normed = returned[:, :D] + dot(logits, router[...], ((1,), (1,)))
        value = hidden[...]
        inverse = inverse_rms(value)
        grad_gain[...] = jnp.sum(grad_normed * value * inverse, axis=0, keepdims=True)
        grad = upstream[...].astype(f32) + rms_backward(value, inverse, gain[...], grad_normed)
        grad_hidden[...] = grad
        grad_branch[...] = grad.astype(bf16)
        wait()

        @tiles(D)
        def _(number):
            at = tile(number)
            grad_mixed[:, at] = dot(grad_branch[...], out_weight[at, :], ((1,), (1,))).astype(bf16)

    shapes = [
        out((count, D), f32), out((count, D)), out((count, D)), out((count, PAD)),
        out((1, D), f32),
    ]
    args = (*parts, hidden, gates, upstream, gain, router, gathered)
    return pl.pallas_call(
        kernel,
        grid_spec=pltpu.PrefetchScalarGridSpec(
            num_scalar_prefetch=1,
            grid=(1,),
            in_specs=[HBM if value is gathered else fixed(value.shape) for value in args],
            out_specs=[fixed(shape.shape) for shape in shapes],
            scratch_shapes=[
                pltpu.VMEM((D, D), bf16),
                pltpu.SemaphoreType.DMA((planes * gathered.shape[0],)),
            ],
        ),
        out_shape=shapes,
        compiler_params=params(),
    )(plane, *args)


def project_backward(step, grad_proj, tokens, slab):
    ranks, rows, _ = grad_proj.shape
    width = slab.shape[1] - PAD

    def kernel(grad_proj, tokens, weight, grad_normed, grad_gain):
        value = tokens[0].astype(f32)
        inverse = inverse_rms(value)
        grad = dot(grad_proj[0], weight[:, :width], ((1,), (1,)))
        grad_normed[...] = grad.astype(bf16)

        @pl.when(pl.program_id(0) == 0)
        def _():
            grad_gain[...] = jnp.zeros_like(grad_gain)

        grad_gain[...] += jnp.sum(grad * value * inverse, axis=0, keepdims=True)

    return pl.pallas_call(
        kernel,
        grid=(ranks,),
        in_specs=[
            leading(grad_proj.shape),
            pl.BlockSpec((1, rows, D), lambda i: (i, step, 0)),
            fixed(slab.shape),
        ],
        out_specs=[pl.BlockSpec((rows, D), lambda i: (i, 0)), fixed((1, D))],
        out_shape=[out((ranks * rows, D)), out((1, D), f32)],
        compiler_params=params(),
    )(grad_proj, tokens, slab)


def shift_rep(value, step):
    count = lax.axis_size("rep")
    return lax.ppermute(value, "rep", [(i, (i + step) % count) for i in range(count)])


def after(value, *others):
    return lax.optimization_barrier((value,) + others)[0]


def two_parts(value):
    high = lax.reduce_precision(value, 8, 7)
    return high.astype(bf16), (value - high).astype(bf16)


def shift_order(count):
    return sorted(range(1, count), key=lambda step: (min(step, count - step), step))


def ring_rep(value, *work):
    count = lax.axis_size("rep")
    rank = lax.axis_index("rep")
    rows = value.shape[0]
    full = jnp.zeros((count * rows,) + value.shape[1:], value.dtype)
    full = lax.dynamic_update_slice_in_dim(full, value, rank * rows, 0)
    for step in range(1, count):
        value, work = lax.optimization_barrier((value, work)) if step == 2 else (value, work)
        value = shift_rep(value, 1)
        full = lax.dynamic_update_slice_in_dim(full, value, (rank - step) % count * rows, 0)
    return full, work


def on_device(
    tokens, cotangent, w_qkv, w_o, w_router, norm_gains, qk_gain, w_in, w_out, segments, routes
):
    planes = lax.axis_size("rep")
    ranks = lax.axis_size("ep")
    plane = lax.axis_index("rep")
    rank = lax.axis_index("ep")
    share = w_in.shape[0]
    own = plane % share
    experts = share * ranks
    where = jnp.stack([rank * share + own, plane, rank % 2]).astype(jnp.int32)
    micro = segments.shape[1]
    mine = tokens.shape[0]
    rows = mine // micro
    length = rows * ranks
    capacity = rows * TOP * 17 // (16 * experts)
    slots = -(-share * capacity // 16) * 16
    width = HEADS // ranks * HD
    qk_gains = qk_gain.astype(f32).reshape(2, HD)
    dense_rows = w_qkv.shape[0]

    def exchange(value, step):
        pairs = [(i, i // share * share + (i % share + step) % share) for i in range(planes)]
        return lax.ppermute(value, "rep", pairs)

    def with_group(value):
        return jnp.stack([value] + [exchange(value, step) for step in range(1, share)])

    def gather_ranks(value):
        return lax.all_gather(value, "ep", axis=0)

    order = shift_order(planes)
    in_parts, out_parts = (
        {
            step: lax.dynamic_index_in_dim(weight, (own + step) % share, 0, keepdims=False)
            for step in [0] + order
        }
        for weight in (w_in, w_out)
    )

    def send(parts, steps):
        return {step: shift_rep(parts[step], step) for step in steps}

    stream = gather_ranks(tokens)
    out_rows = [w_o] + [shift_rep(w_o, step) for step in range(1, planes)]
    upstream_group = with_group(cotangent)
    slab = jnp.concatenate(
        [
            w_qkv.reshape(dense_rows, 3, ranks, width)
            .transpose(2, 0, 1, 3)
            .reshape(ranks, dense_rows, 3 * width),
            jnp.broadcast_to(
                jnp.concatenate(
                    [
                        w_router,
                        norm_gains.reshape(dense_rows, 2),
                        jnp.zeros((dense_rows, PAD - experts - 2), bf16),
                    ],
                    axis=1,
                )[None],
                (ranks, dense_rows, PAD),
            ),
        ],
        axis=2,
    )
    slab = lax.all_to_all(slab, "ep", split_axis=0, concat_axis=0, tiled=True)
    slab = slab.reshape(ranks * dense_rows, 3 * width + PAD)
    out_rows, upstream_group, slab = lax.optimization_barrier((out_rows, upstream_group, slab))
    gathered = gather_ranks(jnp.concatenate(out_rows, axis=0))
    segment = segments[0]
    cosine, sine = jax.vmap(lambda one: rope_tables(doc_positions(one), HD))(segment)
    sine = jnp.where(jnp.arange(HD) < HD // 2, -sine, sine)
    tables = (cosine, sine, segment[:, :, None], segment[:, None, :], qk_gains)
    slab, (tables, in_parts, out_parts) = ring_rep(slab, tables, in_parts, out_parts)
    router = slab[:, 3 * width :]
    gain_pair = router[:, experts : experts + 2].reshape(-1).astype(f32)
    first_gain = gain_pair[None, :D]
    second_gain = gain_pair[None, D:]
    in_parts, out_parts, upstream_group, stream = after(
        (in_parts, out_parts, upstream_group, stream), slab
    )
    in_pieces = {0: in_parts[0], **send(in_parts, order[:1])}
    out_pieces = {0: out_parts[0], **send(out_parts, order[:2])}
    upstream_all = gather_ranks(upstream_group)

    normed, proj = project(stream, first_gain, slab)
    proj = proj.reshape(ranks, micro, rows, 3 * width)
    mixed_h, query, keys, values, lses = attention_forward(proj, *tables)
    mixed = lax.all_to_all(mixed_h, "ep", split_axis=0, concat_axis=3, tiled=True)
    mixed = mixed.reshape(mine, D)
    hidden, payload, gates = route(
        where[1:2], planes, mixed, tokens, gathered, second_gain, router, routes, experts
    )
    normed_two = payload[:, :D]
    payload, in_pieces, out_pieces = lax.optimization_barrier((payload, in_pieces, out_pieces))
    payload = with_group(payload)
    payload, in_parts, out_parts = lax.optimization_barrier((payload, in_parts, out_parts))
    in_pieces.update(send(in_parts, order[1:]))
    in_pieces, out_parts = lax.optimization_barrier((in_pieces, out_parts))
    out_pieces.update(send(out_parts, order[2:]))
    in_pieces = [in_pieces[step] for step in range(planes)]
    out_pieces = [out_pieces[step] for step in range(planes)]
    payload = gather_ranks(payload)

    shape = (ranks, share, micro, rows, -1)
    rows_in, tail, both, active, grad_produced, up_rows, places = expert_forward(
        where, payload.reshape(shape), upstream_all.reshape(shape), in_pieces, slots, experts
    )
    in_rows = micro * ranks * slots
    out_cut = weight_gradient(
        where, planes, active.reshape(in_rows, FF), [grad_produced.reshape(in_rows, D)]
    )

    def sum_rep(parts):
        sums = [
            sum(parts[step].astype(f32) for step in range(first, planes, share))
            for first in range(share)
        ]
        return jnp.stack(
            [
                sum(jnp.where((own - step) % share == j, sums[step], 0.0) for step in range(share))
                for j in range(share)
            ]
        )

    tail, out_cut = lax.optimization_barrier((tail, out_cut))
    out_sent = send(out_cut, order)
    back = []
    returned = []

    def scatter_ranks(value):
        return lax.psum_scatter(value, "ep", scatter_dimension=0)

    def exchange_back(value):
        return [value[0]] + [exchange(value[step], share - step) for step in range(1, share)]

    for step in range(micro):
        back.append(
            expert_backward(
                step, where, tail, both, active, grad_produced, up_rows, places, in_pieces,
                out_pieces, share, rows, experts,
            )
        )
        returned.append(scatter_ranks(back[step][2]))
        if step == 0:
            tail, out_sent[order[0]] = after((tail, out_sent[order[0]]), back[step][2])
        else:
            tail = after(tail, back[step][2])
    rows_in = after(rows_in, tail)
    in_cut = weight_gradient(
        where,
        planes,
        rows_in.reshape(in_rows, D),
        [back[step][3].reshape(in_rows // micro, 2 * FF) for step in range(micro)],
    )
    in_sent = {}

    def swap(value, step):
        return lax.ppermute(value, "ep", [(i, i ^ step) for i in range(ranks)])

    def pair_sum(keep, give):
        return (keep.astype(f32) + swap(give, 1).astype(f32)).astype(bf16)

    def cross(value):
        parts = []
        for step in range(ranks // 2):
            part = lax.dynamic_index_in_dim(value, rank // 2 ^ step, 0, keepdims=False)
            parts.append(swap(part, 2 * step) if step else part)
        return parts

    def total(parts):
        return sum(part.astype(f32) for part in parts)

    grad_inputs, branches, logit_grads, grad_projs = [], [], [], []
    gain_two_sum = gain_one_sum = qk_sum = 0.0
    in_cut, mixtures, out_sent = lax.optimization_barrier(
        (in_cut, [part[:2] for part in back], out_sent)
    )
    mixtures = [pair_sum(*part) for part in mixtures]
    crossed = []
    releases = [order[:1]] + [[]] * (micro - 2) + [order[1:-1]]
    for step in range(micro):
        at = slice(step * rows, (step + 1) * rows)
        parts = after(returned[step], [one[1] for one in grad_inputs])
        parts, in_sent, crossed = lax.optimization_barrier((parts, in_sent, crossed))
        parts = exchange_back(parts)
        parts, in_cut, mixtures = lax.optimization_barrier((parts, in_cut, mixtures))
        in_sent.update(send(in_cut, releases[step]))
        grad_hidden, grad_branch, grad_mixed, grad_logits, gain_two = hidden_backward(
            where[1:2], planes, parts, hidden[at], gates[at], cotangent[at], second_gain,
            router, gathered, experts,
        )
        branches.append(grad_branch)
        logit_grads.append(grad_logits)
        gain_two_sum = gain_two_sum + gain_two
        grad_mixed = lax.all_to_all(grad_mixed, "ep", split_axis=1, concat_axis=0, tiled=True)
        grad_mixed, mixtures = lax.optimization_barrier((grad_mixed, mixtures))
        crossed.append(cross(mixtures[step]))
        grad_proj, grad_qk = attention_backward(
            step, proj, *tables, query, keys, values, lses, grad_mixed
        )
        qk_sum = qk_sum + grad_qk.reshape(-1)
        if step == micro - 1:
            last = in_cut[order[-1]]
            half = last.shape[0] // 2
            grad_proj, in_sent, last, grad_inputs = lax.optimization_barrier(
                (grad_proj, in_sent, last, grad_inputs)
            )
            last_sent = [shift_rep(last[:half], order[-1])]
        grad_projs.append(grad_proj)
        grad_normed, gain_one = project_backward(step, grad_proj, stream, slab)
        gain_one_sum = gain_one_sum + gain_one
        grad_inputs.append(
            (
                grad_hidden,
                grad_normed,
                lax.psum_scatter(grad_normed, "ep", scatter_dimension=0, tiled=True),
            )
        )
    branches = after(jnp.concatenate(branches, axis=0), grad_normed)
    out_sum = dot(mixed, branches, ((0,), (0,))).astype(bf16)
    out_sum = out_sum.reshape(planes, ranks // 2, 2, dense_rows, D)
    out_sum = pair_sum(
        *(
            lax.dynamic_index_in_dim(out_sum, rank % 2 ^ other, 2, keepdims=False).transpose(
                1, 0, 2, 3
            )
            for other in range(2)
        )
    )

    router_sum = dot(normed_two, jnp.concatenate(logit_grads, axis=0), ((0,), (0,)))
    qk_columns = qk_sum.shape[0] // dense_rows
    small = jnp.concatenate(
        [
            router_sum[:, :experts],
            jnp.concatenate([gain_one_sum, gain_two_sum], axis=1).reshape(D, 2),
            jnp.tile(qk_sum.reshape(dense_rows, qk_columns), (planes * ranks, 1)),
        ],
        axis=1,
    )
    count = small.shape[1]

    def halves(value):
        high, low = two_parts(value)
        blank = jnp.zeros((value.shape[0], PAD - 2 * count), bf16)
        return jnp.concatenate([high, low, blank], axis=1)

    def joined(value):
        return value[..., :count].astype(f32) + value[..., count : 2 * count].astype(f32)

    grad_projs, out_sum = lax.optimization_barrier((grad_projs, out_sum))
    out_crossed = cross(out_sum)
    packed = weight_gradient(
        where,
        planes,
        normed.reshape(ranks * mine, D),
        [jnp.stack(grad_projs, axis=1).reshape(ranks * mine, 3 * width)],
        halves(small),
    )
    packed, last_sent, last = lax.optimization_barrier((packed, last_sent, last))
    packed_sent = [packed[0]] + [shift_rep(packed[step], step) for step in range(1, planes)]
    normed_sums = [one[2] for one in grad_inputs]
    packed_sent, normed_sums, last, crossed = lax.optimization_barrier(
        (packed_sent, normed_sums, last, crossed)
    )
    last_sent = last_sent + [shift_rep(last[half:], order[-1])]
    mixture = []
    for parts in crossed:
        parts = total(parts)
        mixture.append(parts[0] + total(exchange_back(parts.astype(bf16))[1:]))
    output = (hidden + jnp.concatenate(mixture, axis=0)).astype(bf16)
    grad_tokens = []
    for step in range(micro):
        grad_hidden, grad_normed = grad_inputs[step][0], normed_sums[step]
        own_stream = tokens[step * rows : (step + 1) * rows].astype(f32)
        grad_tokens.append(
            grad_hidden
            + rms_backward(
                own_stream, inverse_rms(own_stream), first_gain, grad_normed.astype(f32)
            )
        )
    main = total([part[:, : 3 * width] for part in packed_sent]).astype(bf16)
    small = sum(joined(part[:, 3 * width :]) for part in packed_sent)
    packed = jnp.concatenate([main, halves(small)], axis=1).reshape(ranks, dense_rows, -1)
    packed = lax.all_to_all(packed, "ep", split_axis=0, concat_axis=0, tiled=True)
    packed, last_sent = lax.optimization_barrier((packed, last_sent))
    main = packed[..., : 3 * width].astype(f32)
    small = jnp.sum(joined(packed[..., 3 * width :]), axis=0)
    grad_w_qkv = (
        main.reshape(ranks, dense_rows, 3, width).transpose(1, 2, 0, 3).reshape(dense_rows, 3 * D)
    )
    grad_w_out = sum_rep({0: out_cut[0], **out_sent})
    grad_w_in = sum_rep({0: in_cut[0], **in_sent, order[-1]: jnp.concatenate(last_sent, axis=0)})
    out_sum = total(out_crossed)
    grad_w_o = lax.dynamic_index_in_dim(out_sum, plane, 0, keepdims=False)
    out_sum = out_sum.astype(bf16)
    for step in range(1, planes):
        part = lax.dynamic_index_in_dim(out_sum, (plane + step) % planes, 0, keepdims=False)
        grad_w_o = grad_w_o + shift_rep(part, step).astype(f32)
    return (
        output,
        jnp.concatenate(grad_tokens, axis=0),
        grad_w_qkv,
        grad_w_o,
        small[:, :experts],
        small[:, experts : experts + 2].reshape(-1),
        small[:, experts + 2 :].reshape(-1),
        grad_w_in,
        grad_w_out,
    )


def solution(mesh):
    placed = (
        P(("rep", "ep"), None),
        P(("rep", "ep"), None),
        P(("rep", "ep"), None),
        P(("rep", "ep"), None),
        P(("rep", "ep"), None),
        P(("rep", "ep")),
        P(),
        P("ep", "rep", None),
        P("ep", "rep", None),
        P("rep", None, None),
        P(("rep", "ep"), None),
    )
    return jax.shard_map(
        on_device,
        mesh=mesh,
        in_specs=placed,
        out_specs=(
            P(("rep", "ep"), None),
            P(("rep", "ep"), None),
            P(("rep", "ep"), None),
            P(("rep", "ep"), None),
            P(("rep", "ep"), None),
            P(("rep", "ep")),
            P(),
            P("ep", "rep", None),
            P("ep", "rep", None),
        ),
        check_vma=False,
    )
```

```python
import math

import jax
import jax.numpy as jnp
from jax import lax
from jax.experimental import pallas as pl
from jax.experimental.pallas import tpu as pltpu
from jax.sharding import PartitionSpec as P

D = 2048
HEADS = 16
HD = 128
FF = 1024
TOP = 8
HALF = 512
PAD = 128

epsilon = 1e-06
rope_base = 50000.0
bf16 = jnp.bfloat16
f32 = jnp.float32


def dot(a, b, dims=((1,), (0,))):
    return lax.dot_general(a, b, (dims, ((), ())), preferred_element_type=f32)


def inverse_rms(value):
    return lax.rsqrt(jnp.mean(value * value, axis=-1, keepdims=True) + epsilon)


def rms_backward(value, inverse, gain, grad):
    scaled = grad * gain
    inner = jnp.mean(scaled * value, axis=-1, keepdims=True)
    return inverse * (scaled - value * (inverse * inverse * inner))


def doc_positions(segment):
    index = jnp.arange(segment.shape[0], dtype=jnp.int32)
    change = jnp.concatenate([jnp.ones((1,), dtype=jnp.bool_), segment[1:] != segment[:-1]])
    start = lax.cummax(jnp.where(change, index, 0), axis=0)
    return index - start


def rope_tables(position, width):
    steps = jnp.arange(width // 2, dtype=f32) * (2.0 / width)
    rates = jnp.exp(-steps * math.log(rope_base))
    angle = position.astype(f32)[:, None] * rates[None, :]
    angle = jnp.concatenate([angle, angle], axis=-1)
    return (jnp.cos(angle), jnp.sin(angle))


def norm_rope(value, gain, cosine, sine):
    inverse = lax.rsqrt(jnp.mean(value * value, axis=1, keepdims=True) + epsilon)
    value = value * inverse * gain
    return value * cosine + pltpu.roll(value, HD // 2, 1) * sine


def norm_rope_back(value, gain, cosine, sine, grad):
    inverse = lax.rsqrt(jnp.mean(value * value, axis=1, keepdims=True) + epsilon)
    grad = grad * cosine + pltpu.roll(grad * sine, HD // 2, 1)
    normal = value * inverse
    scaled = grad * gain
    inner = jnp.mean(scaled * normal, axis=1, keepdims=True)
    return inverse * (scaled - normal * inner), jnp.sum(grad * normal, axis=0, keepdims=True)


def kept_scores(query, keys, q_seg, k_seg, start):
    scores = dot(query, keys, ((1,), (1,))) * (1.0 / math.sqrt(HD))
    q_index = start + lax.broadcasted_iota(jnp.int32, scores.shape, 0)
    k_index = lax.broadcasted_iota(jnp.int32, scores.shape, 1)
    keep = (jnp.abs(q_index - k_index) <= HALF) & (q_seg == k_seg)
    return jnp.where(keep, scores, -1e30)


BIG = 100 * 1024 * 1024 // 2


def forward_kernel(
    heads, proj, cosine, sine, seg_column, seg_row, gains, mixed, query, keys, values, lses
):
    ranks, _, rows, _ = proj.shape
    length = ranks * rows
    q_block = 2 * rows
    k_seg = seg_row[0]
    for head in range(heads):
        at = slice(head * HD, (head + 1) * HD)

        def raw(part):
            first = (part * heads + head) * HD
            return proj[:, 0, :, first : first + HD].reshape(length, HD)

        query[0, :, at] = norm_rope(raw(0), gains[0:1], cosine[0], sine[0]).astype(bf16)
        keys[0, :, at] = norm_rope(raw(1), gains[1:2], cosine[0], sine[0]).astype(bf16)
        values[0, :, at] = raw(2).astype(bf16)

        @pl.loop(0, length // q_block)
        def one_block(number, head=head, at=at):
            start = pl.multiple_of(number * q_block, q_block)
            here = pl.ds(start, q_block)
            scores = kept_scores(
                query[0, here, at], keys[0, :, at], seg_column[0, here], k_seg, start
            )
            top = jnp.max(scores, axis=1, keepdims=True)
            weights = jnp.exp(scores - top)
            total = jnp.sum(weights, axis=1, keepdims=True)
            lses[0, head, here] = top + jnp.log(total)
            weights = (weights * (1.0 / total)).astype(bf16)
            result = dot(weights, values[0, :, at]).astype(bf16)
            mixed[pl.ds(number * 2, 2), 0, :, at] = result.reshape(2, rows, HD)


def backward_kernel(
    heads, proj, cosine, sine, seg_column, seg_row, gains, query, keys, values, lses, grad_mixed,
    grad_proj, grad_gains, grad_q, grad_k, grad_v,
):
    ranks, _, rows, _ = proj.shape
    length = ranks * rows
    q_block = 2 * rows
    k_seg = seg_row[0]
    scale = 1.0 / math.sqrt(HD)
    sum_q = jnp.zeros((1, HD), f32)
    sum_k = jnp.zeros((1, HD), f32)
    for head in range(heads):
        at = slice(head * HD, (head + 1) * HD)
        grad_k[...] = jnp.zeros_like(grad_k)
        grad_v[...] = jnp.zeros_like(grad_v)

        @pl.loop(0, length // q_block)
        def one_block(number, head=head, at=at):
            start = pl.multiple_of(number * q_block, q_block)
            here = pl.ds(start, q_block)
            q_rows = query[0, here, at]
            g_rows = grad_mixed[here, at]
            k_all = keys[0, :, at]
            scores = kept_scores(q_rows, k_all, seg_column[0, here], k_seg, start)
            weights = jnp.exp(scores - lses[0, head, here])
            grad_weights = dot(g_rows, values[0, :, at], ((1,), (1,)))
            delta = jnp.sum(weights * grad_weights, axis=1, keepdims=True)
            grad_scores = (weights * (grad_weights - delta)).astype(bf16)
            grad_q[here] = dot(grad_scores, k_all) * scale
            grad_k[...] += dot(grad_scores, q_rows, ((0,), (0,)))
            grad_v[...] += dot(weights.astype(bf16), g_rows, ((0,), (0,)))

        def rounded(value):
            return value.astype(bf16).astype(f32)

        def raw(part):
            first = (part * heads + head) * HD
            return proj[:, 0, :, first : first + HD].reshape(length, HD)

        def put(part, value):
            first = (part * heads + head) * HD
            grad_proj[:, :, first : first + HD] = value.astype(bf16).reshape(ranks, rows, HD)

        back_q, gain_q = norm_rope_back(
            raw(0), gains[0:1], cosine[0], sine[0], rounded(grad_q[...])
        )
        back_k, gain_k = norm_rope_back(
            raw(1), gains[1:2], cosine[0], sine[0], rounded(grad_k[...] * scale)
        )
        sum_q, sum_k = sum_q + gain_q, sum_k + gain_k
        put(0, back_q)
        put(1, back_k)
        put(2, grad_v[...])
    grad_gains[0:1] = sum_q
    grad_gains[1:2] = sum_k


def fixed(shape):
    return pl.BlockSpec(shape, lambda *_: (0,) * len(shape), pipeline_mode=pl.Buffered(1))


def leading(shape):
    return pl.BlockSpec((1,) + shape[1:], lambda i: (i,) + (0,) * (len(shape) - 1))


def params():
    return pltpu.CompilerParams(vmem_limit_bytes=BIG)


def cost(products):
    return pl.CostEstimate(flops=20 * products, bytes_accessed=0, transcendentals=0)


def out(shape, dtype=bf16):
    return jax.ShapeDtypeStruct(shape, dtype)


def attention_forward(proj, cosine, sine, seg_column, seg_row, gains):
    ranks, micro, rows, width = proj.shape
    length = ranks * rows
    width = width // 3
    heads = width // HD
    part = out((micro, length, width))
    by_rank = lambda n: pl.BlockSpec((ranks, 1, rows, n), lambda i: (0, i, 0, 0))
    lses = out((micro, heads, length, 1), f32)
    return pl.pallas_call(
        lambda *refs: forward_kernel(heads, *refs),
        grid=(micro,),
        in_specs=[by_rank(3 * width)]
        + [leading(v.shape) for v in (cosine, sine, seg_column, seg_row)]
        + [fixed(gains.shape)],
        out_specs=[by_rank(width)] + [leading(part.shape)] * 3 + [leading(lses.shape)],
        out_shape=[out((ranks, micro, rows, width)), part, part, part, lses],
        compiler_params=params(),
    )(proj, cosine, sine, seg_column, seg_row, gains)


def attention_backward(
    step, proj, cosine, sine, seg_column, seg_row, gains, query, keys, values, lses, grad_mixed
):
    ranks, micro, rows, width = proj.shape
    length = ranks * rows
    heads = width // 3 // HD

    def part(value):
        return pl.BlockSpec((1,) + value.shape[1:], lambda i: (step,) + (0,) * (value.ndim - 1))

    return pl.pallas_call(
        lambda *refs: backward_kernel(heads, *refs),
        grid=(1,),
        in_specs=[pl.BlockSpec((ranks, 1, rows, width), lambda i: (0, step, 0, 0))]
        + [part(v) for v in (cosine, sine, seg_column, seg_row)]
        + [fixed(gains.shape)]
        + [part(v) for v in (query, keys, values, lses)]
        + [fixed(grad_mixed.shape)],
        out_specs=[fixed((ranks, rows, width)), fixed((2, HD))],
        out_shape=[out((ranks, rows, width)), out((2, HD), f32)],
        scratch_shapes=[pltpu.VMEM((length, HD), f32)] * 3,
        compiler_params=params(),
    )(
        proj, cosine, sine, seg_column, seg_row, gains, query, keys, values, lses, grad_mixed
    )


def project(tokens, gain, slab):
    ranks, count, _ = tokens.shape
    width = slab.shape[1] - PAD

    def kernel(value, gain, weight, normed, proj):
        value = value[0].astype(f32)
        result = (value * inverse_rms(value) * gain[...]).astype(bf16)
        normed[0] = result
        proj[0] = dot(result, weight[:, :width])

    return pl.pallas_call(
        kernel,
        grid=(ranks,),
        in_specs=[leading((ranks, count, D)), fixed((1, D)), fixed(slab.shape)],
        out_specs=[leading((ranks, count, D)), leading((ranks, count, width))],
        out_shape=[out((ranks, count, D)), out((ranks, count, width), f32)],
        compiler_params=params(),
    )(tokens, gain, slab)


TILE = 512


def tiles(count):
    return pl.loop(0, count // TILE)


def tile(number):
    return pl.ds(pl.multiple_of(number * TILE, TILE), TILE)


HBM = pl.BlockSpec(memory_space=pl.ANY)


def copies(pairs, sems):
    started = [
        pltpu.make_async_copy(source, target, sems.at[place])
        for place, (source, target) in enumerate(pairs)
    ]
    for copy in started:
        copy.start()

    def wait():
        for copy in started:
            copy.wait()

    return wait


def plane_pairs(plane, pieces, target):
    planes = len(pieces)
    rows = target.shape[0] // planes
    return [
        (piece, target.at[pl.ds((plane + planes - step) % planes * rows, rows)])
        for step, piece in enumerate(pieces)
    ]


def out_weight_pairs(plane, planes, gathered, target):
    ranks = gathered.shape[0]
    rows = D // (planes * ranks)
    return [
        (
            gathered.at[rank, pl.ds(step * rows, rows)],
            target.at[pl.ds(((plane + planes - step) % planes * ranks + rank) * rows, rows)],
        )
        for rank in range(ranks)
        for step in range(planes)
    ]


def route(plane, planes, mixed, tokens, gathered, gain, router, routes, experts):
    count = tokens.shape[0]
    pieces = planes * gathered.shape[0]

    def kernel(
        plane, mixed, tokens, gathered, gain, router, routes, hidden, payload, gates,
        out_weight, sems,
    ):
        copies(out_weight_pairs(plane[0], planes, gathered, out_weight), sems)()

        @tiles(D)
        def _(number):
            at = tile(number)
            hidden[:, at] = tokens[:, at].astype(f32) + dot(mixed[...], out_weight[:, at])

        value = hidden[...]
        normed = (value * inverse_rms(value) * gain[...]).astype(bf16)
        payload[:, :D] = normed
        logits = dot(normed, router[...])
        column = lax.broadcasted_iota(jnp.int32, logits.shape, 1)
        routed = column == routes[:, 0:1]
        for choice in range(1, TOP):
            routed = routed | (column == routes[:, choice : choice + 1])
        logits = jnp.where(routed, logits, -1e30)
        weights = jnp.exp(logits - jnp.max(logits, axis=1, keepdims=True))
        weights = jnp.where(routed, weights, 0.0)
        weights = weights / jnp.sum(weights, axis=1, keepdims=True)
        gates[...] = weights
        high = weights.astype(bf16).astype(f32)
        payload[:, D:] = (high + pltpu.roll(weights - high, experts, 1)).astype(bf16)

    shapes = [out((count, D), f32), out((count, D + PAD)), out((count, PAD), f32)]
    return pl.pallas_call(
        kernel,
        grid_spec=pltpu.PrefetchScalarGridSpec(
            num_scalar_prefetch=1,
            grid=(1,),
            in_specs=[
                HBM if value is gathered else fixed(value.shape)
                for value in (mixed, tokens, gathered, gain, router, routes)
            ],
            out_specs=[fixed(shape.shape) for shape in shapes],
            scratch_shapes=[pltpu.VMEM((D, D), bf16), pltpu.SemaphoreType.DMA((pieces,))],
        ),
        out_shape=shapes,
        compiler_params=params(),
    )(plane, mixed, tokens, gathered, gain, router, routes)


def lane(value, number):
    column = lax.broadcasted_iota(jnp.int32, value.shape, 1)
    return jnp.sum(jnp.where(column == number, value.astype(f32), 0.0), axis=1, keepdims=True)


def one_hot(slot, slots):
    place = lax.broadcasted_iota(jnp.int32, (slots, slot.shape[1]), 0).astype(f32)
    return (place == slot).astype(bf16)


def expert_forward(where, payload, upstream, in_pieces, slots, experts):
    ranks, share, micro, rows, _ = payload.shape
    count = share * rows
    block = 2 * slots

    planes = len(in_pieces)

    def kernel(where, payload, upstream, *refs):
        (
            rows_in, tail, both, active, grad_produced, up_rows, places, in_weight, sems
        ) = refs[planes:]
        number = where[0]

        @pl.when((pl.program_id(0) == 0) & (pl.program_id(1) == 0))
        def _():
            copies(plane_pairs(where[1], refs[:planes], in_weight), sems)()

        for part in range(2):
            here = slice(part * slots, (part + 1) * slots)
            value = payload[part].reshape(count, D + PAD)
            marks = value[:, D:]
            first = lax.broadcasted_iota(jnp.int32, (8, PAD), 1) == number
            taken = dot(first.astype(bf16), marks, ((1,), (1,))) > 0.0
            before = lax.broadcasted_iota(jnp.int32, (count, count), 0)
            behind = lax.broadcasted_iota(jnp.int32, (count, count), 1)
            slot = dot(taken.astype(bf16), (before < behind).astype(bf16))
            select = one_hot(jnp.where(taken, slot, -1.0)[0:1], slots)
            wide = jnp.broadcast_to(lane(marks, number) > 0.0, (count, PAD))
            slot = dot((before > behind).astype(bf16), wide.astype(bf16))
            places[0, 0, part] = jnp.where(wide, slot, -1.0)
            rows_in[0, 0, here] = dot(select, value[:, :D]).astype(bf16)
            marks = dot(select, marks)
            tail[0, 0, here] = marks
            gate = lane(marks, number) + lane(marks, experts + number)
            picked = dot(select, upstream[part].reshape(count, D))
            up_rows[0, 0, here] = picked.astype(bf16)
            grad_produced[0, 0, here] = (gate * picked).astype(bf16)

        for number in range(FF // TILE):
            at = slice(number * TILE, (number + 1) * TILE)
            more = slice(FF + number * TILE, FF + (number + 1) * TILE)
            gate_part = dot(rows_in[0, 0], in_weight[:, at])
            up_part = dot(rows_in[0, 0], in_weight[:, more])
            both[0, 0, :, at] = gate_part
            both[0, 0, :, more] = up_part
            active[0, 0, :, at] = (
                gate_part / (1.0 + jnp.exp(-gate_part)) * up_part
            ).astype(bf16)

    def tokens_spec(width):
        return pl.BlockSpec((2, share, 1, rows, width), lambda m, b, _: (b, 0, m, 0, 0))

    pairs = ranks // 2
    shapes = [
        out((micro, pairs, block, D)),
        out((micro, pairs, block, PAD), f32),
        out((micro, pairs, block, 2 * FF), f32),
        out((micro, pairs, block, FF)),
        out((micro, pairs, block, D)),
        out((micro, pairs, block, D)),
        out((micro, pairs, 2, count, PAD), f32),
    ]
    return pl.pallas_call(
        kernel,
        grid_spec=pltpu.PrefetchScalarGridSpec(
            num_scalar_prefetch=1,
            grid=(micro, pairs),
            in_specs=[tokens_spec(D + PAD), tokens_spec(D)] + [HBM] * planes,
            out_specs=[
                pl.BlockSpec(
                    (1, 1) + s.shape[2:], lambda m, b, _, n=len(s.shape): (m, b) + (0,) * (n - 2)
                )
                for s in shapes
            ],
            scratch_shapes=[pltpu.VMEM((D, 2 * FF), bf16), pltpu.SemaphoreType.DMA((planes,))],
        ),
        out_shape=shapes,
        cost_estimate=cost(micro * pairs * block * D * (2 * FF + 2 * count)),
        compiler_params=params(),
    )(where, payload, upstream, *in_pieces)


def expert_backward(
    step, where, tail, both, active, grad_produced, up_rows, places, in_pieces, out_pieces,
    share, rows, experts,
):
    pairs, block = tail.shape[1:3]
    slots = block // 2
    count = places.shape[3]

    planes = len(in_pieces)

    def kernel(where, tail, both, active, grad_produced, up_rows, places, *refs):
        keep, give, grad_tokens, grad_both, in_weight, out_weight, sems = refs[2 * planes :]
        number = where[0]
        odd = where[2] == 1

        @pl.when(pl.program_id(0) == 0)
        def _():
            copies(
                plane_pairs(where[1], refs[:planes], in_weight)
                + plane_pairs(where[1], refs[planes : 2 * planes], out_weight),
                sems,
            )()

        gate = lane(tail[0, 0], number) + lane(tail[0, 0], experts + number)
        place = lax.broadcasted_iota(jnp.int32, (count, slots), 1).astype(f32)
        selects = [(places[0, 0, part][:, 0:1] == place).astype(bf16) for part in range(2)]

        def spread(value):
            return [
                dot(selects[part], value[part * slots : (part + 1) * slots])
                .astype(bf16)
                .reshape(share, rows, -1)
                for part in range(2)
            ]

        grad_gate = jnp.zeros((block, 1), f32)
        for tile in range(D // TILE):
            at = slice(tile * TILE, (tile + 1) * TILE)
            produced = dot(active[0, 0], out_weight[:, at]).astype(bf16).astype(f32)
            even_rank, odd_rank = spread((gate * produced).astype(bf16))
            keep[0, :, :, at] = jnp.where(odd, odd_rank, even_rank)
            give[0, :, :, at] = jnp.where(odd, even_rank, odd_rank)
            grad_gate = grad_gate + jnp.sum(
                up_rows[0, 0, :, at].astype(f32) * produced, axis=1, keepdims=True
            )

        for tile in range(FF // TILE):
            at = slice(tile * TILE, (tile + 1) * TILE)
            more = slice(FF + tile * TILE, FF + (tile + 1) * TILE)
            grad_active = dot(grad_produced[0, 0], out_weight[at, :], ((1,), (1,)))
            grad_active = grad_active.astype(bf16).astype(f32)
            gate_part = both[0, 0, :, at]
            up_part = both[0, 0, :, more]
            sigma = 1.0 / (1.0 + jnp.exp(-gate_part))
            grad_both[0, :, at] = (
                grad_active * up_part * (sigma * (1.0 + gate_part * (1.0 - sigma)))
            ).astype(bf16)
            grad_both[0, :, more] = (grad_active * (gate_part * sigma)).astype(bf16)

        for tile in range(D // TILE):
            at = slice(tile * TILE, (tile + 1) * TILE)
            grad_rows = dot(grad_both[0], in_weight[at, :], ((1,), (1,))).astype(bf16)
            grad_tokens[0, :, :, at], grad_tokens[1, :, :, at] = spread(grad_rows)

        high = grad_gate.astype(bf16).astype(f32)
        column = lax.broadcasted_iota(jnp.int32, (block, PAD), 1)
        extra = jnp.where(column == number, high, 0.0)
        extra = jnp.where(column == experts + number, grad_gate - high, extra)
        grad_tokens[0, :, :, D:], grad_tokens[1, :, :, D:] = spread(extra.astype(bf16))

    def part(value):
        return pl.BlockSpec(
            (1, 1) + value.shape[2:], lambda b, _: (step, b) + (0,) * (value.ndim - 2)
        )

    def tokens_spec(count, width):
        return pl.BlockSpec((count, share, rows, width), lambda b, _: (b, 0, 0, 0))

    return pl.pallas_call(
        kernel,
        grid_spec=pltpu.PrefetchScalarGridSpec(
            num_scalar_prefetch=1,
            grid=(pairs,),
            in_specs=[part(v) for v in (tail, both, active, grad_produced, up_rows, places)]
            + [HBM] * (2 * planes),
            out_specs=[
                tokens_spec(1, D),
                tokens_spec(1, D),
                tokens_spec(2, D + PAD),
                pl.BlockSpec((1, block, 2 * FF), lambda b, _: (b, 0, 0)),
            ],
            scratch_shapes=[
                pltpu.VMEM((D, 2 * FF), bf16),
                pltpu.VMEM((FF, D), bf16),
                pltpu.SemaphoreType.DMA((2 * planes,)),
            ],
        ),
        out_shape=[
            out((pairs, share, rows, D)),
            out((pairs, share, rows, D)),
            out((2 * pairs, share, rows, D + PAD)),
            out((pairs, block, 2 * FF)),
        ],
        cost_estimate=cost(pairs * block * D * (4 * FF + 2 * count)),
        compiler_params=params(),
    )(
        where, tail, both, active, grad_produced, up_rows, places, *in_pieces, *out_pieces
    )


def weight_gradient(where, planes, left, rights, tail=None, first=0, steps=None):
    steps = planes if steps is None else steps
    count, width = left.shape
    parts = len(rights)
    part_rows = count // parts
    columns = rights[0].shape[1]
    width = width // planes
    step = min(TILE, columns & -columns)
    tails = [] if tail is None else [tail]
    whole = columns + sum(value.shape[1] for value in tails)

    def of_plane(i, where):
        return (where[1] + first + i) % planes

    def kernel(where, left, *refs):
        rights, target = refs[:parts], refs[-1]
        for value in refs[parts:-1]:
            target[0, :, columns:] = value[...]
        for number in range(columns // step):
            at = slice(number * step, (number + 1) * step)
            target[0, :, at] = sum(
                dot(left[part * part_rows : (part + 1) * part_rows], right[:, at], ((0,), (0,)))
                for part, right in enumerate(rights)
            ).astype(bf16)

    return pl.pallas_call(
        kernel,
        grid_spec=pltpu.PrefetchScalarGridSpec(
            num_scalar_prefetch=1,
            grid=(steps,),
            in_specs=[pl.BlockSpec((count, width), lambda i, where: (0, of_plane(i, where)))]
            + [fixed(right.shape) for right in rights]
            + [
                pl.BlockSpec((width, value.shape[1]), lambda i, where: (of_plane(i, where), 0))
                for value in tails
            ],
            out_specs=pl.BlockSpec((1, width, whole), lambda i, _: (i, 0, 0)),
        ),
        out_shape=out((steps, width, whole)),
        cost_estimate=cost(0 if tails else count * steps * width * columns),
        compiler_params=params(),
    )(where, left, *rights, *tails)


def hidden_backward(
    plane, planes, parts, hidden, gates, upstream, gain, router, gathered, experts
):
    count = hidden.shape[0]
    terms = len(parts)

    def kernel(plane, *refs):
        parts = refs[:terms]
        hidden, gates, upstream, gain, router, gathered = refs[terms : terms + 6]
        (
            grad_hidden, grad_branch, grad_mixed, grad_logits, grad_gain, out_weight, sems
        ) = refs[terms + 6 :]
        wait = copies(out_weight_pairs(plane[0], planes, gathered, out_weight), sems)
        returned = sum(part[...].astype(f32) for part in parts)
        tail = returned[:, D:]
        grad_gates = gates[...] * (tail + pltpu.roll(tail, PAD - experts, 1))
        logits = grad_gates - gates[...] * jnp.sum(grad_gates, axis=1, keepdims=True)
        logits = logits.astype(bf16)
        grad_logits[...] = logits
        grad_normed = returned[:, :D] + dot(logits, router[...], ((1,), (1,)))
        value = hidden[...]
        inverse = inverse_rms(value)
        grad_gain[...] = jnp.sum(grad_normed * value * inverse, axis=0, keepdims=True)
        grad = upstream[...].astype(f32) + rms_backward(value, inverse, gain[...], grad_normed)
        grad_hidden[...] = grad
        grad_branch[...] = grad.astype(bf16)
        wait()

        @tiles(D)
        def _(number):
            at = tile(number)
            grad_mixed[:, at] = dot(grad_branch[...], out_weight[at, :], ((1,), (1,))).astype(bf16)

    shapes = [
        out((count, D), f32), out((count, D)), out((count, D)), out((count, PAD)),
        out((1, D), f32),
    ]
    args = (*parts, hidden, gates, upstream, gain, router, gathered)
    return pl.pallas_call(
        kernel,
        grid_spec=pltpu.PrefetchScalarGridSpec(
            num_scalar_prefetch=1,
            grid=(1,),
            in_specs=[HBM if value is gathered else fixed(value.shape) for value in args],
            out_specs=[fixed(shape.shape) for shape in shapes],
            scratch_shapes=[
                pltpu.VMEM((D, D), bf16),
                pltpu.SemaphoreType.DMA((planes * gathered.shape[0],)),
            ],
        ),
        out_shape=shapes,
        compiler_params=params(),
    )(plane, *args)


def project_backward(step, grad_proj, tokens, slab):
    ranks, rows, _ = grad_proj.shape
    width = slab.shape[1] - PAD

    def kernel(grad_proj, tokens, weight, grad_normed, grad_gain):
        value = tokens[0].astype(f32)
        inverse = inverse_rms(value)
        grad = dot(grad_proj[0], weight[:, :width], ((1,), (1,)))
        grad_normed[...] = grad.astype(bf16)

        @pl.when(pl.program_id(0) == 0)
        def _():
            grad_gain[...] = jnp.zeros_like(grad_gain)

        grad_gain[...] += jnp.sum(grad * value * inverse, axis=0, keepdims=True)

    return pl.pallas_call(
        kernel,
        grid=(ranks,),
        in_specs=[
            leading(grad_proj.shape),
            pl.BlockSpec((1, rows, D), lambda i: (i, step, 0)),
            fixed(slab.shape),
        ],
        out_specs=[pl.BlockSpec((rows, D), lambda i: (i, 0)), fixed((1, D))],
        out_shape=[out((ranks * rows, D)), out((1, D), f32)],
        compiler_params=params(),
    )(grad_proj, tokens, slab)


def shift_rep(value, step):
    count = lax.axis_size("rep")
    return lax.ppermute(value, "rep", [(i, (i + step) % count) for i in range(count)])


def after(value, *others):
    return lax.optimization_barrier((value,) + others)[0]


def two_parts(value):
    high = lax.reduce_precision(value, 8, 7)
    return high.astype(bf16), (value - high).astype(bf16)


def shift_order(count):
    return sorted(range(1, count), key=lambda step: (min(step, count - step), step))


def ring_rep(value, *work):
    count = lax.axis_size("rep")
    rank = lax.axis_index("rep")
    rows = value.shape[0]
    full = jnp.zeros((count * rows,) + value.shape[1:], value.dtype)
    full = lax.dynamic_update_slice_in_dim(full, value, rank * rows, 0)
    for step in range(1, count):
        value, work = lax.optimization_barrier((value, work)) if step == 2 else (value, work)
        value = shift_rep(value, 1)
        full = lax.dynamic_update_slice_in_dim(full, value, (rank - step) % count * rows, 0)
    return full, work


def on_device(
    tokens, cotangent, w_qkv, w_o, w_router, norm_gains, qk_gain, w_in, w_out, segments, routes
):
    planes = lax.axis_size("rep")
    ranks = lax.axis_size("ep")
    plane = lax.axis_index("rep")
    rank = lax.axis_index("ep")
    share = w_in.shape[0]
    own = plane % share
    experts = share * ranks
    where = jnp.stack([rank * share + own, plane, rank % 2]).astype(jnp.int32)
    micro = segments.shape[1]
    mine = tokens.shape[0]
    rows = mine // micro
    length = rows * ranks
    capacity = rows * TOP * 17 // (16 * experts)
    slots = -(-share * capacity // 16) * 16
    width = HEADS // ranks * HD
    qk_gains = qk_gain.astype(f32).reshape(2, HD)
    dense_rows = w_qkv.shape[0]

    def exchange(value, step):
        pairs = [(i, i // share * share + (i % share + step) % share) for i in range(planes)]
        return lax.ppermute(value, "rep", pairs)

    def with_group(value):
        return jnp.stack([value] + [exchange(value, step) for step in range(1, share)])

    def gather_ranks(value):
        return lax.all_gather(value, "ep", axis=0)

    order = shift_order(planes)
    in_parts, out_parts = (
        {
            step: lax.dynamic_index_in_dim(weight, (own + step) % share, 0, keepdims=False)
            for step in [0] + order
        }
        for weight in (w_in, w_out)
    )

    def send(parts, steps):
        return {step: shift_rep(parts[step], step) for step in steps}

    stream = gather_ranks(tokens)
    out_rows = [w_o] + [shift_rep(w_o, step) for step in range(1, planes)]
    upstream_group = with_group(cotangent)
    slab = jnp.concatenate(
        [
            w_qkv.reshape(dense_rows, 3, ranks, width)
            .transpose(2, 0, 1, 3)
            .reshape(ranks, dense_rows, 3 * width),
            jnp.broadcast_to(
                jnp.concatenate(
                    [
                        w_router,
                        norm_gains.reshape(dense_rows, 2),
                        jnp.zeros((dense_rows, PAD - experts - 2), bf16),
                    ],
                    axis=1,
                )[None],
                (ranks, dense_rows, PAD),
            ),
        ],
        axis=2,
    )
    slab = lax.all_to_all(slab, "ep", split_axis=0, concat_axis=0, tiled=True)
    slab = slab.reshape(ranks * dense_rows, 3 * width + PAD)
    out_rows, upstream_group, slab = lax.optimization_barrier((out_rows, upstream_group, slab))
    gathered = gather_ranks(jnp.concatenate(out_rows, axis=0))
    segment = segments[0]
    cosine, sine = jax.vmap(lambda one: rope_tables(doc_positions(one), HD))(segment)
    sine = jnp.where(jnp.arange(HD) < HD // 2, -sine, sine)
    tables = (cosine, sine, segment[:, :, None], segment[:, None, :], qk_gains)
    slab, (tables, in_parts, out_parts) = ring_rep(slab, tables, in_parts, out_parts)
    router = slab[:, 3 * width :]
    gain_pair = router[:, experts : experts + 2].reshape(-1).astype(f32)
    first_gain = gain_pair[None, :D]
    second_gain = gain_pair[None, D:]
    in_parts, out_parts, upstream_group, stream = after(
        (in_parts, out_parts, upstream_group, stream), slab
    )
    in_pieces = {0: in_parts[0], **send(in_parts, order[:-1])}
    upstream_all = gather_ranks(upstream_group)

    normed, proj = project(stream, first_gain, slab)
    proj = proj.reshape(ranks, micro, rows, 3 * width)
    mixed_h, query, keys, values, lses = attention_forward(proj, *tables)
    mixed = lax.all_to_all(mixed_h, "ep", split_axis=0, concat_axis=3, tiled=True)
    mixed = mixed.reshape(mine, D)
    hidden, payload, gates = route(
        where[1:2], planes, mixed, tokens, gathered, second_gain, router, routes, experts
    )
    normed_two = payload[:, :D]
    payload, in_pieces = lax.optimization_barrier((payload, in_pieces))
    payload = with_group(payload)
    payload, in_parts, out_parts = lax.optimization_barrier((payload, in_parts, out_parts))
    in_pieces.update(send(in_parts, order[-1:]))
    in_pieces, out_parts = lax.optimization_barrier((in_pieces, out_parts))
    out_pieces = {0: out_parts[0], **send(out_parts, order)}
    in_pieces = [in_pieces[step] for step in range(planes)]
    out_pieces = [out_pieces[step] for step in range(planes)]
    payload = gather_ranks(payload)

    shape = (ranks, share, micro, rows, -1)
    rows_in, tail, both, active, grad_produced, up_rows, places = expert_forward(
        where, payload.reshape(shape), upstream_all.reshape(shape), in_pieces, slots, experts
    )
    in_rows = micro * ranks * slots
    out_cut = weight_gradient(
        where, planes, active.reshape(in_rows, FF), [grad_produced.reshape(in_rows, D)]
    )

    def sum_rep(parts):
        sums = [
            sum(parts[step].astype(f32) for step in range(first, planes, share))
            for first in range(share)
        ]
        return jnp.stack(
            [
                sum(jnp.where((own - step) % share == j, sums[step], 0.0) for step in range(share))
                for j in range(share)
            ]
        )

    tail, out_cut = lax.optimization_barrier((tail, out_cut))
    out_sent = send(out_cut, order)
    back = []
    returned = []

    def scatter_ranks(value):
        return lax.psum_scatter(value, "ep", scatter_dimension=0)

    def exchange_back(value):
        return [value[0]] + [exchange(value[step], share - step) for step in range(1, share)]

    for step in range(micro):
        back.append(
            expert_backward(
                step, where, tail, both, active, grad_produced, up_rows, places, in_pieces,
                out_pieces, share, rows, experts,
            )
        )
        returned.append(scatter_ranks(back[step][2]))
        if step == 0:
            tail, out_sent[order[0]] = after((tail, out_sent[order[0]]), back[step][2])
        else:
            tail = after(tail, back[step][2])
    rows_in = after(rows_in, tail)
    rows_flat = rows_in.reshape(in_rows, D)
    grads_flat = [back[step][3].reshape(in_rows // micro, 2 * FF) for step in range(micro)]
    near = weight_gradient(where, planes, rows_flat, grads_flat, first=order[0], steps=1)
    rows_flat, near = lax.optimization_barrier((rows_flat, near))
    far = weight_gradient(
        where, planes, rows_flat, grads_flat, first=order[0] + 1, steps=planes - 1
    )
    in_cut = {(order[0] + 1 + i) % planes: far[i] for i in range(planes - 1)}
    in_cut[order[0]] = near[0]
    in_sent = send(in_cut, order[:1])

    def swap(value, step):
        return lax.ppermute(value, "ep", [(i, i ^ step) for i in range(ranks)])

    def pair_sum(keep, give):
        return (keep.astype(f32) + swap(give, 1).astype(f32)).astype(bf16)

    def cross(values, places):
        return {
            (number, step): swap(
                lax.dynamic_index_in_dim(values[number], rank // 2 ^ step, 0, keepdims=False),
                2 * step,
            )
            for number, step in places
        }

    places = [(number, step) for number in range(micro) for step in range(1, ranks // 2)]
    cuts = [0, len(places) // 6, len(places) // 3, 2 * len(places) // 3, len(places)]
    shares = [places[start:end] for start, end in zip(cuts, cuts[1:])]

    def total(parts):
        return sum(part.astype(f32) for part in parts)

    grad_inputs, branches, logit_grads, grad_projs = [], [], [], []
    gain_two_sum = gain_one_sum = qk_sum = 0.0
    in_cut, out_sent, in_sent = lax.optimization_barrier((in_cut, out_sent, in_sent))
    mixtures = [part[:2] for part in back]
    releases = [order[1:-1]] + [[]] * (micro - 1)
    for step in range(micro):
        at = slice(step * rows, (step + 1) * rows)
        parts = after(returned[step], [one[1] for one in grad_inputs])
        parts, in_sent = lax.optimization_barrier((parts, in_sent))
        if step == micro - 1:
            crossed = cross(after(mixtures, parts), shares[0])
        parts = exchange_back(parts)
        if step == 0:
            mixtures = [pair_sum(*part) for part in after(mixtures, in_cut)]
        parts, in_cut, mixtures = lax.optimization_barrier((parts, in_cut, mixtures))
        in_sent.update(send(in_cut, releases[step]))
        if step == micro - 1:
            parts, crossed = lax.optimization_barrier((parts, crossed))
            last = in_cut[order[-1]]
            ends = [-(-last.shape[0] * part // 64) * 16 for part in range(5)]
            last = [last[start:end] for start, end in zip(ends, ends[1:])]
            last_sent = [shift_rep(last[0], order[-1])]
        grad_hidden, grad_branch, grad_mixed, grad_logits, gain_two = hidden_backward(
            where[1:2], planes, parts, hidden[at], gates[at], cotangent[at], second_gain,
            router, gathered, experts,
        )
        branches.append(grad_branch)
        logit_grads.append(grad_logits)
        gain_two_sum = gain_two_sum + gain_two
        if step == micro - 1:
            out_sum = dot(mixed, jnp.concatenate(branches, axis=0), ((0,), (0,))).astype(bf16)
            out_sum = out_sum.reshape(planes, ranks, dense_rows, D).transpose(1, 0, 2, 3)
        grad_mixed = lax.all_to_all(grad_mixed, "ep", split_axis=1, concat_axis=0, tiled=True)
        if step == micro - 1:
            grad_mixed, mixtures, last_sent, last, out_sum = lax.optimization_barrier(
                (grad_mixed, mixtures, last_sent, last, out_sum)
            )
            out_sum = lax.psum_scatter(out_sum, "ep", scatter_dimension=0)
            crossed.update(cross(mixtures, shares[1]))
            last_sent.append(shift_rep(last[1], order[-1]))
        grad_proj, grad_qk = attention_backward(
            step, proj, *tables, query, keys, values, lses, grad_mixed
        )
        qk_sum = qk_sum + grad_qk.reshape(-1)
        if step < micro - 1:
            grad_proj, in_sent = lax.optimization_barrier((grad_proj, in_sent))
        else:
            grad_proj, grad_inputs, crossed, mixtures, last_sent, last = (
                lax.optimization_barrier(
                    (grad_proj, grad_inputs, crossed, mixtures, last_sent, last)
                )
            )
            crossed.update(cross(mixtures, shares[2]))
            last_sent.append(shift_rep(last[2], order[-1]))
        grad_projs.append(grad_proj)
        grad_normed, gain_one = project_backward(step, grad_proj, stream, slab)
        gain_one_sum = gain_one_sum + gain_one
        grad_inputs.append(
            (
                grad_hidden,
                grad_normed,
                lax.psum_scatter(grad_normed, "ep", scatter_dimension=0, tiled=True),
            )
        )

    router_sum = dot(normed_two, jnp.concatenate(logit_grads, axis=0), ((0,), (0,)))
    qk_columns = qk_sum.shape[0] // dense_rows
    small = jnp.concatenate(
        [
            router_sum[:, :experts],
            jnp.concatenate([gain_one_sum, gain_two_sum], axis=1).reshape(D, 2),
            jnp.tile(qk_sum.reshape(dense_rows, qk_columns), (planes * ranks, 1)),
        ],
        axis=1,
    )
    count = small.shape[1]

    def halves(value):
        high, low = two_parts(value)
        blank = jnp.zeros((value.shape[0], PAD - 2 * count), bf16)
        return jnp.concatenate([high, low, blank], axis=1)

    def joined(value):
        return value[..., :count].astype(f32) + value[..., count : 2 * count].astype(f32)

    grad_projs, last_sent, last, _ = lax.optimization_barrier(
        (grad_projs, last_sent, last, grad_normed)
    )
    last_sent.append(shift_rep(last[3], order[-1]))
    packed = weight_gradient(
        where,
        planes,
        normed.reshape(ranks * mine, D),
        [jnp.stack(grad_projs, axis=1).reshape(ranks * mine, 3 * width)],
        halves(small),
    )
    packed, crossed, mixtures, last_sent = lax.optimization_barrier(
        (packed, crossed, mixtures, last_sent)
    )
    packed_sent = [packed[0]] + [shift_rep(packed[step], step) for step in range(1, planes)]
    crossed.update(cross(mixtures, shares[3]))
    normed_sums = [one[2] for one in grad_inputs]
    packed_sent, crossed = lax.optimization_barrier((packed_sent, crossed))
    mixture = []
    for number in range(micro):
        parts = total(
            [lax.dynamic_index_in_dim(mixtures[number], rank // 2, 0, keepdims=False)]
            + [crossed[number, step] for step in range(1, ranks // 2)]
        )
        mixture.append(parts[0] + total(exchange_back(parts.astype(bf16))[1:]))
    output = (hidden + jnp.concatenate(mixture, axis=0)).astype(bf16)
    grad_tokens = []
    for step in range(micro):
        grad_hidden, grad_normed = grad_inputs[step][0], normed_sums[step]
        own_stream = tokens[step * rows : (step + 1) * rows].astype(f32)
        grad_tokens.append(
            grad_hidden
            + rms_backward(
                own_stream, inverse_rms(own_stream), first_gain, grad_normed.astype(f32)
            )
        )
    main = total([part[:, : 3 * width] for part in packed_sent]).astype(bf16)
    small = sum(joined(part[:, 3 * width :]) for part in packed_sent)
    packed = jnp.concatenate([main, halves(small)], axis=1).reshape(ranks, dense_rows, -1)
    packed = lax.all_to_all(packed, "ep", split_axis=0, concat_axis=0, tiled=True)
    main = packed[..., : 3 * width].astype(f32)
    small = jnp.sum(joined(packed[..., 3 * width :]), axis=0)
    grad_w_qkv = (
        main.reshape(ranks, dense_rows, 3, width).transpose(1, 2, 0, 3).reshape(dense_rows, 3 * D)
    )
    grad_w_out = sum_rep({0: out_cut[0], **out_sent})
    in_sent[order[-1]] = jnp.concatenate(last_sent, axis=0)
    grad_w_in = sum_rep({0: in_cut[0], **in_sent})
    grad_w_o = lax.dynamic_index_in_dim(out_sum, plane, 0, keepdims=False).astype(f32)
    for step in range(1, planes):
        part = lax.dynamic_index_in_dim(out_sum, (plane + step) % planes, 0, keepdims=False)
        grad_w_o = grad_w_o + shift_rep(part, step).astype(f32)
    return (
        output,
        jnp.concatenate(grad_tokens, axis=0),
        grad_w_qkv,
        grad_w_o,
        small[:, :experts],
        small[:, experts : experts + 2].reshape(-1),
        small[:, experts + 2 :].reshape(-1),
        grad_w_in,
        grad_w_out,
    )


def solution(mesh):
    placed = (
        P(("rep", "ep"), None),
        P(("rep", "ep"), None),
        P(("rep", "ep"), None),
        P(("rep", "ep"), None),
        P(("rep", "ep"), None),
        P(("rep", "ep")),
        P(),
        P("ep", "rep", None),
        P("ep", "rep", None),
        P("rep", None, None),
        P(("rep", "ep"), None),
    )
    return jax.shard_map(
        on_device,
        mesh=mesh,
        in_specs=placed,
        out_specs=(
            P(("rep", "ep"), None),
            P(("rep", "ep"), None),
            P(("rep", "ep"), None),
            P(("rep", "ep"), None),
            P(("rep", "ep"), None),
            P(("rep", "ep")),
            P(),
            P("ep", "rep", None),
            P("ep", "rep", None),
        ),
        check_vma=False,
    )
```

```python
import math

import jax
import jax.numpy as jnp
from jax import lax
from jax.experimental import pallas as pl
from jax.experimental.pallas import tpu as pltpu
from jax.sharding import PartitionSpec as P

D = 2048
HEADS = 16
HD = 128
FF = 1024
TOP = 8
HALF = 512
PAD = 128

epsilon = 1e-06
rope_base = 50000.0
bf16 = jnp.bfloat16
f32 = jnp.float32


def dot(a, b, dims=((1,), (0,))):
    return lax.dot_general(a, b, (dims, ((), ())), preferred_element_type=f32)


def inverse_rms(value):
    return lax.rsqrt(jnp.mean(value * value, axis=-1, keepdims=True) + epsilon)


def rms_backward(value, inverse, gain, grad):
    scaled = grad * gain
    inner = jnp.mean(scaled * value, axis=-1, keepdims=True)
    return inverse * (scaled - value * (inverse * inverse * inner))


def doc_positions(segment):
    index = jnp.arange(segment.shape[0], dtype=jnp.int32)
    change = jnp.concatenate([jnp.ones((1,), dtype=jnp.bool_), segment[1:] != segment[:-1]])
    start = lax.cummax(jnp.where(change, index, 0), axis=0)
    return index - start


def rope_tables(position, width):
    steps = jnp.arange(width // 2, dtype=f32) * (2.0 / width)
    rates = jnp.exp(-steps * math.log(rope_base))
    angle = position.astype(f32)[:, None] * rates[None, :]
    angle = jnp.concatenate([angle, angle], axis=-1)
    return (jnp.cos(angle), jnp.sin(angle))


def norm_rope(value, gain, cosine, sine):
    inverse = lax.rsqrt(jnp.mean(value * value, axis=1, keepdims=True) + epsilon)
    value = value * inverse * gain
    return value * cosine + pltpu.roll(value, HD // 2, 1) * sine


def norm_rope_back(value, gain, cosine, sine, grad):
    inverse = lax.rsqrt(jnp.mean(value * value, axis=1, keepdims=True) + epsilon)
    grad = grad * cosine + pltpu.roll(grad * sine, HD // 2, 1)
    normal = value * inverse
    scaled = grad * gain
    inner = jnp.mean(scaled * normal, axis=1, keepdims=True)
    return inverse * (scaled - normal * inner), jnp.sum(grad * normal, axis=0, keepdims=True)


def kept_scores(query, keys, q_seg, k_seg, start):
    scores = dot(query, keys, ((1,), (1,))) * (1.0 / math.sqrt(HD))
    q_index = start + lax.broadcasted_iota(jnp.int32, scores.shape, 0)
    k_index = lax.broadcasted_iota(jnp.int32, scores.shape, 1)
    keep = (jnp.abs(q_index - k_index) <= HALF) & (q_seg == k_seg)
    return jnp.where(keep, scores, -1e30)


BIG = 100 * 1024 * 1024 // 2


def forward_kernel(
    heads, proj, cosine, sine, seg_column, seg_row, gains, mixed, query, keys, values, lses
):
    ranks, _, rows, _ = proj.shape
    length = ranks * rows
    q_block = 2 * rows
    k_seg = seg_row[0]
    for head in range(heads):
        at = slice(head * HD, (head + 1) * HD)

        def raw(part):
            first = (part * heads + head) * HD
            return proj[:, 0, :, first : first + HD].reshape(length, HD)

        query[0, :, at] = norm_rope(raw(0), gains[0:1], cosine[0], sine[0]).astype(bf16)
        keys[0, :, at] = norm_rope(raw(1), gains[1:2], cosine[0], sine[0]).astype(bf16)
        values[0, :, at] = raw(2).astype(bf16)

        @pl.loop(0, length // q_block)
        def one_block(number, head=head, at=at):
            start = pl.multiple_of(number * q_block, q_block)
            here = pl.ds(start, q_block)
            scores = kept_scores(
                query[0, here, at], keys[0, :, at], seg_column[0, here], k_seg, start
            )
            top = jnp.max(scores, axis=1, keepdims=True)
            weights = jnp.exp(scores - top)
            total = jnp.sum(weights, axis=1, keepdims=True)
            lses[0, head, here] = top + jnp.log(total)
            weights = (weights * (1.0 / total)).astype(bf16)
            result = dot(weights, values[0, :, at]).astype(bf16)
            mixed[pl.ds(number * 2, 2), 0, :, at] = result.reshape(2, rows, HD)


def backward_kernel(
    heads, proj, cosine, sine, seg_column, seg_row, gains, query, keys, values, lses, grad_mixed,
    grad_proj, grad_gains, grad_q, grad_k, grad_v,
):
    ranks, _, rows, _ = proj.shape
    length = ranks * rows
    q_block = 2 * rows
    k_seg = seg_row[0]
    scale = 1.0 / math.sqrt(HD)
    sum_q = jnp.zeros((1, HD), f32)
    sum_k = jnp.zeros((1, HD), f32)
    for head in range(heads):
        at = slice(head * HD, (head + 1) * HD)
        grad_k[...] = jnp.zeros_like(grad_k)
        grad_v[...] = jnp.zeros_like(grad_v)

        @pl.loop(0, length // q_block)
        def one_block(number, head=head, at=at):
            start = pl.multiple_of(number * q_block, q_block)
            here = pl.ds(start, q_block)
            q_rows = query[0, here, at]
            g_rows = grad_mixed[here, at]
            k_all = keys[0, :, at]
            scores = kept_scores(q_rows, k_all, seg_column[0, here], k_seg, start)
            weights = jnp.exp(scores - lses[0, head, here])
            grad_weights = dot(g_rows, values[0, :, at], ((1,), (1,)))
            delta = jnp.sum(weights * grad_weights, axis=1, keepdims=True)
            grad_scores = (weights * (grad_weights - delta)).astype(bf16)
            grad_q[here] = dot(grad_scores, k_all) * scale
            grad_k[...] += dot(grad_scores, q_rows, ((0,), (0,)))
            grad_v[...] += dot(weights.astype(bf16), g_rows, ((0,), (0,)))

        def rounded(value):
            return value.astype(bf16).astype(f32)

        def raw(part):
            first = (part * heads + head) * HD
            return proj[:, 0, :, first : first + HD].reshape(length, HD)

        def put(part, value):
            first = (part * heads + head) * HD
            grad_proj[:, :, first : first + HD] = value.astype(bf16).reshape(ranks, rows, HD)

        back_q, gain_q = norm_rope_back(
            raw(0), gains[0:1], cosine[0], sine[0], rounded(grad_q[...])
        )
        back_k, gain_k = norm_rope_back(
            raw(1), gains[1:2], cosine[0], sine[0], rounded(grad_k[...] * scale)
        )
        sum_q, sum_k = sum_q + gain_q, sum_k + gain_k
        put(0, back_q)
        put(1, back_k)
        put(2, grad_v[...])
    grad_gains[0:1] = sum_q
    grad_gains[1:2] = sum_k


def fixed(shape):
    return pl.BlockSpec(shape, lambda *_: (0,) * len(shape), pipeline_mode=pl.Buffered(1))


def leading(shape):
    return pl.BlockSpec((1,) + shape[1:], lambda i: (i,) + (0,) * (len(shape) - 1))


def params():
    return pltpu.CompilerParams(vmem_limit_bytes=BIG)


def cost(products):
    return pl.CostEstimate(flops=20 * products, bytes_accessed=0, transcendentals=0)


def out(shape, dtype=bf16):
    return jax.ShapeDtypeStruct(shape, dtype)


def attention_forward(proj, cosine, sine, seg_column, seg_row, gains):
    ranks, micro, rows, width = proj.shape
    length = ranks * rows
    width = width // 3
    heads = width // HD
    part = out((micro, length, width))
    by_rank = lambda n: pl.BlockSpec((ranks, 1, rows, n), lambda i: (0, i, 0, 0))
    lses = out((micro, heads, length, 1), f32)
    return pl.pallas_call(
        lambda *refs: forward_kernel(heads, *refs),
        grid=(micro,),
        in_specs=[by_rank(3 * width)]
        + [leading(v.shape) for v in (cosine, sine, seg_column, seg_row)]
        + [fixed(gains.shape)],
        out_specs=[by_rank(width)] + [leading(part.shape)] * 3 + [leading(lses.shape)],
        out_shape=[out((ranks, micro, rows, width)), part, part, part, lses],
        compiler_params=params(),
    )(proj, cosine, sine, seg_column, seg_row, gains)


def attention_backward(
    step, proj, cosine, sine, seg_column, seg_row, gains, query, keys, values, lses, grad_mixed
):
    ranks, micro, rows, width = proj.shape
    length = ranks * rows
    heads = width // 3 // HD

    def part(value):
        return pl.BlockSpec((1,) + value.shape[1:], lambda i: (step,) + (0,) * (value.ndim - 1))

    return pl.pallas_call(
        lambda *refs: backward_kernel(heads, *refs),
        grid=(1,),
        in_specs=[pl.BlockSpec((ranks, 1, rows, width), lambda i: (0, step, 0, 0))]
        + [part(v) for v in (cosine, sine, seg_column, seg_row)]
        + [fixed(gains.shape)]
        + [part(v) for v in (query, keys, values, lses)]
        + [fixed(grad_mixed.shape)],
        out_specs=[fixed((ranks, rows, width)), fixed((2, HD))],
        out_shape=[out((ranks, rows, width)), out((2, HD), f32)],
        scratch_shapes=[pltpu.VMEM((length, HD), f32)] * 3,
        compiler_params=params(),
    )(
        proj, cosine, sine, seg_column, seg_row, gains, query, keys, values, lses, grad_mixed
    )


def project(tokens, gain, slab):
    ranks, count, _ = tokens.shape
    width = slab.shape[1] - PAD

    def kernel(value, gain, weight, normed, proj):
        value = value[0].astype(f32)
        result = (value * inverse_rms(value) * gain[...]).astype(bf16)
        normed[0] = result
        proj[0] = dot(result, weight[:, :width])

    return pl.pallas_call(
        kernel,
        grid=(ranks,),
        in_specs=[leading((ranks, count, D)), fixed((1, D)), fixed(slab.shape)],
        out_specs=[leading((ranks, count, D)), leading((ranks, count, width))],
        out_shape=[out((ranks, count, D)), out((ranks, count, width), f32)],
        compiler_params=params(),
    )(tokens, gain, slab)


TILE = 512


def tiles(count):
    return pl.loop(0, count // TILE)


def tile(number):
    return pl.ds(pl.multiple_of(number * TILE, TILE), TILE)


HBM = pl.BlockSpec(memory_space=pl.ANY)


def copies(pairs, sems):
    started = [
        pltpu.make_async_copy(source, target, sems.at[place])
        for place, (source, target) in enumerate(pairs)
    ]
    for copy in started:
        copy.start()

    def wait():
        for copy in started:
            copy.wait()

    return wait


def plane_pairs(plane, pieces, target):
    planes = len(pieces)
    rows = target.shape[0] // planes
    return [
        (piece, target.at[pl.ds((plane + planes - step) % planes * rows, rows)])
        for step, piece in enumerate(pieces)
    ]


def out_weight_pairs(plane, planes, gathered, target):
    ranks = gathered.shape[0]
    rows = D // (planes * ranks)
    return [
        (
            gathered.at[rank, pl.ds(step * rows, rows)],
            target.at[pl.ds(((plane + planes - step) % planes * ranks + rank) * rows, rows)],
        )
        for rank in range(ranks)
        for step in range(planes)
    ]


def route(plane, planes, mixed, tokens, gathered, gain, router, routes, experts):
    count = tokens.shape[0]
    pieces = planes * gathered.shape[0]

    def kernel(
        plane, mixed, tokens, gathered, gain, router, routes, hidden, payload, gates,
        out_weight, sems,
    ):
        copies(out_weight_pairs(plane[0], planes, gathered, out_weight), sems)()

        @tiles(D)
        def _(number):
            at = tile(number)
            hidden[:, at] = tokens[:, at].astype(f32) + dot(mixed[...], out_weight[:, at])

        value = hidden[...]
        normed = (value * inverse_rms(value) * gain[...]).astype(bf16)
        payload[:, :D] = normed
        logits = dot(normed, router[...])
        column = lax.broadcasted_iota(jnp.int32, logits.shape, 1)
        routed = column == routes[:, 0:1]
        for choice in range(1, TOP):
            routed = routed | (column == routes[:, choice : choice + 1])
        logits = jnp.where(routed, logits, -1e30)
        weights = jnp.exp(logits - jnp.max(logits, axis=1, keepdims=True))
        weights = jnp.where(routed, weights, 0.0)
        weights = weights / jnp.sum(weights, axis=1, keepdims=True)
        gates[...] = weights
        high = weights.astype(bf16).astype(f32)
        payload[:, D:] = (high + pltpu.roll(weights - high, experts, 1)).astype(bf16)

    shapes = [out((count, D), f32), out((count, D + PAD)), out((count, PAD), f32)]
    return pl.pallas_call(
        kernel,
        grid_spec=pltpu.PrefetchScalarGridSpec(
            num_scalar_prefetch=1,
            grid=(1,),
            in_specs=[
                HBM if value is gathered else fixed(value.shape)
                for value in (mixed, tokens, gathered, gain, router, routes)
            ],
            out_specs=[fixed(shape.shape) for shape in shapes],
            scratch_shapes=[pltpu.VMEM((D, D), bf16), pltpu.SemaphoreType.DMA((pieces,))],
        ),
        out_shape=shapes,
        compiler_params=params(),
    )(plane, mixed, tokens, gathered, gain, router, routes)


def lane(value, number):
    column = lax.broadcasted_iota(jnp.int32, value.shape, 1)
    return jnp.sum(jnp.where(column == number, value.astype(f32), 0.0), axis=1, keepdims=True)


def one_hot(slot, slots):
    place = lax.broadcasted_iota(jnp.int32, (slots, slot.shape[1]), 0).astype(f32)
    return (place == slot).astype(bf16)


def expert_forward(where, payload, upstream, in_pieces, slots, experts):
    ranks, share, micro, rows, _ = payload.shape
    count = share * rows
    block = 2 * slots

    planes = len(in_pieces)

    def kernel(where, payload, upstream, *refs):
        (
            rows_in, tail, both, active, grad_produced, up_rows, places, in_weight, sems
        ) = refs[planes:]
        number = where[0]

        @pl.when((pl.program_id(0) == 0) & (pl.program_id(1) == 0))
        def _():
            copies(plane_pairs(where[1], refs[:planes], in_weight), sems)()

        for part in range(2):
            here = slice(part * slots, (part + 1) * slots)
            value = payload[part].reshape(count, D + PAD)
            marks = value[:, D:]
            first = lax.broadcasted_iota(jnp.int32, (8, PAD), 1) == number
            taken = dot(first.astype(bf16), marks, ((1,), (1,))) > 0.0
            before = lax.broadcasted_iota(jnp.int32, (count, count), 0)
            behind = lax.broadcasted_iota(jnp.int32, (count, count), 1)
            slot = dot(taken.astype(bf16), (before < behind).astype(bf16))
            select = one_hot(jnp.where(taken, slot, -1.0)[0:1], slots)
            wide = jnp.broadcast_to(lane(marks, number) > 0.0, (count, PAD))
            slot = dot((before > behind).astype(bf16), wide.astype(bf16))
            places[0, 0, part] = jnp.where(wide, slot, -1.0)
            rows_in[0, 0, here] = dot(select, value[:, :D]).astype(bf16)
            marks = dot(select, marks)
            tail[0, 0, here] = marks
            gate = lane(marks, number) + lane(marks, experts + number)
            picked = dot(select, upstream[part].reshape(count, D))
            up_rows[0, 0, here] = picked.astype(bf16)
            grad_produced[0, 0, here] = (gate * picked).astype(bf16)

        for number in range(FF // TILE):
            at = slice(number * TILE, (number + 1) * TILE)
            more = slice(FF + number * TILE, FF + (number + 1) * TILE)
            gate_part = dot(rows_in[0, 0], in_weight[:, at])
            up_part = dot(rows_in[0, 0], in_weight[:, more])
            both[0, 0, :, at] = gate_part
            both[0, 0, :, more] = up_part
            active[0, 0, :, at] = (
                gate_part / (1.0 + jnp.exp(-gate_part)) * up_part
            ).astype(bf16)

    def tokens_spec(width):
        return pl.BlockSpec((2, share, 1, rows, width), lambda m, b, _: (b, 0, m, 0, 0))

    pairs = ranks // 2
    shapes = [
        out((micro, pairs, block, D)),
        out((micro, pairs, block, PAD), f32),
        out((micro, pairs, block, 2 * FF), f32),
        out((micro, pairs, block, FF)),
        out((micro, pairs, block, D)),
        out((micro, pairs, block, D)),
        out((micro, pairs, 2, count, PAD), f32),
    ]
    return pl.pallas_call(
        kernel,
        grid_spec=pltpu.PrefetchScalarGridSpec(
            num_scalar_prefetch=1,
            grid=(micro, pairs),
            in_specs=[tokens_spec(D + PAD), tokens_spec(D)] + [HBM] * planes,
            out_specs=[
                pl.BlockSpec(
                    (1, 1) + s.shape[2:], lambda m, b, _, n=len(s.shape): (m, b) + (0,) * (n - 2)
                )
                for s in shapes
            ],
            scratch_shapes=[pltpu.VMEM((D, 2 * FF), bf16), pltpu.SemaphoreType.DMA((planes,))],
        ),
        out_shape=shapes,
        cost_estimate=cost(micro * pairs * block * D * (2 * FF + 2 * count)),
        compiler_params=params(),
    )(where, payload, upstream, *in_pieces)


def expert_backward(
    step, where, tail, both, active, grad_produced, up_rows, places, in_pieces, out_pieces,
    share, rows, experts,
):
    pairs, block = tail.shape[1:3]
    slots = block // 2
    count = places.shape[3]

    planes = len(in_pieces)

    def kernel(where, tail, both, active, grad_produced, up_rows, places, *refs):
        keep, give, grad_tokens, grad_both, in_weight, out_weight, sems = refs[2 * planes :]
        number = where[0]
        odd = where[2] == 1

        @pl.when(pl.program_id(0) == 0)
        def _():
            copies(
                plane_pairs(where[1], refs[:planes], in_weight)
                + plane_pairs(where[1], refs[planes : 2 * planes], out_weight),
                sems,
            )()

        gate = lane(tail[0, 0], number) + lane(tail[0, 0], experts + number)
        place = lax.broadcasted_iota(jnp.int32, (count, slots), 1).astype(f32)
        selects = [(places[0, 0, part][:, 0:1] == place).astype(bf16) for part in range(2)]

        def spread(value):
            return [
                dot(selects[part], value[part * slots : (part + 1) * slots])
                .astype(bf16)
                .reshape(share, rows, -1)
                for part in range(2)
            ]

        grad_gate = jnp.zeros((block, 1), f32)
        for tile in range(D // TILE):
            at = slice(tile * TILE, (tile + 1) * TILE)
            produced = dot(active[0, 0], out_weight[:, at]).astype(bf16).astype(f32)
            even_rank, odd_rank = spread((gate * produced).astype(bf16))
            keep[0, :, :, at] = jnp.where(odd, odd_rank, even_rank)
            give[0, :, :, at] = jnp.where(odd, even_rank, odd_rank)
            grad_gate = grad_gate + jnp.sum(
                up_rows[0, 0, :, at].astype(f32) * produced, axis=1, keepdims=True
            )

        for tile in range(FF // TILE):
            at = slice(tile * TILE, (tile + 1) * TILE)
            more = slice(FF + tile * TILE, FF + (tile + 1) * TILE)
            grad_active = dot(grad_produced[0, 0], out_weight[at, :], ((1,), (1,)))
            grad_active = grad_active.astype(bf16).astype(f32)
            gate_part = both[0, 0, :, at]
            up_part = both[0, 0, :, more]
            sigma = 1.0 / (1.0 + jnp.exp(-gate_part))
            grad_both[0, :, at] = (
                grad_active * up_part * (sigma * (1.0 + gate_part * (1.0 - sigma)))
            ).astype(bf16)
            grad_both[0, :, more] = (grad_active * (gate_part * sigma)).astype(bf16)

        for tile in range(D // TILE):
            at = slice(tile * TILE, (tile + 1) * TILE)
            grad_rows = dot(grad_both[0], in_weight[at, :], ((1,), (1,))).astype(bf16)
            grad_tokens[0, :, :, at], grad_tokens[1, :, :, at] = spread(grad_rows)

        high = grad_gate.astype(bf16).astype(f32)
        column = lax.broadcasted_iota(jnp.int32, (block, PAD), 1)
        extra = jnp.where(column == number, high, 0.0)
        extra = jnp.where(column == experts + number, grad_gate - high, extra)
        grad_tokens[0, :, :, D:], grad_tokens[1, :, :, D:] = spread(extra.astype(bf16))

    def part(value):
        return pl.BlockSpec(
            (1, 1) + value.shape[2:], lambda b, _: (step, b) + (0,) * (value.ndim - 2)
        )

    def tokens_spec(count, width):
        return pl.BlockSpec((count, share, rows, width), lambda b, _: (b, 0, 0, 0))

    return pl.pallas_call(
        kernel,
        grid_spec=pltpu.PrefetchScalarGridSpec(
            num_scalar_prefetch=1,
            grid=(pairs,),
            in_specs=[part(v) for v in (tail, both, active, grad_produced, up_rows, places)]
            + [HBM] * (2 * planes),
            out_specs=[
                tokens_spec(1, D),
                tokens_spec(1, D),
                tokens_spec(2, D + PAD),
                pl.BlockSpec((1, block, 2 * FF), lambda b, _: (b, 0, 0)),
            ],
            scratch_shapes=[
                pltpu.VMEM((D, 2 * FF), bf16),
                pltpu.VMEM((FF, D), bf16),
                pltpu.SemaphoreType.DMA((2 * planes,)),
            ],
        ),
        out_shape=[
            out((pairs, share, rows, D)),
            out((pairs, share, rows, D)),
            out((2 * pairs, share, rows, D + PAD)),
            out((pairs, block, 2 * FF)),
        ],
        cost_estimate=cost(pairs * block * D * (4 * FF + 2 * count)),
        compiler_params=params(),
    )(
        where, tail, both, active, grad_produced, up_rows, places, *in_pieces, *out_pieces
    )


def weight_gradient(where, planes, left, rights, tail=None, first=0, steps=None):
    steps = planes if steps is None else steps
    count, width = left.shape
    parts = len(rights)
    part_rows = count // parts
    columns = rights[0].shape[1]
    width = width // planes
    step = min(TILE, columns & -columns)
    tails = [] if tail is None else [tail]
    whole = columns + sum(value.shape[1] for value in tails)

    def of_plane(i, where):
        return (where[1] + first + i) % planes

    def kernel(where, left, *refs):
        rights, tails, targets = refs[:parts], refs[parts:-steps], refs[-steps:]

        def fill(target):
            for value in tails:
                target[:, columns:] = value[...]
            for number in range(columns // step):
                at = slice(number * step, (number + 1) * step)
                target[:, at] = sum(
                    dot(left[part * part_rows : (part + 1) * part_rows], right[:, at], ((0,), (0,)))
                    for part, right in enumerate(rights)
                ).astype(bf16)

        for number, target in enumerate(targets):
            pl.when(pl.program_id(0) == number)(lambda target=target: fill(target))

    return pl.pallas_call(
        kernel,
        grid_spec=pltpu.PrefetchScalarGridSpec(
            num_scalar_prefetch=1,
            grid=(steps,),
            in_specs=[pl.BlockSpec((count, width), lambda i, where: (0, of_plane(i, where)))]
            + [fixed(right.shape) for right in rights]
            + [
                pl.BlockSpec((width, value.shape[1]), lambda i, where: (of_plane(i, where), 0))
                for value in tails
            ],
            out_specs=[fixed((width, whole))] * steps,
        ),
        out_shape=[out((width, whole))] * steps,
        cost_estimate=cost(0 if tails else count * steps * width * columns),
        compiler_params=params(),
    )(where, left, *rights, *tails)


def hidden_backward(
    plane, planes, parts, hidden, gates, upstream, gain, router, gathered, experts
):
    count = hidden.shape[0]
    terms = len(parts)

    def kernel(plane, *refs):
        parts = refs[:terms]
        hidden, gates, upstream, gain, router, gathered = refs[terms : terms + 6]
        (
            grad_hidden, grad_branch, grad_mixed, grad_logits, grad_gain, out_weight, sems
        ) = refs[terms + 6 :]
        wait = copies(out_weight_pairs(plane[0], planes, gathered, out_weight), sems)
        returned = sum(part[...].astype(f32) for part in parts)
        tail = returned[:, D:]
        grad_gates = gates[...] * (tail + pltpu.roll(tail, PAD - experts, 1))
        logits = grad_gates - gates[...] * jnp.sum(grad_gates, axis=1, keepdims=True)
        logits = logits.astype(bf16)
        grad_logits[...] = logits
        grad_normed = returned[:, :D] + dot(logits, router[...], ((1,), (1,)))
        value = hidden[...]
        inverse = inverse_rms(value)
        grad_gain[...] = jnp.sum(grad_normed * value * inverse, axis=0, keepdims=True)
        grad = upstream[...].astype(f32) + rms_backward(value, inverse, gain[...], grad_normed)
        grad_hidden[...] = grad
        grad_branch[...] = grad.astype(bf16)
        wait()

        @tiles(D)
        def _(number):
            at = tile(number)
            grad_mixed[:, at] = dot(grad_branch[...], out_weight[at, :], ((1,), (1,))).astype(bf16)

    shapes = [
        out((count, D), f32), out((count, D)), out((count, D)), out((count, PAD)),
        out((1, D), f32),
    ]
    args = (*parts, hidden, gates, upstream, gain, router, gathered)
    return pl.pallas_call(
        kernel,
        grid_spec=pltpu.PrefetchScalarGridSpec(
            num_scalar_prefetch=1,
            grid=(1,),
            in_specs=[HBM if value is gathered else fixed(value.shape) for value in args],
            out_specs=[fixed(shape.shape) for shape in shapes],
            scratch_shapes=[
                pltpu.VMEM((D, D), bf16),
                pltpu.SemaphoreType.DMA((planes * gathered.shape[0],)),
            ],
        ),
        out_shape=shapes,
        compiler_params=params(),
    )(plane, *args)


def project_backward(step, grad_proj, tokens, slab):
    ranks, rows, _ = grad_proj.shape
    width = slab.shape[1] - PAD

    def kernel(grad_proj, tokens, weight, grad_normed, grad_gain):
        value = tokens[0].astype(f32)
        inverse = inverse_rms(value)
        grad = dot(grad_proj[0], weight[:, :width], ((1,), (1,)))
        grad_normed[...] = grad.astype(bf16)

        @pl.when(pl.program_id(0) == 0)
        def _():
            grad_gain[...] = jnp.zeros_like(grad_gain)

        grad_gain[...] += jnp.sum(grad * value * inverse, axis=0, keepdims=True)

    return pl.pallas_call(
        kernel,
        grid=(ranks,),
        in_specs=[
            leading(grad_proj.shape),
            pl.BlockSpec((1, rows, D), lambda i: (i, step, 0)),
            fixed(slab.shape),
        ],
        out_specs=[pl.BlockSpec((rows, D), lambda i: (i, 0)), fixed((1, D))],
        out_shape=[out((ranks * rows, D)), out((1, D), f32)],
        compiler_params=params(),
    )(grad_proj, tokens, slab)


def shift_rep(value, step):
    count = lax.axis_size("rep")
    return lax.ppermute(value, "rep", [(i, (i + step) % count) for i in range(count)])


def after(value, *others):
    return lax.optimization_barrier((value,) + others)[0]


def two_parts(value):
    high = lax.reduce_precision(value, 8, 7)
    return high.astype(bf16), (value - high).astype(bf16)


def shift_order(count):
    return sorted(range(1, count), key=lambda step: (min(step, count - step), step))


def ring_rep(value, *work):
    count = lax.axis_size("rep")
    rank = lax.axis_index("rep")
    rows = value.shape[0]
    full = jnp.zeros((count * rows,) + value.shape[1:], value.dtype)
    full = lax.dynamic_update_slice_in_dim(full, value, rank * rows, 0)
    for step in range(1, count):
        value, work = lax.optimization_barrier((value, work)) if step == 2 else (value, work)
        value = shift_rep(value, 1)
        full = lax.dynamic_update_slice_in_dim(full, value, (rank - step) % count * rows, 0)
    return full, work


def on_device(
    tokens, cotangent, w_qkv, w_o, w_router, norm_gains, qk_gain, w_in, w_out, segments, routes
):
    planes = lax.axis_size("rep")
    ranks = lax.axis_size("ep")
    plane = lax.axis_index("rep")
    rank = lax.axis_index("ep")
    share = w_in.shape[0]
    own = plane % share
    experts = share * ranks
    where = jnp.stack([rank * share + own, plane, rank % 2]).astype(jnp.int32)
    micro = segments.shape[1]
    mine = tokens.shape[0]
    rows = mine // micro
    length = rows * ranks
    capacity = rows * TOP * 17 // (16 * experts)
    slots = -(-share * capacity // 16) * 16
    width = HEADS // ranks * HD
    qk_gains = qk_gain.astype(f32).reshape(2, HD)
    dense_rows = w_qkv.shape[0]

    def exchange(value, step):
        pairs = [(i, i // share * share + (i % share + step) % share) for i in range(planes)]
        return lax.ppermute(value, "rep", pairs)

    def with_group(value):
        return jnp.stack([value] + [exchange(value, step) for step in range(1, share)])

    def gather_ranks(value):
        return lax.all_gather(value, "ep", axis=0)

    order = shift_order(planes)
    in_parts, out_parts = (
        {
            step: lax.dynamic_index_in_dim(weight, (own + step) % share, 0, keepdims=False)
            for step in [0] + order
        }
        for weight in (w_in, w_out)
    )

    def send(parts, steps):
        return {step: shift_rep(parts[step], step) for step in steps}

    stream = gather_ranks(tokens)
    out_rows = [w_o] + [shift_rep(w_o, step) for step in range(1, planes)]
    upstream_group = with_group(cotangent)
    slab = jnp.concatenate(
        [
            w_qkv.reshape(dense_rows, 3, ranks, width)
            .transpose(2, 0, 1, 3)
            .reshape(ranks, dense_rows, 3 * width),
            jnp.broadcast_to(
                jnp.concatenate(
                    [
                        w_router,
                        norm_gains.reshape(dense_rows, 2),
                        jnp.zeros((dense_rows, PAD - experts - 2), bf16),
                    ],
                    axis=1,
                )[None],
                (ranks, dense_rows, PAD),
            ),
        ],
        axis=2,
    )
    slab = lax.all_to_all(slab, "ep", split_axis=0, concat_axis=0, tiled=True)
    slab = slab.reshape(ranks * dense_rows, 3 * width + PAD)
    out_rows, upstream_group, slab = lax.optimization_barrier((out_rows, upstream_group, slab))
    gathered = gather_ranks(jnp.concatenate(out_rows, axis=0))
    segment = segments[0]
    cosine, sine = jax.vmap(lambda one: rope_tables(doc_positions(one), HD))(segment)
    sine = jnp.where(jnp.arange(HD) < HD // 2, -sine, sine)
    tables = (cosine, sine, segment[:, :, None], segment[:, None, :], qk_gains)
    slab, (tables, in_parts, out_parts) = ring_rep(slab, tables, in_parts, out_parts)
    router = slab[:, 3 * width :]
    gain_pair = router[:, experts : experts + 2].reshape(-1).astype(f32)
    first_gain = gain_pair[None, :D]
    second_gain = gain_pair[None, D:]
    in_parts, out_parts, upstream_group, stream = after(
        (in_parts, out_parts, upstream_group, stream), slab
    )
    in_pieces = {0: in_parts[0], **send(in_parts, order[:-1])}
    upstream_all = gather_ranks(upstream_group)

    normed, proj = project(stream, first_gain, slab)
    proj = proj.reshape(ranks, micro, rows, 3 * width)
    mixed_h, query, keys, values, lses = attention_forward(proj, *tables)
    mixed = lax.all_to_all(mixed_h, "ep", split_axis=0, concat_axis=3, tiled=True)
    mixed = mixed.reshape(mine, D)
    hidden, payload, gates = route(
        where[1:2], planes, mixed, tokens, gathered, second_gain, router, routes, experts
    )
    normed_two = payload[:, :D]
    payload, in_pieces = lax.optimization_barrier((payload, in_pieces))
    payload = with_group(payload)
    payload, in_parts, out_parts = lax.optimization_barrier((payload, in_parts, out_parts))
    in_pieces.update(send(in_parts, order[-1:]))
    in_pieces, out_parts = lax.optimization_barrier((in_pieces, out_parts))
    out_pieces = {0: out_parts[0], **send(out_parts, order)}
    in_pieces = [in_pieces[step] for step in range(planes)]
    out_pieces = [out_pieces[step] for step in range(planes)]
    payload = gather_ranks(payload)

    shape = (ranks, share, micro, rows, -1)
    rows_in, tail, both, active, grad_produced, up_rows, places = expert_forward(
        where, payload.reshape(shape), upstream_all.reshape(shape), in_pieces, slots, experts
    )
    in_rows = micro * ranks * slots
    out_cut = weight_gradient(
        where, planes, active.reshape(in_rows, FF), [grad_produced.reshape(in_rows, D)]
    )

    def sum_rep(parts):
        sums = [
            sum(parts[step].astype(f32) for step in range(first, planes, share))
            for first in range(share)
        ]
        return jnp.stack(
            [
                sum(jnp.where((own - step) % share == j, sums[step], 0.0) for step in range(share))
                for j in range(share)
            ]
        )

    tail, out_cut, out_pieces = lax.optimization_barrier((tail, out_cut, out_pieces))
    out_sent = send(out_cut, order)
    back = []
    returned = []

    def scatter_ranks(value):
        return lax.psum_scatter(value, "ep", scatter_dimension=0)

    def exchange_back(value):
        return [value[0]] + [exchange(value[step], share - step) for step in range(1, share)]

    for step in range(micro):
        back.append(
            expert_backward(
                step, where, tail, both, active, grad_produced, up_rows, places, in_pieces,
                out_pieces, share, rows, experts,
            )
        )
        returned.append(scatter_ranks(back[step][2]))
        if step == 0:
            tail, out_sent[order[0]] = after((tail, out_sent[order[0]]), back[step][2])
        else:
            tail = after(tail, back[step][2])
    rows_in = after(rows_in, tail)
    rows_flat = rows_in.reshape(in_rows, D)
    grads_flat = [back[step][3].reshape(in_rows // micro, 2 * FF) for step in range(micro)]
    near = weight_gradient(where, planes, rows_flat, grads_flat, first=order[0], steps=1)
    rows_flat, near = lax.optimization_barrier((rows_flat, near))
    far = weight_gradient(
        where, planes, rows_flat, grads_flat, first=order[0] + 1, steps=planes - 1
    )
    in_cut = {(order[0] + 1 + i) % planes: part for i, part in enumerate(far)}
    in_cut[order[0]], = near
    in_sent = send(in_cut, order[:1])

    def swap(value, step):
        return lax.ppermute(value, "ep", [(i, i ^ step) for i in range(ranks)])

    def pair_sum(keep, give):
        return (keep.astype(f32) + swap(give, 1).astype(f32)).astype(bf16)

    bits = list(range((ranks // 2).bit_length() - 1))

    def halve(values, phase):
        results = []
        for number, value in enumerate(values):
            way = bits if number % 2 == 0 else bits[::-1]
            bit = way[phase]
            low = 2 ** sum(other < bit for other in way[phase:])
            value = value.reshape((-1, 2, low) + value.shape[1:])
            side = rank // 2 // 2**bit % 2
            keep, give = (
                lax.dynamic_index_in_dim(value, which, 1, keepdims=False).reshape(
                    (-1,) + value.shape[3:]
                )
                for which in (side, 1 - side)
            )
            results.append((keep, swap(give, 2 * 2**bit)))
        return results

    def total(parts):
        return sum(part.astype(f32) for part in parts)

    grad_inputs, branches, logit_grads, grad_projs = [], [], [], []
    gain_two_sum = gain_one_sum = qk_sum = 0.0
    in_cut, out_sent, in_sent = lax.optimization_barrier((in_cut, out_sent, in_sent))
    mixtures = [part[:2] for part in back]
    releases = [order[1:-1]] + [[]] * (micro - 1)
    for step in range(micro):
        at = slice(step * rows, (step + 1) * rows)
        parts = after(returned[step], [one[1] for one in grad_inputs])
        parts, in_sent = lax.optimization_barrier((parts, in_sent))
        parts = exchange_back(parts)
        parts, in_cut, mixtures = lax.optimization_barrier((parts, in_cut, mixtures))
        if step == 0:
            mixtures = [pair_sum(*part) for part in mixtures]
        in_sent.update(send(in_cut, releases[step]))
        if step == micro - 1:
            last = in_cut[order[-1]]
            ends = [-(-last.shape[0] * part // 64) * 16 for part in range(5)]
            last = [last[start:end] for start, end in zip(ends, ends[1:])]
            last_sent = [shift_rep(last[0], order[-1])]
        grad_hidden, grad_branch, grad_mixed, grad_logits, gain_two = hidden_backward(
            where[1:2], planes, parts, hidden[at], gates[at], cotangent[at], second_gain,
            router, gathered, experts,
        )
        branches.append(grad_branch)
        logit_grads.append(grad_logits)
        gain_two_sum = gain_two_sum + gain_two
        if step == micro - 1:
            out_sum = dot(mixed, jnp.concatenate(branches, axis=0), ((0,), (0,))).astype(bf16)
            out_sum = out_sum.reshape(planes, ranks, dense_rows, D).transpose(1, 0, 2, 3)
        grad_mixed = lax.all_to_all(grad_mixed, "ep", split_axis=1, concat_axis=0, tiled=True)
        grad_mixed, mixtures = lax.optimization_barrier((grad_mixed, mixtures))
        if step == micro - 1:
            grad_mixed, mixtures, last_sent, last, out_sum = lax.optimization_barrier(
                (grad_mixed, mixtures, last_sent, last, out_sum)
            )
            out_sum = lax.psum_scatter(out_sum, "ep", scatter_dimension=0)
            last_sent.append(shift_rep(last[1], order[-1]))
        grad_proj, grad_qk = attention_backward(
            step, proj, *tables, query, keys, values, lses, grad_mixed
        )
        qk_sum = qk_sum + grad_qk.reshape(-1)
        if step < micro - 1:
            grad_proj, in_sent = lax.optimization_barrier((grad_proj, in_sent))
        else:
            grad_proj, grad_inputs, last_sent, last = lax.optimization_barrier(
                (grad_proj, grad_inputs, last_sent, last)
            )
            last_sent.append(shift_rep(last[2], order[-1]))
        grad_projs.append(grad_proj)
        grad_normed, gain_one = project_backward(step, grad_proj, stream, slab)
        gain_one_sum = gain_one_sum + gain_one
        grad_inputs.append(
            (
                grad_hidden,
                grad_normed,
                lax.psum_scatter(grad_normed, "ep", scatter_dimension=0, tiled=True),
            )
        )

    router_sum = dot(normed_two, jnp.concatenate(logit_grads, axis=0), ((0,), (0,)))
    qk_columns = qk_sum.shape[0] // dense_rows
    small = jnp.concatenate(
        [
            router_sum[:, :experts],
            jnp.concatenate([gain_one_sum, gain_two_sum], axis=1).reshape(D, 2),
            jnp.tile(qk_sum.reshape(dense_rows, qk_columns), (planes * ranks, 1)),
        ],
        axis=1,
    )
    count = small.shape[1]

    def halves(value):
        high, low = two_parts(value)
        blank = jnp.zeros((value.shape[0], PAD - 2 * count), bf16)
        return jnp.concatenate([high, low, blank], axis=1)

    def joined(value):
        return value[..., :count].astype(f32) + value[..., count : 2 * count].astype(f32)

    grad_projs, last_sent, last, out_cut, out_sent, _ = lax.optimization_barrier(
        (grad_projs, last_sent, last, out_cut, out_sent, grad_normed)
    )
    last_sent.append(shift_rep(last[3], order[-1]))
    packed = weight_gradient(
        where,
        planes,
        normed.reshape(ranks * mine, D),
        [jnp.stack(grad_projs, axis=1).reshape(ranks * mine, 3 * width)],
        halves(small),
    )
    packed, last_sent, out_cut, out_sent, mixtures = lax.optimization_barrier(
        (packed, last_sent, out_cut, out_sent, mixtures)
    )
    packed_sent = [packed[0]] + [shift_rep(packed[step], step) for step in range(1, planes)]
    for phase in range(len(bits)):
        crossed = halve(mixtures, phase)
        if phase < len(bits) - 1:
            mixtures = [total(parts).astype(bf16) for parts in crossed]
    normed_sums = [one[2] for one in grad_inputs]
    packed_sent, crossed = lax.optimization_barrier((packed_sent, crossed))
    mixture = []
    for number in range(micro):
        parts = total(crossed[number])[0]
        mixture.append(parts[0] + total(exchange_back(parts.astype(bf16))[1:]))
    output = (hidden + jnp.concatenate(mixture, axis=0)).astype(bf16)
    grad_tokens = []
    for step in range(micro):
        grad_hidden, grad_normed = grad_inputs[step][0], normed_sums[step]
        own_stream = tokens[step * rows : (step + 1) * rows].astype(f32)
        grad_tokens.append(
            grad_hidden
            + rms_backward(
                own_stream, inverse_rms(own_stream), first_gain, grad_normed.astype(f32)
            )
        )
    main = total([part[:, : 3 * width] for part in packed_sent]).astype(bf16)
    small = sum(joined(part[:, 3 * width :]) for part in packed_sent)
    packed = jnp.concatenate([main, halves(small)], axis=1).reshape(ranks, dense_rows, -1)
    packed = lax.all_to_all(packed, "ep", split_axis=0, concat_axis=0, tiled=True)
    main = packed[..., : 3 * width].astype(f32)
    small = jnp.sum(joined(packed[..., 3 * width :]), axis=0)
    grad_w_qkv = (
        main.reshape(ranks, dense_rows, 3, width).transpose(1, 2, 0, 3).reshape(dense_rows, 3 * D)
    )
    grad_w_out = sum_rep({0: out_cut[0], **out_sent})
    in_sent[order[-1]] = jnp.concatenate(last_sent, axis=0)
    grad_w_in = sum_rep({0: in_cut[0], **in_sent})
    grad_w_o = lax.dynamic_index_in_dim(out_sum, plane, 0, keepdims=False).astype(f32)
    for step in range(1, planes):
        part = lax.dynamic_index_in_dim(out_sum, (plane + step) % planes, 0, keepdims=False)
        grad_w_o = grad_w_o + shift_rep(part, step).astype(f32)
    return (
        output,
        jnp.concatenate(grad_tokens, axis=0),
        grad_w_qkv,
        grad_w_o,
        small[:, :experts],
        small[:, experts : experts + 2].reshape(-1),
        small[:, experts + 2 :].reshape(-1),
        grad_w_in,
        grad_w_out,
    )


def solution(mesh):
    placed = (
        P(("rep", "ep"), None),
        P(("rep", "ep"), None),
        P(("rep", "ep"), None),
        P(("rep", "ep"), None),
        P(("rep", "ep"), None),
        P(("rep", "ep")),
        P(),
        P("ep", "rep", None),
        P("ep", "rep", None),
        P("rep", None, None),
        P(("rep", "ep"), None),
    )
    return jax.shard_map(
        on_device,
        mesh=mesh,
        in_specs=placed,
        out_specs=(
            P(("rep", "ep"), None),
            P(("rep", "ep"), None),
            P(("rep", "ep"), None),
            P(("rep", "ep"), None),
            P(("rep", "ep"), None),
            P(("rep", "ep")),
            P(),
            P("ep", "rep", None),
            P("ep", "rep", None),
        ),
        check_vma=False,
    )
```

```python
import math

import jax
import jax.numpy as jnp
from jax import lax
from jax.experimental import pallas as pl
from jax.experimental.pallas import tpu as pltpu
from jax.sharding import PartitionSpec as P

D = 2048
HEADS = 16
HD = 128
FF = 1024
TOP = 8
HALF = 512
PAD = 128

epsilon = 1e-06
rope_base = 50000.0
bf16 = jnp.bfloat16
f32 = jnp.float32


def dot(a, b, dims=((1,), (0,))):
    return lax.dot_general(a, b, (dims, ((), ())), preferred_element_type=f32)


def inverse_rms(value):
    return lax.rsqrt(jnp.mean(value * value, axis=-1, keepdims=True) + epsilon)


def rms_backward(value, inverse, gain, grad):
    scaled = grad * gain
    inner = jnp.mean(scaled * value, axis=-1, keepdims=True)
    return inverse * (scaled - value * (inverse * inverse * inner))


def doc_positions(segment):
    index = jnp.arange(segment.shape[0], dtype=jnp.int32)
    change = jnp.concatenate([jnp.ones((1,), dtype=jnp.bool_), segment[1:] != segment[:-1]])
    start = lax.cummax(jnp.where(change, index, 0), axis=0)
    return index - start


def rope_tables(position, width):
    steps = jnp.arange(width // 2, dtype=f32) * (2.0 / width)
    rates = jnp.exp(-steps * math.log(rope_base))
    angle = position.astype(f32)[:, None] * rates[None, :]
    angle = jnp.concatenate([angle, angle], axis=-1)
    return (jnp.cos(angle), jnp.sin(angle))


def norm_rope(value, gain, cosine, sine):
    inverse = lax.rsqrt(jnp.mean(value * value, axis=1, keepdims=True) + epsilon)
    value = value * inverse * gain
    return value * cosine + pltpu.roll(value, HD // 2, 1) * sine


def norm_rope_back(value, gain, cosine, sine, grad):
    inverse = lax.rsqrt(jnp.mean(value * value, axis=1, keepdims=True) + epsilon)
    grad = grad * cosine + pltpu.roll(grad * sine, HD // 2, 1)
    normal = value * inverse
    scaled = grad * gain
    inner = jnp.mean(scaled * normal, axis=1, keepdims=True)
    return inverse * (scaled - normal * inner), jnp.sum(grad * normal, axis=0, keepdims=True)


def kept_scores(query, keys, q_seg, k_seg, start):
    scores = dot(query, keys, ((1,), (1,))) * (1.0 / math.sqrt(HD))
    q_index = start + lax.broadcasted_iota(jnp.int32, scores.shape, 0)
    k_index = lax.broadcasted_iota(jnp.int32, scores.shape, 1)
    keep = (jnp.abs(q_index - k_index) <= HALF) & (q_seg == k_seg)
    return jnp.where(keep, scores, -1e30)


BIG = 100 * 1024 * 1024 // 2


def forward_kernel(
    heads, proj, cosine, sine, seg_column, seg_row, gains, mixed, query, keys, values, lses
):
    ranks, _, rows, _ = proj.shape
    length = ranks * rows
    q_block = 2 * rows
    k_seg = seg_row[0]
    for head in range(heads):
        at = slice(head * HD, (head + 1) * HD)

        def raw(part):
            first = (part * heads + head) * HD
            return proj[:, 0, :, first : first + HD].reshape(length, HD)

        query[0, :, at] = norm_rope(raw(0), gains[0:1], cosine[0], sine[0]).astype(bf16)
        keys[0, :, at] = norm_rope(raw(1), gains[1:2], cosine[0], sine[0]).astype(bf16)
        values[0, :, at] = raw(2).astype(bf16)

        @pl.loop(0, length // q_block)
        def one_block(number, head=head, at=at):
            start = pl.multiple_of(number * q_block, q_block)
            here = pl.ds(start, q_block)
            scores = kept_scores(
                query[0, here, at], keys[0, :, at], seg_column[0, here], k_seg, start
            )
            top = jnp.max(scores, axis=1, keepdims=True)
            weights = jnp.exp(scores - top)
            total = jnp.sum(weights, axis=1, keepdims=True)
            lses[0, head, here] = top + jnp.log(total)
            weights = (weights * (1.0 / total)).astype(bf16)
            result = dot(weights, values[0, :, at]).astype(bf16)
            mixed[pl.ds(number * 2, 2), 0, :, at] = result.reshape(2, rows, HD)


def backward_kernel(
    heads, proj, cosine, sine, seg_column, seg_row, gains, query, keys, values, lses, grad_mixed,
    grad_proj, grad_gains, grad_q, grad_k, grad_v,
):
    ranks, _, rows, _ = proj.shape
    length = ranks * rows
    q_block = 2 * rows
    k_seg = seg_row[0]
    scale = 1.0 / math.sqrt(HD)
    sum_q = jnp.zeros((1, HD), f32)
    sum_k = jnp.zeros((1, HD), f32)
    for head in range(heads):
        at = slice(head * HD, (head + 1) * HD)
        grad_k[...] = jnp.zeros_like(grad_k)
        grad_v[...] = jnp.zeros_like(grad_v)

        @pl.loop(0, length // q_block)
        def one_block(number, head=head, at=at):
            start = pl.multiple_of(number * q_block, q_block)
            here = pl.ds(start, q_block)
            q_rows = query[0, here, at]
            g_rows = grad_mixed[here, at]
            k_all = keys[0, :, at]
            scores = kept_scores(q_rows, k_all, seg_column[0, here], k_seg, start)
            weights = jnp.exp(scores - lses[0, head, here])
            grad_weights = dot(g_rows, values[0, :, at], ((1,), (1,)))
            delta = jnp.sum(weights * grad_weights, axis=1, keepdims=True)
            grad_scores = (weights * (grad_weights - delta)).astype(bf16)
            grad_q[here] = dot(grad_scores, k_all) * scale
            grad_k[...] += dot(grad_scores, q_rows, ((0,), (0,)))
            grad_v[...] += dot(weights.astype(bf16), g_rows, ((0,), (0,)))

        def rounded(value):
            return value.astype(bf16).astype(f32)

        def raw(part):
            first = (part * heads + head) * HD
            return proj[:, 0, :, first : first + HD].reshape(length, HD)

        def put(part, value):
            first = (part * heads + head) * HD
            grad_proj[:, :, first : first + HD] = value.astype(bf16).reshape(ranks, rows, HD)

        back_q, gain_q = norm_rope_back(
            raw(0), gains[0:1], cosine[0], sine[0], rounded(grad_q[...])
        )
        back_k, gain_k = norm_rope_back(
            raw(1), gains[1:2], cosine[0], sine[0], rounded(grad_k[...] * scale)
        )
        sum_q, sum_k = sum_q + gain_q, sum_k + gain_k
        put(0, back_q)
        put(1, back_k)
        put(2, grad_v[...])
    grad_gains[0:1] = sum_q
    grad_gains[1:2] = sum_k


def fixed(shape):
    return pl.BlockSpec(shape, lambda *_: (0,) * len(shape), pipeline_mode=pl.Buffered(1))


def leading(shape):
    return pl.BlockSpec((1,) + shape[1:], lambda i: (i,) + (0,) * (len(shape) - 1))


def params():
    return pltpu.CompilerParams(vmem_limit_bytes=BIG)


def cost(products):
    return pl.CostEstimate(flops=20 * products, bytes_accessed=0, transcendentals=0)


def out(shape, dtype=bf16):
    return jax.ShapeDtypeStruct(shape, dtype)


def attention_forward(proj, cosine, sine, seg_column, seg_row, gains):
    ranks, micro, rows, width = proj.shape
    length = ranks * rows
    width = width // 3
    heads = width // HD
    part = out((micro, length, width))
    by_rank = lambda n: pl.BlockSpec((ranks, 1, rows, n), lambda i: (0, i, 0, 0))
    lses = out((micro, heads, length, 1), f32)
    return pl.pallas_call(
        lambda *refs: forward_kernel(heads, *refs),
        grid=(micro,),
        in_specs=[by_rank(3 * width)]
        + [leading(v.shape) for v in (cosine, sine, seg_column, seg_row)]
        + [fixed(gains.shape)],
        out_specs=[by_rank(width)] + [leading(part.shape)] * 3 + [leading(lses.shape)],
        out_shape=[out((ranks, micro, rows, width)), part, part, part, lses],
        compiler_params=params(),
    )(proj, cosine, sine, seg_column, seg_row, gains)


def attention_backward(
    step, proj, cosine, sine, seg_column, seg_row, gains, query, keys, values, lses, grad_mixed
):
    ranks, micro, rows, width = proj.shape
    length = ranks * rows
    heads = width // 3 // HD

    def part(value):
        return pl.BlockSpec((1,) + value.shape[1:], lambda i: (step,) + (0,) * (value.ndim - 1))

    return pl.pallas_call(
        lambda *refs: backward_kernel(heads, *refs),
        grid=(1,),
        in_specs=[pl.BlockSpec((ranks, 1, rows, width), lambda i: (0, step, 0, 0))]
        + [part(v) for v in (cosine, sine, seg_column, seg_row)]
        + [fixed(gains.shape)]
        + [part(v) for v in (query, keys, values, lses)]
        + [fixed(grad_mixed.shape)],
        out_specs=[fixed((ranks, rows, width)), fixed((2, HD))],
        out_shape=[out((ranks, rows, width)), out((2, HD), f32)],
        scratch_shapes=[pltpu.VMEM((length, HD), f32)] * 3,
        compiler_params=params(),
    )(
        proj, cosine, sine, seg_column, seg_row, gains, query, keys, values, lses, grad_mixed
    )


def project(tokens, gain, slab):
    ranks, count, _ = tokens.shape
    width = slab.shape[1] - PAD

    def kernel(value, gain, weight, normed, proj):
        value = value[0].astype(f32)
        result = (value * inverse_rms(value) * gain[...]).astype(bf16)
        normed[0] = result
        proj[0] = dot(result, weight[:, :width])

    return pl.pallas_call(
        kernel,
        grid=(ranks,),
        in_specs=[leading((ranks, count, D)), fixed((1, D)), fixed(slab.shape)],
        out_specs=[leading((ranks, count, D)), leading((ranks, count, width))],
        out_shape=[out((ranks, count, D)), out((ranks, count, width), f32)],
        compiler_params=params(),
    )(tokens, gain, slab)


TILE = 512


def tiles(count):
    return pl.loop(0, count // TILE)


def tile(number):
    return pl.ds(pl.multiple_of(number * TILE, TILE), TILE)


HBM = pl.BlockSpec(memory_space=pl.ANY)


def copies(pairs, sems):
    started = [
        pltpu.make_async_copy(source, target, sems.at[place])
        for place, (source, target) in enumerate(pairs)
    ]
    for copy in started:
        copy.start()

    def wait():
        for copy in started:
            copy.wait()

    return wait


def plane_pairs(plane, pieces, target):
    planes = len(pieces)
    rows = target.shape[0] // planes
    return [
        (piece, target.at[pl.ds((plane + planes - step) % planes * rows, rows)])
        for step, piece in enumerate(pieces)
    ]


def out_weight_pairs(plane, planes, gathered, target):
    ranks = gathered.shape[0]
    rows = D // (planes * ranks)
    return [
        (
            gathered.at[rank, pl.ds(step * rows, rows)],
            target.at[pl.ds(((plane + planes - step) % planes * ranks + rank) * rows, rows)],
        )
        for rank in range(ranks)
        for step in range(planes)
    ]


def route(plane, planes, mixed, tokens, gathered, gain, router, routes, experts):
    count = tokens.shape[0]
    pieces = planes * gathered.shape[0]

    def kernel(
        plane, mixed, tokens, gathered, gain, router, routes, hidden, payload, gates,
        out_weight, sems,
    ):
        copies(out_weight_pairs(plane[0], planes, gathered, out_weight), sems)()

        @tiles(D)
        def _(number):
            at = tile(number)
            hidden[:, at] = tokens[:, at].astype(f32) + dot(mixed[...], out_weight[:, at])

        value = hidden[...]
        normed = (value * inverse_rms(value) * gain[...]).astype(bf16)
        payload[:, :D] = normed
        logits = dot(normed, router[...])
        column = lax.broadcasted_iota(jnp.int32, logits.shape, 1)
        routed = column == routes[:, 0:1]
        for choice in range(1, TOP):
            routed = routed | (column == routes[:, choice : choice + 1])
        logits = jnp.where(routed, logits, -1e30)
        weights = jnp.exp(logits - jnp.max(logits, axis=1, keepdims=True))
        weights = jnp.where(routed, weights, 0.0)
        weights = weights / jnp.sum(weights, axis=1, keepdims=True)
        gates[...] = weights
        high = weights.astype(bf16).astype(f32)
        payload[:, D:] = (high + pltpu.roll(weights - high, experts, 1)).astype(bf16)

    shapes = [out((count, D), f32), out((count, D + PAD)), out((count, PAD), f32)]
    return pl.pallas_call(
        kernel,
        grid_spec=pltpu.PrefetchScalarGridSpec(
            num_scalar_prefetch=1,
            grid=(1,),
            in_specs=[
                HBM if value is gathered else fixed(value.shape)
                for value in (mixed, tokens, gathered, gain, router, routes)
            ],
            out_specs=[fixed(shape.shape) for shape in shapes],
            scratch_shapes=[pltpu.VMEM((D, D), bf16), pltpu.SemaphoreType.DMA((pieces,))],
        ),
        out_shape=shapes,
        compiler_params=params(),
    )(plane, mixed, tokens, gathered, gain, router, routes)


def lane(value, number):
    column = lax.broadcasted_iota(jnp.int32, value.shape, 1)
    return jnp.sum(jnp.where(column == number, value.astype(f32), 0.0), axis=1, keepdims=True)


def one_hot(slot, slots):
    place = lax.broadcasted_iota(jnp.int32, (slots, slot.shape[1]), 0).astype(f32)
    return (place == slot).astype(bf16)


def expert_forward(where, payload, upstream, in_pieces, slots, experts):
    ranks, share, micro, rows, _ = payload.shape
    count = share * rows
    block = 2 * slots

    planes = len(in_pieces)

    def kernel(where, payload, upstream, *refs):
        (
            rows_in, tail, both, active, grad_produced, up_rows, places, in_weight, sems
        ) = refs[planes:]
        number = where[0]

        @pl.when((pl.program_id(0) == 0) & (pl.program_id(1) == 0))
        def _():
            copies(plane_pairs(where[1], refs[:planes], in_weight), sems)()

        for part in range(2):
            here = slice(part * slots, (part + 1) * slots)
            value = payload[part].reshape(count, D + PAD)
            marks = value[:, D:]
            first = lax.broadcasted_iota(jnp.int32, (8, PAD), 1) == number
            taken = dot(first.astype(bf16), marks, ((1,), (1,))) > 0.0
            before = lax.broadcasted_iota(jnp.int32, (count, count), 0)
            behind = lax.broadcasted_iota(jnp.int32, (count, count), 1)
            slot = dot(taken.astype(bf16), (before < behind).astype(bf16))
            select = one_hot(jnp.where(taken, slot, -1.0)[0:1], slots)
            wide = jnp.broadcast_to(lane(marks, number) > 0.0, (count, PAD))
            slot = dot((before > behind).astype(bf16), wide.astype(bf16))
            places[0, 0, part] = jnp.where(wide, slot, -1.0)
            rows_in[0, 0, here] = dot(select, value[:, :D]).astype(bf16)
            marks = dot(select, marks)
            tail[0, 0, here] = marks
            gate = lane(marks, number) + lane(marks, experts + number)
            picked = dot(select, upstream[part].reshape(count, D))
            up_rows[0, 0, here] = picked.astype(bf16)
            grad_produced[0, 0, here] = (gate * picked).astype(bf16)

        for number in range(FF // TILE):
            at = slice(number * TILE, (number + 1) * TILE)
            more = slice(FF + number * TILE, FF + (number + 1) * TILE)
            gate_part = dot(rows_in[0, 0], in_weight[:, at])
            up_part = dot(rows_in[0, 0], in_weight[:, more])
            both[0, 0, :, at] = gate_part
            both[0, 0, :, more] = up_part
            active[0, 0, :, at] = (
                gate_part / (1.0 + jnp.exp(-gate_part)) * up_part
            ).astype(bf16)

    def tokens_spec(width):
        return pl.BlockSpec((2, share, 1, rows, width), lambda m, b, _: (b, 0, m, 0, 0))

    pairs = ranks // 2
    shapes = [
        out((micro, pairs, block, D)),
        out((micro, pairs, block, PAD), f32),
        out((micro, pairs, block, 2 * FF), f32),
        out((micro, pairs, block, FF)),
        out((micro, pairs, block, D)),
        out((micro, pairs, block, D)),
        out((micro, pairs, 2, count, PAD), f32),
    ]
    return pl.pallas_call(
        kernel,
        grid_spec=pltpu.PrefetchScalarGridSpec(
            num_scalar_prefetch=1,
            grid=(micro, pairs),
            in_specs=[tokens_spec(D + PAD), tokens_spec(D)] + [HBM] * planes,
            out_specs=[
                pl.BlockSpec(
                    (1, 1) + s.shape[2:], lambda m, b, _, n=len(s.shape): (m, b) + (0,) * (n - 2)
                )
                for s in shapes
            ],
            scratch_shapes=[pltpu.VMEM((D, 2 * FF), bf16), pltpu.SemaphoreType.DMA((planes,))],
        ),
        out_shape=shapes,
        cost_estimate=cost(micro * pairs * block * D * (2 * FF + 2 * count)),
        compiler_params=params(),
    )(where, payload, upstream, *in_pieces)


def expert_backward(
    step, where, tail, both, active, grad_produced, up_rows, places, in_pieces, out_pieces,
    share, rows, experts,
):
    pairs, block = tail.shape[1:3]
    slots = block // 2
    count = places.shape[3]

    planes = len(in_pieces)

    def kernel(where, tail, both, active, grad_produced, up_rows, places, *refs):
        keep, give, grad_tokens, grad_both, in_weight, out_weight, sems = refs[2 * planes :]
        number = where[0]
        odd = where[2] == 1

        @pl.when(pl.program_id(0) == 0)
        def _():
            copies(
                plane_pairs(where[1], refs[:planes], in_weight)
                + plane_pairs(where[1], refs[planes : 2 * planes], out_weight),
                sems,
            )()

        gate = lane(tail[0, 0], number) + lane(tail[0, 0], experts + number)
        place = lax.broadcasted_iota(jnp.int32, (count, slots), 1).astype(f32)
        selects = [(places[0, 0, part][:, 0:1] == place).astype(bf16) for part in range(2)]

        def spread(value):
            return [
                dot(selects[part], value[part * slots : (part + 1) * slots])
                .astype(bf16)
                .reshape(share, rows, -1)
                for part in range(2)
            ]

        grad_gate = jnp.zeros((block, 1), f32)
        for tile in range(D // TILE):
            at = slice(tile * TILE, (tile + 1) * TILE)
            produced = dot(active[0, 0], out_weight[:, at]).astype(bf16).astype(f32)
            even_rank, odd_rank = spread((gate * produced).astype(bf16))
            keep[0, :, :, at] = jnp.where(odd, odd_rank, even_rank)
            give[0, :, :, at] = jnp.where(odd, even_rank, odd_rank)
            grad_gate = grad_gate + jnp.sum(
                up_rows[0, 0, :, at].astype(f32) * produced, axis=1, keepdims=True
            )

        for tile in range(FF // TILE):
            at = slice(tile * TILE, (tile + 1) * TILE)
            more = slice(FF + tile * TILE, FF + (tile + 1) * TILE)
            grad_active = dot(grad_produced[0, 0], out_weight[at, :], ((1,), (1,)))
            grad_active = grad_active.astype(bf16).astype(f32)
            gate_part = both[0, 0, :, at]
            up_part = both[0, 0, :, more]
            sigma = 1.0 / (1.0 + jnp.exp(-gate_part))
            grad_both[0, :, at] = (
                grad_active * up_part * (sigma * (1.0 + gate_part * (1.0 - sigma)))
            ).astype(bf16)
            grad_both[0, :, more] = (grad_active * (gate_part * sigma)).astype(bf16)

        for tile in range(D // TILE):
            at = slice(tile * TILE, (tile + 1) * TILE)
            grad_rows = dot(grad_both[0], in_weight[at, :], ((1,), (1,))).astype(bf16)
            grad_tokens[0, :, :, at], grad_tokens[1, :, :, at] = spread(grad_rows)

        high = grad_gate.astype(bf16).astype(f32)
        column = lax.broadcasted_iota(jnp.int32, (block, PAD), 1)
        extra = jnp.where(column == number, high, 0.0)
        extra = jnp.where(column == experts + number, grad_gate - high, extra)
        grad_tokens[0, :, :, D:], grad_tokens[1, :, :, D:] = spread(extra.astype(bf16))

    def part(value):
        return pl.BlockSpec(
            (1, 1) + value.shape[2:], lambda b, _: (step, b) + (0,) * (value.ndim - 2)
        )

    def tokens_spec(count, width):
        return pl.BlockSpec((count, share, rows, width), lambda b, _: (b, 0, 0, 0))

    return pl.pallas_call(
        kernel,
        grid_spec=pltpu.PrefetchScalarGridSpec(
            num_scalar_prefetch=1,
            grid=(pairs,),
            in_specs=[part(v) for v in (tail, both, active, grad_produced, up_rows, places)]
            + [HBM] * (2 * planes),
            out_specs=[
                tokens_spec(1, D),
                tokens_spec(1, D),
                tokens_spec(2, D + PAD),
                pl.BlockSpec((1, block, 2 * FF), lambda b, _: (b, 0, 0)),
            ],
            scratch_shapes=[
                pltpu.VMEM((D, 2 * FF), bf16),
                pltpu.VMEM((FF, D), bf16),
                pltpu.SemaphoreType.DMA((2 * planes,)),
            ],
        ),
        out_shape=[
            out((pairs, share, rows, D)),
            out((pairs, share, rows, D)),
            out((2 * pairs, share, rows, D + PAD)),
            out((pairs, block, 2 * FF)),
        ],
        cost_estimate=cost(pairs * block * D * (4 * FF + 2 * count)),
        compiler_params=params(),
    )(
        where, tail, both, active, grad_produced, up_rows, places, *in_pieces, *out_pieces
    )


def weight_gradient(where, planes, left, rights, tail=None, first=0, steps=None):
    steps = planes if steps is None else steps
    count, width = left.shape
    parts = len(rights)
    part_rows = count // parts
    columns = rights[0].shape[1]
    width = width // planes
    step = min(TILE, columns & -columns)
    tails = [] if tail is None else [tail]
    whole = columns + sum(value.shape[1] for value in tails)

    def of_plane(i, where):
        return (where[1] + first + i) % planes

    def kernel(where, left, *refs):
        rights, tails, targets = refs[:parts], refs[parts:-steps], refs[-steps:]

        def fill(target):
            for value in tails:
                target[:, columns:] = value[...]
            for number in range(columns // step):
                at = slice(number * step, (number + 1) * step)
                target[:, at] = sum(
                    dot(left[part * part_rows : (part + 1) * part_rows], right[:, at], ((0,), (0,)))
                    for part, right in enumerate(rights)
                ).astype(bf16)

        for number, target in enumerate(targets):
            pl.when(pl.program_id(0) == number)(lambda target=target: fill(target))

    return pl.pallas_call(
        kernel,
        grid_spec=pltpu.PrefetchScalarGridSpec(
            num_scalar_prefetch=1,
            grid=(steps,),
            in_specs=[pl.BlockSpec((count, width), lambda i, where: (0, of_plane(i, where)))]
            + [fixed(right.shape) for right in rights]
            + [
                pl.BlockSpec((width, value.shape[1]), lambda i, where: (of_plane(i, where), 0))
                for value in tails
            ],
            out_specs=[fixed((width, whole))] * steps,
        ),
        out_shape=[out((width, whole))] * steps,
        cost_estimate=cost(0 if tails else count * steps * width * columns),
        compiler_params=params(),
    )(where, left, *rights, *tails)


def hidden_backward(
    plane, planes, parts, hidden, gates, upstream, gain, router, gathered, experts
):
    count = hidden.shape[0]
    terms = len(parts)

    def kernel(plane, *refs):
        parts = refs[:terms]
        hidden, gates, upstream, gain, router, gathered = refs[terms : terms + 6]
        (
            grad_hidden, grad_branch, grad_mixed, grad_logits, grad_gain, out_weight, sems
        ) = refs[terms + 6 :]
        wait = copies(out_weight_pairs(plane[0], planes, gathered, out_weight), sems)
        returned = sum(part[...].astype(f32) for part in parts)
        tail = returned[:, D:]
        grad_gates = gates[...] * (tail + pltpu.roll(tail, PAD - experts, 1))
        logits = grad_gates - gates[...] * jnp.sum(grad_gates, axis=1, keepdims=True)
        logits = logits.astype(bf16)
        grad_logits[...] = logits
        grad_normed = returned[:, :D] + dot(logits, router[...], ((1,), (1,)))
        value = hidden[...]
        inverse = inverse_rms(value)
        grad_gain[...] = jnp.sum(grad_normed * value * inverse, axis=0, keepdims=True)
        grad = upstream[...].astype(f32) + rms_backward(value, inverse, gain[...], grad_normed)
        grad_hidden[...] = grad
        grad_branch[...] = grad.astype(bf16)
        wait()

        @tiles(D)
        def _(number):
            at = tile(number)
            grad_mixed[:, at] = dot(grad_branch[...], out_weight[at, :], ((1,), (1,))).astype(bf16)

    shapes = [
        out((count, D), f32), out((count, D)), out((count, D)), out((count, PAD)),
        out((1, D), f32),
    ]
    args = (*parts, hidden, gates, upstream, gain, router, gathered)
    return pl.pallas_call(
        kernel,
        grid_spec=pltpu.PrefetchScalarGridSpec(
            num_scalar_prefetch=1,
            grid=(1,),
            in_specs=[HBM if value is gathered else fixed(value.shape) for value in args],
            out_specs=[fixed(shape.shape) for shape in shapes],
            scratch_shapes=[
                pltpu.VMEM((D, D), bf16),
                pltpu.SemaphoreType.DMA((planes * gathered.shape[0],)),
            ],
        ),
        out_shape=shapes,
        compiler_params=params(),
    )(plane, *args)


def project_backward(step, grad_proj, tokens, slab):
    ranks, rows, _ = grad_proj.shape
    width = slab.shape[1] - PAD

    def kernel(grad_proj, tokens, weight, grad_normed, grad_gain):
        value = tokens[0].astype(f32)
        inverse = inverse_rms(value)
        grad = dot(grad_proj[0], weight[:, :width], ((1,), (1,)))
        grad_normed[...] = grad.astype(bf16)

        @pl.when(pl.program_id(0) == 0)
        def _():
            grad_gain[...] = jnp.zeros_like(grad_gain)

        grad_gain[...] += jnp.sum(grad * value * inverse, axis=0, keepdims=True)

    return pl.pallas_call(
        kernel,
        grid=(ranks,),
        in_specs=[
            leading(grad_proj.shape),
            pl.BlockSpec((1, rows, D), lambda i: (i, step, 0)),
            fixed(slab.shape),
        ],
        out_specs=[pl.BlockSpec((rows, D), lambda i: (i, 0)), fixed((1, D))],
        out_shape=[out((ranks * rows, D)), out((1, D), f32)],
        compiler_params=params(),
    )(grad_proj, tokens, slab)


def cut_heads(weight, tail, ranks):
    rows = weight.shape[0]
    width = D // ranks

    def kernel(weight, tail, target):
        for rank in range(ranks):
            for part in range(3):
                at = part * D + rank * width
                target[rank, :, part * width : (part + 1) * width] = weight[:, at : at + width]
            target[rank, :, 3 * width :] = tail[...]

    return pl.pallas_call(
        kernel,
        out_shape=out((ranks, rows, 3 * width + PAD)),
        compiler_params=params(),
    )(weight, tail)


def unpack(packed, count):
    ranks, rows, columns = packed.shape
    width = (columns - PAD) // 3

    def kernel(packed, main, small):
        for rank in range(ranks):
            for part in range(3):
                at = part * D + rank * width
                main[:, at : at + width] = packed[rank, :, part * width : (part + 1) * width].astype(
                    f32
                )
        tails = sum(packed[rank, :, 3 * width :].astype(f32) for rank in range(ranks))
        small[...] = tails + pltpu.roll(tails, PAD - count, 1)

    return pl.pallas_call(
        kernel,
        out_shape=[out((rows, 3 * D), f32), out((rows, PAD), f32)],
        compiler_params=params(),
    )(packed)


def shift_rep(value, step):
    count = lax.axis_size("rep")
    return lax.ppermute(value, "rep", [(i, (i + step) % count) for i in range(count)])


def after(value, *others):
    return lax.optimization_barrier((value,) + others)[0]


def two_parts(value):
    high = lax.reduce_precision(value, 8, 7)
    return high.astype(bf16), (value - high).astype(bf16)


def shift_order(count):
    return sorted(range(1, count), key=lambda step: (min(step, count - step), step))


def ring_rep(value, *work):
    count = lax.axis_size("rep")
    rank = lax.axis_index("rep")
    rows = value.shape[0]
    full = jnp.zeros((count * rows,) + value.shape[1:], value.dtype)
    full = lax.dynamic_update_slice_in_dim(full, value, rank * rows, 0)
    for step in range(1, count):
        value, work = lax.optimization_barrier((value, work)) if step == count - 1 else (value, work)
        value = shift_rep(value, 1)
        full = lax.dynamic_update_slice_in_dim(full, value, (rank - step) % count * rows, 0)
    return full, work


def on_device(
    tokens, cotangent, w_qkv, w_o, w_router, norm_gains, qk_gain, w_in, w_out, segments, routes
):
    planes = lax.axis_size("rep")
    ranks = lax.axis_size("ep")
    plane = lax.axis_index("rep")
    rank = lax.axis_index("ep")
    share = w_in.shape[0]
    own = plane % share
    experts = share * ranks
    where = jnp.stack([rank * share + own, plane, rank % 2]).astype(jnp.int32)
    micro = segments.shape[1]
    mine = tokens.shape[0]
    rows = mine // micro
    length = rows * ranks
    capacity = rows * TOP * 17 // (16 * experts)
    slots = -(-share * capacity // 16) * 16
    width = HEADS // ranks * HD
    qk_gains = qk_gain.astype(f32).reshape(2, HD)
    dense_rows = w_qkv.shape[0]

    def exchange(value, step):
        pairs = [(i, i // share * share + (i % share + step) % share) for i in range(planes)]
        return lax.ppermute(value, "rep", pairs)

    def with_group(value):
        return jnp.stack([value] + [exchange(value, step) for step in range(1, share)])

    def gather_ranks(value):
        return lax.all_gather(value, "ep", axis=0)

    order = shift_order(planes)
    in_parts, out_parts = (
        {
            step: lax.dynamic_index_in_dim(weight, (own + step) % share, 0, keepdims=False)
            for step in [0] + order
        }
        for weight in (w_in, w_out)
    )

    def send(parts, steps):
        return {step: shift_rep(parts[step], step) for step in steps}

    stream = gather_ranks(tokens)
    out_rows = [w_o] + [shift_rep(w_o, step) for step in range(1, planes)]
    upstream_group = with_group(cotangent)
    slab = cut_heads(
        w_qkv,
        jnp.concatenate(
            [
                w_router,
                norm_gains.reshape(dense_rows, 2),
                jnp.zeros((dense_rows, PAD - experts - 2), bf16),
            ],
            axis=1,
        ),
        ranks,
    )
    slab = lax.all_to_all(slab, "ep", split_axis=0, concat_axis=0, tiled=True)
    slab = slab.reshape(ranks * dense_rows, 3 * width + PAD)
    out_rows, upstream_group, slab = lax.optimization_barrier((out_rows, upstream_group, slab))
    gathered = gather_ranks(jnp.concatenate(out_rows, axis=0))
    segment = segments[0]
    cosine, sine = jax.vmap(lambda one: rope_tables(doc_positions(one), HD))(segment)
    sine = jnp.where(jnp.arange(HD) < HD // 2, -sine, sine)
    tables = (cosine, sine, segment[:, :, None], segment[:, None, :], qk_gains)
    slab, (tables, in_parts, out_parts) = ring_rep(slab, tables, in_parts, out_parts)
    router = slab[:, 3 * width :]
    gain_pair = router[:, experts : experts + 2].reshape(-1).astype(f32)
    first_gain = gain_pair[None, :D]
    second_gain = gain_pair[None, D:]
    in_parts, out_parts, upstream_group, stream = after(
        (in_parts, out_parts, upstream_group, stream), slab
    )
    in_pieces = {0: in_parts[0], **send(in_parts, order[:-1])}
    upstream_all = gather_ranks(upstream_group)

    normed, proj = project(stream, first_gain, slab)
    proj = proj.reshape(ranks, micro, rows, 3 * width)
    mixed_h, query, keys, values, lses = attention_forward(proj, *tables)
    mixed = lax.all_to_all(mixed_h, "ep", split_axis=0, concat_axis=3, tiled=True)
    mixed = mixed.reshape(mine, D)
    hidden, payload, gates = route(
        where[1:2], planes, mixed, tokens, gathered, second_gain, router, routes, experts
    )
    normed_two = payload[:, :D]
    payload, in_pieces = lax.optimization_barrier((payload, in_pieces))
    payload = with_group(payload)
    payload, in_parts, out_parts = lax.optimization_barrier((payload, in_parts, out_parts))
    in_pieces.update(send(in_parts, order[-1:]))
    in_pieces, out_parts = lax.optimization_barrier((in_pieces, out_parts))
    out_pieces = {0: out_parts[0], **send(out_parts, order)}
    in_pieces = [in_pieces[step] for step in range(planes)]
    out_pieces = [out_pieces[step] for step in range(planes)]
    payload = gather_ranks(payload)

    shape = (ranks, share, micro, rows, -1)
    rows_in, tail, both, active, grad_produced, up_rows, places = expert_forward(
        where, payload.reshape(shape), upstream_all.reshape(shape), in_pieces, slots, experts
    )
    in_rows = micro * ranks * slots
    out_cut = weight_gradient(
        where, planes, active.reshape(in_rows, FF), [grad_produced.reshape(in_rows, D)]
    )

    def sum_rep(parts):
        sums = [
            sum(parts[step].astype(f32) for step in range(first, planes, share))
            for first in range(share)
        ]
        return jnp.stack(
            [
                sum(jnp.where((own - step) % share == j, sums[step], 0.0) for step in range(share))
                for j in range(share)
            ]
        )

    tail, out_cut, out_pieces = lax.optimization_barrier((tail, out_cut, out_pieces))
    out_sent = send(out_cut, order)
    back = []
    returned = []

    def scatter_ranks(value):
        return lax.psum_scatter(value, "ep", scatter_dimension=0)

    def exchange_back(value):
        return [value[0]] + [exchange(value[step], share - step) for step in range(1, share)]

    for step in range(micro):
        back.append(
            expert_backward(
                step, where, tail, both, active, grad_produced, up_rows, places, in_pieces,
                out_pieces, share, rows, experts,
            )
        )
        returned.append(scatter_ranks(back[step][2]))
        if step == 0:
            short = {near: out_sent[near] for near in order[:2]}
            tail, short = after((tail, short), back[step][2])
            out_sent.update(short)
        else:
            tail = after(tail, back[step][2])
    rows_in = after(rows_in, tail)
    rows_flat = rows_in.reshape(in_rows, D)
    grads_flat = [back[step][3].reshape(in_rows // micro, 2 * FF) for step in range(micro)]
    near = weight_gradient(where, planes, rows_flat, grads_flat, first=order[0], steps=1)
    rows_flat, near = lax.optimization_barrier((rows_flat, near))
    far = weight_gradient(
        where, planes, rows_flat, grads_flat, first=order[0] + 1, steps=planes - 1
    )
    in_cut = {(order[0] + 1 + i) % planes: part for i, part in enumerate(far)}
    in_cut[order[0]], = near
    in_sent = send(in_cut, order[:1])

    def swap(value, step):
        return lax.ppermute(value, "ep", [(i, i ^ step) for i in range(ranks)])

    def pair_sum(keep, give):
        return (keep.astype(f32) + swap(give, 1).astype(f32)).astype(bf16)

    bits = list(range((ranks // 2).bit_length() - 1))

    def halve(values, phase):
        results = []
        for number, value in enumerate(values):
            way = bits if number % 2 == 0 else bits[::-1]
            bit = way[phase]
            low = 2 ** sum(other < bit for other in way[phase:])
            value = value.reshape((-1, 2, low) + value.shape[1:])
            side = rank // 2 // 2**bit % 2
            keep, give = (
                lax.dynamic_index_in_dim(value, which, 1, keepdims=False).reshape(
                    (-1,) + value.shape[3:]
                )
                for which in (side, 1 - side)
            )
            results.append((keep, swap(give, 2 * 2**bit)))
        return results

    def total(parts):
        return sum(part.astype(f32) for part in parts)

    grad_inputs, branches, logit_grads, grad_projs = [], [], [], []
    gain_two_sum = gain_one_sum = qk_sum = 0.0
    in_cut, out_sent, in_sent = lax.optimization_barrier((in_cut, out_sent, in_sent))
    mixtures = [part[:2] for part in back]
    releases = [order[1:-1]] + [[]] * (micro - 1)
    for step in range(micro):
        at = slice(step * rows, (step + 1) * rows)
        parts = after(returned[step], [one[1] for one in grad_inputs])
        parts, in_sent = lax.optimization_barrier((parts, in_sent))
        parts = exchange_back(parts)
        parts, in_cut, mixtures = lax.optimization_barrier((parts, in_cut, mixtures))
        if step == 0:
            mixtures = [pair_sum(*part) for part in mixtures]
        in_sent.update(send(in_cut, releases[step]))
        if step == micro - 1:
            last = in_cut[order[-1]]
            ends = [-(-last.shape[0] * eighths // 128) * 16 for eighths in (0, 3, 5, 8)]
            last = [last[start:end] for start, end in zip(ends, ends[1:])]
            last_sent = [shift_rep(last[0], order[-1])]
        grad_hidden, grad_branch, grad_mixed, grad_logits, gain_two = hidden_backward(
            where[1:2], planes, parts, hidden[at], gates[at], cotangent[at], second_gain,
            router, gathered, experts,
        )
        branches.append(grad_branch)
        logit_grads.append(grad_logits)
        gain_two_sum = gain_two_sum + gain_two
        if step == micro - 1:
            out_sum = dot(mixed, jnp.concatenate(branches, axis=0), ((0,), (0,))).astype(bf16)
            out_sum = out_sum.reshape(planes, ranks, dense_rows, D).transpose(1, 0, 2, 3)
        grad_mixed = lax.all_to_all(grad_mixed, "ep", split_axis=1, concat_axis=0, tiled=True)
        grad_mixed, mixtures = lax.optimization_barrier((grad_mixed, mixtures))
        if step == micro - 1:
            grad_mixed, mixtures, last_sent, last, out_sum = lax.optimization_barrier(
                (grad_mixed, mixtures, last_sent, last, out_sum)
            )
            out_sum = lax.psum_scatter(out_sum, "ep", scatter_dimension=0)
            last_sent.append(shift_rep(last[1], order[-1]))
        grad_proj, grad_qk = attention_backward(
            step, proj, *tables, query, keys, values, lses, grad_mixed
        )
        qk_sum = qk_sum + grad_qk.reshape(-1)
        if step < micro - 1:
            grad_proj, in_sent = lax.optimization_barrier((grad_proj, in_sent))
        else:
            grad_proj, grad_inputs, last_sent, last = lax.optimization_barrier(
                (grad_proj, grad_inputs, last_sent, last)
            )
        grad_projs.append(grad_proj)
        grad_normed, gain_one = project_backward(step, grad_proj, stream, slab)
        gain_one_sum = gain_one_sum + gain_one
        grad_inputs.append(
            (
                grad_hidden,
                grad_normed,
                lax.psum_scatter(grad_normed, "ep", scatter_dimension=0, tiled=True),
            )
        )

    router_sum = dot(normed_two, jnp.concatenate(logit_grads, axis=0), ((0,), (0,)))
    qk_columns = qk_sum.shape[0] // dense_rows
    small = jnp.concatenate(
        [
            router_sum[:, :experts],
            jnp.concatenate([gain_one_sum, gain_two_sum], axis=1).reshape(D, 2),
            jnp.tile(qk_sum.reshape(dense_rows, qk_columns), (planes * ranks, 1)),
        ],
        axis=1,
    )
    count = small.shape[1]

    def halves(value):
        high, low = two_parts(value)
        blank = jnp.zeros((value.shape[0], PAD - 2 * count), bf16)
        return jnp.concatenate([high, low, blank], axis=1)

    def joined(value):
        return value[..., :count].astype(f32) + value[..., count : 2 * count].astype(f32)

    grad_projs, last, out_cut, out_sent, _ = lax.optimization_barrier(
        (grad_projs, last, out_cut, out_sent, grad_normed)
    )
    last_sent.append(shift_rep(last[2], order[-1]))
    packed = weight_gradient(
        where,
        planes,
        normed.reshape(ranks * mine, D),
        [jnp.stack(grad_projs, axis=1).reshape(ranks * mine, 3 * width)],
        halves(small),
    )
    packed, last_sent, out_cut, out_sent, mixtures = lax.optimization_barrier(
        (packed, last_sent, out_cut, out_sent, mixtures)
    )
    packed_sent = [packed[0]] + [shift_rep(packed[step], step) for step in range(1, planes)]
    for phase in range(len(bits)):
        crossed = halve(mixtures, phase)
        if phase < len(bits) - 1:
            mixtures = [total(parts).astype(bf16) for parts in crossed]
    normed_sums = [one[2] for one in grad_inputs]
    normed_sums = [one[2] for one in grad_inputs]
    grad_tokens = []
    for step in range(micro):
        own_stream = tokens[step * rows : (step + 1) * rows].astype(f32)
        grad_tokens.append(
            grad_inputs[step][0]
            + rms_backward(
                own_stream, inverse_rms(own_stream), first_gain, normed_sums[step].astype(f32)
            )
        )
    grad_tokens = jnp.concatenate(grad_tokens, axis=0)
    packed_sent, grad_tokens = lax.optimization_barrier((packed_sent, grad_tokens))
    crossed, out_sum = lax.optimization_barrier((crossed, out_sum))
    mixture = []
    for number in range(micro):
        parts = total(crossed[number])[0]
        mixture.append((parts[0], exchange_back(parts.astype(bf16))[1:]))
    own_sum = lax.dynamic_index_in_dim(out_sum, plane, 0, keepdims=False)
    out_sent_back = [
        shift_rep(
            lax.dynamic_index_in_dim(out_sum, (plane + step) % planes, 0, keepdims=False), step
        )
        for step in range(1, planes)
    ]
    main = total([part[:, : 3 * width] for part in packed_sent]).astype(bf16)
    small = sum(joined(part[:, 3 * width :]) for part in packed_sent)
    packed = jnp.concatenate([main, halves(small)], axis=1).reshape(ranks, dense_rows, -1)
    packed = lax.all_to_all(packed, "ep", split_axis=0, concat_axis=0, tiled=True)
    packed, mixture, out_sent_back = lax.optimization_barrier((packed, mixture, out_sent_back))
    output = jnp.concatenate([mine_part + total(others) for mine_part, others in mixture], axis=0)
    output = (hidden + output).astype(bf16)
    grad_w_o = total([own_sum, *out_sent_back])
    grad_w_qkv, small = unpack(packed, count)
    grad_w_out = sum_rep({0: out_cut[0], **out_sent})
    in_sent[order[-1]] = jnp.concatenate(last_sent, axis=0)
    grad_w_in = sum_rep({0: in_cut[0], **in_sent})
    return (
        output,
        grad_tokens,
        grad_w_qkv,
        grad_w_o,
        small[:, :experts],
        small[:, experts : experts + 2].reshape(-1),
        small[:, experts + 2 : count].reshape(-1),
        grad_w_in,
        grad_w_out,
    )


def solution(mesh):
    placed = (
        P(("rep", "ep"), None),
        P(("rep", "ep"), None),
        P(("rep", "ep"), None),
        P(("rep", "ep"), None),
        P(("rep", "ep"), None),
        P(("rep", "ep")),
        P(),
        P("ep", "rep", None),
        P("ep", "rep", None),
        P("rep", None, None),
        P(("rep", "ep"), None),
    )
    return jax.shard_map(
        on_device,
        mesh=mesh,
        in_specs=placed,
        out_specs=(
            P(("rep", "ep"), None),
            P(("rep", "ep"), None),
            P(("rep", "ep"), None),
            P(("rep", "ep"), None),
            P(("rep", "ep"), None),
            P(("rep", "ep")),
            P(),
            P("ep", "rep", None),
            P("ep", "rep", None),
        ),
        check_vma=False,
    )
```

```python
import math

import jax
import jax.numpy as jnp
from jax import lax
from jax.experimental import pallas as pl
from jax.experimental.pallas import tpu as pltpu
from jax.sharding import PartitionSpec as P

D = 2048
HEADS = 16
HD = 128
FF = 1024
TOP = 8
HALF = 512
PAD = 128

epsilon = 1e-06
rope_base = 50000.0
bf16 = jnp.bfloat16
f32 = jnp.float32


def dot(a, b, dims=((1,), (0,))):
    return lax.dot_general(a, b, (dims, ((), ())), preferred_element_type=f32)


def inverse_rms(value):
    return lax.rsqrt(jnp.mean(value * value, axis=-1, keepdims=True) + epsilon)


def rms_backward(value, inverse, gain, grad):
    scaled = grad * gain
    inner = jnp.mean(scaled * value, axis=-1, keepdims=True)
    return inverse * (scaled - value * (inverse * inverse * inner))


def doc_positions(segment):
    index = jnp.arange(segment.shape[0], dtype=jnp.int32)
    change = jnp.concatenate([jnp.ones((1,), dtype=jnp.bool_), segment[1:] != segment[:-1]])
    start = lax.cummax(jnp.where(change, index, 0), axis=0)
    return index - start


def rope_tables(position, width):
    steps = jnp.arange(width // 2, dtype=f32) * (2.0 / width)
    rates = jnp.exp(-steps * math.log(rope_base))
    angle = position.astype(f32)[:, None] * rates[None, :]
    angle = jnp.concatenate([angle, angle], axis=-1)
    return (jnp.cos(angle), jnp.sin(angle))


def norm_rope(value, gain, cosine, sine):
    inverse = lax.rsqrt(jnp.mean(value * value, axis=1, keepdims=True) + epsilon)
    value = value * inverse * gain
    return value * cosine + pltpu.roll(value, HD // 2, 1) * sine


def norm_rope_back(value, gain, cosine, sine, grad):
    inverse = lax.rsqrt(jnp.mean(value * value, axis=1, keepdims=True) + epsilon)
    grad = grad * cosine + pltpu.roll(grad * sine, HD // 2, 1)
    normal = value * inverse
    scaled = grad * gain
    inner = jnp.mean(scaled * normal, axis=1, keepdims=True)
    return inverse * (scaled - normal * inner), jnp.sum(grad * normal, axis=0, keepdims=True)


def kept_scores(query, keys, q_seg, k_seg, start):
    scores = dot(query, keys, ((1,), (1,))) * (1.0 / math.sqrt(HD))
    q_index = start + lax.broadcasted_iota(jnp.int32, scores.shape, 0)
    k_index = lax.broadcasted_iota(jnp.int32, scores.shape, 1)
    keep = (jnp.abs(q_index - k_index) <= HALF) & (q_seg == k_seg)
    return jnp.where(keep, scores, -1e30)


BIG = 100 * 1024 * 1024 // 2


def forward_kernel(
    heads, proj, cosine, sine, seg_column, seg_row, gains, mixed, query, keys, values, lses
):
    ranks, _, rows, _ = proj.shape
    length = ranks * rows
    q_block = 2 * rows
    k_seg = seg_row[0]
    for head in range(heads):
        at = slice(head * HD, (head + 1) * HD)

        def raw(part):
            first = (part * heads + head) * HD
            return proj[:, 0, :, first : first + HD].reshape(length, HD)

        query[0, :, at] = norm_rope(raw(0), gains[0:1], cosine[0], sine[0]).astype(bf16)
        keys[0, :, at] = norm_rope(raw(1), gains[1:2], cosine[0], sine[0]).astype(bf16)
        values[0, :, at] = raw(2).astype(bf16)

        @pl.loop(0, length // q_block)
        def one_block(number, head=head, at=at):
            start = pl.multiple_of(number * q_block, q_block)
            here = pl.ds(start, q_block)
            scores = kept_scores(
                query[0, here, at], keys[0, :, at], seg_column[0, here], k_seg, start
            )
            top = jnp.max(scores, axis=1, keepdims=True)
            weights = jnp.exp(scores - top)
            total = jnp.sum(weights, axis=1, keepdims=True)
            lses[0, head, here] = top + jnp.log(total)
            weights = (weights * (1.0 / total)).astype(bf16)
            result = dot(weights, values[0, :, at]).astype(bf16)
            mixed[pl.ds(number * 2, 2), 0, :, at] = result.reshape(2, rows, HD)


def backward_kernel(
    heads, proj, cosine, sine, seg_column, seg_row, gains, query, keys, values, lses, grad_mixed,
    grad_proj, grad_gains, grad_q, grad_k, grad_v,
):
    ranks, _, rows, _ = proj.shape
    length = ranks * rows
    q_block = 2 * rows
    k_seg = seg_row[0]
    scale = 1.0 / math.sqrt(HD)
    sum_q = jnp.zeros((1, HD), f32)
    sum_k = jnp.zeros((1, HD), f32)
    for head in range(heads):
        at = slice(head * HD, (head + 1) * HD)
        grad_k[...] = jnp.zeros_like(grad_k)
        grad_v[...] = jnp.zeros_like(grad_v)

        @pl.loop(0, length // q_block)
        def one_block(number, head=head, at=at):
            start = pl.multiple_of(number * q_block, q_block)
            here = pl.ds(start, q_block)
            q_rows = query[0, here, at]
            g_rows = grad_mixed[here, at]
            k_all = keys[0, :, at]
            scores = kept_scores(q_rows, k_all, seg_column[0, here], k_seg, start)
            weights = jnp.exp(scores - lses[0, head, here])
            grad_weights = dot(g_rows, values[0, :, at], ((1,), (1,)))
            delta = jnp.sum(weights * grad_weights, axis=1, keepdims=True)
            grad_scores = (weights * (grad_weights - delta)).astype(bf16)
            grad_q[here] = dot(grad_scores, k_all) * scale
            grad_k[...] += dot(grad_scores, q_rows, ((0,), (0,)))
            grad_v[...] += dot(weights.astype(bf16), g_rows, ((0,), (0,)))

        def rounded(value):
            return value.astype(bf16).astype(f32)

        def raw(part):
            first = (part * heads + head) * HD
            return proj[:, 0, :, first : first + HD].reshape(length, HD)

        def put(part, value):
            first = (part * heads + head) * HD
            grad_proj[:, :, first : first + HD] = value.astype(bf16).reshape(ranks, rows, HD)

        back_q, gain_q = norm_rope_back(
            raw(0), gains[0:1], cosine[0], sine[0], rounded(grad_q[...])
        )
        back_k, gain_k = norm_rope_back(
            raw(1), gains[1:2], cosine[0], sine[0], rounded(grad_k[...] * scale)
        )
        sum_q, sum_k = sum_q + gain_q, sum_k + gain_k
        put(0, back_q)
        put(1, back_k)
        put(2, grad_v[...])
    grad_gains[0:1] = sum_q
    grad_gains[1:2] = sum_k


def fixed(shape):
    return pl.BlockSpec(shape, lambda *_: (0,) * len(shape), pipeline_mode=pl.Buffered(1))


def leading(shape):
    return pl.BlockSpec((1,) + shape[1:], lambda i: (i,) + (0,) * (len(shape) - 1))


def params():
    return pltpu.CompilerParams(vmem_limit_bytes=BIG)


def cost(products):
    return pl.CostEstimate(flops=20 * products, bytes_accessed=0, transcendentals=0)


def out(shape, dtype=bf16):
    return jax.ShapeDtypeStruct(shape, dtype)


def attention_forward(proj, cosine, sine, seg_column, seg_row, gains):
    ranks, micro, rows, width = proj.shape
    length = ranks * rows
    width = width // 3
    heads = width // HD
    part = out((micro, length, width))
    by_rank = lambda n: pl.BlockSpec((ranks, 1, rows, n), lambda i: (0, i, 0, 0))
    lses = out((micro, heads, length, 1), f32)
    return pl.pallas_call(
        lambda *refs: forward_kernel(heads, *refs),
        grid=(micro,),
        in_specs=[by_rank(3 * width)]
        + [leading(v.shape) for v in (cosine, sine, seg_column, seg_row)]
        + [fixed(gains.shape)],
        out_specs=[by_rank(width)] + [leading(part.shape)] * 3 + [leading(lses.shape)],
        out_shape=[out((ranks, micro, rows, width)), part, part, part, lses],
        compiler_params=params(),
    )(proj, cosine, sine, seg_column, seg_row, gains)


def attention_backward(
    step, proj, cosine, sine, seg_column, seg_row, gains, query, keys, values, lses, grad_mixed
):
    ranks, micro, rows, width = proj.shape
    length = ranks * rows
    heads = width // 3 // HD

    def part(value):
        return pl.BlockSpec((1,) + value.shape[1:], lambda i: (step,) + (0,) * (value.ndim - 1))

    return pl.pallas_call(
        lambda *refs: backward_kernel(heads, *refs),
        grid=(1,),
        in_specs=[pl.BlockSpec((ranks, 1, rows, width), lambda i: (0, step, 0, 0))]
        + [part(v) for v in (cosine, sine, seg_column, seg_row)]
        + [fixed(gains.shape)]
        + [part(v) for v in (query, keys, values, lses)]
        + [fixed(grad_mixed.shape)],
        out_specs=[fixed((ranks, rows, width)), fixed((2, HD))],
        out_shape=[out((ranks, rows, width)), out((2, HD), f32)],
        scratch_shapes=[pltpu.VMEM((length, HD), f32)] * 3,
        compiler_params=params(),
    )(
        proj, cosine, sine, seg_column, seg_row, gains, query, keys, values, lses, grad_mixed
    )


def project(tokens, gain, slab):
    ranks, count, _ = tokens.shape
    width = slab.shape[1] - PAD

    def kernel(value, gain, weight, normed, proj):
        value = value[0].astype(f32)
        result = (value * inverse_rms(value) * gain[...]).astype(bf16)
        normed[0] = result
        proj[0] = dot(result, weight[:, :width])

    return pl.pallas_call(
        kernel,
        grid=(ranks,),
        in_specs=[leading((ranks, count, D)), fixed((1, D)), fixed(slab.shape)],
        out_specs=[leading((ranks, count, D)), leading((ranks, count, width))],
        out_shape=[out((ranks, count, D)), out((ranks, count, width), f32)],
        compiler_params=params(),
    )(tokens, gain, slab)


TILE = 512


def tiles(count):
    return pl.loop(0, count // TILE)


def tile(number):
    return pl.ds(pl.multiple_of(number * TILE, TILE), TILE)


HBM = pl.BlockSpec(memory_space=pl.ANY)


def copies(pairs, sems):
    started = [
        pltpu.make_async_copy(source, target, sems.at[place])
        for place, (source, target) in enumerate(pairs)
    ]
    for copy in started:
        copy.start()

    def wait():
        for copy in started:
            copy.wait()

    return wait


def plane_pairs(plane, pieces, target):
    planes = len(pieces)
    rows = target.shape[0] // planes
    return [
        (piece, target.at[pl.ds(lax.bitwise_xor(plane, jnp.int32(step)) * rows, rows)])
        for step, piece in enumerate(pieces)
    ]


def out_weight_pairs(plane, planes, gathered, target):
    ranks = gathered.shape[0]
    rows = D // (planes * ranks)
    return [
        (
            gathered.at[rank, pl.ds(step * rows, rows)],
            target.at[
                pl.ds((lax.bitwise_xor(plane, jnp.int32(step)) * ranks + rank) * rows, rows)
            ],
        )
        for rank in range(ranks)
        for step in range(planes)
    ]


def route(plane, planes, mixed, tokens, gathered, gain, router, routes, experts):
    count = tokens.shape[0]
    pieces = planes * gathered.shape[0]

    def kernel(
        plane, mixed, tokens, gathered, gain, router, routes, hidden, payload, gates,
        out_weight, sems,
    ):
        copies(out_weight_pairs(plane[0], planes, gathered, out_weight), sems)()

        @tiles(D)
        def _(number):
            at = tile(number)
            hidden[:, at] = tokens[:, at].astype(f32) + dot(mixed[...], out_weight[:, at])

        value = hidden[...]
        normed = (value * inverse_rms(value) * gain[...]).astype(bf16)
        payload[:, :D] = normed
        logits = dot(normed, router[...])
        column = lax.broadcasted_iota(jnp.int32, logits.shape, 1)
        routed = column == routes[:, 0:1]
        for choice in range(1, TOP):
            routed = routed | (column == routes[:, choice : choice + 1])
        logits = jnp.where(routed, logits, -1e30)
        weights = jnp.exp(logits - jnp.max(logits, axis=1, keepdims=True))
        weights = jnp.where(routed, weights, 0.0)
        weights = weights / jnp.sum(weights, axis=1, keepdims=True)
        gates[...] = weights
        high = weights.astype(bf16).astype(f32)
        payload[:, D:] = (high + pltpu.roll(weights - high, experts, 1)).astype(bf16)

    shapes = [out((count, D), f32), out((count, D + PAD)), out((count, PAD), f32)]
    return pl.pallas_call(
        kernel,
        grid_spec=pltpu.PrefetchScalarGridSpec(
            num_scalar_prefetch=1,
            grid=(1,),
            in_specs=[
                HBM if value is gathered else fixed(value.shape)
                for value in (mixed, tokens, gathered, gain, router, routes)
            ],
            out_specs=[fixed(shape.shape) for shape in shapes],
            scratch_shapes=[pltpu.VMEM((D, D), bf16), pltpu.SemaphoreType.DMA((pieces,))],
        ),
        out_shape=shapes,
        compiler_params=params(),
    )(plane, mixed, tokens, gathered, gain, router, routes)


def lane(value, number):
    column = lax.broadcasted_iota(jnp.int32, value.shape, 1)
    return jnp.sum(jnp.where(column == number, value.astype(f32), 0.0), axis=1, keepdims=True)


def one_hot(slot, slots):
    place = lax.broadcasted_iota(jnp.int32, (slots, slot.shape[1]), 0).astype(f32)
    return (place == slot).astype(bf16)


def expert_forward(where, payload, upstream, in_pieces, slots, experts):
    ranks, share, micro, rows, _ = payload.shape
    count = share * rows
    block = 2 * slots

    planes = len(in_pieces)

    def kernel(where, payload, upstream, *refs):
        (
            rows_in, tail, both, active, grad_produced, up_rows, places, in_weight, sems
        ) = refs[planes:]
        number = where[0]

        @pl.when((pl.program_id(0) == 0) & (pl.program_id(1) == 0))
        def _():
            copies(plane_pairs(where[1], refs[:planes], in_weight), sems)()

        for part in range(2):
            here = slice(part * slots, (part + 1) * slots)
            value = payload[part].reshape(count, D + PAD)
            marks = value[:, D:]
            first = lax.broadcasted_iota(jnp.int32, (8, PAD), 1) == number
            taken = dot(first.astype(bf16), marks, ((1,), (1,))) > 0.0
            before = lax.broadcasted_iota(jnp.int32, (count, count), 0)
            behind = lax.broadcasted_iota(jnp.int32, (count, count), 1)
            slot = dot(taken.astype(bf16), (before < behind).astype(bf16))
            select = one_hot(jnp.where(taken, slot, -1.0)[0:1], slots)
            wide = jnp.broadcast_to(lane(marks, number) > 0.0, (count, PAD))
            slot = dot((before > behind).astype(bf16), wide.astype(bf16))
            places[0, 0, part] = jnp.where(wide, slot, -1.0)
            rows_in[0, 0, here] = dot(select, value[:, :D]).astype(bf16)
            marks = dot(select, marks)
            tail[0, 0, here] = marks
            gate = lane(marks, number) + lane(marks, experts + number)
            picked = dot(select, upstream[part].reshape(count, D))
            up_rows[0, 0, here] = picked.astype(bf16)
            grad_produced[0, 0, here] = (gate * picked).astype(bf16)

        for number in range(FF // TILE):
            at = slice(number * TILE, (number + 1) * TILE)
            more = slice(FF + number * TILE, FF + (number + 1) * TILE)
            gate_part = dot(rows_in[0, 0], in_weight[:, at])
            up_part = dot(rows_in[0, 0], in_weight[:, more])
            both[0, 0, :, at] = gate_part
            both[0, 0, :, more] = up_part
            active[0, 0, :, at] = (
                gate_part / (1.0 + jnp.exp(-gate_part)) * up_part
            ).astype(bf16)

    def tokens_spec(width):
        return pl.BlockSpec((2, share, 1, rows, width), lambda m, b, _: (b, 0, m, 0, 0))

    pairs = ranks // 2
    shapes = [
        out((micro, pairs, block, D)),
        out((micro, pairs, block, PAD), f32),
        out((micro, pairs, block, 2 * FF), f32),
        out((micro, pairs, block, FF)),
        out((micro, pairs, block, D)),
        out((micro, pairs, block, D)),
        out((micro, pairs, 2, count, PAD), f32),
    ]
    return pl.pallas_call(
        kernel,
        grid_spec=pltpu.PrefetchScalarGridSpec(
            num_scalar_prefetch=1,
            grid=(micro, pairs),
            in_specs=[tokens_spec(D + PAD), tokens_spec(D)] + [HBM] * planes,
            out_specs=[
                pl.BlockSpec(
                    (1, 1) + s.shape[2:], lambda m, b, _, n=len(s.shape): (m, b) + (0,) * (n - 2)
                )
                for s in shapes
            ],
            scratch_shapes=[pltpu.VMEM((D, 2 * FF), bf16), pltpu.SemaphoreType.DMA((planes,))],
        ),
        out_shape=shapes,
        cost_estimate=cost(micro * pairs * block * D * (2 * FF + 2 * count)),
        compiler_params=params(),
    )(where, payload, upstream, *in_pieces)


def expert_backward(
    step, where, tail, both, active, grad_produced, up_rows, places, in_pieces, out_pieces,
    share, rows, experts,
):
    pairs, block = tail.shape[1:3]
    slots = block // 2
    count = places.shape[3]

    planes = len(in_pieces)

    def kernel(where, tail, both, active, grad_produced, up_rows, places, *refs):
        keep, give, grad_tokens, grad_both, in_weight, out_weight, sems = refs[2 * planes :]
        number = where[0]
        odd = where[2] == 1

        @pl.when(pl.program_id(0) == 0)
        def _():
            copies(
                plane_pairs(where[1], refs[:planes], in_weight)
                + plane_pairs(where[1], refs[planes : 2 * planes], out_weight),
                sems,
            )()

        gate = lane(tail[0, 0], number) + lane(tail[0, 0], experts + number)
        place = lax.broadcasted_iota(jnp.int32, (count, slots), 1).astype(f32)
        selects = [(places[0, 0, part][:, 0:1] == place).astype(bf16) for part in range(2)]

        def spread(value):
            return [
                dot(selects[part], value[part * slots : (part + 1) * slots])
                .astype(bf16)
                .reshape(share, rows, -1)
                for part in range(2)
            ]

        grad_gate = jnp.zeros((block, 1), f32)
        for tile in range(D // TILE):
            at = slice(tile * TILE, (tile + 1) * TILE)
            produced = dot(active[0, 0], out_weight[:, at]).astype(bf16).astype(f32)
            even_rank, odd_rank = spread((gate * produced).astype(bf16))
            keep[0, :, :, at] = jnp.where(odd, odd_rank, even_rank)
            give[0, :, :, at] = jnp.where(odd, even_rank, odd_rank)
            grad_gate = grad_gate + jnp.sum(
                up_rows[0, 0, :, at].astype(f32) * produced, axis=1, keepdims=True
            )

        for tile in range(FF // TILE):
            at = slice(tile * TILE, (tile + 1) * TILE)
            more = slice(FF + tile * TILE, FF + (tile + 1) * TILE)
            grad_active = dot(grad_produced[0, 0], out_weight[at, :], ((1,), (1,)))
            grad_active = grad_active.astype(bf16).astype(f32)
            gate_part = both[0, 0, :, at]
            up_part = both[0, 0, :, more]
            sigma = 1.0 / (1.0 + jnp.exp(-gate_part))
            grad_both[0, :, at] = (
                grad_active * up_part * (sigma * (1.0 + gate_part * (1.0 - sigma)))
            ).astype(bf16)
            grad_both[0, :, more] = (grad_active * (gate_part * sigma)).astype(bf16)

        for tile in range(D // TILE):
            at = slice(tile * TILE, (tile + 1) * TILE)
            grad_rows = dot(grad_both[0], in_weight[at, :], ((1,), (1,))).astype(bf16)
            grad_tokens[0, :, :, at], grad_tokens[1, :, :, at] = spread(grad_rows)

        high = grad_gate.astype(bf16).astype(f32)
        column = lax.broadcasted_iota(jnp.int32, (block, PAD), 1)
        extra = jnp.where(column == number, high, 0.0)
        extra = jnp.where(column == experts + number, grad_gate - high, extra)
        grad_tokens[0, :, :, D:], grad_tokens[1, :, :, D:] = spread(extra.astype(bf16))

    def part(value):
        return pl.BlockSpec(
            (1, 1) + value.shape[2:], lambda b, _: (step, b) + (0,) * (value.ndim - 2)
        )

    def tokens_spec(count, width):
        return pl.BlockSpec((count, share, rows, width), lambda b, _: (b, 0, 0, 0))

    return pl.pallas_call(
        kernel,
        grid_spec=pltpu.PrefetchScalarGridSpec(
            num_scalar_prefetch=1,
            grid=(pairs,),
            in_specs=[part(v) for v in (tail, both, active, grad_produced, up_rows, places)]
            + [HBM] * (2 * planes),
            out_specs=[
                tokens_spec(1, D),
                tokens_spec(1, D),
                tokens_spec(2, D + PAD),
                pl.BlockSpec((1, block, 2 * FF), lambda b, _: (b, 0, 0)),
            ],
            scratch_shapes=[
                pltpu.VMEM((D, 2 * FF), bf16),
                pltpu.VMEM((FF, D), bf16),
                pltpu.SemaphoreType.DMA((2 * planes,)),
            ],
        ),
        out_shape=[
            out((pairs, share, rows, D)),
            out((pairs, share, rows, D)),
            out((2 * pairs, share, rows, D + PAD)),
            out((pairs, block, 2 * FF)),
        ],
        cost_estimate=cost(pairs * block * D * (4 * FF + 2 * count)),
        compiler_params=params(),
    )(
        where, tail, both, active, grad_produced, up_rows, places, *in_pieces, *out_pieces
    )


def weight_gradient(where, planes, left, rights, tail=None, first=0, steps=None):
    steps = planes if steps is None else steps
    count, width = left.shape
    parts = len(rights)
    part_rows = count // parts
    columns = rights[0].shape[1]
    width = width // planes
    step = min(TILE, columns & -columns)
    tails = [] if tail is None else [tail]
    whole = columns + sum(value.shape[1] for value in tails)

    def of_plane(i, where):
        return lax.bitwise_xor(where[1], jnp.int32(first + i))

    def kernel(where, left, *refs):
        rights, tails, targets = refs[:parts], refs[parts:-steps], refs[-steps:]

        def fill(target):
            for value in tails:
                target[:, columns:] = value[...]
            for number in range(columns // step):
                at = slice(number * step, (number + 1) * step)
                target[:, at] = sum(
                    dot(left[part * part_rows : (part + 1) * part_rows], right[:, at], ((0,), (0,)))
                    for part, right in enumerate(rights)
                ).astype(bf16)

        for number, target in enumerate(targets):
            pl.when(pl.program_id(0) == number)(lambda target=target: fill(target))

    return pl.pallas_call(
        kernel,
        grid_spec=pltpu.PrefetchScalarGridSpec(
            num_scalar_prefetch=1,
            grid=(steps,),
            in_specs=[pl.BlockSpec((count, width), lambda i, where: (0, of_plane(i, where)))]
            + [fixed(right.shape) for right in rights]
            + [
                pl.BlockSpec((width, value.shape[1]), lambda i, where: (of_plane(i, where), 0))
                for value in tails
            ],
            out_specs=[fixed((width, whole))] * steps,
        ),
        out_shape=[out((width, whole))] * steps,
        cost_estimate=cost(0 if tails else count * steps * width * columns),
        compiler_params=params(),
    )(where, left, *rights, *tails)


def hidden_backward(
    plane, planes, parts, hidden, gates, upstream, gain, router, gathered, experts
):
    count = hidden.shape[0]
    terms = len(parts)

    def kernel(plane, *refs):
        parts = refs[:terms]
        hidden, gates, upstream, gain, router, gathered = refs[terms : terms + 6]
        (
            grad_hidden, grad_branch, grad_mixed, grad_logits, grad_gain, out_weight, sems
        ) = refs[terms + 6 :]
        wait = copies(out_weight_pairs(plane[0], planes, gathered, out_weight), sems)
        returned = sum(part[...].astype(f32) for part in parts)
        tail = returned[:, D:]
        grad_gates = gates[...] * (tail + pltpu.roll(tail, PAD - experts, 1))
        logits = grad_gates - gates[...] * jnp.sum(grad_gates, axis=1, keepdims=True)
        logits = logits.astype(bf16)
        grad_logits[...] = logits
        grad_normed = returned[:, :D] + dot(logits, router[...], ((1,), (1,)))
        value = hidden[...]
        inverse = inverse_rms(value)
        grad_gain[...] = jnp.sum(grad_normed * value * inverse, axis=0, keepdims=True)
        grad = upstream[...].astype(f32) + rms_backward(value, inverse, gain[...], grad_normed)
        grad_hidden[...] = grad
        grad_branch[...] = grad.astype(bf16)
        wait()

        @tiles(D)
        def _(number):
            at = tile(number)
            grad_mixed[:, at] = dot(grad_branch[...], out_weight[at, :], ((1,), (1,))).astype(bf16)

    shapes = [
        out((count, D), f32), out((count, D)), out((count, D)), out((count, PAD)),
        out((1, D), f32),
    ]
    args = (*parts, hidden, gates, upstream, gain, router, gathered)
    return pl.pallas_call(
        kernel,
        grid_spec=pltpu.PrefetchScalarGridSpec(
            num_scalar_prefetch=1,
            grid=(1,),
            in_specs=[HBM if value is gathered else fixed(value.shape) for value in args],
            out_specs=[fixed(shape.shape) for shape in shapes],
            scratch_shapes=[
                pltpu.VMEM((D, D), bf16),
                pltpu.SemaphoreType.DMA((planes * gathered.shape[0],)),
            ],
        ),
        out_shape=shapes,
        compiler_params=params(),
    )(plane, *args)


def project_backward(step, grad_proj, tokens, slab):
    ranks, rows, _ = grad_proj.shape
    width = slab.shape[1] - PAD

    def kernel(grad_proj, tokens, weight, grad_normed, grad_gain):
        value = tokens[0].astype(f32)
        inverse = inverse_rms(value)
        grad = dot(grad_proj[0], weight[:, :width], ((1,), (1,)))
        grad_normed[...] = grad.astype(bf16)

        @pl.when(pl.program_id(0) == 0)
        def _():
            grad_gain[...] = jnp.zeros_like(grad_gain)

        grad_gain[...] += jnp.sum(grad * value * inverse, axis=0, keepdims=True)

    return pl.pallas_call(
        kernel,
        grid=(ranks,),
        in_specs=[
            leading(grad_proj.shape),
            pl.BlockSpec((1, rows, D), lambda i: (i, step, 0)),
            fixed(slab.shape),
        ],
        out_specs=[pl.BlockSpec((rows, D), lambda i: (i, 0)), fixed((1, D))],
        out_shape=[out((ranks * rows, D)), out((1, D), f32)],
        compiler_params=params(),
    )(grad_proj, tokens, slab)


def cut_heads(weight, tail, ranks):
    rows = weight.shape[0]
    width = D // ranks

    def kernel(weight, tail, target):
        for rank in range(ranks):
            for part in range(3):
                at = part * D + rank * width
                target[rank, :, part * width : (part + 1) * width] = weight[:, at : at + width]
            target[rank, :, 3 * width :] = tail[...]

    return pl.pallas_call(
        kernel,
        out_shape=out((ranks, rows, 3 * width + PAD)),
        compiler_params=params(),
    )(weight, tail)


def unpack(packed, count):
    ranks, rows, columns = packed.shape
    width = (columns - PAD) // 3

    def kernel(packed, main, small):
        for rank in range(ranks):
            for part in range(3):
                at = part * D + rank * width
                main[:, at : at + width] = packed[rank, :, part * width : (part + 1) * width].astype(
                    f32
                )
        tails = sum(packed[rank, :, 3 * width :].astype(f32) for rank in range(ranks))
        small[...] = tails + pltpu.roll(tails, PAD - count, 1)

    return pl.pallas_call(
        kernel,
        out_shape=[out((rows, 3 * D), f32), out((rows, PAD), f32)],
        compiler_params=params(),
    )(packed)


def shift_rep(value, step):
    count = lax.axis_size("rep")
    return lax.ppermute(value, "rep", [(i, (i + step) % count) for i in range(count)])


def cross_rep(value, bits):
    return lax.ppermute(value, "rep", [(i, i ^ bits) for i in range(lax.axis_size("rep"))])


def after(value, *others):
    return lax.optimization_barrier((value,) + others)[0]


def two_parts(value):
    high = lax.reduce_precision(value, 8, 7)
    return high.astype(bf16), (value - high).astype(bf16)


def ring_rep(value, *work):
    count = lax.axis_size("rep")
    rank = lax.axis_index("rep")
    rows = value.shape[0]
    full = jnp.zeros((count * rows,) + value.shape[1:], value.dtype)
    full = lax.dynamic_update_slice_in_dim(full, value, rank * rows, 0)
    for step in range(1, count):
        value, work = lax.optimization_barrier((value, work)) if step == count - 1 else (value, work)
        value = shift_rep(value, 1)
        full = lax.dynamic_update_slice_in_dim(full, value, (rank - step) % count * rows, 0)
    return full, work


def on_device(
    tokens, cotangent, w_qkv, w_o, w_router, norm_gains, qk_gain, w_in, w_out, segments, routes
):
    planes = lax.axis_size("rep")
    ranks = lax.axis_size("ep")
    plane = lax.axis_index("rep")
    rank = lax.axis_index("ep")
    share = w_in.shape[0]
    own = plane % share
    experts = share * ranks
    where = jnp.stack([rank * share + own, plane, rank % 2]).astype(jnp.int32)
    micro = segments.shape[1]
    mine = tokens.shape[0]
    rows = mine // micro
    length = rows * ranks
    capacity = rows * TOP * 17 // (16 * experts)
    slots = -(-share * capacity // 16) * 16
    width = HEADS // ranks * HD
    qk_gains = qk_gain.astype(f32).reshape(2, HD)
    dense_rows = w_qkv.shape[0]

    def exchange(value, step):
        pairs = [(i, i // share * share + (i % share + step) % share) for i in range(planes)]
        return lax.ppermute(value, "rep", pairs)

    def with_group(value):
        return jnp.stack([value] + [exchange(value, step) for step in range(1, share)])

    def gather_ranks(value):
        return lax.all_gather(value, "ep", axis=0)

    assert planes & (planes - 1) == 0 and share & (share - 1) == 0
    near, half, last_step = 1, planes // 2, planes - 1
    in_parts, out_parts = (
        {
            step: lax.dynamic_index_in_dim(weight, own ^ step % share, 0, keepdims=False)
            for step in range(planes)
        }
        for weight in (w_in, w_out)
    )

    def send(parts, steps):
        return {step: cross_rep(parts[step], step) for step in steps}

    stream = gather_ranks(tokens)
    out_rows = [w_o] + [cross_rep(w_o, step) for step in range(1, planes)]
    upstream_group = with_group(cotangent)
    slab = cut_heads(
        w_qkv,
        jnp.concatenate(
            [
                w_router,
                norm_gains.reshape(dense_rows, 2),
                jnp.zeros((dense_rows, PAD - experts - 2), bf16),
            ],
            axis=1,
        ),
        ranks,
    )
    slab = lax.all_to_all(slab, "ep", split_axis=0, concat_axis=0, tiled=True)
    slab = slab.reshape(ranks * dense_rows, 3 * width + PAD)
    out_rows, upstream_group, slab = lax.optimization_barrier((out_rows, upstream_group, slab))
    gathered = gather_ranks(jnp.concatenate(out_rows, axis=0))
    segment = segments[0]
    cosine, sine = jax.vmap(lambda one: rope_tables(doc_positions(one), HD))(segment)
    sine = jnp.where(jnp.arange(HD) < HD // 2, -sine, sine)
    tables = (cosine, sine, segment[:, :, None], segment[:, None, :], qk_gains)
    slab, (tables, in_parts, out_parts) = ring_rep(slab, tables, in_parts, out_parts)
    router = slab[:, 3 * width :]
    gain_pair = router[:, experts : experts + 2].reshape(-1).astype(f32)
    first_gain = gain_pair[None, :D]
    second_gain = gain_pair[None, D:]
    in_parts, out_parts, upstream_group, stream = after(
        (in_parts, out_parts, upstream_group, stream), slab
    )
    in_pieces = {0: in_parts[0], **send(in_parts, range(last_step - 1, 0, -1))}
    upstream_all = gather_ranks(upstream_group)

    normed, proj = project(stream, first_gain, slab)
    proj = proj.reshape(ranks, micro, rows, 3 * width)
    mixed_h, query, keys, values, lses = attention_forward(proj, *tables)
    mixed = lax.all_to_all(mixed_h, "ep", split_axis=0, concat_axis=3, tiled=True)
    mixed = mixed.reshape(mine, D)
    hidden, payload, gates = route(
        where[1:2], planes, mixed, tokens, gathered, second_gain, router, routes, experts
    )
    normed_two = payload[:, :D]
    payload, in_pieces = lax.optimization_barrier((payload, in_pieces))
    payload = with_group(payload)
    payload, in_parts, out_parts = lax.optimization_barrier((payload, in_parts, out_parts))
    in_pieces.update(send(in_parts, [last_step]))
    in_pieces, out_parts = lax.optimization_barrier((in_pieces, out_parts))
    out_pieces = {0: out_parts[0], **send(out_parts, range(1, planes))}
    in_pieces = [in_pieces[step] for step in range(planes)]
    out_pieces = [out_pieces[step] for step in range(planes)]
    payload = gather_ranks(payload)

    shape = (ranks, share, micro, rows, -1)
    rows_in, tail, both, active, grad_produced, up_rows, places = expert_forward(
        where, payload.reshape(shape), upstream_all.reshape(shape), in_pieces, slots, experts
    )
    in_rows = micro * ranks * slots
    out_cut = weight_gradient(
        where, planes, active.reshape(in_rows, FF), [grad_produced.reshape(in_rows, D)]
    )

    def sum_rep(parts):
        sums = [
            sum(parts[step].astype(f32) for step in range(first, planes, share))
            for first in range(share)
        ]
        return jnp.stack(
            [
                sum(jnp.where(own ^ step == j, sums[step], 0.0) for step in range(share))
                for j in range(share)
            ]
        )

    tail, out_cut, out_pieces = lax.optimization_barrier((tail, out_cut, out_pieces))
    out_sent = send(out_cut, range(1, planes))
    back = []
    returned = []

    def scatter_ranks(value):
        return lax.psum_scatter(value, "ep", scatter_dimension=0)

    def exchange_back(value):
        return [value[0]] + [exchange(value[step], share - step) for step in range(1, share)]

    for step in range(micro):
        back.append(
            expert_backward(
                step, where, tail, both, active, grad_produced, up_rows, places, in_pieces,
                out_pieces, share, rows, experts,
            )
        )
        returned.append(scatter_ranks(back[step][2]))
        if step == 0:
            ended = {bits: out_sent[bits] for bits in (near, last_step)}
            tail, ended = after((tail, ended), back[step][2])
            out_sent.update(ended)
        else:
            tail = after(tail, back[step][2])
    rows_in = after(rows_in, tail)
    rows_flat = rows_in.reshape(in_rows, D)
    grads_flat = [back[step][3].reshape(in_rows // micro, 2 * FF) for step in range(micro)]
    (in_last,) = weight_gradient(
        where, planes, rows_flat, grads_flat, first=last_step, steps=1
    )
    rows_flat, in_last = lax.optimization_barrier((rows_flat, in_last))
    in_cut = weight_gradient(where, planes, rows_flat, grads_flat, steps=last_step)

    def cuts(value, *places):
        ends = [-(-value.shape[0] * place // 512) * 16 for place in (0, *places, 32)]
        return [value[start:end] for start, end in zip(ends, ends[1:])]

    in_last = cuts(in_last, 11, 19, 26)
    last_sent = [cross_rep(in_last[0], last_step)]

    def swap(value, step):
        return lax.ppermute(value, "ep", [(i, i ^ step) for i in range(ranks)])

    def pair_sum(keep, give):
        return (keep.astype(f32) + swap(give, 1).astype(f32)).astype(bf16)

    bits = list(range((ranks // 2).bit_length() - 1))

    def halve(values, phase):
        results = []
        for number, value in enumerate(values):
            way = bits if number % 2 == 0 else bits[::-1]
            bit = way[phase]
            low = 2 ** sum(other < bit for other in way[phase:])
            value = value.reshape((-1, 2, low) + value.shape[1:])
            side = rank // 2 // 2**bit % 2
            keep, give = (
                lax.dynamic_index_in_dim(value, which, 1, keepdims=False).reshape(
                    (-1,) + value.shape[3:]
                )
                for which in (side, 1 - side)
            )
            results.append((keep, swap(give, 2 * 2**bit)))
        return results

    def total(parts):
        return sum(part.astype(f32) for part in parts)

    grad_inputs, branches, logit_grads, grad_projs = [], [], [], []
    gain_two_sum = gain_one_sum = qk_sum = 0.0
    in_cut, out_sent, last_sent, in_last = lax.optimization_barrier(
        (in_cut, out_sent, last_sent, in_last)
    )
    mixtures = [part[:2] for part in back]
    for step in range(micro):
        at = slice(step * rows, (step + 1) * rows)
        parts = after(returned[step], [one[1] for one in grad_inputs])
        parts, last_sent = lax.optimization_barrier((parts, last_sent))
        parts = exchange_back(parts)
        parts, in_cut, mixtures, in_last = lax.optimization_barrier(
            (parts, in_cut, mixtures, in_last)
        )
        if step == 0:
            mixtures = [pair_sum(*part) for part in mixtures]
            last_sent.append(cross_rep(in_last[1], last_step))
        if step == micro - 1:
            rest = [cuts(value, 12, 20) for value in in_cut[1:]]
            rest_sent = [[cross_rep(part[0], i + 1) for i, part in enumerate(rest)]]
        grad_hidden, grad_branch, grad_mixed, grad_logits, gain_two = hidden_backward(
            where[1:2], planes, parts, hidden[at], gates[at], cotangent[at], second_gain,
            router, gathered, experts,
        )
        branches.append(grad_branch)
        logit_grads.append(grad_logits)
        gain_two_sum = gain_two_sum + gain_two
        if step == micro - 1:
            out_sum = dot(mixed, jnp.concatenate(branches, axis=0), ((0,), (0,))).astype(bf16)
            out_sum = out_sum.reshape(planes, ranks, dense_rows, D).transpose(1, 0, 2, 3)
        grad_mixed = lax.all_to_all(grad_mixed, "ep", split_axis=1, concat_axis=0, tiled=True)
        grad_mixed, mixtures, last_sent, in_last = lax.optimization_barrier(
            (grad_mixed, mixtures, last_sent, in_last)
        )
        if step == 0:
            last_sent.append(cross_rep(in_last[2], last_step))
        if step == micro - 1:
            grad_mixed, mixtures, rest_sent, rest, out_sum = lax.optimization_barrier(
                (grad_mixed, mixtures, rest_sent, rest, out_sum)
            )
            out_sum = lax.psum_scatter(out_sum, "ep", scatter_dimension=0)
            rest_sent.append([cross_rep(part[1], i + 1) for i, part in enumerate(rest)])
        grad_proj, grad_qk = attention_backward(
            step, proj, *tables, query, keys, values, lses, grad_mixed
        )
        qk_sum = qk_sum + grad_qk.reshape(-1)
        if step < micro - 1:
            grad_proj, last_sent, in_last = lax.optimization_barrier(
                (grad_proj, last_sent, in_last)
            )
            if step == 0:
                last_sent.append(cross_rep(in_last[3], last_step))
        else:
            grad_proj, grad_inputs, rest_sent, rest = lax.optimization_barrier(
                (grad_proj, grad_inputs, rest_sent, rest)
            )
        grad_projs.append(grad_proj)
        grad_normed, gain_one = project_backward(step, grad_proj, stream, slab)
        gain_one_sum = gain_one_sum + gain_one
        grad_inputs.append(
            (
                grad_hidden,
                grad_normed,
                lax.psum_scatter(grad_normed, "ep", scatter_dimension=0, tiled=True),
            )
        )

    router_sum = dot(normed_two, jnp.concatenate(logit_grads, axis=0), ((0,), (0,)))
    qk_columns = qk_sum.shape[0] // dense_rows
    small = jnp.concatenate(
        [
            router_sum[:, :experts],
            jnp.concatenate([gain_one_sum, gain_two_sum], axis=1).reshape(D, 2),
            jnp.tile(qk_sum.reshape(dense_rows, qk_columns), (planes * ranks, 1)),
        ],
        axis=1,
    )
    count = small.shape[1]

    def halves(value):
        high, low = two_parts(value)
        blank = jnp.zeros((value.shape[0], PAD - 2 * count), bf16)
        return jnp.concatenate([high, low, blank], axis=1)

    def joined(value):
        return value[..., :count].astype(f32) + value[..., count : 2 * count].astype(f32)

    grad_projs, rest, out_cut, out_sent, _ = lax.optimization_barrier(
        (grad_projs, rest, out_cut, out_sent, grad_normed)
    )
    rest_sent.append([cross_rep(part[2], i + 1) for i, part in enumerate(rest)])
    packed = weight_gradient(
        where,
        planes,
        normed.reshape(ranks * mine, D),
        [jnp.stack(grad_projs, axis=1).reshape(ranks * mine, 3 * width)],
        halves(small),
    )
    packed, rest_sent, out_cut, out_sent, mixtures = lax.optimization_barrier(
        (packed, rest_sent, out_cut, out_sent, mixtures)
    )
    packed_sent = [packed[0]] + [cross_rep(packed[step], step) for step in range(1, planes)]
    for phase in range(len(bits)):
        crossed = halve(mixtures, phase)
        if phase < len(bits) - 1:
            mixtures = [total(parts).astype(bf16) for parts in crossed]
    normed_sums = [one[2] for one in grad_inputs]
    normed_sums = [one[2] for one in grad_inputs]
    grad_tokens = []
    for step in range(micro):
        own_stream = tokens[step * rows : (step + 1) * rows].astype(f32)
        grad_tokens.append(
            grad_inputs[step][0]
            + rms_backward(
                own_stream, inverse_rms(own_stream), first_gain, normed_sums[step].astype(f32)
            )
        )
    grad_tokens = jnp.concatenate(grad_tokens, axis=0)
    packed_sent, grad_tokens = lax.optimization_barrier((packed_sent, grad_tokens))
    crossed, out_sum = lax.optimization_barrier((crossed, out_sum))
    mixture = []
    for number in range(micro):
        parts = total(crossed[number])[0]
        mixture.append((parts[0], exchange_back(parts.astype(bf16))[1:]))
    own_sum = lax.dynamic_index_in_dim(out_sum, plane, 0, keepdims=False)
    out_sent_back = [
        cross_rep(lax.dynamic_index_in_dim(out_sum, plane ^ step, 0, keepdims=False), step)
        for step in range(1, planes)
    ]
    main = total([part[:, : 3 * width] for part in packed_sent]).astype(bf16)
    small = sum(joined(part[:, 3 * width :]) for part in packed_sent)
    packed = jnp.concatenate([main, halves(small)], axis=1).reshape(ranks, dense_rows, -1)
    packed = lax.all_to_all(packed, "ep", split_axis=0, concat_axis=0, tiled=True)
    packed, mixture, out_sent_back = lax.optimization_barrier((packed, mixture, out_sent_back))
    output = jnp.concatenate([mine_part + total(others) for mine_part, others in mixture], axis=0)
    output = (hidden + output).astype(bf16)
    grad_w_o = total([own_sum, *out_sent_back])
    grad_w_qkv, small = unpack(packed, count)
    grad_w_out = sum_rep({0: out_cut[0], **out_sent})
    in_sent = {
        i + 1: jnp.concatenate([parts[i] for parts in rest_sent], axis=0)
        for i in range(planes - 2)
    }
    in_sent[last_step] = jnp.concatenate(last_sent, axis=0)
    grad_w_in = sum_rep({0: in_cut[0], **in_sent})
    return (
        output,
        grad_tokens,
        grad_w_qkv,
        grad_w_o,
        small[:, :experts],
        small[:, experts : experts + 2].reshape(-1),
        small[:, experts + 2 : count].reshape(-1),
        grad_w_in,
        grad_w_out,
    )


def solution(mesh):
    placed = (
        P(("rep", "ep"), None),
        P(("rep", "ep"), None),
        P(("rep", "ep"), None),
        P(("rep", "ep"), None),
        P(("rep", "ep"), None),
        P(("rep", "ep")),
        P(),
        P("ep", "rep", None),
        P("ep", "rep", None),
        P("rep", None, None),
        P(("rep", "ep"), None),
    )
    return jax.shard_map(
        on_device,
        mesh=mesh,
        in_specs=placed,
        out_specs=(
            P(("rep", "ep"), None),
            P(("rep", "ep"), None),
            P(("rep", "ep"), None),
            P(("rep", "ep"), None),
            P(("rep", "ep"), None),
            P(("rep", "ep")),
            P(),
            P("ep", "rep", None),
            P("ep", "rep", None),
        ),
        check_vma=False,
    )
```

```python
import math

import jax
import jax.numpy as jnp
from jax import lax
from jax.experimental import pallas as pl
from jax.experimental.pallas import tpu as pltpu
from jax.sharding import PartitionSpec as P

D = 2048
HEADS = 16
HD = 128
FF = 1024
TOP = 8
HALF = 512
PAD = 128

epsilon = 1e-06
rope_base = 50000.0
bf16 = jnp.bfloat16
f32 = jnp.float32


def dot(a, b, dims=((1,), (0,))):
    return lax.dot_general(a, b, (dims, ((), ())), preferred_element_type=f32)


def inverse_rms(value):
    return lax.rsqrt(jnp.mean(value * value, axis=-1, keepdims=True) + epsilon)


def rms_backward(value, inverse, gain, grad):
    scaled = grad * gain
    inner = jnp.mean(scaled * value, axis=-1, keepdims=True)
    return inverse * (scaled - value * (inverse * inverse * inner))


def doc_positions(segment):
    index = jnp.arange(segment.shape[0], dtype=jnp.int32)
    change = jnp.concatenate([jnp.ones((1,), dtype=jnp.bool_), segment[1:] != segment[:-1]])
    start = lax.cummax(jnp.where(change, index, 0), axis=0)
    return index - start


def rope_tables(position, width):
    steps = jnp.arange(width // 2, dtype=f32) * (2.0 / width)
    rates = jnp.exp(-steps * math.log(rope_base))
    angle = position.astype(f32)[:, None] * rates[None, :]
    angle = jnp.concatenate([angle, angle], axis=-1)
    return (jnp.cos(angle), jnp.sin(angle))


def norm_rope(value, gain, cosine, sine):
    inverse = lax.rsqrt(jnp.mean(value * value, axis=1, keepdims=True) + epsilon)
    value = value * inverse * gain
    return value * cosine + pltpu.roll(value, HD // 2, 1) * sine


def norm_rope_back(value, gain, cosine, sine, grad):
    inverse = lax.rsqrt(jnp.mean(value * value, axis=1, keepdims=True) + epsilon)
    grad = grad * cosine + pltpu.roll(grad * sine, HD // 2, 1)
    normal = value * inverse
    scaled = grad * gain
    inner = jnp.mean(scaled * normal, axis=1, keepdims=True)
    return inverse * (scaled - normal * inner), jnp.sum(grad * normal, axis=0, keepdims=True)


def kept_scores(query, keys, q_seg, k_seg, start):
    scores = dot(query, keys, ((1,), (1,))) * (1.0 / math.sqrt(HD))
    q_index = start + lax.broadcasted_iota(jnp.int32, scores.shape, 0)
    k_index = lax.broadcasted_iota(jnp.int32, scores.shape, 1)
    keep = (jnp.abs(q_index - k_index) <= HALF) & (q_seg == k_seg)
    return jnp.where(keep, scores, -1e30)


BIG = 100 * 1024 * 1024 // 2


def forward_kernel(
    heads, proj, cosine, sine, seg_column, seg_row, gains, mixed, query, keys, values, lses
):
    ranks, _, rows, _ = proj.shape
    length = ranks * rows
    q_block = 2 * rows
    k_seg = seg_row[0]
    for head in range(heads):
        at = slice(head * HD, (head + 1) * HD)

        def raw(part):
            first = (part * heads + head) * HD
            return proj[:, 0, :, first : first + HD].reshape(length, HD)

        query[0, :, at] = norm_rope(raw(0), gains[0:1], cosine[0], sine[0]).astype(bf16)
        keys[0, :, at] = norm_rope(raw(1), gains[1:2], cosine[0], sine[0]).astype(bf16)
        values[0, :, at] = raw(2).astype(bf16)

        @pl.loop(0, length // q_block)
        def one_block(number, head=head, at=at):
            start = pl.multiple_of(number * q_block, q_block)
            here = pl.ds(start, q_block)
            scores = kept_scores(
                query[0, here, at], keys[0, :, at], seg_column[0, here], k_seg, start
            )
            top = jnp.max(scores, axis=1, keepdims=True)
            weights = jnp.exp(scores - top)
            total = jnp.sum(weights, axis=1, keepdims=True)
            lses[0, head, here] = top + jnp.log(total)
            weights = (weights * (1.0 / total)).astype(bf16)
            result = dot(weights, values[0, :, at]).astype(bf16)
            mixed[pl.ds(number * 2, 2), 0, :, at] = result.reshape(2, rows, HD)


def backward_kernel(
    heads, proj, cosine, sine, seg_column, seg_row, gains, query, keys, values, lses, grad_mixed,
    grad_proj, grad_gains, grad_q, grad_k, grad_v,
):
    ranks, _, rows, _ = proj.shape
    length = ranks * rows
    q_block = 2 * rows
    k_seg = seg_row[0]
    scale = 1.0 / math.sqrt(HD)
    sum_q = jnp.zeros((1, HD), f32)
    sum_k = jnp.zeros((1, HD), f32)
    for head in range(heads):
        at = slice(head * HD, (head + 1) * HD)
        grad_k[...] = jnp.zeros_like(grad_k)
        grad_v[...] = jnp.zeros_like(grad_v)

        @pl.loop(0, length // q_block)
        def one_block(number, head=head, at=at):
            start = pl.multiple_of(number * q_block, q_block)
            here = pl.ds(start, q_block)
            q_rows = query[0, here, at]
            g_rows = grad_mixed[here, at]
            k_all = keys[0, :, at]
            scores = kept_scores(q_rows, k_all, seg_column[0, here], k_seg, start)
            weights = jnp.exp(scores - lses[0, head, here])
            grad_weights = dot(g_rows, values[0, :, at], ((1,), (1,)))
            delta = jnp.sum(weights * grad_weights, axis=1, keepdims=True)
            grad_scores = (weights * (grad_weights - delta)).astype(bf16)
            grad_q[here] = dot(grad_scores, k_all) * scale
            grad_k[...] += dot(grad_scores, q_rows, ((0,), (0,)))
            grad_v[...] += dot(weights.astype(bf16), g_rows, ((0,), (0,)))

        def rounded(value):
            return value.astype(bf16).astype(f32)

        def raw(part):
            first = (part * heads + head) * HD
            return proj[:, 0, :, first : first + HD].reshape(length, HD)

        def put(part, value):
            first = (part * heads + head) * HD
            grad_proj[:, :, first : first + HD] = value.astype(bf16).reshape(ranks, rows, HD)

        back_q, gain_q = norm_rope_back(
            raw(0), gains[0:1], cosine[0], sine[0], rounded(grad_q[...])
        )
        back_k, gain_k = norm_rope_back(
            raw(1), gains[1:2], cosine[0], sine[0], rounded(grad_k[...] * scale)
        )
        sum_q, sum_k = sum_q + gain_q, sum_k + gain_k
        put(0, back_q)
        put(1, back_k)
        put(2, grad_v[...])
    grad_gains[0:1] = sum_q
    grad_gains[1:2] = sum_k


def fixed(shape):
    return pl.BlockSpec(shape, lambda *_: (0,) * len(shape), pipeline_mode=pl.Buffered(1))


def leading(shape):
    return pl.BlockSpec((1,) + shape[1:], lambda i: (i,) + (0,) * (len(shape) - 1))


def params():
    return pltpu.CompilerParams(vmem_limit_bytes=BIG)


def cost(products):
    return pl.CostEstimate(flops=20 * products, bytes_accessed=0, transcendentals=0)


def out(shape, dtype=bf16):
    return jax.ShapeDtypeStruct(shape, dtype)


def attention_forward(proj, cosine, sine, seg_column, seg_row, gains):
    ranks, micro, rows, width = proj.shape
    length = ranks * rows
    width = width // 3
    heads = width // HD
    part = out((micro, length, width))
    by_rank = lambda n: pl.BlockSpec((ranks, 1, rows, n), lambda i: (0, i, 0, 0))
    lses = out((micro, heads, length, 1), f32)
    return pl.pallas_call(
        lambda *refs: forward_kernel(heads, *refs),
        grid=(micro,),
        in_specs=[by_rank(3 * width)]
        + [leading(v.shape) for v in (cosine, sine, seg_column, seg_row)]
        + [fixed(gains.shape)],
        out_specs=[by_rank(width)] + [leading(part.shape)] * 3 + [leading(lses.shape)],
        out_shape=[out((ranks, micro, rows, width)), part, part, part, lses],
        compiler_params=params(),
    )(proj, cosine, sine, seg_column, seg_row, gains)


def attention_backward(
    step, proj, cosine, sine, seg_column, seg_row, gains, query, keys, values, lses, grad_mixed
):
    ranks, micro, rows, width = proj.shape
    length = ranks * rows
    heads = width // 3 // HD

    def part(value):
        return pl.BlockSpec((1,) + value.shape[1:], lambda i: (step,) + (0,) * (value.ndim - 1))

    return pl.pallas_call(
        lambda *refs: backward_kernel(heads, *refs),
        grid=(1,),
        in_specs=[pl.BlockSpec((ranks, 1, rows, width), lambda i: (0, step, 0, 0))]
        + [part(v) for v in (cosine, sine, seg_column, seg_row)]
        + [fixed(gains.shape)]
        + [part(v) for v in (query, keys, values, lses)]
        + [fixed(grad_mixed.shape)],
        out_specs=[fixed((ranks, rows, width)), fixed((2, HD))],
        out_shape=[out((ranks, rows, width)), out((2, HD), f32)],
        scratch_shapes=[pltpu.VMEM((length, HD), f32)] * 3,
        compiler_params=params(),
    )(
        proj, cosine, sine, seg_column, seg_row, gains, query, keys, values, lses, grad_mixed
    )


def project(tokens, gain, slab):
    ranks, count, _ = tokens.shape
    width = slab.shape[1] - PAD

    def kernel(value, gain, weight, normed, proj):
        value = value[0].astype(f32)
        result = (value * inverse_rms(value) * gain[...]).astype(bf16)
        normed[0] = result
        proj[0] = dot(result, weight[:, :width])

    return pl.pallas_call(
        kernel,
        grid=(ranks,),
        in_specs=[leading((ranks, count, D)), fixed((1, D)), fixed(slab.shape)],
        out_specs=[leading((ranks, count, D)), leading((ranks, count, width))],
        out_shape=[out((ranks, count, D)), out((ranks, count, width), f32)],
        compiler_params=params(),
    )(tokens, gain, slab)


TILE = 512


def tiles(count):
    return pl.loop(0, count // TILE)


def tile(number):
    return pl.ds(pl.multiple_of(number * TILE, TILE), TILE)


HBM = pl.BlockSpec(memory_space=pl.ANY)


def copies(pairs, sems):
    started = [
        pltpu.make_async_copy(source, target, sems.at[place])
        for place, (source, target) in enumerate(pairs)
    ]
    for copy in started:
        copy.start()

    def wait():
        for copy in started:
            copy.wait()

    return wait


def plane_pairs(plane, pieces, target):
    planes = len(pieces)
    rows = target.shape[0] // planes
    return [
        (piece, target.at[pl.ds(lax.bitwise_xor(plane, jnp.int32(step)) * rows, rows)])
        for step, piece in enumerate(pieces)
    ]


def out_weight_pairs(plane, planes, gathered, target):
    ranks = gathered.shape[0]
    rows = D // (planes * ranks)
    return [
        (
            gathered.at[rank, pl.ds(step * rows, rows)],
            target.at[
                pl.ds((lax.bitwise_xor(plane, jnp.int32(step)) * ranks + rank) * rows, rows)
            ],
        )
        for rank in range(ranks)
        for step in range(planes)
    ]


def route(plane, planes, mixed, tokens, gathered, gain, router, routes, experts):
    count = tokens.shape[0]
    pieces = planes * gathered.shape[0]

    def kernel(
        plane, mixed, tokens, gathered, gain, router, routes, hidden, payload, gates,
        out_weight, sems,
    ):
        copies(out_weight_pairs(plane[0], planes, gathered, out_weight), sems)()

        @tiles(D)
        def _(number):
            at = tile(number)
            hidden[:, at] = tokens[:, at].astype(f32) + dot(mixed[...], out_weight[:, at])

        value = hidden[...]
        normed = (value * inverse_rms(value) * gain[...]).astype(bf16)
        payload[:, :D] = normed
        logits = dot(normed, router[...])
        column = lax.broadcasted_iota(jnp.int32, logits.shape, 1)
        routed = column == routes[:, 0:1]
        for choice in range(1, TOP):
            routed = routed | (column == routes[:, choice : choice + 1])
        logits = jnp.where(routed, logits, -1e30)
        weights = jnp.exp(logits - jnp.max(logits, axis=1, keepdims=True))
        weights = jnp.where(routed, weights, 0.0)
        weights = weights / jnp.sum(weights, axis=1, keepdims=True)
        gates[...] = weights
        high = weights.astype(bf16).astype(f32)
        payload[:, D:] = (high + pltpu.roll(weights - high, experts, 1)).astype(bf16)

    shapes = [out((count, D), f32), out((count, D + PAD)), out((count, PAD), f32)]
    return pl.pallas_call(
        kernel,
        grid_spec=pltpu.PrefetchScalarGridSpec(
            num_scalar_prefetch=1,
            grid=(1,),
            in_specs=[
                HBM if value is gathered else fixed(value.shape)
                for value in (mixed, tokens, gathered, gain, router, routes)
            ],
            out_specs=[fixed(shape.shape) for shape in shapes],
            scratch_shapes=[pltpu.VMEM((D, D), bf16), pltpu.SemaphoreType.DMA((pieces,))],
        ),
        out_shape=shapes,
        compiler_params=params(),
    )(plane, mixed, tokens, gathered, gain, router, routes)


def lane(value, number):
    column = lax.broadcasted_iota(jnp.int32, value.shape, 1)
    return jnp.sum(jnp.where(column == number, value.astype(f32), 0.0), axis=1, keepdims=True)


def one_hot(slot, slots):
    place = lax.broadcasted_iota(jnp.int32, (slots, slot.shape[1]), 0).astype(f32)
    return (place == slot).astype(bf16)


def expert_forward(where, payload, upstream, in_pieces, slots, experts):
    ranks, share, micro, rows, _ = payload.shape
    count = share * rows
    block = 2 * slots

    planes = len(in_pieces)

    def kernel(where, payload, upstream, *refs):
        (
            rows_in, tail, both, active, grad_produced, up_rows, places, in_weight, sems
        ) = refs[planes:]
        number = where[0]

        @pl.when((pl.program_id(0) == 0) & (pl.program_id(1) == 0))
        def _():
            copies(plane_pairs(where[1], refs[:planes], in_weight), sems)()

        for part in range(2):
            here = slice(part * slots, (part + 1) * slots)
            value = payload[part].reshape(count, D + PAD)
            marks = value[:, D:]
            first = lax.broadcasted_iota(jnp.int32, (8, PAD), 1) == number
            taken = dot(first.astype(bf16), marks, ((1,), (1,))) > 0.0
            before = lax.broadcasted_iota(jnp.int32, (count, count), 0)
            behind = lax.broadcasted_iota(jnp.int32, (count, count), 1)
            slot = dot(taken.astype(bf16), (before < behind).astype(bf16))
            select = one_hot(jnp.where(taken, slot, -1.0)[0:1], slots)
            wide = jnp.broadcast_to(lane(marks, number) > 0.0, (count, PAD))
            slot = dot((before > behind).astype(bf16), wide.astype(bf16))
            places[0, 0, part] = jnp.where(wide, slot, -1.0)
            rows_in[0, 0, here] = dot(select, value[:, :D]).astype(bf16)
            marks = dot(select, marks)
            tail[0, 0, here] = marks
            gate = lane(marks, number) + lane(marks, experts + number)
            picked = dot(select, upstream[part].reshape(count, D))
            up_rows[0, 0, here] = picked.astype(bf16)
            grad_produced[0, 0, here] = (gate * picked).astype(bf16)

        for number in range(FF // TILE):
            at = slice(number * TILE, (number + 1) * TILE)
            more = slice(FF + number * TILE, FF + (number + 1) * TILE)
            gate_part = dot(rows_in[0, 0], in_weight[:, at])
            up_part = dot(rows_in[0, 0], in_weight[:, more])
            both[0, 0, :, at] = gate_part
            both[0, 0, :, more] = up_part
            active[0, 0, :, at] = (
                gate_part / (1.0 + jnp.exp(-gate_part)) * up_part
            ).astype(bf16)

    def tokens_spec(width):
        return pl.BlockSpec((2, share, 1, rows, width), lambda m, b, _: (b, 0, m, 0, 0))

    pairs = ranks // 2
    shapes = [
        out((micro, pairs, block, D)),
        out((micro, pairs, block, PAD), f32),
        out((micro, pairs, block, 2 * FF), f32),
        out((micro, pairs, block, FF)),
        out((micro, pairs, block, D)),
        out((micro, pairs, block, D)),
        out((micro, pairs, 2, count, PAD), f32),
    ]
    return pl.pallas_call(
        kernel,
        grid_spec=pltpu.PrefetchScalarGridSpec(
            num_scalar_prefetch=1,
            grid=(micro, pairs),
            in_specs=[tokens_spec(D + PAD), tokens_spec(D)] + [HBM] * planes,
            out_specs=[
                pl.BlockSpec(
                    (1, 1) + s.shape[2:], lambda m, b, _, n=len(s.shape): (m, b) + (0,) * (n - 2)
                )
                for s in shapes
            ],
            scratch_shapes=[pltpu.VMEM((D, 2 * FF), bf16), pltpu.SemaphoreType.DMA((planes,))],
        ),
        out_shape=shapes,
        cost_estimate=cost(micro * pairs * block * D * (2 * FF + 2 * count)),
        compiler_params=params(),
    )(where, payload, upstream, *in_pieces)


def expert_backward(
    step, where, tail, both, active, grad_produced, up_rows, places, in_pieces, out_pieces,
    share, rows, experts,
):
    pairs, block = tail.shape[1:3]
    slots = block // 2
    count = places.shape[3]

    planes = len(in_pieces)

    def kernel(where, tail, both, active, grad_produced, up_rows, places, *refs):
        keep, give, grad_tokens, grad_both, in_weight, out_weight, sems = refs[2 * planes :]
        number = where[0]
        odd = where[2] == 1

        @pl.when(pl.program_id(0) == 0)
        def _():
            copies(
                plane_pairs(where[1], refs[:planes], in_weight)
                + plane_pairs(where[1], refs[planes : 2 * planes], out_weight),
                sems,
            )()

        gate = lane(tail[0, 0], number) + lane(tail[0, 0], experts + number)
        place = lax.broadcasted_iota(jnp.int32, (count, slots), 1).astype(f32)
        selects = [(places[0, 0, part][:, 0:1] == place).astype(bf16) for part in range(2)]

        def spread(value):
            return [
                dot(selects[part], value[part * slots : (part + 1) * slots])
                .astype(bf16)
                .reshape(share, rows, -1)
                for part in range(2)
            ]

        grad_gate = jnp.zeros((block, 1), f32)
        for tile in range(D // TILE):
            at = slice(tile * TILE, (tile + 1) * TILE)
            produced = dot(active[0, 0], out_weight[:, at]).astype(bf16).astype(f32)
            even_rank, odd_rank = spread((gate * produced).astype(bf16))
            keep[0, :, :, at] = jnp.where(odd, odd_rank, even_rank)
            give[0, :, :, at] = jnp.where(odd, even_rank, odd_rank)
            grad_gate = grad_gate + jnp.sum(
                up_rows[0, 0, :, at].astype(f32) * produced, axis=1, keepdims=True
            )

        for tile in range(FF // TILE):
            at = slice(tile * TILE, (tile + 1) * TILE)
            more = slice(FF + tile * TILE, FF + (tile + 1) * TILE)
            grad_active = dot(grad_produced[0, 0], out_weight[at, :], ((1,), (1,)))
            grad_active = grad_active.astype(bf16).astype(f32)
            gate_part = both[0, 0, :, at]
            up_part = both[0, 0, :, more]
            sigma = 1.0 / (1.0 + jnp.exp(-gate_part))
            grad_both[0, :, at] = (
                grad_active * up_part * (sigma * (1.0 + gate_part * (1.0 - sigma)))
            ).astype(bf16)
            grad_both[0, :, more] = (grad_active * (gate_part * sigma)).astype(bf16)

        for tile in range(D // TILE):
            at = slice(tile * TILE, (tile + 1) * TILE)
            grad_rows = dot(grad_both[0], in_weight[at, :], ((1,), (1,))).astype(bf16)
            grad_tokens[0, :, :, at], grad_tokens[1, :, :, at] = spread(grad_rows)

        high = grad_gate.astype(bf16).astype(f32)
        column = lax.broadcasted_iota(jnp.int32, (block, PAD), 1)
        extra = jnp.where(column == number, high, 0.0)
        extra = jnp.where(column == experts + number, grad_gate - high, extra)
        grad_tokens[0, :, :, D:], grad_tokens[1, :, :, D:] = spread(extra.astype(bf16))

    def part(value):
        return pl.BlockSpec(
            (1, 1) + value.shape[2:], lambda b, _: (step, b) + (0,) * (value.ndim - 2)
        )

    def tokens_spec(count, width):
        return pl.BlockSpec((count, share, rows, width), lambda b, _: (b, 0, 0, 0))

    return pl.pallas_call(
        kernel,
        grid_spec=pltpu.PrefetchScalarGridSpec(
            num_scalar_prefetch=1,
            grid=(pairs,),
            in_specs=[part(v) for v in (tail, both, active, grad_produced, up_rows, places)]
            + [HBM] * (2 * planes),
            out_specs=[
                tokens_spec(1, D),
                tokens_spec(1, D),
                tokens_spec(2, D + PAD),
                pl.BlockSpec((1, block, 2 * FF), lambda b, _: (b, 0, 0)),
            ],
            scratch_shapes=[
                pltpu.VMEM((D, 2 * FF), bf16),
                pltpu.VMEM((FF, D), bf16),
                pltpu.SemaphoreType.DMA((2 * planes,)),
            ],
        ),
        out_shape=[
            out((pairs, share, rows, D)),
            out((pairs, share, rows, D)),
            out((2 * pairs, share, rows, D + PAD)),
            out((pairs, block, 2 * FF)),
        ],
        cost_estimate=cost(pairs * block * D * (4 * FF + 2 * count)),
        compiler_params=params(),
    )(
        where, tail, both, active, grad_produced, up_rows, places, *in_pieces, *out_pieces
    )


def weight_gradient(where, planes, left, rights, tail=None, first=0, steps=None, shift=False):
    steps = planes if steps is None else steps
    count, width = left.shape
    parts = len(rights)
    part_rows = count // parts
    columns = rights[0].shape[1]
    width = width // planes
    step = min(TILE, columns & -columns)
    tails = [] if tail is None else [tail]
    whole = columns + sum(value.shape[1] for value in tails)

    def of_plane(i, where):
        return (where[1] + first + i) % planes if shift else lax.bitwise_xor(where[1], first + i)

    def kernel(where, left, *refs):
        rights, tails, targets = refs[:parts], refs[parts:-steps], refs[-steps:]

        def fill(target):
            for value in tails:
                target[:, columns:] = value[...]
            for number in range(columns // step):
                at = slice(number * step, (number + 1) * step)
                target[:, at] = sum(
                    dot(left[part * part_rows : (part + 1) * part_rows], right[:, at], ((0,), (0,)))
                    for part, right in enumerate(rights)
                ).astype(bf16)

        for number, target in enumerate(targets):
            pl.when(pl.program_id(0) == number)(lambda target=target: fill(target))

    return pl.pallas_call(
        kernel,
        grid_spec=pltpu.PrefetchScalarGridSpec(
            num_scalar_prefetch=1,
            grid=(steps,),
            in_specs=[pl.BlockSpec((count, width), lambda i, where: (0, of_plane(i, where)))]
            + [fixed(right.shape) for right in rights]
            + [
                pl.BlockSpec((width, value.shape[1]), lambda i, where: (of_plane(i, where), 0))
                for value in tails
            ],
            out_specs=[fixed((width, whole))] * steps,
        ),
        out_shape=[out((width, whole))] * steps,
        cost_estimate=cost(0 if tails else count * steps * width * columns),
        compiler_params=params(),
    )(where, left, *rights, *tails)


def hidden_backward(
    plane, planes, parts, hidden, gates, upstream, gain, router, gathered, experts
):
    count = hidden.shape[0]
    terms = len(parts)

    def kernel(plane, *refs):
        parts = refs[:terms]
        hidden, gates, upstream, gain, router, gathered = refs[terms : terms + 6]
        (
            grad_hidden, grad_branch, grad_mixed, grad_logits, grad_gain, out_weight, sems
        ) = refs[terms + 6 :]
        wait = copies(out_weight_pairs(plane[0], planes, gathered, out_weight), sems)
        returned = sum(part[...].astype(f32) for part in parts)
        tail = returned[:, D:]
        grad_gates = gates[...] * (tail + pltpu.roll(tail, PAD - experts, 1))
        logits = grad_gates - gates[...] * jnp.sum(grad_gates, axis=1, keepdims=True)
        logits = logits.astype(bf16)
        grad_logits[...] = logits
        grad_normed = returned[:, :D] + dot(logits, router[...], ((1,), (1,)))
        value = hidden[...]
        inverse = inverse_rms(value)
        grad_gain[...] = jnp.sum(grad_normed * value * inverse, axis=0, keepdims=True)
        grad = upstream[...].astype(f32) + rms_backward(value, inverse, gain[...], grad_normed)
        grad_hidden[...] = grad
        grad_branch[...] = grad.astype(bf16)
        wait()

        @tiles(D)
        def _(number):
            at = tile(number)
            grad_mixed[:, at] = dot(grad_branch[...], out_weight[at, :], ((1,), (1,))).astype(bf16)

    shapes = [
        out((count, D), f32), out((count, D)), out((count, D)), out((count, PAD)),
        out((1, D), f32),
    ]
    args = (*parts, hidden, gates, upstream, gain, router, gathered)
    return pl.pallas_call(
        kernel,
        grid_spec=pltpu.PrefetchScalarGridSpec(
            num_scalar_prefetch=1,
            grid=(1,),
            in_specs=[HBM if value is gathered else fixed(value.shape) for value in args],
            out_specs=[fixed(shape.shape) for shape in shapes],
            scratch_shapes=[
                pltpu.VMEM((D, D), bf16),
                pltpu.SemaphoreType.DMA((planes * gathered.shape[0],)),
            ],
        ),
        out_shape=shapes,
        compiler_params=params(),
    )(plane, *args)


def project_backward(step, grad_proj, tokens, slab):
    ranks, rows, _ = grad_proj.shape
    width = slab.shape[1] - PAD

    def kernel(grad_proj, tokens, weight, grad_normed, grad_gain):
        value = tokens[0].astype(f32)
        inverse = inverse_rms(value)
        grad = dot(grad_proj[0], weight[:, :width], ((1,), (1,)))
        grad_normed[...] = grad.astype(bf16)

        @pl.when(pl.program_id(0) == 0)
        def _():
            grad_gain[...] = jnp.zeros_like(grad_gain)

        grad_gain[...] += jnp.sum(grad * value * inverse, axis=0, keepdims=True)

    return pl.pallas_call(
        kernel,
        grid=(ranks,),
        in_specs=[
            leading(grad_proj.shape),
            pl.BlockSpec((1, rows, D), lambda i: (i, step, 0)),
            fixed(slab.shape),
        ],
        out_specs=[pl.BlockSpec((rows, D), lambda i: (i, 0)), fixed((1, D))],
        out_shape=[out((ranks * rows, D)), out((1, D), f32)],
        compiler_params=params(),
    )(grad_proj, tokens, slab)


def cut_heads(weight, tail, ranks):
    rows = weight.shape[0]
    width = D // ranks

    def kernel(weight, tail, target):
        for rank in range(ranks):
            for part in range(3):
                at = part * D + rank * width
                target[rank, :, part * width : (part + 1) * width] = weight[:, at : at + width]
            target[rank, :, 3 * width :] = tail[...]

    return pl.pallas_call(
        kernel,
        out_shape=out((ranks, rows, 3 * width + PAD)),
        compiler_params=params(),
    )(weight, tail)


def unpack(packed, count):
    ranks, rows, columns = packed.shape
    width = (columns - PAD) // 3

    def kernel(packed, main, small):
        for rank in range(ranks):
            for part in range(3):
                at = part * D + rank * width
                main[:, at : at + width] = packed[rank, :, part * width : (part + 1) * width].astype(
                    f32
                )
        tails = sum(packed[rank, :, 3 * width :].astype(f32) for rank in range(ranks))
        small[...] = tails + pltpu.roll(tails, PAD - count, 1)

    return pl.pallas_call(
        kernel,
        out_shape=[out((rows, 3 * D), f32), out((rows, PAD), f32)],
        compiler_params=params(),
    )(packed)


def shift_rep(value, step):
    count = lax.axis_size("rep")
    return lax.ppermute(value, "rep", [(i, (i + step) % count) for i in range(count)])


def cross_rep(value, bits):
    return lax.ppermute(value, "rep", [(i, i ^ bits) for i in range(lax.axis_size("rep"))])


def after(value, *others):
    return lax.optimization_barrier((value,) + others)[0]


def two_parts(value):
    high = lax.reduce_precision(value, 8, 7)
    return high.astype(bf16), (value - high).astype(bf16)


def ring_rep(value, *work):
    count = lax.axis_size("rep")
    rank = lax.axis_index("rep")
    rows = value.shape[0]
    full = jnp.zeros((count * rows,) + value.shape[1:], value.dtype)
    full = lax.dynamic_update_slice_in_dim(full, value, rank * rows, 0)
    for step in range(1, count):
        value, work = lax.optimization_barrier((value, work)) if step == count - 1 else (value, work)
        value = shift_rep(value, 1)
        full = lax.dynamic_update_slice_in_dim(full, value, (rank - step) % count * rows, 0)
    return full, work


def on_device(
    tokens, cotangent, w_qkv, w_o, w_router, norm_gains, qk_gain, w_in, w_out, segments, routes
):
    planes = lax.axis_size("rep")
    ranks = lax.axis_size("ep")
    plane = lax.axis_index("rep")
    rank = lax.axis_index("ep")
    share = w_in.shape[0]
    own = plane % share
    experts = share * ranks
    where = jnp.stack([rank * share + own, plane, rank % 2]).astype(jnp.int32)
    micro = segments.shape[1]
    mine = tokens.shape[0]
    rows = mine // micro
    length = rows * ranks
    capacity = rows * TOP * 17 // (16 * experts)
    slots = -(-share * capacity // 16) * 16
    width = HEADS // ranks * HD
    qk_gains = qk_gain.astype(f32).reshape(2, HD)
    dense_rows = w_qkv.shape[0]

    def exchange(value, step):
        pairs = [(i, i // share * share + (i % share + step) % share) for i in range(planes)]
        return lax.ppermute(value, "rep", pairs)

    def with_group(value):
        return jnp.stack([value] + [exchange(value, step) for step in range(1, share)])

    def gather_ranks(value):
        return lax.all_gather(value, "ep", axis=0)

    assert planes & (planes - 1) == 0 and share & (share - 1) == 0
    near, half, last_step = 1, planes // 2, planes - 1
    in_parts, out_parts = (
        {
            step: lax.dynamic_index_in_dim(weight, own ^ step % share, 0, keepdims=False)
            for step in range(planes)
        }
        for weight in (w_in, w_out)
    )

    def send(parts, steps):
        return {step: cross_rep(parts[step], step) for step in steps}

    stream = gather_ranks(tokens)
    out_rows = [w_o] + [cross_rep(w_o, step) for step in range(1, planes)]
    upstream_group = with_group(cotangent)
    slab = cut_heads(
        w_qkv,
        jnp.concatenate(
            [
                w_router,
                norm_gains.reshape(dense_rows, 2),
                jnp.zeros((dense_rows, PAD - experts - 2), bf16),
            ],
            axis=1,
        ),
        ranks,
    )
    slab = lax.all_to_all(slab, "ep", split_axis=0, concat_axis=0, tiled=True)
    slab = slab.reshape(ranks * dense_rows, 3 * width + PAD)
    out_rows, upstream_group, slab = lax.optimization_barrier((out_rows, upstream_group, slab))
    gathered = gather_ranks(jnp.concatenate(out_rows, axis=0))
    segment = segments[0]
    cosine, sine = jax.vmap(lambda one: rope_tables(doc_positions(one), HD))(segment)
    sine = jnp.where(jnp.arange(HD) < HD // 2, -sine, sine)
    tables = (cosine, sine, segment[:, :, None], segment[:, None, :], qk_gains)
    slab, (tables, in_parts, out_parts) = ring_rep(slab, tables, in_parts, out_parts)
    router = slab[:, 3 * width :]
    gain_pair = router[:, experts : experts + 2].reshape(-1).astype(f32)
    first_gain = gain_pair[None, :D]
    second_gain = gain_pair[None, D:]
    in_parts, out_parts, upstream_group, stream = after(
        (in_parts, out_parts, upstream_group, stream), slab
    )
    in_pieces = {0: in_parts[0], **send(in_parts, range(last_step - 1, 0, -1))}
    upstream_all = gather_ranks(upstream_group)

    normed, proj = project(stream, first_gain, slab)
    proj = proj.reshape(ranks, micro, rows, 3 * width)
    mixed_h, query, keys, values, lses = attention_forward(proj, *tables)
    mixed = lax.all_to_all(mixed_h, "ep", split_axis=0, concat_axis=3, tiled=True)
    mixed = mixed.reshape(mine, D)
    hidden, payload, gates = route(
        where[1:2], planes, mixed, tokens, gathered, second_gain, router, routes, experts
    )
    normed_two = payload[:, :D]
    payload, in_pieces = lax.optimization_barrier((payload, in_pieces))
    payload = with_group(payload)
    payload, in_parts, out_parts = lax.optimization_barrier((payload, in_parts, out_parts))
    in_pieces.update(send(in_parts, [last_step]))
    in_pieces, out_parts = lax.optimization_barrier((in_pieces, out_parts))
    out_pieces = {0: out_parts[0], **send(out_parts, range(1, planes))}
    in_pieces = [in_pieces[step] for step in range(planes)]
    out_pieces = [out_pieces[step] for step in range(planes)]
    payload = gather_ranks(payload)

    shape = (ranks, share, micro, rows, -1)
    rows_in, tail, both, active, grad_produced, up_rows, places = expert_forward(
        where, payload.reshape(shape), upstream_all.reshape(shape), in_pieces, slots, experts
    )
    in_rows = micro * ranks * slots
    out_cut = weight_gradient(
        where, planes, active.reshape(in_rows, FF), [grad_produced.reshape(in_rows, D)]
    )

    def sum_rep(parts, shift=False):
        sums = [
            sum(parts[step].astype(f32) for step in range(first, planes, share))
            for first in range(share)
        ]
        return jnp.stack(
            [
                sum(
                    jnp.where(((own - step) % share if shift else own ^ step) == j, sums[step], 0.0)
                    for step in range(share)
                )
                for j in range(share)
            ]
        )

    tail, out_cut = lax.optimization_barrier((tail, out_cut))
    out_sent = send(out_cut, [near])
    tail, out_cut, out_pieces = lax.optimization_barrier((tail, out_cut, out_pieces))
    out_sent.update(send(out_cut, range(2, planes)))
    back = []
    returned = []

    def scatter_ranks(value):
        return lax.psum_scatter(value, "ep", scatter_dimension=0)

    def exchange_back(value):
        return [value[0]] + [exchange(value[step], share - step) for step in range(1, share)]

    for step in range(micro):
        back.append(
            expert_backward(
                step, where, tail, both, active, grad_produced, up_rows, places, in_pieces,
                out_pieces, share, rows, experts,
            )
        )
        returned.append(scatter_ranks(back[step][2]))
        if step == 0:
            ended = {bits: out_sent[bits] for bits in (near, last_step)}
            tail, ended = after((tail, ended), back[step][2])
            out_sent.update(ended)
        else:
            tail = after(tail, back[step][2])
    rows_in = after(rows_in, tail)
    rows_flat = rows_in.reshape(in_rows, D)
    grads_flat = [back[step][3].reshape(in_rows // micro, 2 * FF) for step in range(micro)]
    (in_near,) = weight_gradient(
        where, planes, rows_flat, grads_flat, first=1, steps=1, shift=True
    )
    rows_flat, in_near = lax.optimization_barrier((rows_flat, in_near))
    *in_rest, in_back, in_own = weight_gradient(
        where, planes, rows_flat, grads_flat, first=2, steps=last_step, shift=True
    )
    in_sent = {0: in_own, 1: shift_rep(in_near, 1)}

    def cuts(value, *places):
        ends = [-(-value.shape[0] * place // 512) * 16 for place in (0, *places, 32)]
        return [value[start:end] for start, end in zip(ends, ends[1:])]

    def swap(value, step):
        return lax.ppermute(value, "ep", [(i, i ^ step) for i in range(ranks)])

    def pair_sum(keep, give):
        return (keep.astype(f32) + swap(give, 1).astype(f32)).astype(bf16)

    bits = list(range((ranks // 2).bit_length() - 1))

    def halve(values, phase):
        results = []
        for number, value in enumerate(values):
            way = bits if number % 2 == 0 else bits[::-1]
            bit = way[phase]
            low = 2 ** sum(other < bit for other in way[phase:])
            value = value.reshape((-1, 2, low) + value.shape[1:])
            side = rank // 2 // 2**bit % 2
            keep, give = (
                lax.dynamic_index_in_dim(value, which, 1, keepdims=False).reshape(
                    (-1,) + value.shape[3:]
                )
                for which in (side, 1 - side)
            )
            results.append((keep, swap(give, 2 * 2**bit)))
        return results

    def total(parts):
        return sum(part.astype(f32) for part in parts)

    grad_inputs, branches, logit_grads, grad_projs = [], [], [], []
    gain_two_sum = gain_one_sum = qk_sum = 0.0
    in_rest, in_back, out_sent, in_sent = lax.optimization_barrier(
        (in_rest, in_back, out_sent, in_sent)
    )
    mixtures = [part[:2] for part in back]
    for step in range(micro):
        at = slice(step * rows, (step + 1) * rows)
        parts = after(returned[step], [one[1] for one in grad_inputs])
        parts, in_sent = lax.optimization_barrier((parts, in_sent))
        if step == micro - 1:
            crossed = halve(after(mixtures, parts), 0)
        parts = exchange_back(parts)
        parts, in_rest, in_back, mixtures = lax.optimization_barrier(
            (parts, in_rest, in_back, mixtures)
        )
        if step == 0:
            mixtures = [pair_sum(*part) for part in mixtures]
            in_sent[last_step] = shift_rep(in_back, last_step)
        if step == micro - 1:
            rest = [cuts(value, 12, 20) for value in in_rest]
            rest_sent = [[shift_rep(part[0], i + 2) for i, part in enumerate(rest)]]
        grad_hidden, grad_branch, grad_mixed, grad_logits, gain_two = hidden_backward(
            where[1:2], planes, parts, hidden[at], gates[at], cotangent[at], second_gain,
            router, gathered, experts,
        )
        branches.append(grad_branch)
        logit_grads.append(grad_logits)
        gain_two_sum = gain_two_sum + gain_two
        if step == micro - 1:
            out_sum = dot(mixed, jnp.concatenate(branches, axis=0), ((0,), (0,))).astype(bf16)
            out_sum = out_sum.reshape(planes, ranks, dense_rows, D).transpose(1, 0, 2, 3)
        grad_mixed = lax.all_to_all(grad_mixed, "ep", split_axis=1, concat_axis=0, tiled=True)
        grad_mixed, mixtures = lax.optimization_barrier((grad_mixed, mixtures))
        if step == micro - 1:
            grad_mixed, crossed, rest_sent, rest, out_sum = lax.optimization_barrier(
                (grad_mixed, crossed, rest_sent, rest, out_sum)
            )
            out_sum = lax.psum_scatter(out_sum, "ep", scatter_dimension=0)
            rest_sent.append([shift_rep(part[1], i + 2) for i, part in enumerate(rest)])
        grad_proj, grad_qk = attention_backward(
            step, proj, *tables, query, keys, values, lses, grad_mixed
        )
        qk_sum = qk_sum + grad_qk.reshape(-1)
        if step < micro - 1:
            grad_proj, in_sent = lax.optimization_barrier((grad_proj, in_sent))
        else:
            grad_proj, grad_inputs, rest_sent, rest = lax.optimization_barrier(
                (grad_proj, grad_inputs, rest_sent, rest)
            )
        grad_projs.append(grad_proj)
        grad_normed, gain_one = project_backward(step, grad_proj, stream, slab)
        gain_one_sum = gain_one_sum + gain_one
        grad_inputs.append(
            (
                grad_hidden,
                grad_normed,
                lax.psum_scatter(grad_normed, "ep", scatter_dimension=0, tiled=True),
            )
        )

    router_sum = dot(normed_two, jnp.concatenate(logit_grads, axis=0), ((0,), (0,)))
    qk_columns = qk_sum.shape[0] // dense_rows
    small = jnp.concatenate(
        [
            router_sum[:, :experts],
            jnp.concatenate([gain_one_sum, gain_two_sum], axis=1).reshape(D, 2),
            jnp.tile(qk_sum.reshape(dense_rows, qk_columns), (planes * ranks, 1)),
        ],
        axis=1,
    )
    count = small.shape[1]

    def halves(value):
        high, low = two_parts(value)
        blank = jnp.zeros((value.shape[0], PAD - 2 * count), bf16)
        return jnp.concatenate([high, low, blank], axis=1)

    def joined(value):
        return value[..., :count].astype(f32) + value[..., count : 2 * count].astype(f32)

    grad_projs, rest, out_cut, out_sent, _ = lax.optimization_barrier(
        (grad_projs, rest, out_cut, out_sent, grad_normed)
    )
    rest_sent.append([shift_rep(part[2], i + 2) for i, part in enumerate(rest)])
    packed = weight_gradient(
        where,
        planes,
        normed.reshape(ranks * mine, D),
        [jnp.stack(grad_projs, axis=1).reshape(ranks * mine, 3 * width)],
        halves(small),
    )
    for phase in range(1, len(bits)):
        mixtures = [total(parts).astype(bf16) for parts in crossed]
        crossed = halve(mixtures, phase)
    packed, rest_sent, out_cut, out_sent, crossed = lax.optimization_barrier(
        (packed, rest_sent, out_cut, out_sent, crossed)
    )
    packed_sent = [packed[0]] + [cross_rep(packed[step], step) for step in range(1, planes)]
    normed_sums = [one[2] for one in grad_inputs]
    normed_sums = [one[2] for one in grad_inputs]
    grad_tokens = []
    for step in range(micro):
        own_stream = tokens[step * rows : (step + 1) * rows].astype(f32)
        grad_tokens.append(
            grad_inputs[step][0]
            + rms_backward(
                own_stream, inverse_rms(own_stream), first_gain, normed_sums[step].astype(f32)
            )
        )
    grad_tokens = jnp.concatenate(grad_tokens, axis=0)
    packed_sent, grad_tokens = lax.optimization_barrier((packed_sent, grad_tokens))
    mixture = []
    for number in range(micro):
        parts = total(crossed[number])[0]
        mixture.append((parts[0], exchange_back(parts.astype(bf16))[1:]))
    own_sum = lax.dynamic_index_in_dim(out_sum, plane, 0, keepdims=False)
    out_sent_back = [
        cross_rep(lax.dynamic_index_in_dim(out_sum, plane ^ step, 0, keepdims=False), step)
        for step in range(1, planes)
    ]
    main = total([part[:, : 3 * width] for part in packed_sent]).astype(bf16)
    small = sum(joined(part[:, 3 * width :]) for part in packed_sent)
    packed = jnp.concatenate([main, halves(small)], axis=1).reshape(ranks, dense_rows, -1)
    packed = lax.all_to_all(packed, "ep", split_axis=0, concat_axis=0, tiled=True)
    packed, mixture, out_sent_back = lax.optimization_barrier((packed, mixture, out_sent_back))
    output = jnp.concatenate([mine_part + total(others) for mine_part, others in mixture], axis=0)
    output = (hidden + output).astype(bf16)
    grad_w_o = total([own_sum, *out_sent_back])
    grad_w_qkv, small = unpack(packed, count)
    grad_w_out = sum_rep({0: out_cut[0], **out_sent})
    for i in range(planes - 3):
        in_sent[i + 2] = jnp.concatenate([parts[i] for parts in rest_sent], axis=0)
    grad_w_in = sum_rep(in_sent, shift=True)
    return (
        output,
        grad_tokens,
        grad_w_qkv,
        grad_w_o,
        small[:, :experts],
        small[:, experts : experts + 2].reshape(-1),
        small[:, experts + 2 : count].reshape(-1),
        grad_w_in,
        grad_w_out,
    )


def solution(mesh):
    placed = (
        P(("rep", "ep"), None),
        P(("rep", "ep"), None),
        P(("rep", "ep"), None),
        P(("rep", "ep"), None),
        P(("rep", "ep"), None),
        P(("rep", "ep")),
        P(),
        P("ep", "rep", None),
        P("ep", "rep", None),
        P("rep", None, None),
        P(("rep", "ep"), None),
    )
    return jax.shard_map(
        on_device,
        mesh=mesh,
        in_specs=placed,
        out_specs=(
            P(("rep", "ep"), None),
            P(("rep", "ep"), None),
            P(("rep", "ep"), None),
            P(("rep", "ep"), None),
            P(("rep", "ep"), None),
            P(("rep", "ep")),
            P(),
            P("ep", "rep", None),
            P("ep", "rep", None),
        ),
        check_vma=False,
    )
```

```python
import math

import jax
import jax.numpy as jnp
from jax import lax
from jax.experimental import pallas as pl
from jax.experimental.pallas import tpu as pltpu
from jax.sharding import PartitionSpec as P

D = 2048
HEADS = 16
HD = 128
FF = 1024
TOP = 8
HALF = 512
PAD = 128

epsilon = 1e-06
rope_base = 50000.0
bf16 = jnp.bfloat16
f32 = jnp.float32


def dot(a, b, dims=((1,), (0,))):
    return lax.dot_general(a, b, (dims, ((), ())), preferred_element_type=f32)


def inverse_rms(value):
    return lax.rsqrt(jnp.mean(value * value, axis=-1, keepdims=True) + epsilon)


def rms_backward(value, inverse, gain, grad):
    scaled = grad * gain
    inner = jnp.mean(scaled * value, axis=-1, keepdims=True)
    return inverse * (scaled - value * (inverse * inverse * inner))


def doc_positions(segment):
    index = jnp.arange(segment.shape[0], dtype=jnp.int32)
    change = jnp.concatenate([jnp.ones((1,), dtype=jnp.bool_), segment[1:] != segment[:-1]])
    start = lax.cummax(jnp.where(change, index, 0), axis=0)
    return index - start


def rope_tables(position, width):
    steps = jnp.arange(width // 2, dtype=f32) * (2.0 / width)
    rates = jnp.exp(-steps * math.log(rope_base))
    angle = position.astype(f32)[:, None] * rates[None, :]
    angle = jnp.concatenate([angle, angle], axis=-1)
    return (jnp.cos(angle), jnp.sin(angle))


def norm_rope(value, gain, cosine, sine):
    inverse = lax.rsqrt(jnp.mean(value * value, axis=1, keepdims=True) + epsilon)
    value = value * inverse * gain
    return value * cosine + pltpu.roll(value, HD // 2, 1) * sine


def norm_rope_back(value, gain, cosine, sine, grad):
    inverse = lax.rsqrt(jnp.mean(value * value, axis=1, keepdims=True) + epsilon)
    grad = grad * cosine + pltpu.roll(grad * sine, HD // 2, 1)
    normal = value * inverse
    scaled = grad * gain
    inner = jnp.mean(scaled * normal, axis=1, keepdims=True)
    return inverse * (scaled - normal * inner), jnp.sum(grad * normal, axis=0, keepdims=True)


def kept_scores(query, keys, q_seg, k_seg, start):
    scores = dot(query, keys, ((1,), (1,))) * (1.0 / math.sqrt(HD))
    q_index = start + lax.broadcasted_iota(jnp.int32, scores.shape, 0)
    k_index = lax.broadcasted_iota(jnp.int32, scores.shape, 1)
    keep = (jnp.abs(q_index - k_index) <= HALF) & (q_seg == k_seg)
    return jnp.where(keep, scores, -1e30)


BIG = 100 * 1024 * 1024 // 2


def forward_kernel(
    heads, proj, cosine, sine, seg_column, seg_row, gains, mixed, query, keys, values, lses
):
    ranks, _, rows, _ = proj.shape
    length = ranks * rows
    q_block = 2 * rows
    k_seg = seg_row[0]
    for head in range(heads):
        at = slice(head * HD, (head + 1) * HD)

        def raw(part):
            first = (part * heads + head) * HD
            return proj[:, 0, :, first : first + HD].reshape(length, HD)

        query[0, :, at] = norm_rope(raw(0), gains[0:1], cosine[0], sine[0]).astype(bf16)
        keys[0, :, at] = norm_rope(raw(1), gains[1:2], cosine[0], sine[0]).astype(bf16)
        values[0, :, at] = raw(2).astype(bf16)

        @pl.loop(0, length // q_block)
        def one_block(number, head=head, at=at):
            start = pl.multiple_of(number * q_block, q_block)
            here = pl.ds(start, q_block)
            scores = kept_scores(
                query[0, here, at], keys[0, :, at], seg_column[0, here], k_seg, start
            )
            top = jnp.max(scores, axis=1, keepdims=True)
            weights = jnp.exp(scores - top)
            total = jnp.sum(weights, axis=1, keepdims=True)
            lses[0, head, here] = top + jnp.log(total)
            weights = (weights * (1.0 / total)).astype(bf16)
            result = dot(weights, values[0, :, at]).astype(bf16)
            mixed[pl.ds(number * 2, 2), 0, :, at] = result.reshape(2, rows, HD)


def backward_kernel(
    heads, proj, cosine, sine, seg_column, seg_row, gains, query, keys, values, lses, grad_mixed,
    grad_proj, grad_gains, grad_q, grad_k, grad_v,
):
    ranks, _, rows, _ = proj.shape
    length = ranks * rows
    q_block = 2 * rows
    k_seg = seg_row[0]
    scale = 1.0 / math.sqrt(HD)
    sum_q = jnp.zeros((1, HD), f32)
    sum_k = jnp.zeros((1, HD), f32)
    for head in range(heads):
        at = slice(head * HD, (head + 1) * HD)
        grad_k[...] = jnp.zeros_like(grad_k)
        grad_v[...] = jnp.zeros_like(grad_v)

        @pl.loop(0, length // q_block)
        def one_block(number, head=head, at=at):
            start = pl.multiple_of(number * q_block, q_block)
            here = pl.ds(start, q_block)
            q_rows = query[0, here, at]
            g_rows = grad_mixed[here, at]
            k_all = keys[0, :, at]
            scores = kept_scores(q_rows, k_all, seg_column[0, here], k_seg, start)
            weights = jnp.exp(scores - lses[0, head, here])
            grad_weights = dot(g_rows, values[0, :, at], ((1,), (1,)))
            delta = jnp.sum(weights * grad_weights, axis=1, keepdims=True)
            grad_scores = (weights * (grad_weights - delta)).astype(bf16)
            grad_q[here] = dot(grad_scores, k_all) * scale
            grad_k[...] += dot(grad_scores, q_rows, ((0,), (0,)))
            grad_v[...] += dot(weights.astype(bf16), g_rows, ((0,), (0,)))

        def rounded(value):
            return value.astype(bf16).astype(f32)

        def raw(part):
            first = (part * heads + head) * HD
            return proj[:, 0, :, first : first + HD].reshape(length, HD)

        def put(part, value):
            first = (part * heads + head) * HD
            grad_proj[:, :, first : first + HD] = value.astype(bf16).reshape(ranks, rows, HD)

        back_q, gain_q = norm_rope_back(
            raw(0), gains[0:1], cosine[0], sine[0], rounded(grad_q[...])
        )
        back_k, gain_k = norm_rope_back(
            raw(1), gains[1:2], cosine[0], sine[0], rounded(grad_k[...] * scale)
        )
        sum_q, sum_k = sum_q + gain_q, sum_k + gain_k
        put(0, back_q)
        put(1, back_k)
        put(2, grad_v[...])
    grad_gains[0:1] = sum_q
    grad_gains[1:2] = sum_k


def fixed(shape):
    return pl.BlockSpec(shape, lambda *_: (0,) * len(shape), pipeline_mode=pl.Buffered(1))


def leading(shape):
    return pl.BlockSpec((1,) + shape[1:], lambda i: (i,) + (0,) * (len(shape) - 1))


def params():
    return pltpu.CompilerParams(vmem_limit_bytes=BIG)


def cost(products):
    return pl.CostEstimate(flops=20 * products, bytes_accessed=0, transcendentals=0)


def out(shape, dtype=bf16):
    return jax.ShapeDtypeStruct(shape, dtype)


def attention_forward(proj, cosine, sine, seg_column, seg_row, gains):
    ranks, micro, rows, width = proj.shape
    length = ranks * rows
    width = width // 3
    heads = width // HD
    part = out((micro, length, width))
    by_rank = lambda n: pl.BlockSpec((ranks, 1, rows, n), lambda i: (0, i, 0, 0))
    lses = out((micro, heads, length, 1), f32)
    return pl.pallas_call(
        lambda *refs: forward_kernel(heads, *refs),
        grid=(micro,),
        in_specs=[by_rank(3 * width)]
        + [leading(v.shape) for v in (cosine, sine, seg_column, seg_row)]
        + [fixed(gains.shape)],
        out_specs=[by_rank(width)] + [leading(part.shape)] * 3 + [leading(lses.shape)],
        out_shape=[out((ranks, micro, rows, width)), part, part, part, lses],
        compiler_params=params(),
    )(proj, cosine, sine, seg_column, seg_row, gains)


def attention_backward(
    step, proj, cosine, sine, seg_column, seg_row, gains, query, keys, values, lses, grad_mixed
):
    ranks, micro, rows, width = proj.shape
    length = ranks * rows
    heads = width // 3 // HD

    def part(value):
        return pl.BlockSpec((1,) + value.shape[1:], lambda i: (step,) + (0,) * (value.ndim - 1))

    return pl.pallas_call(
        lambda *refs: backward_kernel(heads, *refs),
        grid=(1,),
        in_specs=[pl.BlockSpec((ranks, 1, rows, width), lambda i: (0, step, 0, 0))]
        + [part(v) for v in (cosine, sine, seg_column, seg_row)]
        + [fixed(gains.shape)]
        + [part(v) for v in (query, keys, values, lses)]
        + [fixed(grad_mixed.shape)],
        out_specs=[fixed((ranks, rows, width)), fixed((2, HD))],
        out_shape=[out((ranks, rows, width)), out((2, HD), f32)],
        scratch_shapes=[pltpu.VMEM((length, HD), f32)] * 3,
        compiler_params=params(),
    )(
        proj, cosine, sine, seg_column, seg_row, gains, query, keys, values, lses, grad_mixed
    )


def project(micro, tokens, gain, slab):
    ranks, count, _ = tokens.shape
    rows = count // micro
    width = slab.shape[1] - PAD

    def kernel(value, gain, weight, normed, proj):
        value = value[0].astype(f32)
        result = (value * inverse_rms(value) * gain[...]).astype(bf16)
        normed[...] = result.reshape(micro, 1, rows, D)
        proj[0] = dot(result, weight[:, :width])

    return pl.pallas_call(
        kernel,
        grid=(ranks,),
        in_specs=[leading((ranks, count, D)), fixed((1, D)), fixed(slab.shape)],
        out_specs=[
            pl.BlockSpec((micro, 1, rows, D), lambda i: (0, i, 0, 0)),
            leading((ranks, count, width)),
        ],
        out_shape=[out((micro, ranks, rows, D)), out((ranks, count, width), f32)],
        compiler_params=params(),
    )(tokens, gain, slab)


TILE = 512


def tiles(count):
    return pl.loop(0, count // TILE)


def tile(number):
    return pl.ds(pl.multiple_of(number * TILE, TILE), TILE)


HBM = pl.BlockSpec(memory_space=pl.ANY)


def copies(pairs, sems):
    started = [
        pltpu.make_async_copy(source, target, sems.at[place])
        for place, (source, target) in enumerate(pairs)
    ]
    for copy in started:
        copy.start()

    def wait():
        for copy in started:
            copy.wait()

    return wait


def plane_pairs(plane, pieces, target):
    planes = len(pieces)
    rows = target.shape[0] // planes
    return [
        (piece, target.at[pl.ds(lax.bitwise_xor(plane, jnp.int32(step)) * rows, rows)])
        for step, piece in enumerate(pieces)
    ]


def out_weight_pairs(plane, planes, gathered, target):
    ranks = gathered.shape[0]
    rows = D // (planes * ranks)
    return [
        (
            gathered.at[rank, pl.ds(step * rows, rows)],
            target.at[
                pl.ds((lax.bitwise_xor(plane, jnp.int32(step)) * ranks + rank) * rows, rows)
            ],
        )
        for rank in range(ranks)
        for step in range(planes)
    ]


def route(plane, planes, mixed, tokens, gathered, gain, router, routes, experts):
    count = tokens.shape[0]
    pieces = planes * gathered.shape[0]

    def kernel(
        plane, mixed, tokens, gathered, gain, router, routes, hidden, payload, gates,
        out_weight, sems,
    ):
        copies(out_weight_pairs(plane[0], planes, gathered, out_weight), sems)()

        @tiles(D)
        def _(number):
            at = tile(number)
            hidden[:, at] = tokens[:, at].astype(f32) + dot(mixed[...], out_weight[:, at])

        value = hidden[...]
        normed = (value * inverse_rms(value) * gain[...]).astype(bf16)
        payload[:, :D] = normed
        logits = dot(normed, router[...])
        column = lax.broadcasted_iota(jnp.int32, logits.shape, 1)
        routed = column == routes[:, 0:1]
        for choice in range(1, TOP):
            routed = routed | (column == routes[:, choice : choice + 1])
        logits = jnp.where(routed, logits, -1e30)
        weights = jnp.exp(logits - jnp.max(logits, axis=1, keepdims=True))
        weights = jnp.where(routed, weights, 0.0)
        weights = weights / jnp.sum(weights, axis=1, keepdims=True)
        gates[...] = weights
        high = weights.astype(bf16).astype(f32)
        payload[:, D:] = (high + pltpu.roll(weights - high, experts, 1)).astype(bf16)

    shapes = [out((count, D), f32), out((count, D + PAD)), out((count, PAD), f32)]
    return pl.pallas_call(
        kernel,
        grid_spec=pltpu.PrefetchScalarGridSpec(
            num_scalar_prefetch=1,
            grid=(1,),
            in_specs=[
                HBM if value is gathered else fixed(value.shape)
                for value in (mixed, tokens, gathered, gain, router, routes)
            ],
            out_specs=[fixed(shape.shape) for shape in shapes],
            scratch_shapes=[pltpu.VMEM((D, D), bf16), pltpu.SemaphoreType.DMA((pieces,))],
        ),
        out_shape=shapes,
        compiler_params=params(),
    )(plane, mixed, tokens, gathered, gain, router, routes)


def lane(value, number):
    column = lax.broadcasted_iota(jnp.int32, value.shape, 1)
    return jnp.sum(jnp.where(column == number, value.astype(f32), 0.0), axis=1, keepdims=True)


def one_hot(slot, slots):
    place = lax.broadcasted_iota(jnp.int32, (slots, slot.shape[1]), 0).astype(f32)
    return (place == slot).astype(bf16)


def expert_forward(where, payload, upstream, in_pieces, slots, experts):
    ranks, share, micro, rows, _ = payload.shape
    count = share * rows
    block = 2 * slots

    planes = len(in_pieces)

    def kernel(where, payload, upstream, *refs):
        (
            rows_in, tail, both, active, grad_produced, up_rows, places, in_weight, sems
        ) = refs[planes:]
        number = where[0]

        @pl.when((pl.program_id(0) == 0) & (pl.program_id(1) == 0))
        def _():
            copies(plane_pairs(where[1], refs[:planes], in_weight), sems)()

        for part in range(2):
            here = slice(part * slots, (part + 1) * slots)
            value = payload[part].reshape(count, D + PAD)
            marks = value[:, D:]
            first = lax.broadcasted_iota(jnp.int32, (8, PAD), 1) == number
            taken = dot(first.astype(bf16), marks, ((1,), (1,))) > 0.0
            before = lax.broadcasted_iota(jnp.int32, (count, count), 0)
            behind = lax.broadcasted_iota(jnp.int32, (count, count), 1)
            slot = dot(taken.astype(bf16), (before < behind).astype(bf16))
            select = one_hot(jnp.where(taken, slot, -1.0)[0:1], slots)
            wide = jnp.broadcast_to(lane(marks, number) > 0.0, (count, PAD))
            slot = dot((before > behind).astype(bf16), wide.astype(bf16))
            places[0, 0, part] = jnp.where(wide, slot, -1.0)
            rows_in[0, 0, here] = dot(select, value[:, :D]).astype(bf16)
            marks = dot(select, marks)
            tail[0, 0, here] = marks
            gate = lane(marks, number) + lane(marks, experts + number)
            picked = dot(select, upstream[part].reshape(count, D))
            up_rows[0, 0, here] = picked.astype(bf16)
            grad_produced[0, 0, here] = (gate * picked).astype(bf16)

        for number in range(FF // TILE):
            at = slice(number * TILE, (number + 1) * TILE)
            more = slice(FF + number * TILE, FF + (number + 1) * TILE)
            gate_part = dot(rows_in[0, 0], in_weight[:, at])
            up_part = dot(rows_in[0, 0], in_weight[:, more])
            both[0, 0, :, at] = gate_part
            both[0, 0, :, more] = up_part
            active[0, 0, :, at] = (
                gate_part / (1.0 + jnp.exp(-gate_part)) * up_part
            ).astype(bf16)

    def tokens_spec(width):
        return pl.BlockSpec((2, share, 1, rows, width), lambda m, b, _: (b, 0, m, 0, 0))

    pairs = ranks // 2
    shapes = [
        out((micro, pairs, block, D)),
        out((micro, pairs, block, PAD), f32),
        out((micro, pairs, block, 2 * FF), f32),
        out((micro, pairs, block, FF)),
        out((micro, pairs, block, D)),
        out((micro, pairs, block, D)),
        out((micro, pairs, 2, count, PAD), f32),
    ]
    return pl.pallas_call(
        kernel,
        grid_spec=pltpu.PrefetchScalarGridSpec(
            num_scalar_prefetch=1,
            grid=(micro, pairs),
            in_specs=[tokens_spec(D + PAD), tokens_spec(D)] + [HBM] * planes,
            out_specs=[
                pl.BlockSpec(
                    (1, 1) + s.shape[2:], lambda m, b, _, n=len(s.shape): (m, b) + (0,) * (n - 2)
                )
                for s in shapes
            ],
            scratch_shapes=[pltpu.VMEM((D, 2 * FF), bf16), pltpu.SemaphoreType.DMA((planes,))],
        ),
        out_shape=shapes,
        cost_estimate=cost(micro * pairs * block * D * (2 * FF + 2 * count)),
        compiler_params=params(),
    )(where, payload, upstream, *in_pieces)


def expert_backward(
    step, where, tail, both, active, grad_produced, up_rows, places, in_pieces, out_pieces,
    share, rows, experts,
):
    pairs, block = tail.shape[1:3]
    slots = block // 2
    count = places.shape[3]

    planes = len(in_pieces)

    def kernel(where, tail, both, active, grad_produced, up_rows, places, *refs):
        keep, give, grad_tokens, grad_both, in_weight, out_weight, sems = refs[2 * planes :]
        number = where[0]
        odd = where[2] == 1

        @pl.when(pl.program_id(0) == 0)
        def _():
            copies(
                plane_pairs(where[1], refs[:planes], in_weight)
                + plane_pairs(where[1], refs[planes : 2 * planes], out_weight),
                sems,
            )()

        gate = lane(tail[0, 0], number) + lane(tail[0, 0], experts + number)
        place = lax.broadcasted_iota(jnp.int32, (count, slots), 1).astype(f32)
        selects = [(places[0, 0, part][:, 0:1] == place).astype(bf16) for part in range(2)]

        def spread(value):
            return [
                dot(selects[part], value[part * slots : (part + 1) * slots])
                .astype(bf16)
                .reshape(share, rows, -1)
                for part in range(2)
            ]

        grad_gate = jnp.zeros((block, 1), f32)
        for tile in range(D // TILE):
            at = slice(tile * TILE, (tile + 1) * TILE)
            produced = dot(active[0, 0], out_weight[:, at]).astype(bf16).astype(f32)
            even_rank, odd_rank = spread((gate * produced).astype(bf16))
            keep[0, :, :, at] = jnp.where(odd, odd_rank, even_rank)
            give[0, :, :, at] = jnp.where(odd, even_rank, odd_rank)
            grad_gate = grad_gate + jnp.sum(
                up_rows[0, 0, :, at].astype(f32) * produced, axis=1, keepdims=True
            )

        for tile in range(FF // TILE):
            at = slice(tile * TILE, (tile + 1) * TILE)
            more = slice(FF + tile * TILE, FF + (tile + 1) * TILE)
            grad_active = dot(grad_produced[0, 0], out_weight[at, :], ((1,), (1,)))
            grad_active = grad_active.astype(bf16).astype(f32)
            gate_part = both[0, 0, :, at]
            up_part = both[0, 0, :, more]
            sigma = 1.0 / (1.0 + jnp.exp(-gate_part))
            grad_both[0, :, at] = (
                grad_active * up_part * (sigma * (1.0 + gate_part * (1.0 - sigma)))
            ).astype(bf16)
            grad_both[0, :, more] = (grad_active * (gate_part * sigma)).astype(bf16)

        for tile in range(D // TILE):
            at = slice(tile * TILE, (tile + 1) * TILE)
            grad_rows = dot(grad_both[0], in_weight[at, :], ((1,), (1,))).astype(bf16)
            grad_tokens[0, :, :, at], grad_tokens[1, :, :, at] = spread(grad_rows)

        high = grad_gate.astype(bf16).astype(f32)
        column = lax.broadcasted_iota(jnp.int32, (block, PAD), 1)
        extra = jnp.where(column == number, high, 0.0)
        extra = jnp.where(column == experts + number, grad_gate - high, extra)
        grad_tokens[0, :, :, D:], grad_tokens[1, :, :, D:] = spread(extra.astype(bf16))

    def part(value):
        return pl.BlockSpec(
            (1, 1) + value.shape[2:], lambda b, _: (step, b) + (0,) * (value.ndim - 2)
        )

    def tokens_spec(count, width):
        return pl.BlockSpec((count, share, rows, width), lambda b, _: (b, 0, 0, 0))

    return pl.pallas_call(
        kernel,
        grid_spec=pltpu.PrefetchScalarGridSpec(
            num_scalar_prefetch=1,
            grid=(pairs,),
            in_specs=[part(v) for v in (tail, both, active, grad_produced, up_rows, places)]
            + [HBM] * (2 * planes),
            out_specs=[
                tokens_spec(1, D),
                tokens_spec(1, D),
                tokens_spec(2, D + PAD),
                pl.BlockSpec((1, block, 2 * FF), lambda b, _: (b, 0, 0)),
            ],
            scratch_shapes=[
                pltpu.VMEM((D, 2 * FF), bf16),
                pltpu.VMEM((FF, D), bf16),
                pltpu.SemaphoreType.DMA((2 * planes,)),
            ],
        ),
        out_shape=[
            out((pairs, share, rows, D)),
            out((pairs, share, rows, D)),
            out((2 * pairs, share, rows, D + PAD)),
            out((pairs, block, 2 * FF)),
        ],
        cost_estimate=cost(pairs * block * D * (4 * FF + 2 * count)),
        compiler_params=params(),
    )(
        where, tail, both, active, grad_produced, up_rows, places, *in_pieces, *out_pieces
    )


def weight_gradient(where, planes, left, rights, tail=None, first=0, steps=None, shift=False):
    steps = planes if steps is None else steps
    count, width = left.shape
    parts = len(rights)
    part_rows = count // parts
    columns = rights[0].shape[1]
    width = width // planes
    step = min(TILE, columns & -columns)
    tails = [] if tail is None else [tail]
    whole = columns + sum(value.shape[1] for value in tails)

    def of_plane(i, where):
        return (where[1] + first + i) % planes if shift else lax.bitwise_xor(where[1], first + i)

    def kernel(where, left, *refs):
        rights, tails, targets = refs[:parts], refs[parts:-steps], refs[-steps:]

        def fill(target):
            for value in tails:
                target[:, columns:] = value[...]
            for number in range(columns // step):
                at = slice(number * step, (number + 1) * step)
                target[:, at] = sum(
                    dot(left[part * part_rows : (part + 1) * part_rows], right[:, at], ((0,), (0,)))
                    for part, right in enumerate(rights)
                ).astype(bf16)

        for number, target in enumerate(targets):
            pl.when(pl.program_id(0) == number)(lambda target=target: fill(target))

    return pl.pallas_call(
        kernel,
        grid_spec=pltpu.PrefetchScalarGridSpec(
            num_scalar_prefetch=1,
            grid=(steps,),
            in_specs=[pl.BlockSpec((count, width), lambda i, where: (0, of_plane(i, where)))]
            + [fixed(right.shape) for right in rights]
            + [
                pl.BlockSpec((width, value.shape[1]), lambda i, where: (of_plane(i, where), 0))
                for value in tails
            ],
            out_specs=[fixed((width, whole))] * steps,
        ),
        out_shape=[out((width, whole))] * steps,
        cost_estimate=cost(0 if tails else count * steps * width * columns),
        compiler_params=params(),
    )(where, left, *rights, *tails)


def hidden_backward(
    plane, planes, parts, hidden, gates, upstream, gain, router, gathered, experts
):
    count = hidden.shape[0]
    terms = len(parts)

    def kernel(plane, *refs):
        parts = refs[:terms]
        hidden, gates, upstream, gain, router, gathered = refs[terms : terms + 6]
        (
            grad_hidden, grad_branch, grad_mixed, grad_logits, grad_gain, out_weight, sems
        ) = refs[terms + 6 :]
        wait = copies(out_weight_pairs(plane[0], planes, gathered, out_weight), sems)
        returned = sum(part[...].astype(f32) for part in parts)
        tail = returned[:, D:]
        grad_gates = gates[...] * (tail + pltpu.roll(tail, PAD - experts, 1))
        logits = grad_gates - gates[...] * jnp.sum(grad_gates, axis=1, keepdims=True)
        logits = logits.astype(bf16)
        grad_logits[...] = logits
        grad_normed = returned[:, :D] + dot(logits, router[...], ((1,), (1,)))
        value = hidden[...]
        inverse = inverse_rms(value)
        grad_gain[...] = jnp.sum(grad_normed * value * inverse, axis=0, keepdims=True)
        grad = upstream[...].astype(f32) + rms_backward(value, inverse, gain[...], grad_normed)
        grad_hidden[...] = grad
        grad_branch[...] = grad.astype(bf16)
        wait()

        @tiles(D)
        def _(number):
            at = tile(number)
            grad_mixed[:, at] = dot(grad_branch[...], out_weight[at, :], ((1,), (1,))).astype(bf16)

    shapes = [
        out((count, D), f32), out((count, D)), out((count, D)), out((count, PAD)),
        out((1, D), f32),
    ]
    args = (*parts, hidden, gates, upstream, gain, router, gathered)
    return pl.pallas_call(
        kernel,
        grid_spec=pltpu.PrefetchScalarGridSpec(
            num_scalar_prefetch=1,
            grid=(1,),
            in_specs=[HBM if value is gathered else fixed(value.shape) for value in args],
            out_specs=[fixed(shape.shape) for shape in shapes],
            scratch_shapes=[
                pltpu.VMEM((D, D), bf16),
                pltpu.SemaphoreType.DMA((planes * gathered.shape[0],)),
            ],
        ),
        out_shape=shapes,
        compiler_params=params(),
    )(plane, *args)


def project_backward(step, grad_proj, tokens, slab):
    ranks, rows, _ = grad_proj.shape
    width = slab.shape[1] - PAD

    def kernel(grad_proj, tokens, weight, grad_normed, grad_gain):
        value = tokens[0].astype(f32)
        inverse = inverse_rms(value)
        grad = dot(grad_proj[0], weight[:, :width], ((1,), (1,)))
        grad_normed[...] = grad.astype(bf16)

        @pl.when(pl.program_id(0) == 0)
        def _():
            grad_gain[...] = jnp.zeros_like(grad_gain)

        grad_gain[...] += jnp.sum(grad * value * inverse, axis=0, keepdims=True)

    return pl.pallas_call(
        kernel,
        grid=(ranks,),
        in_specs=[
            leading(grad_proj.shape),
            pl.BlockSpec((1, rows, D), lambda i: (i, step, 0)),
            fixed(slab.shape),
        ],
        out_specs=[pl.BlockSpec((rows, D), lambda i: (i, 0)), fixed((1, D))],
        out_shape=[out((ranks * rows, D)), out((1, D), f32)],
        compiler_params=params(),
    )(grad_proj, tokens, slab)


def cut_heads(weight, tail, ranks):
    rows = weight.shape[0]
    width = D // ranks

    def kernel(weight, tail, target):
        for rank in range(ranks):
            for part in range(3):
                at = part * D + rank * width
                target[rank, :, part * width : (part + 1) * width] = weight[:, at : at + width]
            target[rank, :, 3 * width :] = tail[...]

    return pl.pallas_call(
        kernel,
        out_shape=out((ranks, rows, 3 * width + PAD)),
        compiler_params=params(),
    )(weight, tail)


def unpack(packed, count):
    ranks, rows, columns = packed.shape
    width = (columns - PAD) // 3

    def kernel(packed, main, small):
        for rank in range(ranks):
            for part in range(3):
                at = part * D + rank * width
                main[:, at : at + width] = packed[rank, :, part * width : (part + 1) * width].astype(
                    f32
                )
        tails = sum(packed[rank, :, 3 * width :].astype(f32) for rank in range(ranks))
        small[...] = tails + pltpu.roll(tails, PAD - count, 1)

    return pl.pallas_call(
        kernel,
        out_shape=[out((rows, 3 * D), f32), out((rows, PAD), f32)],
        compiler_params=params(),
    )(packed)


def shift_rep(value, step):
    count = lax.axis_size("rep")
    return lax.ppermute(value, "rep", [(i, (i + step) % count) for i in range(count)])


def cross_rep(value, bits):
    return lax.ppermute(value, "rep", [(i, i ^ bits) for i in range(lax.axis_size("rep"))])


def after(value, *others):
    return lax.optimization_barrier((value,) + others)[0]


def two_parts(value):
    high = lax.reduce_precision(value, 8, 7)
    return high.astype(bf16), (value - high).astype(bf16)


def ring_rep(value, *work):
    count = lax.axis_size("rep")
    rank = lax.axis_index("rep")
    rows = value.shape[0]
    full = jnp.zeros((count * rows,) + value.shape[1:], value.dtype)
    full = lax.dynamic_update_slice_in_dim(full, value, rank * rows, 0)
    for step in range(1, count):
        value, work = lax.optimization_barrier((value, work)) if step == count - 1 else (value, work)
        value = shift_rep(value, 1)
        full = lax.dynamic_update_slice_in_dim(full, value, (rank - step) % count * rows, 0)
    return full, work


def on_device(
    tokens, cotangent, w_qkv, w_o, w_router, norm_gains, qk_gain, w_in, w_out, segments, routes
):
    planes = lax.axis_size("rep")
    ranks = lax.axis_size("ep")
    plane = lax.axis_index("rep")
    rank = lax.axis_index("ep")
    share = w_in.shape[0]
    own = plane % share
    experts = share * ranks
    where = jnp.stack([rank * share + own, plane, rank % 2]).astype(jnp.int32)
    micro = segments.shape[1]
    mine = tokens.shape[0]
    rows = mine // micro
    length = rows * ranks
    capacity = rows * TOP * 17 // (16 * experts)
    slots = -(-share * capacity // 16) * 16
    width = HEADS // ranks * HD
    qk_gains = qk_gain.astype(f32).reshape(2, HD)
    dense_rows = w_qkv.shape[0]

    def exchange(value, step):
        pairs = [(i, i // share * share + (i % share + step) % share) for i in range(planes)]
        return lax.ppermute(value, "rep", pairs)

    def with_group(value):
        return jnp.stack([value] + [exchange(value, step) for step in range(1, share)])

    def gather_ranks(value):
        return lax.all_gather(value, "ep", axis=0)

    assert planes & (planes - 1) == 0 and share & (share - 1) == 0
    last_step = planes - 1
    in_parts, out_parts = (
        {
            step: lax.dynamic_index_in_dim(weight, own ^ step % share, 0, keepdims=False)
            for step in range(planes)
        }
        for weight in (w_in, w_out)
    )

    def send(parts, steps):
        return {step: cross_rep(parts[step], step) for step in steps}

    stream = gather_ranks(tokens)
    out_rows = [w_o] + [cross_rep(w_o, step) for step in range(1, planes)]
    upstream_group = with_group(cotangent)
    slab = cut_heads(
        w_qkv,
        jnp.concatenate(
            [
                w_router,
                norm_gains.reshape(dense_rows, 2),
                jnp.zeros((dense_rows, PAD - experts - 2), bf16),
            ],
            axis=1,
        ),
        ranks,
    )
    slab = lax.all_to_all(slab, "ep", split_axis=0, concat_axis=0, tiled=True)
    slab = slab.reshape(ranks * dense_rows, 3 * width + PAD)
    out_rows, upstream_group, slab = lax.optimization_barrier((out_rows, upstream_group, slab))
    gathered = gather_ranks(jnp.concatenate(out_rows, axis=0))
    segment = segments[0]
    cosine, sine = jax.vmap(lambda one: rope_tables(doc_positions(one), HD))(segment)
    sine = jnp.where(jnp.arange(HD) < HD // 2, -sine, sine)
    tables = (cosine, sine, segment[:, :, None], segment[:, None, :], qk_gains)
    slab, (tables, in_parts, out_parts) = ring_rep(slab, tables, in_parts, out_parts)
    router = slab[:, 3 * width :]
    gain_pair = router[:, experts : experts + 2].reshape(-1).astype(f32)
    first_gain = gain_pair[None, :D]
    second_gain = gain_pair[None, D:]
    in_parts, out_parts, upstream_group, stream = after(
        (in_parts, out_parts, upstream_group, stream), slab
    )
    in_pieces = {0: in_parts[0], **send(in_parts, range(last_step - 1, 0, -1))}
    upstream_all = gather_ranks(upstream_group)

    normed, proj = project(micro, stream, first_gain, slab)
    proj = proj.reshape(ranks, micro, rows, 3 * width)
    mixed_h, query, keys, values, lses = attention_forward(proj, *tables)
    mixed = lax.all_to_all(mixed_h, "ep", split_axis=0, concat_axis=3, tiled=True)
    mixed = mixed.reshape(mine, D)
    hidden, payload, gates = route(
        where[1:2], planes, mixed, tokens, gathered, second_gain, router, routes, experts
    )
    normed_two = payload[:, :D]
    payload, in_pieces = lax.optimization_barrier((payload, in_pieces))
    payload = with_group(payload)
    payload, in_parts, out_parts = lax.optimization_barrier((payload, in_parts, out_parts))
    in_pieces.update(send(in_parts, [last_step]))
    in_pieces, out_parts = lax.optimization_barrier((in_pieces, out_parts))
    out_pieces = {0: out_parts[0], **send(out_parts, range(1, planes))}
    in_pieces = [in_pieces[step] for step in range(planes)]
    out_pieces = [out_pieces[step] for step in range(planes)]
    payload = gather_ranks(payload)

    shape = (ranks, share, micro, rows, -1)
    rows_in, tail, both, active, grad_produced, up_rows, places = expert_forward(
        where, payload.reshape(shape), upstream_all.reshape(shape), in_pieces, slots, experts
    )
    in_rows = micro * ranks * slots
    out_cut = weight_gradient(
        where, planes, active.reshape(in_rows, FF), [grad_produced.reshape(in_rows, D)]
    )

    def sum_rep(parts, shift=False):
        sums = [
            sum(parts[step].astype(f32) for step in range(first, planes, share))
            for first in range(share)
        ]
        return jnp.stack(
            [
                sum(
                    jnp.where(((own - step) % share if shift else own ^ step) == j, sums[step], 0.0)
                    for step in range(share)
                )
                for j in range(share)
            ]
        )

    tail, out_cut, out_pieces = lax.optimization_barrier((tail, out_cut, out_pieces))
    out_sent = send(out_cut, range(1, planes))
    def swap(value, step):
        return lax.ppermute(value, "ep", [(i, i ^ step) for i in range(ranks)])

    def pair_sum(keep, give):
        return (keep.astype(f32) + swap(give, 1).astype(f32)).astype(bf16)

    bits = list(range((ranks // 2).bit_length() - 1))

    def halve(number, value, phase):
        way = bits if number % 2 == 0 else bits[::-1]
        bit = way[phase]
        low = 2 ** sum(other < bit for other in way[phase:])
        value = value.reshape((-1, 2, low) + value.shape[1:])
        side = rank // 2 // 2**bit % 2
        keep, give = (
            lax.dynamic_index_in_dim(value, which, 1, keepdims=False).reshape((-1,) + value.shape[3:])
            for which in (side, 1 - side)
        )
        return keep, swap(give, 2 * 2**bit)

    def total(parts):
        return sum(part.astype(f32) for part in parts)

    back = []
    returned = []

    def scatter_ranks(value):
        return lax.psum_scatter(value, "ep", scatter_dimension=0)

    def exchange_back(value):
        return [value[0]] + [exchange(value[step], share - step) for step in range(1, share)]

    for step in range(micro):
        back.append(
            expert_backward(
                step, where, tail, both, active, grad_produced, up_rows, places, in_pieces,
                out_pieces, share, rows, experts,
            )
        )
        returned.append(scatter_ranks(back[step][2]))
        if step == 0:
            tail, out_sent[last_step] = after((tail, out_sent[last_step]), back[step][2])
        else:
            tail = after(tail, back[step][2])
    early = [pair_sum(*part[:2]) for part in back[:-1]]
    rows_in, tail, early = lax.optimization_barrier((rows_in, tail, early))
    crossed = [halve(number, value, 0) for number, value in enumerate(early)]
    rows_flat = rows_in.reshape(in_rows, D)
    grads_flat = [back[step][3].reshape(in_rows // micro, 2 * FF) for step in range(micro)]
    (in_near,) = weight_gradient(
        where, planes, rows_flat, grads_flat, first=1, steps=1, shift=True
    )
    rows_flat, in_near = lax.optimization_barrier((rows_flat, in_near))
    *in_rest, in_back, in_own = weight_gradient(
        where, planes, rows_flat, grads_flat, first=2, steps=last_step, shift=True
    )
    in_sent = {0: in_own, 1: shift_rep(in_near, 1)}

    def cuts(value, *places):
        ends = [-(-value.shape[0] * place // 512) * 16 for place in (0, *places, 32)]
        return [value[start:end] for start, end in zip(ends, ends[1:])]

    grad_inputs, branches, logit_grads, grad_projs = [], [], [], []
    gain_two_sum = gain_one_sum = qk_sum = 0.0
    in_rest, in_back, out_sent, in_sent, crossed = lax.optimization_barrier(
        (in_rest, in_back, out_sent, in_sent, crossed)
    )
    late = back[-1][:2]
    for step in range(micro):
        at = slice(step * rows, (step + 1) * rows)
        parts = after(returned[step], [one[1] for one in grad_inputs])
        parts, in_sent = lax.optimization_barrier((parts, in_sent))
        if step == micro - 1:
            crossed.append(halve(step, after(late, parts), 0))
        parts = exchange_back(parts)
        parts, in_rest, in_back, late = lax.optimization_barrier((parts, in_rest, in_back, late))
        if step == 0:
            late = pair_sum(*late)
            in_sent[last_step] = shift_rep(in_back, last_step)
        if step == micro - 1:
            rest = [cuts(value, 12, 20) for value in in_rest]
            rest_sent = [[shift_rep(part[0], i + 2) for i, part in enumerate(rest)]]
        grad_hidden, grad_branch, grad_mixed, grad_logits, gain_two = hidden_backward(
            where[1:2], planes, parts, hidden[at], gates[at], cotangent[at], second_gain,
            router, gathered, experts,
        )
        branches.append(grad_branch)
        logit_grads.append(grad_logits)
        gain_two_sum = gain_two_sum + gain_two
        if step == micro - 1:
            out_sum = dot(mixed, jnp.concatenate(branches, axis=0), ((0,), (0,))).astype(bf16)
            out_sum = out_sum.reshape(planes, ranks, dense_rows, D).transpose(1, 0, 2, 3)
        grad_mixed = lax.all_to_all(grad_mixed, "ep", split_axis=1, concat_axis=0, tiled=True)
        grad_mixed, late = lax.optimization_barrier((grad_mixed, late))
        if step == micro - 1:
            grad_mixed, rest_sent, rest, out_sum, crossed = lax.optimization_barrier(
                (grad_mixed, rest_sent, rest, out_sum, crossed)
            )
            out_sum = lax.psum_scatter(out_sum, "ep", scatter_dimension=0)
            rest_sent.append([shift_rep(part[1], i + 2) for i, part in enumerate(rest)])
        grad_proj, grad_qk = attention_backward(
            step, proj, *tables, query, keys, values, lses, grad_mixed
        )
        qk_sum = qk_sum + grad_qk.reshape(-1)
        if step < micro - 1:
            grad_proj, in_sent = lax.optimization_barrier((grad_proj, in_sent))
        else:
            grad_proj, grad_inputs, rest_sent, rest = lax.optimization_barrier(
                (grad_proj, grad_inputs, rest_sent, rest)
            )
        grad_projs.append(grad_proj)
        grad_normed, gain_one = project_backward(step, grad_proj, stream, slab)
        gain_one_sum = gain_one_sum + gain_one
        grad_inputs.append(
            (
                grad_hidden,
                grad_normed,
                lax.psum_scatter(grad_normed, "ep", scatter_dimension=0, tiled=True),
            )
        )

    router_sum = dot(normed_two, jnp.concatenate(logit_grads, axis=0), ((0,), (0,)))
    qk_columns = qk_sum.shape[0] // dense_rows
    small = jnp.concatenate(
        [
            router_sum[:, :experts],
            jnp.concatenate([gain_one_sum, gain_two_sum], axis=1).reshape(D, 2),
            jnp.tile(qk_sum.reshape(dense_rows, qk_columns), (planes * ranks, 1)),
        ],
        axis=1,
    )
    count = small.shape[1]

    def halves(value):
        high, low = two_parts(value)
        blank = jnp.zeros((value.shape[0], PAD - 2 * count), bf16)
        return jnp.concatenate([high, low, blank], axis=1)

    def joined(value):
        return value[..., :count].astype(f32) + value[..., count : 2 * count].astype(f32)

    grad_projs, rest, out_cut, out_sent, _ = lax.optimization_barrier(
        (grad_projs, rest, out_cut, out_sent, grad_normed)
    )
    rest_sent.append([shift_rep(part[2], i + 2) for i, part in enumerate(rest)])
    packed = weight_gradient(
        where,
        planes,
        normed.reshape(ranks * mine, D),
        [grad.reshape(length, 3 * width) for grad in grad_projs],
        halves(small),
    )
    packed, rest_sent, out_cut, out_sent, crossed = lax.optimization_barrier(
        (packed, rest_sent, out_cut, out_sent, crossed)
    )
    packed_sent = [packed[0]] + [cross_rep(packed[step], step) for step in range(1, planes)]
    normed_sums = [one[2] for one in grad_inputs]
    normed_sums = [one[2] for one in grad_inputs]
    grad_tokens = []
    for step in range(micro):
        own_stream = tokens[step * rows : (step + 1) * rows].astype(f32)
        grad_tokens.append(
            grad_inputs[step][0]
            + rms_backward(
                own_stream, inverse_rms(own_stream), first_gain, normed_sums[step].astype(f32)
            )
        )
    grad_tokens = jnp.concatenate(grad_tokens, axis=0)
    packed_sent, grad_tokens = lax.optimization_barrier((packed_sent, grad_tokens))
    for phase in range(1, len(bits)):
        mixtures = [total(parts).astype(bf16) for parts in crossed]
        crossed = [halve(number, value, phase) for number, value in enumerate(mixtures)]
    mixture = []
    for number in range(micro):
        parts = total(crossed[number])[0]
        mixture.append((parts[0], exchange_back(parts.astype(bf16))[1:]))
    own_sum = lax.dynamic_index_in_dim(out_sum, plane, 0, keepdims=False)
    out_sent_back = [
        cross_rep(lax.dynamic_index_in_dim(out_sum, plane ^ step, 0, keepdims=False), step)
        for step in range(1, planes)
    ]
    main = total([part[:, : 3 * width] for part in packed_sent]).astype(bf16)
    small = sum(joined(part[:, 3 * width :]) for part in packed_sent)
    packed = jnp.concatenate([main, halves(small)], axis=1).reshape(ranks, dense_rows, -1)
    packed = lax.all_to_all(packed, "ep", split_axis=0, concat_axis=0, tiled=True)
    packed, mixture, out_sent_back = lax.optimization_barrier((packed, mixture, out_sent_back))
    output = jnp.concatenate([mine_part + total(others) for mine_part, others in mixture], axis=0)
    output = (hidden + output).astype(bf16)
    grad_w_o = total([own_sum, *out_sent_back])
    grad_w_qkv, small = unpack(packed, count)
    grad_w_out = sum_rep({0: out_cut[0], **out_sent})
    for i in range(planes - 3):
        in_sent[i + 2] = jnp.concatenate([parts[i] for parts in rest_sent], axis=0)
    grad_w_in = sum_rep(in_sent, shift=True)
    return (
        output,
        grad_tokens,
        grad_w_qkv,
        grad_w_o,
        small[:, :experts],
        small[:, experts : experts + 2].reshape(-1),
        small[:, experts + 2 : count].reshape(-1),
        grad_w_in,
        grad_w_out,
    )


def solution(mesh):
    placed = (
        P(("rep", "ep"), None),
        P(("rep", "ep"), None),
        P(("rep", "ep"), None),
        P(("rep", "ep"), None),
        P(("rep", "ep"), None),
        P(("rep", "ep")),
        P(),
        P("ep", "rep", None),
        P("ep", "rep", None),
        P("rep", None, None),
        P(("rep", "ep"), None),
    )
    return jax.shard_map(
        on_device,
        mesh=mesh,
        in_specs=placed,
        out_specs=(
            P(("rep", "ep"), None),
            P(("rep", "ep"), None),
            P(("rep", "ep"), None),
            P(("rep", "ep"), None),
            P(("rep", "ep"), None),
            P(("rep", "ep")),
            P(),
            P("ep", "rep", None),
            P("ep", "rep", None),
        ),
        check_vma=False,
    )
```

```python
import math

import jax
import jax.numpy as jnp
from jax import lax
from jax.experimental import pallas as pl
from jax.experimental.pallas import tpu as pltpu
from jax.sharding import PartitionSpec as P

D = 2048
HEADS = 16
HD = 128
FF = 1024
TOP = 8
HALF = 512
PAD = 128

epsilon = 1e-06
rope_base = 50000.0
bf16 = jnp.bfloat16
f32 = jnp.float32


def dot(a, b, dims=((1,), (0,))):
    return lax.dot_general(a, b, (dims, ((), ())), preferred_element_type=f32)


def inverse_rms(value):
    return lax.rsqrt(jnp.mean(value * value, axis=-1, keepdims=True) + epsilon)


def rms_backward(value, inverse, gain, grad):
    scaled = grad * gain
    inner = jnp.mean(scaled * value, axis=-1, keepdims=True)
    return inverse * (scaled - value * (inverse * inverse * inner))


def doc_positions(segment):
    index = jnp.arange(segment.shape[0], dtype=jnp.int32)
    change = jnp.concatenate([jnp.ones((1,), dtype=jnp.bool_), segment[1:] != segment[:-1]])
    start = lax.cummax(jnp.where(change, index, 0), axis=0)
    return index - start


def rope_tables(position, width):
    steps = jnp.arange(width // 2, dtype=f32) * (2.0 / width)
    rates = jnp.exp(-steps * math.log(rope_base))
    angle = position.astype(f32)[:, None] * rates[None, :]
    angle = jnp.concatenate([angle, angle], axis=-1)
    return (jnp.cos(angle), jnp.sin(angle))


def norm_rope(value, gain, cosine, sine):
    inverse = lax.rsqrt(jnp.mean(value * value, axis=1, keepdims=True) + epsilon)
    value = value * inverse * gain
    return value * cosine + pltpu.roll(value, HD // 2, 1) * sine


def norm_rope_back(value, gain, cosine, sine, grad):
    inverse = lax.rsqrt(jnp.mean(value * value, axis=1, keepdims=True) + epsilon)
    grad = grad * cosine + pltpu.roll(grad * sine, HD // 2, 1)
    normal = value * inverse
    scaled = grad * gain
    inner = jnp.mean(scaled * normal, axis=1, keepdims=True)
    return inverse * (scaled - normal * inner), jnp.sum(grad * normal, axis=0, keepdims=True)


def kept_scores(query, keys, q_seg, k_seg, start):
    scores = dot(query, keys, ((1,), (1,))) * (1.0 / math.sqrt(HD))
    q_index = start + lax.broadcasted_iota(jnp.int32, scores.shape, 0)
    k_index = lax.broadcasted_iota(jnp.int32, scores.shape, 1)
    keep = (jnp.abs(q_index - k_index) <= HALF) & (q_seg == k_seg)
    return jnp.where(keep, scores, -1e30)


BIG = 100 * 1024 * 1024 // 2


def forward_kernel(
    heads, proj, cosine, sine, seg_column, seg_row, gains, mixed, query, keys, values, lses
):
    ranks, _, rows, _ = proj.shape
    length = ranks * rows
    q_block = 2 * rows
    k_seg = seg_row[0]
    for head in range(heads):
        at = slice(head * HD, (head + 1) * HD)

        def raw(part):
            first = (part * heads + head) * HD
            return proj[:, 0, :, first : first + HD].reshape(length, HD)

        query[0, :, at] = norm_rope(raw(0), gains[0:1], cosine[0], sine[0]).astype(bf16)
        keys[0, :, at] = norm_rope(raw(1), gains[1:2], cosine[0], sine[0]).astype(bf16)
        values[0, :, at] = raw(2).astype(bf16)

        @pl.loop(0, length // q_block)
        def one_block(number, head=head, at=at):
            start = pl.multiple_of(number * q_block, q_block)
            here = pl.ds(start, q_block)
            scores = kept_scores(
                query[0, here, at], keys[0, :, at], seg_column[0, here], k_seg, start
            )
            top = jnp.max(scores, axis=1, keepdims=True)
            weights = jnp.exp(scores - top)
            total = jnp.sum(weights, axis=1, keepdims=True)
            lses[0, head, here] = top + jnp.log(total)
            weights = (weights * (1.0 / total)).astype(bf16)
            result = dot(weights, values[0, :, at]).astype(bf16)
            mixed[pl.ds(number * 2, 2), 0, :, at] = result.reshape(2, rows, HD)


def backward_kernel(
    heads, proj, cosine, sine, seg_column, seg_row, gains, query, keys, values, lses, grad_mixed,
    grad_proj, grad_gains, grad_q, grad_k, grad_v,
):
    ranks, _, rows, _ = proj.shape
    length = ranks * rows
    q_block = 2 * rows
    k_seg = seg_row[0]
    scale = 1.0 / math.sqrt(HD)
    sum_q = jnp.zeros((1, HD), f32)
    sum_k = jnp.zeros((1, HD), f32)
    for head in range(heads):
        at = slice(head * HD, (head + 1) * HD)
        grad_k[...] = jnp.zeros_like(grad_k)
        grad_v[...] = jnp.zeros_like(grad_v)

        @pl.loop(0, length // q_block)
        def one_block(number, head=head, at=at):
            start = pl.multiple_of(number * q_block, q_block)
            here = pl.ds(start, q_block)
            q_rows = query[0, here, at]
            g_rows = grad_mixed[here, at]
            k_all = keys[0, :, at]
            scores = kept_scores(q_rows, k_all, seg_column[0, here], k_seg, start)
            weights = jnp.exp(scores - lses[0, head, here])
            grad_weights = dot(g_rows, values[0, :, at], ((1,), (1,)))
            delta = jnp.sum(weights * grad_weights, axis=1, keepdims=True)
            grad_scores = (weights * (grad_weights - delta)).astype(bf16)
            grad_q[here] = dot(grad_scores, k_all) * scale
            grad_k[...] += dot(grad_scores, q_rows, ((0,), (0,)))
            grad_v[...] += dot(weights.astype(bf16), g_rows, ((0,), (0,)))

        def rounded(value):
            return value.astype(bf16).astype(f32)

        def raw(part):
            first = (part * heads + head) * HD
            return proj[:, 0, :, first : first + HD].reshape(length, HD)

        def put(part, value):
            first = (part * heads + head) * HD
            grad_proj[:, :, first : first + HD] = value.astype(bf16).reshape(ranks, rows, HD)

        back_q, gain_q = norm_rope_back(
            raw(0), gains[0:1], cosine[0], sine[0], rounded(grad_q[...])
        )
        back_k, gain_k = norm_rope_back(
            raw(1), gains[1:2], cosine[0], sine[0], rounded(grad_k[...] * scale)
        )
        sum_q, sum_k = sum_q + gain_q, sum_k + gain_k
        put(0, back_q)
        put(1, back_k)
        put(2, grad_v[...])
    grad_gains[0:1] = sum_q
    grad_gains[1:2] = sum_k


def fixed(shape):
    return pl.BlockSpec(shape, lambda *_: (0,) * len(shape), pipeline_mode=pl.Buffered(1))


def leading(shape):
    return pl.BlockSpec((1,) + shape[1:], lambda i: (i,) + (0,) * (len(shape) - 1))


def params():
    return pltpu.CompilerParams(vmem_limit_bytes=BIG)


def cost(products):
    return pl.CostEstimate(flops=20 * products, bytes_accessed=0, transcendentals=0)


def out(shape, dtype=bf16):
    return jax.ShapeDtypeStruct(shape, dtype)


def attention_forward(proj, cosine, sine, seg_column, seg_row, gains):
    ranks, micro, rows, width = proj.shape
    length = ranks * rows
    width = width // 3
    heads = width // HD
    part = out((micro, length, width))
    by_rank = lambda n: pl.BlockSpec((ranks, 1, rows, n), lambda i: (0, i, 0, 0))
    lses = out((micro, heads, length, 1), f32)
    return pl.pallas_call(
        lambda *refs: forward_kernel(heads, *refs),
        grid=(micro,),
        in_specs=[by_rank(3 * width)]
        + [leading(v.shape) for v in (cosine, sine, seg_column, seg_row)]
        + [fixed(gains.shape)],
        out_specs=[by_rank(width)] + [leading(part.shape)] * 3 + [leading(lses.shape)],
        out_shape=[out((ranks, micro, rows, width)), part, part, part, lses],
        compiler_params=params(),
    )(proj, cosine, sine, seg_column, seg_row, gains)


def attention_backward(
    step, proj, cosine, sine, seg_column, seg_row, gains, query, keys, values, lses, grad_mixed
):
    ranks, micro, rows, width = proj.shape
    length = ranks * rows
    heads = width // 3 // HD

    def part(value):
        return pl.BlockSpec((1,) + value.shape[1:], lambda i: (step,) + (0,) * (value.ndim - 1))

    return pl.pallas_call(
        lambda *refs: backward_kernel(heads, *refs),
        grid=(1,),
        in_specs=[pl.BlockSpec((ranks, 1, rows, width), lambda i: (0, step, 0, 0))]
        + [part(v) for v in (cosine, sine, seg_column, seg_row)]
        + [fixed(gains.shape)]
        + [part(v) for v in (query, keys, values, lses)]
        + [fixed(grad_mixed.shape)],
        out_specs=[fixed((ranks, rows, width)), fixed((2, HD))],
        out_shape=[out((ranks, rows, width)), out((2, HD), f32)],
        scratch_shapes=[pltpu.VMEM((length, HD), f32)] * 3,
        compiler_params=params(),
    )(
        proj, cosine, sine, seg_column, seg_row, gains, query, keys, values, lses, grad_mixed
    )


def project(micro, tokens, gain, slab):
    ranks, count, _ = tokens.shape
    rows = count // micro
    width = slab.shape[1] - PAD

    def kernel(value, gain, weight, normed, proj):
        value = value[0].astype(f32)
        result = (value * inverse_rms(value) * gain[...]).astype(bf16)
        normed[...] = result.reshape(micro, 1, rows, D)
        proj[0] = dot(result, weight[:, :width])

    return pl.pallas_call(
        kernel,
        grid=(ranks,),
        in_specs=[leading((ranks, count, D)), fixed((1, D)), fixed(slab.shape)],
        out_specs=[
            pl.BlockSpec((micro, 1, rows, D), lambda i: (0, i, 0, 0)),
            leading((ranks, count, width)),
        ],
        out_shape=[out((micro, ranks, rows, D)), out((ranks, count, width), f32)],
        compiler_params=params(),
    )(tokens, gain, slab)


TILE = 512


def tiles(count):
    return pl.loop(0, count // TILE)


def tile(number):
    return pl.ds(pl.multiple_of(number * TILE, TILE), TILE)


HBM = pl.BlockSpec(memory_space=pl.ANY)


def copies(pairs, sems):
    started = [
        pltpu.make_async_copy(source, target, sems.at[place])
        for place, (source, target) in enumerate(pairs)
    ]
    for copy in started:
        copy.start()

    def wait():
        for copy in started:
            copy.wait()

    return wait


def plane_pairs(plane, pieces, target):
    planes = len(pieces)
    rows = target.shape[0] // planes
    return [
        (piece, target.at[pl.ds(lax.bitwise_xor(plane, jnp.int32(step)) * rows, rows)])
        for step, piece in enumerate(pieces)
    ]


def out_weight_pairs(plane, planes, gathered, target):
    ranks = gathered.shape[0]
    rows = D // (planes * ranks)
    return [
        (
            gathered.at[rank, pl.ds(step * rows, rows)],
            target.at[
                pl.ds((lax.bitwise_xor(plane, jnp.int32(step)) * ranks + rank) * rows, rows)
            ],
        )
        for rank in range(ranks)
        for step in range(planes)
    ]


def route(plane, planes, mixed, tokens, gathered, gain, router, routes, experts):
    count = tokens.shape[0]
    pieces = planes * gathered.shape[0]

    def kernel(
        plane, mixed, tokens, gathered, gain, router, routes, hidden, payload, gates,
        out_weight, sems,
    ):
        copies(out_weight_pairs(plane[0], planes, gathered, out_weight), sems)()

        @tiles(D)
        def _(number):
            at = tile(number)
            hidden[:, at] = tokens[:, at].astype(f32) + dot(mixed[...], out_weight[:, at])

        value = hidden[...]
        normed = (value * inverse_rms(value) * gain[...]).astype(bf16)
        payload[:, :D] = normed
        logits = dot(normed, router[...])
        column = lax.broadcasted_iota(jnp.int32, logits.shape, 1)
        routed = column == routes[:, 0:1]
        for choice in range(1, TOP):
            routed = routed | (column == routes[:, choice : choice + 1])
        logits = jnp.where(routed, logits, -1e30)
        weights = jnp.exp(logits - jnp.max(logits, axis=1, keepdims=True))
        weights = jnp.where(routed, weights, 0.0)
        weights = weights / jnp.sum(weights, axis=1, keepdims=True)
        gates[...] = weights
        high = weights.astype(bf16).astype(f32)
        payload[:, D:] = (high + pltpu.roll(weights - high, experts, 1)).astype(bf16)

    shapes = [out((count, D), f32), out((count, D + PAD)), out((count, PAD), f32)]
    return pl.pallas_call(
        kernel,
        grid_spec=pltpu.PrefetchScalarGridSpec(
            num_scalar_prefetch=1,
            grid=(1,),
            in_specs=[
                HBM if value is gathered else fixed(value.shape)
                for value in (mixed, tokens, gathered, gain, router, routes)
            ],
            out_specs=[fixed(shape.shape) for shape in shapes],
            scratch_shapes=[pltpu.VMEM((D, D), bf16), pltpu.SemaphoreType.DMA((pieces,))],
        ),
        out_shape=shapes,
        compiler_params=params(),
    )(plane, mixed, tokens, gathered, gain, router, routes)


def lane(value, number):
    column = lax.broadcasted_iota(jnp.int32, value.shape, 1)
    return jnp.sum(jnp.where(column == number, value.astype(f32), 0.0), axis=1, keepdims=True)


def one_hot(slot, slots):
    place = lax.broadcasted_iota(jnp.int32, (slots, slot.shape[1]), 0).astype(f32)
    return (place == slot).astype(bf16)


def expert_forward(where, payload, upstream, in_pieces, slots, experts):
    ranks, share, micro, rows, _ = payload.shape
    count = share * rows
    block = 2 * slots

    planes = len(in_pieces)

    def kernel(where, payload, upstream, *refs):
        (
            rows_in, tail, both, active, grad_produced, up_rows, places, in_weight, sems
        ) = refs[planes:]
        number = where[0]

        @pl.when((pl.program_id(0) == 0) & (pl.program_id(1) == 0))
        def _():
            copies(plane_pairs(where[1], refs[:planes], in_weight), sems)()

        for part in range(2):
            here = slice(part * slots, (part + 1) * slots)
            value = payload[part].reshape(count, D + PAD)
            marks = value[:, D:]
            first = lax.broadcasted_iota(jnp.int32, (8, PAD), 1) == number
            taken = dot(first.astype(bf16), marks, ((1,), (1,))) > 0.0
            before = lax.broadcasted_iota(jnp.int32, (count, count), 0)
            behind = lax.broadcasted_iota(jnp.int32, (count, count), 1)
            slot = dot(taken.astype(bf16), (before < behind).astype(bf16))
            select = one_hot(jnp.where(taken, slot, -1.0)[0:1], slots)
            wide = jnp.broadcast_to(lane(marks, number) > 0.0, (count, PAD))
            slot = dot((before > behind).astype(bf16), wide.astype(bf16))
            places[0, 0, part] = jnp.where(wide, slot, -1.0)
            rows_in[0, 0, here] = dot(select, value[:, :D]).astype(bf16)
            marks = dot(select, marks)
            tail[0, 0, here] = marks
            gate = lane(marks, number) + lane(marks, experts + number)
            picked = dot(select, upstream[part].reshape(count, D))
            up_rows[0, 0, here] = picked.astype(bf16)
            grad_produced[0, 0, here] = (gate * picked).astype(bf16)

        for number in range(FF // TILE):
            at = slice(number * TILE, (number + 1) * TILE)
            more = slice(FF + number * TILE, FF + (number + 1) * TILE)
            gate_part = dot(rows_in[0, 0], in_weight[:, at])
            up_part = dot(rows_in[0, 0], in_weight[:, more])
            both[0, 0, :, at] = gate_part
            both[0, 0, :, more] = up_part
            active[0, 0, :, at] = (
                gate_part / (1.0 + jnp.exp(-gate_part)) * up_part
            ).astype(bf16)

    def tokens_spec(width):
        return pl.BlockSpec((2, share, 1, rows, width), lambda m, b, _: (b, 0, m, 0, 0))

    pairs = ranks // 2
    shapes = [
        out((micro, pairs, block, D)),
        out((micro, pairs, block, PAD), f32),
        out((micro, pairs, block, 2 * FF), f32),
        out((micro, pairs, block, FF)),
        out((micro, pairs, block, D)),
        out((micro, pairs, block, D)),
        out((micro, pairs, 2, count, PAD), f32),
    ]
    return pl.pallas_call(
        kernel,
        grid_spec=pltpu.PrefetchScalarGridSpec(
            num_scalar_prefetch=1,
            grid=(micro, pairs),
            in_specs=[tokens_spec(D + PAD), tokens_spec(D)] + [HBM] * planes,
            out_specs=[
                pl.BlockSpec(
                    (1, 1) + s.shape[2:], lambda m, b, _, n=len(s.shape): (m, b) + (0,) * (n - 2)
                )
                for s in shapes
            ],
            scratch_shapes=[pltpu.VMEM((D, 2 * FF), bf16), pltpu.SemaphoreType.DMA((planes,))],
        ),
        out_shape=shapes,
        cost_estimate=cost(micro * pairs * block * D * (2 * FF + 2 * count)),
        compiler_params=params(),
    )(where, payload, upstream, *in_pieces)


def expert_backward(
    step, where, tail, both, active, grad_produced, up_rows, places, in_pieces, out_pieces,
    share, rows, experts,
):
    pairs, block = tail.shape[1:3]
    slots = block // 2
    count = places.shape[3]

    planes = len(in_pieces)

    def kernel(where, tail, both, active, grad_produced, up_rows, places, *refs):
        keep, give, grad_tokens, grad_both, in_weight, out_weight, sems = refs[2 * planes :]
        number = where[0]
        odd = where[2] == 1

        @pl.when(pl.program_id(0) == 0)
        def _():
            copies(
                plane_pairs(where[1], refs[:planes], in_weight)
                + plane_pairs(where[1], refs[planes : 2 * planes], out_weight),
                sems,
            )()

        gate = lane(tail[0, 0], number) + lane(tail[0, 0], experts + number)
        place = lax.broadcasted_iota(jnp.int32, (count, slots), 1).astype(f32)
        selects = [(places[0, 0, part][:, 0:1] == place).astype(bf16) for part in range(2)]

        def spread(value):
            return [
                dot(selects[part], value[part * slots : (part + 1) * slots])
                .astype(bf16)
                .reshape(share, rows, -1)
                for part in range(2)
            ]

        grad_gate = jnp.zeros((block, 1), f32)
        for tile in range(D // TILE):
            at = slice(tile * TILE, (tile + 1) * TILE)
            produced = dot(active[0, 0], out_weight[:, at]).astype(bf16).astype(f32)
            even_rank, odd_rank = spread((gate * produced).astype(bf16))
            keep[0, :, :, at] = jnp.where(odd, odd_rank, even_rank)
            give[0, :, :, at] = jnp.where(odd, even_rank, odd_rank)
            grad_gate = grad_gate + jnp.sum(
                up_rows[0, 0, :, at].astype(f32) * produced, axis=1, keepdims=True
            )

        for tile in range(FF // TILE):
            at = slice(tile * TILE, (tile + 1) * TILE)
            more = slice(FF + tile * TILE, FF + (tile + 1) * TILE)
            grad_active = dot(grad_produced[0, 0], out_weight[at, :], ((1,), (1,)))
            grad_active = grad_active.astype(bf16).astype(f32)
            gate_part = both[0, 0, :, at]
            up_part = both[0, 0, :, more]
            sigma = 1.0 / (1.0 + jnp.exp(-gate_part))
            grad_both[0, :, at] = (
                grad_active * up_part * (sigma * (1.0 + gate_part * (1.0 - sigma)))
            ).astype(bf16)
            grad_both[0, :, more] = (grad_active * (gate_part * sigma)).astype(bf16)

        for tile in range(D // TILE):
            at = slice(tile * TILE, (tile + 1) * TILE)
            grad_rows = dot(grad_both[0], in_weight[at, :], ((1,), (1,))).astype(bf16)
            grad_tokens[0, :, :, at], grad_tokens[1, :, :, at] = spread(grad_rows)

        high = grad_gate.astype(bf16).astype(f32)
        column = lax.broadcasted_iota(jnp.int32, (block, PAD), 1)
        extra = jnp.where(column == number, high, 0.0)
        extra = jnp.where(column == experts + number, grad_gate - high, extra)
        grad_tokens[0, :, :, D:], grad_tokens[1, :, :, D:] = spread(extra.astype(bf16))

    def part(value):
        return pl.BlockSpec(
            (1, 1) + value.shape[2:], lambda b, _: (step, b) + (0,) * (value.ndim - 2)
        )

    def tokens_spec(count, width):
        return pl.BlockSpec((count, share, rows, width), lambda b, _: (b, 0, 0, 0))

    return pl.pallas_call(
        kernel,
        grid_spec=pltpu.PrefetchScalarGridSpec(
            num_scalar_prefetch=1,
            grid=(pairs,),
            in_specs=[part(v) for v in (tail, both, active, grad_produced, up_rows, places)]
            + [HBM] * (2 * planes),
            out_specs=[
                tokens_spec(1, D),
                tokens_spec(1, D),
                tokens_spec(2, D + PAD),
                pl.BlockSpec((1, block, 2 * FF), lambda b, _: (b, 0, 0)),
            ],
            scratch_shapes=[
                pltpu.VMEM((D, 2 * FF), bf16),
                pltpu.VMEM((FF, D), bf16),
                pltpu.SemaphoreType.DMA((2 * planes,)),
            ],
        ),
        out_shape=[
            out((pairs, share, rows, D)),
            out((pairs, share, rows, D)),
            out((2 * pairs, share, rows, D + PAD)),
            out((pairs, block, 2 * FF)),
        ],
        cost_estimate=cost(pairs * block * D * (4 * FF + 2 * count)),
        compiler_params=params(),
    )(
        where, tail, both, active, grad_produced, up_rows, places, *in_pieces, *out_pieces
    )


def weight_gradient(where, planes, left, rights, tail=None, first=0, steps=None, shift=False):
    steps = planes if steps is None else steps
    count, width = left.shape
    parts = len(rights)
    part_rows = count // parts
    columns = rights[0].shape[1]
    width = width // planes
    step = min(TILE, columns & -columns)
    tails = [] if tail is None else [tail]
    whole = columns + sum(value.shape[1] for value in tails)

    def of_plane(i, where):
        return (where[1] + first + i) % planes if shift else lax.bitwise_xor(where[1], first + i)

    def kernel(where, left, *refs):
        rights, tails, targets = refs[:parts], refs[parts:-steps], refs[-steps:]

        def fill(target):
            for value in tails:
                target[:, columns:] = value[...]
            for number in range(columns // step):
                at = slice(number * step, (number + 1) * step)
                target[:, at] = sum(
                    dot(left[part * part_rows : (part + 1) * part_rows], right[:, at], ((0,), (0,)))
                    for part, right in enumerate(rights)
                ).astype(bf16)

        for number, target in enumerate(targets):
            pl.when(pl.program_id(0) == number)(lambda target=target: fill(target))

    return pl.pallas_call(
        kernel,
        grid_spec=pltpu.PrefetchScalarGridSpec(
            num_scalar_prefetch=1,
            grid=(steps,),
            in_specs=[pl.BlockSpec((count, width), lambda i, where: (0, of_plane(i, where)))]
            + [fixed(right.shape) for right in rights]
            + [
                pl.BlockSpec((width, value.shape[1]), lambda i, where: (of_plane(i, where), 0))
                for value in tails
            ],
            out_specs=[fixed((width, whole))] * steps,
        ),
        out_shape=[out((width, whole))] * steps,
        cost_estimate=cost(0 if tails else count * steps * width * columns),
        compiler_params=params(),
    )(where, left, *rights, *tails)


def hidden_backward(
    plane, planes, parts, hidden, gates, upstream, gain, router, gathered, experts
):
    count = hidden.shape[0]
    terms = len(parts)

    def kernel(plane, *refs):
        parts = refs[:terms]
        hidden, gates, upstream, gain, router, gathered = refs[terms : terms + 6]
        (
            grad_hidden, grad_branch, grad_mixed, grad_logits, grad_gain, out_weight, sems
        ) = refs[terms + 6 :]
        wait = copies(out_weight_pairs(plane[0], planes, gathered, out_weight), sems)
        returned = sum(part[...].astype(f32) for part in parts)
        tail = returned[:, D:]
        grad_gates = gates[...] * (tail + pltpu.roll(tail, PAD - experts, 1))
        logits = grad_gates - gates[...] * jnp.sum(grad_gates, axis=1, keepdims=True)
        logits = logits.astype(bf16)
        grad_logits[...] = logits
        grad_normed = returned[:, :D] + dot(logits, router[...], ((1,), (1,)))
        value = hidden[...]
        inverse = inverse_rms(value)
        grad_gain[...] = jnp.sum(grad_normed * value * inverse, axis=0, keepdims=True)
        grad = upstream[...].astype(f32) + rms_backward(value, inverse, gain[...], grad_normed)
        grad_hidden[...] = grad
        grad_branch[...] = grad.astype(bf16)
        wait()

        @tiles(D)
        def _(number):
            at = tile(number)
            grad_mixed[:, at] = dot(grad_branch[...], out_weight[at, :], ((1,), (1,))).astype(bf16)

    shapes = [
        out((count, D), f32), out((count, D)), out((count, D)), out((count, PAD)),
        out((1, D), f32),
    ]
    args = (*parts, hidden, gates, upstream, gain, router, gathered)
    return pl.pallas_call(
        kernel,
        grid_spec=pltpu.PrefetchScalarGridSpec(
            num_scalar_prefetch=1,
            grid=(1,),
            in_specs=[HBM if value is gathered else fixed(value.shape) for value in args],
            out_specs=[fixed(shape.shape) for shape in shapes],
            scratch_shapes=[
                pltpu.VMEM((D, D), bf16),
                pltpu.SemaphoreType.DMA((planes * gathered.shape[0],)),
            ],
        ),
        out_shape=shapes,
        compiler_params=params(),
    )(plane, *args)


def project_backward(step, grad_proj, tokens, slab):
    ranks, rows, _ = grad_proj.shape
    width = slab.shape[1] - PAD

    def kernel(grad_proj, tokens, weight, grad_normed, grad_gain):
        value = tokens[0].astype(f32)
        inverse = inverse_rms(value)
        grad = dot(grad_proj[0], weight[:, :width], ((1,), (1,)))
        grad_normed[...] = grad.astype(bf16)

        @pl.when(pl.program_id(0) == 0)
        def _():
            grad_gain[...] = jnp.zeros_like(grad_gain)

        grad_gain[...] += jnp.sum(grad * value * inverse, axis=0, keepdims=True)

    return pl.pallas_call(
        kernel,
        grid=(ranks,),
        in_specs=[
            leading(grad_proj.shape),
            pl.BlockSpec((1, rows, D), lambda i: (i, step, 0)),
            fixed(slab.shape),
        ],
        out_specs=[pl.BlockSpec((rows, D), lambda i: (i, 0)), fixed((1, D))],
        out_shape=[out((ranks * rows, D)), out((1, D), f32)],
        compiler_params=params(),
    )(grad_proj, tokens, slab)


def cut_heads(weight, tail, ranks):
    rows = weight.shape[0]
    width = D // ranks

    def kernel(weight, tail, target):
        for rank in range(ranks):
            for part in range(3):
                at = part * D + rank * width
                target[rank, :, part * width : (part + 1) * width] = weight[:, at : at + width]
            target[rank, :, 3 * width :] = tail[...]

    return pl.pallas_call(
        kernel,
        out_shape=out((ranks, rows, 3 * width + PAD)),
        compiler_params=params(),
    )(weight, tail)


def unpack(packed, count):
    ranks, rows, columns = packed.shape
    width = (columns - PAD) // 3

    def kernel(packed, main, small):
        for rank in range(ranks):
            for part in range(3):
                at = part * D + rank * width
                main[:, at : at + width] = packed[rank, :, part * width : (part + 1) * width].astype(
                    f32
                )
        tails = sum(packed[rank, :, 3 * width :].astype(f32) for rank in range(ranks))
        small[...] = tails + pltpu.roll(tails, PAD - count, 1)

    return pl.pallas_call(
        kernel,
        out_shape=[out((rows, 3 * D), f32), out((rows, PAD), f32)],
        compiler_params=params(),
    )(packed)


def shift_rep(value, step):
    count = lax.axis_size("rep")
    return lax.ppermute(value, "rep", [(i, (i + step) % count) for i in range(count)])


def cross_rep(value, bits):
    return lax.ppermute(value, "rep", [(i, i ^ bits) for i in range(lax.axis_size("rep"))])


def after(value, *others):
    return lax.optimization_barrier((value,) + others)[0]


def two_parts(value):
    high = lax.reduce_precision(value, 8, 7)
    return high.astype(bf16), (value - high).astype(bf16)


def ring_rep(value, *work):
    count = lax.axis_size("rep")
    rank = lax.axis_index("rep")
    rows = value.shape[0]
    full = jnp.zeros((count * rows,) + value.shape[1:], value.dtype)
    full = lax.dynamic_update_slice_in_dim(full, value, rank * rows, 0)
    for step in range(1, count):
        value, work = lax.optimization_barrier((value, work)) if step == count - 1 else (value, work)
        value = shift_rep(value, 1)
        full = lax.dynamic_update_slice_in_dim(full, value, (rank - step) % count * rows, 0)
    return full, work


def on_device(
    tokens, cotangent, w_qkv, w_o, w_router, norm_gains, qk_gain, w_in, w_out, segments, routes
):
    planes = lax.axis_size("rep")
    ranks = lax.axis_size("ep")
    plane = lax.axis_index("rep")
    rank = lax.axis_index("ep")
    share = w_in.shape[0]
    own = plane % share
    experts = share * ranks
    where = jnp.stack([rank * share + own, plane, rank % 2]).astype(jnp.int32)
    micro = segments.shape[1]
    mine = tokens.shape[0]
    rows = mine // micro
    length = rows * ranks
    capacity = rows * TOP * 17 // (16 * experts)
    slots = -(-share * capacity // 16) * 16
    width = HEADS // ranks * HD
    qk_gains = qk_gain.astype(f32).reshape(2, HD)
    dense_rows = w_qkv.shape[0]

    def exchange(value, step):
        pairs = [(i, i // share * share + (i % share + step) % share) for i in range(planes)]
        return lax.ppermute(value, "rep", pairs)

    def with_group(value):
        return jnp.stack([value] + [exchange(value, step) for step in range(1, share)])

    def gather_ranks(value):
        return lax.all_gather(value, "ep", axis=0)

    assert planes & (planes - 1) == 0 and share & (share - 1) == 0
    last_step = planes - 1
    in_parts, out_parts = (
        {
            step: lax.dynamic_index_in_dim(weight, own ^ step % share, 0, keepdims=False)
            for step in range(planes)
        }
        for weight in (w_in, w_out)
    )

    def send(parts, steps):
        return {step: cross_rep(parts[step], step) for step in steps}

    stream = gather_ranks(tokens)
    out_rows = [w_o] + [cross_rep(w_o, step) for step in range(1, planes)]
    upstream_group = with_group(cotangent)
    slab = cut_heads(
        w_qkv,
        jnp.concatenate(
            [
                w_router,
                norm_gains.reshape(dense_rows, 2),
                jnp.zeros((dense_rows, PAD - experts - 2), bf16),
            ],
            axis=1,
        ),
        ranks,
    )
    slab = lax.all_to_all(slab, "ep", split_axis=0, concat_axis=0, tiled=True)
    slab = slab.reshape(ranks * dense_rows, 3 * width + PAD)
    out_rows, upstream_group, slab = lax.optimization_barrier((out_rows, upstream_group, slab))
    gathered = gather_ranks(jnp.concatenate(out_rows, axis=0))
    segment = segments[0]
    cosine, sine = jax.vmap(lambda one: rope_tables(doc_positions(one), HD))(segment)
    sine = jnp.where(jnp.arange(HD) < HD // 2, -sine, sine)
    tables = (cosine, sine, segment[:, :, None], segment[:, None, :], qk_gains)
    slab, (tables, in_parts, out_parts) = ring_rep(slab, tables, in_parts, out_parts)
    router = slab[:, 3 * width :]
    gain_pair = router[:, experts : experts + 2].reshape(-1).astype(f32)
    first_gain = gain_pair[None, :D]
    second_gain = gain_pair[None, D:]
    in_parts, out_parts, upstream_group, stream = after(
        (in_parts, out_parts, upstream_group, stream), slab
    )
    in_pieces = {0: in_parts[0], **send(in_parts, range(last_step - 1, 0, -1))}
    upstream_all = gather_ranks(upstream_group)

    normed, proj = project(micro, stream, first_gain, slab)
    proj = proj.reshape(ranks, micro, rows, 3 * width)
    mixed_h, query, keys, values, lses = attention_forward(proj, *tables)
    mixed = lax.all_to_all(mixed_h, "ep", split_axis=0, concat_axis=3, tiled=True)
    mixed = mixed.reshape(mine, D)
    hidden, payload, gates = route(
        where[1:2], planes, mixed, tokens, gathered, second_gain, router, routes, experts
    )
    normed_two = payload[:, :D]
    payload, in_pieces = lax.optimization_barrier((payload, in_pieces))
    payload = with_group(payload)
    payload, in_parts, out_parts = lax.optimization_barrier((payload, in_parts, out_parts))
    in_pieces.update(send(in_parts, [last_step]))
    in_pieces, out_parts = lax.optimization_barrier((in_pieces, out_parts))
    out_pieces = {0: out_parts[0], **send(out_parts, range(1, planes))}
    in_pieces = [in_pieces[step] for step in range(planes)]
    out_pieces = [out_pieces[step] for step in range(planes)]
    payload = gather_ranks(payload)

    shape = (ranks, share, micro, rows, -1)
    rows_in, tail, both, active, grad_produced, up_rows, places = expert_forward(
        where, payload.reshape(shape), upstream_all.reshape(shape), in_pieces, slots, experts
    )
    in_rows = micro * ranks * slots
    out_cut = weight_gradient(
        where, planes, active.reshape(in_rows, FF), [grad_produced.reshape(in_rows, D)]
    )

    def sum_rep(parts, shift=False):
        sums = [
            sum(parts[step].astype(f32) for step in range(first, planes, share))
            for first in range(share)
        ]
        return jnp.stack(
            [
                sum(
                    jnp.where(((own - step) % share if shift else own ^ step) == j, sums[step], 0.0)
                    for step in range(share)
                )
                for j in range(share)
            ]
        )

    tail, out_cut, out_pieces = lax.optimization_barrier((tail, out_cut, out_pieces))
    first = cross_rep(out_cut[1][:16], 1)
    tail, out_cut, first = lax.optimization_barrier((tail, out_cut, first))
    out_sent = send([out_cut[0], out_cut[1][16:], *out_cut[2:]], range(1, planes))
    back = []
    returned = []

    def scatter_ranks(value):
        return lax.psum_scatter(value, "ep", scatter_dimension=0)

    def exchange_back(value):
        return [value[0]] + [exchange(value[step], share - step) for step in range(1, share)]

    for step in range(micro):
        back.append(
            expert_backward(
                step, where, tail, both, active, grad_produced, up_rows, places, in_pieces,
                out_pieces, share, rows, experts,
            )
        )
        returned.append(scatter_ranks(back[step][2]))
        if step == 0:
            tail, out_sent[last_step] = after((tail, out_sent[last_step]), back[step][2])
        else:
            tail = after(tail, back[step][2])
    rows_in = after(rows_in, tail)
    rows_flat = rows_in.reshape(in_rows, D)
    grads_flat = [back[step][3].reshape(in_rows // micro, 2 * FF) for step in range(micro)]
    (in_near,) = weight_gradient(
        where, planes, rows_flat, grads_flat, first=1, steps=1, shift=True
    )
    rows_flat, in_near = lax.optimization_barrier((rows_flat, in_near))
    *in_rest, in_back, in_own = weight_gradient(
        where, planes, rows_flat, grads_flat, first=2, steps=last_step, shift=True
    )
    in_sent = {0: in_own, 1: shift_rep(in_near, 1)}

    def cuts(value, *places):
        ends = [-(-value.shape[0] * place // 512) * 16 for place in (0, *places, 32)]
        return [value[start:end] for start, end in zip(ends, ends[1:])]

    def swap(value, step):
        return lax.ppermute(value, "ep", [(i, i ^ step) for i in range(ranks)])

    bits = list(range((ranks // 2).bit_length() - 1))

    def cut_pairs(number, value, phase):
        way = bits if number % 2 == 0 else bits[::-1]
        bit = way[phase]
        low = 2 ** sum(other < bit for other in way[phase:])
        value = value.reshape((-1, 2, low) + value.shape[1:])
        side = rank // 2 // 2**bit % 2
        return [
            lax.dynamic_index_in_dim(value, which, 1, keepdims=False).reshape((-1,) + value.shape[3:])
            for which in (side, 1 - side)
        ]

    def pair_sum(number, keep, give):
        got = swap(give, 1)
        return [
            total(parts).astype(bf16)
            for parts in zip(cut_pairs(number, keep, 0), cut_pairs(number, got, 0))
        ]

    def halve(number, halves, phase):
        return halves[0], swap(halves[1], 2 * 2 ** (bits if number % 2 == 0 else bits[::-1])[phase])

    def total(parts):
        return sum(part.astype(f32) for part in parts)

    grad_inputs, branches, logit_grads, grad_projs = [], [], [], []
    gain_two_sum = gain_one_sum = qk_sum = 0.0
    in_rest, in_back, out_sent, in_sent = lax.optimization_barrier(
        (in_rest, in_back, out_sent, in_sent)
    )
    mixtures = [part[:2] for part in back]
    for step in range(micro):
        at = slice(step * rows, (step + 1) * rows)
        parts = after(returned[step], [one[1] for one in grad_inputs])
        parts, in_sent = lax.optimization_barrier((parts, in_sent))
        if step == micro - 1:
            mixtures = after(mixtures, parts)
            crossed = [halve(number, value, 0) for number, value in enumerate(mixtures)]
        parts = exchange_back(parts)
        parts, in_rest, in_back, mixtures = lax.optimization_barrier(
            (parts, in_rest, in_back, mixtures)
        )
        if step == 0:
            mixtures = [pair_sum(number, *part) for number, part in enumerate(mixtures)]
            in_sent[last_step] = shift_rep(in_back, last_step)
        if step == micro - 1:
            rest = [cuts(value, 12, 20) for value in in_rest]
            rest_sent = [[shift_rep(part[0], i + 2) for i, part in enumerate(rest)]]
        grad_hidden, grad_branch, grad_mixed, grad_logits, gain_two = hidden_backward(
            where[1:2], planes, parts, hidden[at], gates[at], cotangent[at], second_gain,
            router, gathered, experts,
        )
        branches.append(grad_branch)
        logit_grads.append(grad_logits)
        gain_two_sum = gain_two_sum + gain_two
        if step == micro - 1:
            out_sum = dot(mixed, jnp.concatenate(branches, axis=0), ((0,), (0,))).astype(bf16)
            out_sum = out_sum.reshape(planes, ranks, dense_rows, D).transpose(1, 0, 2, 3)
        grad_mixed = lax.all_to_all(grad_mixed, "ep", split_axis=1, concat_axis=0, tiled=True)
        grad_mixed, mixtures = lax.optimization_barrier((grad_mixed, mixtures))
        if step == micro - 1:
            grad_mixed, crossed, rest_sent, rest, out_sum = lax.optimization_barrier(
                (grad_mixed, crossed, rest_sent, rest, out_sum)
            )
            out_sum = lax.psum_scatter(out_sum, "ep", scatter_dimension=0)
            rest_sent.append([shift_rep(part[1], i + 2) for i, part in enumerate(rest)])
        grad_proj, grad_qk = attention_backward(
            step, proj, *tables, query, keys, values, lses, grad_mixed
        )
        qk_sum = qk_sum + grad_qk.reshape(-1)
        if step < micro - 1:
            grad_proj, in_sent = lax.optimization_barrier((grad_proj, in_sent))
        else:
            grad_proj, grad_inputs, rest_sent, rest = lax.optimization_barrier(
                (grad_proj, grad_inputs, rest_sent, rest)
            )
        grad_projs.append(grad_proj)
        grad_normed, gain_one = project_backward(step, grad_proj, stream, slab)
        gain_one_sum = gain_one_sum + gain_one
        grad_inputs.append(
            (
                grad_hidden,
                grad_normed,
                lax.psum_scatter(grad_normed, "ep", scatter_dimension=0, tiled=True),
            )
        )

    router_sum = dot(normed_two, jnp.concatenate(logit_grads, axis=0), ((0,), (0,)))
    qk_columns = qk_sum.shape[0] // dense_rows
    small = jnp.concatenate(
        [
            router_sum[:, :experts],
            jnp.concatenate([gain_one_sum, gain_two_sum], axis=1).reshape(D, 2),
            jnp.tile(qk_sum.reshape(dense_rows, qk_columns), (planes * ranks, 1)),
        ],
        axis=1,
    )
    count = small.shape[1]

    def halves(value):
        high, low = two_parts(value)
        blank = jnp.zeros((value.shape[0], PAD - 2 * count), bf16)
        return jnp.concatenate([high, low, blank], axis=1)

    def joined(value):
        return value[..., :count].astype(f32) + value[..., count : 2 * count].astype(f32)

    grad_projs, rest, out_cut, out_sent, _ = lax.optimization_barrier(
        (grad_projs, rest, out_cut, out_sent, grad_normed)
    )
    rest_sent.append([shift_rep(part[2], i + 2) for i, part in enumerate(rest)])
    packed = weight_gradient(
        where,
        planes,
        normed.reshape(ranks * mine, D),
        [grad.reshape(length, 3 * width) for grad in grad_projs],
        halves(small),
    )
    packed, rest_sent, out_cut, out_sent, crossed = lax.optimization_barrier(
        (packed, rest_sent, out_cut, out_sent, crossed)
    )
    packed_sent = [packed[0]] + [cross_rep(packed[step], step) for step in range(1, planes)]
    normed_sums = [one[2] for one in grad_inputs]
    normed_sums = [one[2] for one in grad_inputs]
    grad_tokens = []
    for step in range(micro):
        own_stream = tokens[step * rows : (step + 1) * rows].astype(f32)
        grad_tokens.append(
            grad_inputs[step][0]
            + rms_backward(
                own_stream, inverse_rms(own_stream), first_gain, normed_sums[step].astype(f32)
            )
        )
    grad_tokens = jnp.concatenate(grad_tokens, axis=0)
    packed_sent, grad_tokens = lax.optimization_barrier((packed_sent, grad_tokens))
    for phase in range(1, len(bits)):
        mixtures = [total(parts).astype(bf16) for parts in crossed]
        crossed = [
            halve(number, cut_pairs(number, value, phase), phase)
            for number, value in enumerate(mixtures)
        ]
    mixture = []
    for number in range(micro):
        parts = total(crossed[number])[0]
        mixture.append((parts[0], exchange_back(parts.astype(bf16))[1:]))
    own_sum = lax.dynamic_index_in_dim(out_sum, plane, 0, keepdims=False)
    out_sent_back = [
        cross_rep(lax.dynamic_index_in_dim(out_sum, plane ^ step, 0, keepdims=False), step)
        for step in range(1, planes)
    ]
    main = total([part[:, : 3 * width] for part in packed_sent]).astype(bf16)
    small = sum(joined(part[:, 3 * width :]) for part in packed_sent)
    packed = jnp.concatenate([main, halves(small)], axis=1).reshape(ranks, dense_rows, -1)
    packed = lax.all_to_all(packed, "ep", split_axis=0, concat_axis=0, tiled=True)
    packed, mixture, out_sent_back = lax.optimization_barrier((packed, mixture, out_sent_back))
    output = jnp.concatenate([mine_part + total(others) for mine_part, others in mixture], axis=0)
    output = (hidden + output).astype(bf16)
    grad_w_o = total([own_sum, *out_sent_back])
    grad_w_qkv, small = unpack(packed, count)
    out_sent[1] = jnp.concatenate([first, out_sent[1]], axis=0)
    grad_w_out = sum_rep({0: out_cut[0], **out_sent})
    for i in range(planes - 3):
        in_sent[i + 2] = jnp.concatenate([parts[i] for parts in rest_sent], axis=0)
    grad_w_in = sum_rep(in_sent, shift=True)
    return (
        output,
        grad_tokens,
        grad_w_qkv,
        grad_w_o,
        small[:, :experts],
        small[:, experts : experts + 2].reshape(-1),
        small[:, experts + 2 : count].reshape(-1),
        grad_w_in,
        grad_w_out,
    )


def solution(mesh):
    placed = (
        P(("rep", "ep"), None),
        P(("rep", "ep"), None),
        P(("rep", "ep"), None),
        P(("rep", "ep"), None),
        P(("rep", "ep"), None),
        P(("rep", "ep")),
        P(),
        P("ep", "rep", None),
        P("ep", "rep", None),
        P("rep", None, None),
        P(("rep", "ep"), None),
    )
    return jax.shard_map(
        on_device,
        mesh=mesh,
        in_specs=placed,
        out_specs=(
            P(("rep", "ep"), None),
            P(("rep", "ep"), None),
            P(("rep", "ep"), None),
            P(("rep", "ep"), None),
            P(("rep", "ep"), None),
            P(("rep", "ep")),
            P(),
            P("ep", "rep", None),
            P("ep", "rep", None),
        ),
        check_vma=False,
    )
```

```python
import math

import jax
import jax.numpy as jnp
from jax import lax
from jax.experimental import pallas as pl
from jax.experimental.pallas import tpu as pltpu
from jax.sharding import PartitionSpec as P

D = 2048
HEADS = 16
HD = 128
FF = 1024
TOP = 8
HALF = 512
PAD = 128

epsilon = 1e-06
rope_base = 50000.0
bf16 = jnp.bfloat16
f32 = jnp.float32


def dot(a, b, dims=((1,), (0,))):
    return lax.dot_general(a, b, (dims, ((), ())), preferred_element_type=f32)


def inverse_rms(value):
    return lax.rsqrt(jnp.mean(value * value, axis=-1, keepdims=True) + epsilon)


def rms_backward(value, inverse, gain, grad):
    scaled = grad * gain
    inner = jnp.mean(scaled * value, axis=-1, keepdims=True)
    return inverse * (scaled - value * (inverse * inverse * inner))


def doc_positions(segment):
    index = jnp.arange(segment.shape[0], dtype=jnp.int32)
    change = jnp.concatenate([jnp.ones((1,), dtype=jnp.bool_), segment[1:] != segment[:-1]])
    start = lax.cummax(jnp.where(change, index, 0), axis=0)
    return index - start


def rope_tables(position, width):
    steps = jnp.arange(width // 2, dtype=f32) * (2.0 / width)
    rates = jnp.exp(-steps * math.log(rope_base))
    angle = position.astype(f32)[:, None] * rates[None, :]
    angle = jnp.concatenate([angle, angle], axis=-1)
    return (jnp.cos(angle), jnp.sin(angle))


def norm_rope(value, gain, cosine, sine):
    inverse = lax.rsqrt(jnp.mean(value * value, axis=1, keepdims=True) + epsilon)
    value = value * inverse * gain
    return value * cosine + pltpu.roll(value, HD // 2, 1) * sine


def norm_rope_back(value, gain, cosine, sine, grad):
    inverse = lax.rsqrt(jnp.mean(value * value, axis=1, keepdims=True) + epsilon)
    grad = grad * cosine + pltpu.roll(grad * sine, HD // 2, 1)
    normal = value * inverse
    scaled = grad * gain
    inner = jnp.mean(scaled * normal, axis=1, keepdims=True)
    return inverse * (scaled - normal * inner), jnp.sum(grad * normal, axis=0, keepdims=True)


def kept_scores(query, keys, q_seg, k_seg, start):
    scores = dot(query, keys, ((1,), (1,))) * (1.0 / math.sqrt(HD))
    q_index = start + lax.broadcasted_iota(jnp.int32, scores.shape, 0)
    k_index = lax.broadcasted_iota(jnp.int32, scores.shape, 1)
    keep = (jnp.abs(q_index - k_index) <= HALF) & (q_seg == k_seg)
    return jnp.where(keep, scores, -1e30)


BIG = 100 * 1024 * 1024 // 2


def forward_kernel(
    heads, proj, cosine, sine, seg_column, seg_row, gains, mixed, query, keys, values, lses
):
    ranks, _, rows, _ = proj.shape
    length = ranks * rows
    q_block = 2 * rows
    k_seg = seg_row[0]
    for head in range(heads):
        at = slice(head * HD, (head + 1) * HD)

        def raw(part):
            first = (part * heads + head) * HD
            return proj[:, 0, :, first : first + HD].reshape(length, HD)

        query[0, :, at] = norm_rope(raw(0), gains[0:1], cosine[0], sine[0]).astype(bf16)
        keys[0, :, at] = norm_rope(raw(1), gains[1:2], cosine[0], sine[0]).astype(bf16)
        values[0, :, at] = raw(2).astype(bf16)

        @pl.loop(0, length // q_block)
        def one_block(number, head=head, at=at):
            start = pl.multiple_of(number * q_block, q_block)
            here = pl.ds(start, q_block)
            scores = kept_scores(
                query[0, here, at], keys[0, :, at], seg_column[0, here], k_seg, start
            )
            top = jnp.max(scores, axis=1, keepdims=True)
            weights = jnp.exp(scores - top)
            total = jnp.sum(weights, axis=1, keepdims=True)
            lses[0, head, here] = top + jnp.log(total)
            weights = (weights * (1.0 / total)).astype(bf16)
            result = dot(weights, values[0, :, at]).astype(bf16)
            mixed[pl.ds(number * 2, 2), 0, :, at] = result.reshape(2, rows, HD)


def backward_kernel(
    heads, proj, cosine, sine, seg_column, seg_row, gains, query, keys, values, lses, grad_mixed,
    grad_proj, grad_gains, grad_q, grad_k, grad_v,
):
    ranks, _, rows, _ = proj.shape
    length = ranks * rows
    q_block = 2 * rows
    k_seg = seg_row[0]
    scale = 1.0 / math.sqrt(HD)
    sum_q = jnp.zeros((1, HD), f32)
    sum_k = jnp.zeros((1, HD), f32)
    for head in range(heads):
        at = slice(head * HD, (head + 1) * HD)
        grad_k[...] = jnp.zeros_like(grad_k)
        grad_v[...] = jnp.zeros_like(grad_v)

        @pl.loop(0, length // q_block)
        def one_block(number, head=head, at=at):
            start = pl.multiple_of(number * q_block, q_block)
            here = pl.ds(start, q_block)
            q_rows = query[0, here, at]
            g_rows = grad_mixed[here, at]
            k_all = keys[0, :, at]
            scores = kept_scores(q_rows, k_all, seg_column[0, here], k_seg, start)
            weights = jnp.exp(scores - lses[0, head, here])
            grad_weights = dot(g_rows, values[0, :, at], ((1,), (1,)))
            delta = jnp.sum(weights * grad_weights, axis=1, keepdims=True)
            grad_scores = (weights * (grad_weights - delta)).astype(bf16)
            grad_q[here] = dot(grad_scores, k_all) * scale
            grad_k[...] += dot(grad_scores, q_rows, ((0,), (0,)))
            grad_v[...] += dot(weights.astype(bf16), g_rows, ((0,), (0,)))

        def rounded(value):
            return value.astype(bf16).astype(f32)

        def raw(part):
            first = (part * heads + head) * HD
            return proj[:, 0, :, first : first + HD].reshape(length, HD)

        def put(part, value):
            first = (part * heads + head) * HD
            grad_proj[:, :, first : first + HD] = value.astype(bf16).reshape(ranks, rows, HD)

        back_q, gain_q = norm_rope_back(
            raw(0), gains[0:1], cosine[0], sine[0], rounded(grad_q[...])
        )
        back_k, gain_k = norm_rope_back(
            raw(1), gains[1:2], cosine[0], sine[0], rounded(grad_k[...] * scale)
        )
        sum_q, sum_k = sum_q + gain_q, sum_k + gain_k
        put(0, back_q)
        put(1, back_k)
        put(2, grad_v[...])
    grad_gains[0:1] = sum_q
    grad_gains[1:2] = sum_k


def fixed(shape):
    return pl.BlockSpec(shape, lambda *_: (0,) * len(shape), pipeline_mode=pl.Buffered(1))


def leading(shape):
    return pl.BlockSpec((1,) + shape[1:], lambda i: (i,) + (0,) * (len(shape) - 1))


def params():
    return pltpu.CompilerParams(vmem_limit_bytes=BIG)


def cost(products):
    return pl.CostEstimate(flops=20 * products, bytes_accessed=0, transcendentals=0)


def out(shape, dtype=bf16):
    return jax.ShapeDtypeStruct(shape, dtype)


def attention_forward(proj, cosine, sine, seg_column, seg_row, gains):
    ranks, micro, rows, width = proj.shape
    length = ranks * rows
    width = width // 3
    heads = width // HD
    part = out((micro, length, width))
    by_rank = lambda n: pl.BlockSpec((ranks, 1, rows, n), lambda i: (0, i, 0, 0))
    lses = out((micro, heads, length, 1), f32)
    return pl.pallas_call(
        lambda *refs: forward_kernel(heads, *refs),
        grid=(micro,),
        in_specs=[by_rank(3 * width)]
        + [leading(v.shape) for v in (cosine, sine, seg_column, seg_row)]
        + [fixed(gains.shape)],
        out_specs=[by_rank(width)] + [leading(part.shape)] * 3 + [leading(lses.shape)],
        out_shape=[out((ranks, micro, rows, width)), part, part, part, lses],
        compiler_params=params(),
    )(proj, cosine, sine, seg_column, seg_row, gains)


def attention_backward(
    step, proj, cosine, sine, seg_column, seg_row, gains, query, keys, values, lses, grad_mixed
):
    ranks, micro, rows, width = proj.shape
    length = ranks * rows
    heads = width // 3 // HD

    def part(value):
        return pl.BlockSpec((1,) + value.shape[1:], lambda i: (step,) + (0,) * (value.ndim - 1))

    return pl.pallas_call(
        lambda *refs: backward_kernel(heads, *refs),
        grid=(1,),
        in_specs=[pl.BlockSpec((ranks, 1, rows, width), lambda i: (0, step, 0, 0))]
        + [part(v) for v in (cosine, sine, seg_column, seg_row)]
        + [fixed(gains.shape)]
        + [part(v) for v in (query, keys, values, lses)]
        + [fixed(grad_mixed.shape)],
        out_specs=[fixed((ranks, rows, width)), fixed((2, HD))],
        out_shape=[out((ranks, rows, width)), out((2, HD), f32)],
        scratch_shapes=[pltpu.VMEM((length, HD), f32)] * 3,
        compiler_params=params(),
    )(
        proj, cosine, sine, seg_column, seg_row, gains, query, keys, values, lses, grad_mixed
    )


def project(micro, tokens, gain, slab):
    ranks, count, _ = tokens.shape
    rows = count // micro
    width = slab.shape[1] - PAD

    def kernel(value, gain, weight, normed, proj):
        value = value[0].astype(f32)
        result = (value * inverse_rms(value) * gain[...]).astype(bf16)
        normed[...] = result.reshape(micro, 1, rows, D)
        proj[0] = dot(result, weight[:, :width])

    return pl.pallas_call(
        kernel,
        grid=(ranks,),
        in_specs=[leading((ranks, count, D)), fixed((1, D)), fixed(slab.shape)],
        out_specs=[
            pl.BlockSpec((micro, 1, rows, D), lambda i: (0, i, 0, 0)),
            leading((ranks, count, width)),
        ],
        out_shape=[out((micro, ranks, rows, D)), out((ranks, count, width), f32)],
        compiler_params=params(),
    )(tokens, gain, slab)


TILE = 512


def tiles(count):
    return pl.loop(0, count // TILE)


def tile(number):
    return pl.ds(pl.multiple_of(number * TILE, TILE), TILE)


HBM = pl.BlockSpec(memory_space=pl.ANY)


def copies(pairs, sems):
    started = [
        pltpu.make_async_copy(source, target, sems.at[place])
        for place, (source, target) in enumerate(pairs)
    ]
    for copy in started:
        copy.start()

    def wait():
        for copy in started:
            copy.wait()

    return wait


def plane_pairs(plane, pieces, target):
    planes = len(pieces)
    rows = target.shape[0] // planes
    return [
        (piece, target.at[pl.ds(lax.bitwise_xor(plane, jnp.int32(step)) * rows, rows)])
        for step, piece in enumerate(pieces)
    ]


def out_weight_pairs(plane, planes, gathered, target):
    ranks = gathered.shape[0]
    rows = D // (planes * ranks)
    return [
        (
            gathered.at[rank, pl.ds(step * rows, rows)],
            target.at[
                pl.ds((lax.bitwise_xor(plane, jnp.int32(step)) * ranks + rank) * rows, rows)
            ],
        )
        for rank in range(ranks)
        for step in range(planes)
    ]


def route(plane, planes, mixed, tokens, gathered, gain, router, routes, experts):
    count = tokens.shape[0]
    pieces = planes * gathered.shape[0]

    def kernel(
        plane, mixed, tokens, gathered, gain, router, routes, hidden, payload, gates,
        out_weight, sems,
    ):
        copies(out_weight_pairs(plane[0], planes, gathered, out_weight), sems)()

        @tiles(D)
        def _(number):
            at = tile(number)
            hidden[:, at] = tokens[:, at].astype(f32) + dot(mixed[...], out_weight[:, at])

        value = hidden[...]
        normed = (value * inverse_rms(value) * gain[...]).astype(bf16)
        payload[:, :D] = normed
        logits = dot(normed, router[...])
        column = lax.broadcasted_iota(jnp.int32, logits.shape, 1)
        routed = column == routes[:, 0:1]
        for choice in range(1, TOP):
            routed = routed | (column == routes[:, choice : choice + 1])
        logits = jnp.where(routed, logits, -1e30)
        weights = jnp.exp(logits - jnp.max(logits, axis=1, keepdims=True))
        weights = jnp.where(routed, weights, 0.0)
        weights = weights / jnp.sum(weights, axis=1, keepdims=True)
        gates[...] = weights
        high = weights.astype(bf16).astype(f32)
        payload[:, D:] = (high + pltpu.roll(weights - high, experts, 1)).astype(bf16)

    shapes = [out((count, D), f32), out((count, D + PAD)), out((count, PAD), f32)]
    return pl.pallas_call(
        kernel,
        grid_spec=pltpu.PrefetchScalarGridSpec(
            num_scalar_prefetch=1,
            grid=(1,),
            in_specs=[
                HBM if value is gathered else fixed(value.shape)
                for value in (mixed, tokens, gathered, gain, router, routes)
            ],
            out_specs=[fixed(shape.shape) for shape in shapes],
            scratch_shapes=[pltpu.VMEM((D, D), bf16), pltpu.SemaphoreType.DMA((pieces,))],
        ),
        out_shape=shapes,
        compiler_params=params(),
    )(plane, mixed, tokens, gathered, gain, router, routes)


def lane(value, number):
    column = lax.broadcasted_iota(jnp.int32, value.shape, 1)
    return jnp.sum(jnp.where(column == number, value.astype(f32), 0.0), axis=1, keepdims=True)


def one_hot(slot, slots):
    place = lax.broadcasted_iota(jnp.int32, (slots, slot.shape[1]), 0).astype(f32)
    return (place == slot).astype(bf16)


def expert_forward(where, payload, upstream, in_pieces, slots, experts):
    ranks, share, micro, rows, _ = payload.shape
    count = share * rows
    block = 2 * slots

    planes = len(in_pieces)

    def kernel(where, payload, upstream, *refs):
        (
            rows_in, tail, both, active, grad_produced, up_rows, places, in_weight, sems
        ) = refs[planes:]
        number = where[0]

        @pl.when((pl.program_id(0) == 0) & (pl.program_id(1) == 0))
        def _():
            copies(plane_pairs(where[1], refs[:planes], in_weight), sems)()

        for part in range(2):
            here = slice(part * slots, (part + 1) * slots)
            value = payload[part].reshape(count, D + PAD)
            marks = value[:, D:]
            first = lax.broadcasted_iota(jnp.int32, (8, PAD), 1) == number
            taken = dot(first.astype(bf16), marks, ((1,), (1,))) > 0.0
            before = lax.broadcasted_iota(jnp.int32, (count, count), 0)
            behind = lax.broadcasted_iota(jnp.int32, (count, count), 1)
            slot = dot(taken.astype(bf16), (before < behind).astype(bf16))
            select = one_hot(jnp.where(taken, slot, -1.0)[0:1], slots)
            wide = jnp.broadcast_to(lane(marks, number) > 0.0, (count, PAD))
            slot = dot((before > behind).astype(bf16), wide.astype(bf16))
            places[0, 0, part] = jnp.where(wide, slot, -1.0)
            rows_in[0, 0, here] = dot(select, value[:, :D]).astype(bf16)
            marks = dot(select, marks)
            tail[0, 0, here] = marks
            gate = lane(marks, number) + lane(marks, experts + number)
            picked = dot(select, upstream[part].reshape(count, D))
            up_rows[0, 0, here] = picked.astype(bf16)
            grad_produced[0, 0, here] = (gate * picked).astype(bf16)

        for number in range(FF // TILE):
            at = slice(number * TILE, (number + 1) * TILE)
            more = slice(FF + number * TILE, FF + (number + 1) * TILE)
            gate_part = dot(rows_in[0, 0], in_weight[:, at])
            up_part = dot(rows_in[0, 0], in_weight[:, more])
            both[0, 0, :, at] = gate_part
            both[0, 0, :, more] = up_part
            active[0, 0, :, at] = (
                gate_part / (1.0 + jnp.exp(-gate_part)) * up_part
            ).astype(bf16)

    def tokens_spec(width):
        return pl.BlockSpec((2, share, 1, rows, width), lambda m, b, _: (b, 0, m, 0, 0))

    pairs = ranks // 2
    shapes = [
        out((micro, pairs, block, D)),
        out((micro, pairs, block, PAD), f32),
        out((micro, pairs, block, 2 * FF), f32),
        out((micro, pairs, block, FF)),
        out((micro, pairs, block, D)),
        out((micro, pairs, block, D)),
        out((micro, pairs, 2, count, PAD), f32),
    ]
    return pl.pallas_call(
        kernel,
        grid_spec=pltpu.PrefetchScalarGridSpec(
            num_scalar_prefetch=1,
            grid=(micro, pairs),
            in_specs=[tokens_spec(D + PAD), tokens_spec(D)] + [HBM] * planes,
            out_specs=[
                pl.BlockSpec(
                    (1, 1) + s.shape[2:], lambda m, b, _, n=len(s.shape): (m, b) + (0,) * (n - 2)
                )
                for s in shapes
            ],
            scratch_shapes=[pltpu.VMEM((D, 2 * FF), bf16), pltpu.SemaphoreType.DMA((planes,))],
        ),
        out_shape=shapes,
        cost_estimate=cost(micro * pairs * block * D * (2 * FF + 2 * count)),
        compiler_params=params(),
    )(where, payload, upstream, *in_pieces)


def expert_backward(
    step, where, tail, both, active, grad_produced, up_rows, places, in_pieces, out_pieces,
    share, rows, experts,
):
    pairs, block = tail.shape[1:3]
    slots = block // 2
    count = places.shape[3]

    planes = len(in_pieces)

    def kernel(where, tail, both, active, grad_produced, up_rows, places, *refs):
        keep, give, grad_tokens, grad_both, in_weight, out_weight, sems = refs[2 * planes :]
        number = where[0]
        odd = where[2] == 1

        @pl.when(pl.program_id(0) == 0)
        def _():
            copies(
                plane_pairs(where[1], refs[:planes], in_weight)
                + plane_pairs(where[1], refs[planes : 2 * planes], out_weight),
                sems,
            )()

        gate = lane(tail[0, 0], number) + lane(tail[0, 0], experts + number)
        place = lax.broadcasted_iota(jnp.int32, (count, slots), 1).astype(f32)
        selects = [(places[0, 0, part][:, 0:1] == place).astype(bf16) for part in range(2)]

        def spread(value):
            return [
                dot(selects[part], value[part * slots : (part + 1) * slots])
                .astype(bf16)
                .reshape(share, rows, -1)
                for part in range(2)
            ]

        grad_gate = jnp.zeros((block, 1), f32)
        for tile in range(D // TILE):
            at = slice(tile * TILE, (tile + 1) * TILE)
            produced = dot(active[0, 0], out_weight[:, at]).astype(bf16).astype(f32)
            even_rank, odd_rank = spread((gate * produced).astype(bf16))
            keep[0, :, :, at] = jnp.where(odd, odd_rank, even_rank)
            give[0, :, :, at] = jnp.where(odd, even_rank, odd_rank)
            grad_gate = grad_gate + jnp.sum(
                up_rows[0, 0, :, at].astype(f32) * produced, axis=1, keepdims=True
            )

        for tile in range(FF // TILE):
            at = slice(tile * TILE, (tile + 1) * TILE)
            more = slice(FF + tile * TILE, FF + (tile + 1) * TILE)
            grad_active = dot(grad_produced[0, 0], out_weight[at, :], ((1,), (1,)))
            grad_active = grad_active.astype(bf16).astype(f32)
            gate_part = both[0, 0, :, at]
            up_part = both[0, 0, :, more]
            sigma = 1.0 / (1.0 + jnp.exp(-gate_part))
            grad_both[0, :, at] = (
                grad_active * up_part * (sigma * (1.0 + gate_part * (1.0 - sigma)))
            ).astype(bf16)
            grad_both[0, :, more] = (grad_active * (gate_part * sigma)).astype(bf16)

        for tile in range(D // TILE):
            at = slice(tile * TILE, (tile + 1) * TILE)
            grad_rows = dot(grad_both[0], in_weight[at, :], ((1,), (1,))).astype(bf16)
            grad_tokens[0, :, :, at], grad_tokens[1, :, :, at] = spread(grad_rows)

        high = grad_gate.astype(bf16).astype(f32)
        column = lax.broadcasted_iota(jnp.int32, (block, PAD), 1)
        extra = jnp.where(column == number, high, 0.0)
        extra = jnp.where(column == experts + number, grad_gate - high, extra)
        grad_tokens[0, :, :, D:], grad_tokens[1, :, :, D:] = spread(extra.astype(bf16))

    def part(value):
        return pl.BlockSpec(
            (1, 1) + value.shape[2:], lambda b, _: (step, b) + (0,) * (value.ndim - 2)
        )

    def tokens_spec(count, width):
        return pl.BlockSpec((count, share, rows, width), lambda b, _: (b, 0, 0, 0))

    return pl.pallas_call(
        kernel,
        grid_spec=pltpu.PrefetchScalarGridSpec(
            num_scalar_prefetch=1,
            grid=(pairs,),
            in_specs=[part(v) for v in (tail, both, active, grad_produced, up_rows, places)]
            + [HBM] * (2 * planes),
            out_specs=[
                tokens_spec(1, D),
                tokens_spec(1, D),
                tokens_spec(2, D + PAD),
                pl.BlockSpec((1, block, 2 * FF), lambda b, _: (b, 0, 0)),
            ],
            scratch_shapes=[
                pltpu.VMEM((D, 2 * FF), bf16),
                pltpu.VMEM((FF, D), bf16),
                pltpu.SemaphoreType.DMA((2 * planes,)),
            ],
        ),
        out_shape=[
            out((pairs, share, rows, D)),
            out((pairs, share, rows, D)),
            out((2 * pairs, share, rows, D + PAD)),
            out((pairs, block, 2 * FF)),
        ],
        cost_estimate=cost(pairs * block * D * (4 * FF + 2 * count)),
        compiler_params=params(),
    )(
        where, tail, both, active, grad_produced, up_rows, places, *in_pieces, *out_pieces
    )


def weight_gradient(where, planes, left, rights, tail=None, first=0, steps=None, shift=False):
    steps = planes if steps is None else steps
    count, width = left.shape
    parts = len(rights)
    part_rows = count // parts
    columns = rights[0].shape[1]
    width = width // planes
    step = min(TILE, columns & -columns)
    tails = [] if tail is None else [tail]
    whole = columns + sum(value.shape[1] for value in tails)

    def of_plane(i, where):
        return (where[1] + first + i) % planes if shift else lax.bitwise_xor(where[1], first + i)

    def kernel(where, left, *refs):
        rights, tails, targets = refs[:parts], refs[parts:-steps], refs[-steps:]

        def fill(target):
            for value in tails:
                target[:, columns:] = value[...]
            for number in range(columns // step):
                at = slice(number * step, (number + 1) * step)
                target[:, at] = sum(
                    dot(left[part * part_rows : (part + 1) * part_rows], right[:, at], ((0,), (0,)))
                    for part, right in enumerate(rights)
                ).astype(bf16)

        for number, target in enumerate(targets):
            pl.when(pl.program_id(0) == number)(lambda target=target: fill(target))

    return pl.pallas_call(
        kernel,
        grid_spec=pltpu.PrefetchScalarGridSpec(
            num_scalar_prefetch=1,
            grid=(steps,),
            in_specs=[pl.BlockSpec((count, width), lambda i, where: (0, of_plane(i, where)))]
            + [fixed(right.shape) for right in rights]
            + [
                pl.BlockSpec((width, value.shape[1]), lambda i, where: (of_plane(i, where), 0))
                for value in tails
            ],
            out_specs=[fixed((width, whole))] * steps,
        ),
        out_shape=[out((width, whole))] * steps,
        cost_estimate=cost(0 if tails else count * steps * width * columns),
        compiler_params=params(),
    )(where, left, *rights, *tails)


def hidden_backward(
    step, plane, planes, parts, hidden, gates, upstream, gain, router, gathered, experts
):
    first = parts[0].shape
    count = first[1]
    terms = len(parts)

    def kernel(plane, *refs):
        parts = refs[:terms]
        hidden, gates, upstream, gain, router, gathered = refs[terms : terms + 6]
        (
            grad_hidden, grad_branch, grad_mixed, grad_logits, grad_gain, out_weight, sems
        ) = refs[terms + 6 :]
        wait = copies(out_weight_pairs(plane[0], planes, gathered, out_weight), sems)
        returned = sum(part[...].astype(f32) for part in parts[1:]) + parts[0][0].astype(f32)
        tail = returned[:, D:]
        grad_gates = gates[...] * (tail + pltpu.roll(tail, PAD - experts, 1))
        logits = grad_gates - gates[...] * jnp.sum(grad_gates, axis=1, keepdims=True)
        logits = logits.astype(bf16)
        grad_logits[...] = logits
        grad_normed = returned[:, :D] + dot(logits, router[...], ((1,), (1,)))
        value = hidden[...]
        inverse = inverse_rms(value)
        grad_gain[...] = jnp.sum(grad_normed * value * inverse, axis=0, keepdims=True)
        grad = upstream[...].astype(f32) + rms_backward(value, inverse, gain[...], grad_normed)
        grad_hidden[...] = grad
        grad_branch[...] = grad.astype(bf16)
        wait()

        @tiles(D)
        def _(number):
            at = tile(number)
            grad_mixed[:, at] = dot(grad_branch[...], out_weight[at, :], ((1,), (1,))).astype(bf16)

    shapes = [
        out((count, D), f32), out((count, D)), out((count, D)), out((count, PAD)),
        out((1, D), f32),
    ]
    args = (*parts, hidden, gates, upstream, gain, router, gathered)

    def spec(value):
        if value is gathered:
            return HBM
        if value is parts[0]:
            return pl.BlockSpec((1,) + first[1:], lambda *_: (0, 0, 0))
        if any(value is rows for rows in (hidden, gates, upstream)):
            return pl.BlockSpec((count, value.shape[1]), lambda *_: (step, 0))
        return fixed(value.shape)

    return pl.pallas_call(
        kernel,
        grid_spec=pltpu.PrefetchScalarGridSpec(
            num_scalar_prefetch=1,
            grid=(1,),
            in_specs=[spec(value) for value in args],
            out_specs=[fixed(shape.shape) for shape in shapes],
            scratch_shapes=[
                pltpu.VMEM((D, D), bf16),
                pltpu.SemaphoreType.DMA((planes * gathered.shape[0],)),
            ],
        ),
        out_shape=shapes,
        compiler_params=params(),
    )(plane, *args)


def project_backward(step, grad_proj, tokens, slab):
    ranks, rows, _ = grad_proj.shape
    width = slab.shape[1] - PAD

    def kernel(grad_proj, tokens, weight, grad_normed, grad_gain):
        value = tokens[...].reshape(2 * rows, D).astype(f32)
        inverse = inverse_rms(value)
        grad = dot(grad_proj[...].reshape(2 * rows, width), weight[:, :width], ((1,), (1,)))
        grad_normed[...] = grad.astype(bf16)

        @pl.when(pl.program_id(0) == 0)
        def _():
            grad_gain[...] = jnp.zeros_like(grad_gain)

        grad_gain[...] += jnp.sum(grad * value * inverse, axis=0, keepdims=True)

    return pl.pallas_call(
        kernel,
        grid=(ranks // 2,),
        in_specs=[
            pl.BlockSpec((2, rows, width), lambda i: (i, 0, 0)),
            pl.BlockSpec((2, rows, D), lambda i: (i, step, 0)),
            fixed(slab.shape),
        ],
        out_specs=[pl.BlockSpec((2 * rows, D), lambda i: (i, 0)), fixed((1, D))],
        out_shape=[out((ranks * rows, D)), out((1, D), f32)],
        compiler_params=params(),
    )(grad_proj, tokens, slab)


def cut_heads(weight, tail, ranks):
    rows = weight.shape[0]
    width = D // ranks

    def kernel(weight, tail, target):
        for rank in range(ranks):
            for part in range(3):
                at = part * D + rank * width
                target[rank, :, part * width : (part + 1) * width] = weight[:, at : at + width]
            target[rank, :, 3 * width :] = tail[...]

    return pl.pallas_call(
        kernel,
        out_shape=out((ranks, rows, 3 * width + PAD)),
        compiler_params=params(),
    )(weight, tail)


def unpack(packed, count):
    ranks, rows, columns = packed.shape
    width = (columns - PAD) // 3

    def kernel(packed, main, small):
        for rank in range(ranks):
            for part in range(3):
                at = part * D + rank * width
                main[:, at : at + width] = packed[rank, :, part * width : (part + 1) * width].astype(
                    f32
                )
        tails = sum(packed[rank, :, 3 * width :].astype(f32) for rank in range(ranks))
        small[...] = tails + pltpu.roll(tails, PAD - count, 1)

    return pl.pallas_call(
        kernel,
        out_shape=[out((rows, 3 * D), f32), out((rows, PAD), f32)],
        compiler_params=params(),
    )(packed)


def shift_rep(value, step):
    count = lax.axis_size("rep")
    return lax.ppermute(value, "rep", [(i, (i + step) % count) for i in range(count)])


def cross_rep(value, bits):
    return lax.ppermute(value, "rep", [(i, i ^ bits) for i in range(lax.axis_size("rep"))])


def after(value, *others):
    return lax.optimization_barrier((value,) + others)[0]


def two_parts(value):
    high = lax.reduce_precision(value, 8, 7)
    return high.astype(bf16), (value - high).astype(bf16)


def ring_rep(value, *work):
    count = lax.axis_size("rep")
    rank = lax.axis_index("rep")
    rows = value.shape[0]
    full = jnp.zeros((count * rows,) + value.shape[1:], value.dtype)
    full = lax.dynamic_update_slice_in_dim(full, value, rank * rows, 0)
    for step in range(1, count):
        value, work = lax.optimization_barrier((value, work)) if step == count - 1 else (value, work)
        value = shift_rep(value, 1)
        full = lax.dynamic_update_slice_in_dim(full, value, (rank - step) % count * rows, 0)
    return full, work


def on_device(
    tokens, cotangent, w_qkv, w_o, w_router, norm_gains, qk_gain, w_in, w_out, segments, routes
):
    planes = lax.axis_size("rep")
    ranks = lax.axis_size("ep")
    plane = lax.axis_index("rep")
    rank = lax.axis_index("ep")
    share = w_in.shape[0]
    own = plane % share
    experts = share * ranks
    where = jnp.stack([rank * share + own, plane, rank % 2]).astype(jnp.int32)
    micro = segments.shape[1]
    mine = tokens.shape[0]
    rows = mine // micro
    length = rows * ranks
    capacity = rows * TOP * 17 // (16 * experts)
    slots = -(-share * capacity // 16) * 16
    width = HEADS // ranks * HD
    qk_gains = qk_gain.astype(f32).reshape(2, HD)
    dense_rows = w_qkv.shape[0]

    def exchange(value, step):
        pairs = [(i, i // share * share + (i % share + step) % share) for i in range(planes)]
        return lax.ppermute(value, "rep", pairs)

    def with_group(value):
        return jnp.stack([value] + [exchange(value, step) for step in range(1, share)])

    def gather_ranks(value):
        return lax.all_gather(value, "ep", axis=0)

    assert planes & (planes - 1) == 0 and share & (share - 1) == 0
    last_step = planes - 1
    in_parts, out_parts = (
        {
            step: lax.dynamic_index_in_dim(weight, own ^ step % share, 0, keepdims=False)
            for step in range(planes)
        }
        for weight in (w_in, w_out)
    )

    def send(parts, steps):
        return {step: cross_rep(parts[step], step) for step in steps}

    stream = gather_ranks(tokens)
    out_rows = [w_o] + [cross_rep(w_o, step) for step in range(1, planes)]
    upstream_group = with_group(cotangent)
    slab = cut_heads(
        w_qkv,
        jnp.concatenate(
            [
                w_router,
                norm_gains.reshape(dense_rows, 2),
                jnp.zeros((dense_rows, PAD - experts - 2), bf16),
            ],
            axis=1,
        ),
        ranks,
    )
    slab = lax.all_to_all(slab, "ep", split_axis=0, concat_axis=0, tiled=True)
    slab = slab.reshape(ranks * dense_rows, 3 * width + PAD)
    out_rows, upstream_group, slab = lax.optimization_barrier((out_rows, upstream_group, slab))
    gathered = gather_ranks(jnp.concatenate(out_rows, axis=0))
    segment = segments[0]
    cosine, sine = jax.vmap(lambda one: rope_tables(doc_positions(one), HD))(segment)
    sine = jnp.where(jnp.arange(HD) < HD // 2, -sine, sine)
    tables = (cosine, sine, segment[:, :, None], segment[:, None, :], qk_gains)
    slab, (tables, in_parts, out_parts) = ring_rep(slab, tables, in_parts, out_parts)
    router = slab[:, 3 * width :]
    gain_pair = router[:, experts : experts + 2].reshape(-1).astype(f32)
    first_gain = gain_pair[None, :D]
    second_gain = gain_pair[None, D:]
    in_parts, out_parts, upstream_group, stream = after(
        (in_parts, out_parts, upstream_group, stream), slab
    )
    in_pieces = {0: in_parts[0], **send(in_parts, range(last_step - 1, 0, -1))}
    upstream_all = gather_ranks(upstream_group)

    normed, proj = project(micro, stream, first_gain, slab)
    proj = proj.reshape(ranks, micro, rows, 3 * width)
    mixed_h, query, keys, values, lses = attention_forward(proj, *tables)
    mixed = lax.all_to_all(mixed_h, "ep", split_axis=0, concat_axis=3, tiled=True)
    mixed = mixed.reshape(mine, D)
    hidden, payload, gates = route(
        where[1:2], planes, mixed, tokens, gathered, second_gain, router, routes, experts
    )
    normed_two = payload[:, :D]
    payload, in_pieces = lax.optimization_barrier((payload, in_pieces))
    payload = with_group(payload)
    payload, in_parts, out_parts = lax.optimization_barrier((payload, in_parts, out_parts))
    in_pieces.update(send(in_parts, [last_step]))
    in_pieces, out_parts = lax.optimization_barrier((in_pieces, out_parts))
    out_pieces = {0: out_parts[0], **send(out_parts, range(1, planes))}
    in_pieces = [in_pieces[step] for step in range(planes)]
    out_pieces = [out_pieces[step] for step in range(planes)]
    payload = gather_ranks(payload)

    shape = (ranks, share, micro, rows, -1)
    rows_in, tail, both, active, grad_produced, up_rows, places = expert_forward(
        where, payload.reshape(shape), upstream_all.reshape(shape), in_pieces, slots, experts
    )
    in_rows = micro * ranks * slots
    out_cut = weight_gradient(
        where, planes, active.reshape(in_rows, FF), [grad_produced.reshape(in_rows, D)]
    )

    def sum_rep(parts, shift=False):
        sums = [
            sum(parts[step].astype(f32) for step in range(first, planes, share))
            for first in range(share)
        ]
        return jnp.stack(
            [
                sum(
                    jnp.where(((own - step) % share if shift else own ^ step) == j, sums[step], 0.0)
                    for step in range(share)
                )
                for j in range(share)
            ]
        )

    tail, out_cut, out_pieces = lax.optimization_barrier((tail, out_cut, out_pieces))
    first = cross_rep(out_cut[1][:16], 1)
    tail, out_cut, first = lax.optimization_barrier((tail, out_cut, first))
    out_sent = send([out_cut[0], out_cut[1][16:], *out_cut[2:]], range(1, planes))
    back = []
    returned = []

    def scatter_ranks(value):
        return lax.psum_scatter(value, "ep", scatter_dimension=0)

    def exchange_back(value):
        return [value] + [exchange(value[step], share - step) for step in range(1, share)]

    for step in range(micro):
        back.append(
            expert_backward(
                step, where, tail, both, active, grad_produced, up_rows, places, in_pieces,
                out_pieces, share, rows, experts,
            )
        )
        returned.append(scatter_ranks(back[step][2]))
        if step == 0:
            tail, out_sent[last_step] = after((tail, out_sent[last_step]), back[step][2])
        else:
            tail = after(tail, back[step][2])
    rows_in = after(rows_in, tail)
    rows_flat = rows_in.reshape(in_rows, D)
    grads_flat = [back[step][3].reshape(in_rows // micro, 2 * FF) for step in range(micro)]
    (in_near,) = weight_gradient(
        where, planes, rows_flat, grads_flat, first=1, steps=1, shift=True
    )
    rows_flat, in_near = lax.optimization_barrier((rows_flat, in_near))
    *in_rest, in_back, in_own = weight_gradient(
        where, planes, rows_flat, grads_flat, first=2, steps=last_step, shift=True
    )
    in_sent = {0: in_own, 1: shift_rep(in_near, 1)}

    def cuts(value, *places):
        ends = [-(-value.shape[0] * place // 512) * 16 for place in (0, *places, 32)]
        return [value[start:end] for start, end in zip(ends, ends[1:])]

    def swap(value, step):
        return lax.ppermute(value, "ep", [(i, i ^ step) for i in range(ranks)])

    bits = list(range((ranks // 2).bit_length() - 1))

    def cut_pairs(number, value, phase):
        way = bits if number % 2 == 0 else bits[::-1]
        bit = way[phase]
        low = 2 ** sum(other < bit for other in way[phase:])
        value = value.reshape((-1, 2, low) + value.shape[1:])
        side = rank // 2 // 2**bit % 2
        return [
            lax.dynamic_index_in_dim(value, which, 1, keepdims=False).reshape((-1,) + value.shape[3:])
            for which in (side, 1 - side)
        ]

    def pair_sum(number, keep, give):
        got = swap(give, 1)
        return [
            total(parts).astype(bf16)
            for parts in zip(cut_pairs(number, keep, 0), cut_pairs(number, got, 0))
        ]

    def halve(number, halves, phase):
        return halves[0], swap(halves[1], 2 * 2 ** (bits if number % 2 == 0 else bits[::-1])[phase])

    def total(parts):
        return sum(part.astype(f32) for part in parts)

    grad_inputs, branches, logit_grads, grad_projs = [], [], [], []
    gain_two_sum = gain_one_sum = qk_sum = 0.0
    in_rest, in_back, out_sent, in_sent = lax.optimization_barrier(
        (in_rest, in_back, out_sent, in_sent)
    )
    mixtures = [part[:2] for part in back]
    for step in range(micro):
        parts = after(returned[step], [one[1] for one in grad_inputs])
        parts, in_sent = lax.optimization_barrier((parts, in_sent))
        if step == micro - 1:
            mixtures = after(mixtures, parts)
            crossed = [halve(number, value, 0) for number, value in enumerate(mixtures)]
        parts = exchange_back(parts)
        parts, in_rest, in_back, mixtures = lax.optimization_barrier(
            (parts, in_rest, in_back, mixtures)
        )
        if step == 0:
            mixtures = [pair_sum(number, *part) for number, part in enumerate(mixtures)]
            in_sent[last_step] = shift_rep(in_back, last_step)
        if step == micro - 1:
            rest = [cuts(value, 20, 28) for value in in_rest]
            rest_sent = [[shift_rep(part[0], i + 2) for i, part in enumerate(rest)]]
        grad_hidden, grad_branch, grad_mixed, grad_logits, gain_two = hidden_backward(
            step, where[1:2], planes, parts, hidden, gates, cotangent, second_gain, router, gathered,
            experts,
        )
        branches.append(grad_branch)
        logit_grads.append(grad_logits)
        gain_two_sum = gain_two_sum + gain_two
        if step == micro - 1:
            out_sum = dot(mixed, jnp.concatenate(branches, axis=0), ((0,), (0,))).astype(bf16)
            out_sum = out_sum.reshape(planes, ranks, dense_rows, D).transpose(1, 0, 2, 3)
        grad_mixed = lax.all_to_all(grad_mixed, "ep", split_axis=1, concat_axis=0, tiled=True)
        grad_mixed, mixtures = lax.optimization_barrier((grad_mixed, mixtures))
        if step == micro - 1:
            grad_mixed, crossed, rest_sent, rest, out_sum = lax.optimization_barrier(
                (grad_mixed, crossed, rest_sent, rest, out_sum)
            )
            out_sum = lax.psum_scatter(out_sum, "ep", scatter_dimension=0)
            rest_sent.append([shift_rep(part[1], i + 2) for i, part in enumerate(rest)])
        grad_proj, grad_qk = attention_backward(
            step, proj, *tables, query, keys, values, lses, grad_mixed
        )
        qk_sum = qk_sum + grad_qk.reshape(-1)
        if step < micro - 1:
            grad_proj, in_sent = lax.optimization_barrier((grad_proj, in_sent))
        else:
            grad_proj, grad_inputs, rest_sent, rest = lax.optimization_barrier(
                (grad_proj, grad_inputs, rest_sent, rest)
            )
        grad_projs.append(grad_proj)
        grad_normed, gain_one = project_backward(step, grad_proj, stream, slab)
        gain_one_sum = gain_one_sum + gain_one
        grad_inputs.append(
            (
                grad_hidden,
                grad_normed,
                lax.psum_scatter(grad_normed, "ep", scatter_dimension=0, tiled=True),
            )
        )

    router_sum = dot(normed_two, jnp.concatenate(logit_grads, axis=0), ((0,), (0,)))
    qk_columns = qk_sum.shape[0] // dense_rows
    small = jnp.concatenate(
        [
            router_sum[:, :experts],
            jnp.concatenate([gain_one_sum, gain_two_sum], axis=1).reshape(D, 2),
            jnp.tile(qk_sum.reshape(dense_rows, qk_columns), (planes * ranks, 1)),
        ],
        axis=1,
    )
    count = small.shape[1]

    def halves(value):
        high, low = two_parts(value)
        blank = jnp.zeros((value.shape[0], PAD - 2 * count), bf16)
        return jnp.concatenate([high, low, blank], axis=1)

    def joined(value):
        return value[..., :count].astype(f32) + value[..., count : 2 * count].astype(f32)

    grad_projs, rest, out_cut, out_sent, _ = lax.optimization_barrier(
        (grad_projs, rest, out_cut, out_sent, grad_normed)
    )
    rest_sent.append([shift_rep(part[2], i + 2) for i, part in enumerate(rest)])
    packed = weight_gradient(
        where,
        planes,
        normed.reshape(ranks * mine, D),
        [grad.reshape(length, 3 * width) for grad in grad_projs],
        halves(small),
    )
    packed, rest_sent, out_cut, out_sent, crossed = lax.optimization_barrier(
        (packed, rest_sent, out_cut, out_sent, crossed)
    )
    packed_sent = [packed[0]] + [cross_rep(packed[step], step) for step in range(1, planes)]
    normed_sums = [one[2] for one in grad_inputs]
    normed_sums = [one[2] for one in grad_inputs]
    grad_tokens = []
    for step in range(micro):
        own_stream = tokens[step * rows : (step + 1) * rows].astype(f32)
        grad_tokens.append(
            grad_inputs[step][0]
            + rms_backward(
                own_stream, inverse_rms(own_stream), first_gain, normed_sums[step].astype(f32)
            )
        )
    grad_tokens = jnp.concatenate(grad_tokens, axis=0)
    packed_sent, grad_tokens = lax.optimization_barrier((packed_sent, grad_tokens))
    for phase in range(1, len(bits)):
        mixtures = [total(parts).astype(bf16) for parts in crossed]
        crossed = [
            halve(number, cut_pairs(number, value, phase), phase)
            for number, value in enumerate(mixtures)
        ]
    mixture = []
    for number in range(micro):
        parts = total(crossed[number])[0]
        mixture.append((parts[0], exchange_back(parts.astype(bf16))[1:]))
    own_sum = lax.dynamic_index_in_dim(out_sum, plane, 0, keepdims=False)
    out_sent_back = [
        cross_rep(lax.dynamic_index_in_dim(out_sum, plane ^ step, 0, keepdims=False), step)
        for step in range(1, planes)
    ]
    main = total([part[:, : 3 * width] for part in packed_sent]).astype(bf16)
    small = sum(joined(part[:, 3 * width :]) for part in packed_sent)
    packed = jnp.concatenate([main, halves(small)], axis=1).reshape(ranks, dense_rows, -1)
    packed = lax.all_to_all(packed, "ep", split_axis=0, concat_axis=0, tiled=True)
    packed, mixture, out_sent_back = lax.optimization_barrier((packed, mixture, out_sent_back))
    output = jnp.concatenate([mine_part + total(others) for mine_part, others in mixture], axis=0)
    output = (hidden + output).astype(bf16)
    grad_w_o = total([own_sum, *out_sent_back])
    grad_w_qkv, small = unpack(packed, count)
    out_sent[1] = jnp.concatenate([first, out_sent[1]], axis=0)
    grad_w_out = sum_rep({0: out_cut[0], **out_sent})
    for i in range(planes - 3):
        in_sent[i + 2] = jnp.concatenate([parts[i] for parts in rest_sent], axis=0)
    grad_w_in = sum_rep(in_sent, shift=True)
    return (
        output,
        grad_tokens,
        grad_w_qkv,
        grad_w_o,
        small[:, :experts],
        small[:, experts : experts + 2].reshape(-1),
        small[:, experts + 2 : count].reshape(-1),
        grad_w_in,
        grad_w_out,
    )


def solution(mesh):
    placed = (
        P(("rep", "ep"), None),
        P(("rep", "ep"), None),
        P(("rep", "ep"), None),
        P(("rep", "ep"), None),
        P(("rep", "ep"), None),
        P(("rep", "ep")),
        P(),
        P("ep", "rep", None),
        P("ep", "rep", None),
        P("rep", None, None),
        P(("rep", "ep"), None),
    )
    return jax.shard_map(
        on_device,
        mesh=mesh,
        in_specs=placed,
        out_specs=(
            P(("rep", "ep"), None),
            P(("rep", "ep"), None),
            P(("rep", "ep"), None),
            P(("rep", "ep"), None),
            P(("rep", "ep"), None),
            P(("rep", "ep")),
            P(),
            P("ep", "rep", None),
            P("ep", "rep", None),
        ),
        check_vma=False,
    )
```

```python
import math

import jax
import jax.numpy as jnp
from jax import lax
from jax.experimental import pallas as pl
from jax.experimental.pallas import tpu as pltpu
from jax.sharding import PartitionSpec as P

D = 2048
HEADS = 16
HD = 128
FF = 1024
TOP = 8
HALF = 512
PAD = 128

epsilon = 1e-06
rope_base = 50000.0
bf16 = jnp.bfloat16
f32 = jnp.float32


def dot(a, b, dims=((1,), (0,))):
    return lax.dot_general(a, b, (dims, ((), ())), preferred_element_type=f32)


def inverse_rms(value):
    return lax.rsqrt(jnp.mean(value * value, axis=-1, keepdims=True) + epsilon)


def rms_backward(value, inverse, gain, grad):
    scaled = grad * gain
    inner = jnp.mean(scaled * value, axis=-1, keepdims=True)
    return inverse * (scaled - value * (inverse * inverse * inner))


def doc_positions(segment):
    index = jnp.arange(segment.shape[0], dtype=jnp.int32)
    change = jnp.concatenate([jnp.ones((1,), dtype=jnp.bool_), segment[1:] != segment[:-1]])
    start = lax.cummax(jnp.where(change, index, 0), axis=0)
    return index - start


def rope_tables(position, width):
    steps = jnp.arange(width // 2, dtype=f32) * (2.0 / width)
    rates = jnp.exp(-steps * math.log(rope_base))
    angle = position.astype(f32)[:, None] * rates[None, :]
    angle = jnp.concatenate([angle, angle], axis=-1)
    return (jnp.cos(angle), jnp.sin(angle))


def norm_rope(value, gain, cosine, sine):
    inverse = lax.rsqrt(jnp.mean(value * value, axis=1, keepdims=True) + epsilon)
    value = value * inverse * gain
    return value * cosine + pltpu.roll(value, HD // 2, 1) * sine


def norm_rope_back(value, gain, cosine, sine, grad):
    inverse = lax.rsqrt(jnp.mean(value * value, axis=1, keepdims=True) + epsilon)
    grad = grad * cosine + pltpu.roll(grad * sine, HD // 2, 1)
    normal = value * inverse
    scaled = grad * gain
    inner = jnp.mean(scaled * normal, axis=1, keepdims=True)
    return inverse * (scaled - normal * inner), jnp.sum(grad * normal, axis=0, keepdims=True)


def kept_scores(query, keys, q_seg, k_seg, start):
    scores = dot(query, keys, ((1,), (1,))) * (1.0 / math.sqrt(HD))
    q_index = start + lax.broadcasted_iota(jnp.int32, scores.shape, 0)
    k_index = lax.broadcasted_iota(jnp.int32, scores.shape, 1)
    keep = (jnp.abs(q_index - k_index) <= HALF) & (q_seg == k_seg)
    return jnp.where(keep, scores, -1e30)


BIG = 100 * 1024 * 1024 // 2


def forward_kernel(
    heads, proj, cosine, sine, seg_column, seg_row, gains, mixed, query, keys, values, lses
):
    ranks, _, rows, _ = proj.shape
    length = ranks * rows
    q_block = 2 * rows
    k_seg = seg_row[0]
    for head in range(heads):
        at = slice(head * HD, (head + 1) * HD)

        def raw(part):
            first = (part * heads + head) * HD
            return proj[:, 0, :, first : first + HD].reshape(length, HD)

        query[0, :, at] = norm_rope(raw(0), gains[0:1], cosine[0], sine[0]).astype(bf16)
        keys[0, :, at] = norm_rope(raw(1), gains[1:2], cosine[0], sine[0]).astype(bf16)
        values[0, :, at] = raw(2).astype(bf16)

        @pl.loop(0, length // q_block)
        def one_block(number, head=head, at=at):
            start = pl.multiple_of(number * q_block, q_block)
            here = pl.ds(start, q_block)
            scores = kept_scores(
                query[0, here, at], keys[0, :, at], seg_column[0, here], k_seg, start
            )
            top = jnp.max(scores, axis=1, keepdims=True)
            weights = jnp.exp(scores - top)
            total = jnp.sum(weights, axis=1, keepdims=True)
            lses[0, head, here] = top + jnp.log(total)
            weights = (weights * (1.0 / total)).astype(bf16)
            result = dot(weights, values[0, :, at]).astype(bf16)
            mixed[pl.ds(number * 2, 2), 0, :, at] = result.reshape(2, rows, HD)


def backward_kernel(
    heads, proj, cosine, sine, seg_column, seg_row, gains, query, keys, values, lses, grad_mixed,
    grad_proj, grad_gains, grad_q, grad_k, grad_v,
):
    ranks, _, rows, _ = proj.shape
    length = ranks * rows
    q_block = 2 * rows
    k_seg = seg_row[0]
    scale = 1.0 / math.sqrt(HD)
    sum_q = jnp.zeros((1, HD), f32)
    sum_k = jnp.zeros((1, HD), f32)
    for head in range(heads):
        at = slice(head * HD, (head + 1) * HD)
        grad_k[...] = jnp.zeros_like(grad_k)
        grad_v[...] = jnp.zeros_like(grad_v)

        @pl.loop(0, length // q_block)
        def one_block(number, head=head, at=at):
            start = pl.multiple_of(number * q_block, q_block)
            here = pl.ds(start, q_block)
            q_rows = query[0, here, at]
            g_rows = grad_mixed[here, at]
            k_all = keys[0, :, at]
            scores = kept_scores(q_rows, k_all, seg_column[0, here], k_seg, start)
            weights = jnp.exp(scores - lses[0, head, here])
            grad_weights = dot(g_rows, values[0, :, at], ((1,), (1,)))
            delta = jnp.sum(weights * grad_weights, axis=1, keepdims=True)
            grad_scores = (weights * (grad_weights - delta)).astype(bf16)
            grad_q[here] = dot(grad_scores, k_all) * scale
            grad_k[...] += dot(grad_scores, q_rows, ((0,), (0,)))
            grad_v[...] += dot(weights.astype(bf16), g_rows, ((0,), (0,)))

        def rounded(value):
            return value.astype(bf16).astype(f32)

        def raw(part):
            first = (part * heads + head) * HD
            return proj[:, 0, :, first : first + HD].reshape(length, HD)

        def put(part, value):
            first = (part * heads + head) * HD
            grad_proj[:, :, first : first + HD] = value.astype(bf16).reshape(ranks, rows, HD)

        back_q, gain_q = norm_rope_back(
            raw(0), gains[0:1], cosine[0], sine[0], rounded(grad_q[...])
        )
        back_k, gain_k = norm_rope_back(
            raw(1), gains[1:2], cosine[0], sine[0], rounded(grad_k[...] * scale)
        )
        sum_q, sum_k = sum_q + gain_q, sum_k + gain_k
        put(0, back_q)
        put(1, back_k)
        put(2, grad_v[...])
    grad_gains[0:1] = sum_q
    grad_gains[1:2] = sum_k


def fixed(shape):
    return pl.BlockSpec(shape, lambda *_: (0,) * len(shape), pipeline_mode=pl.Buffered(1))


def leading(shape):
    return pl.BlockSpec((1,) + shape[1:], lambda i: (i,) + (0,) * (len(shape) - 1))


def params():
    return pltpu.CompilerParams(vmem_limit_bytes=BIG)


def cost(products):
    return pl.CostEstimate(flops=20 * products, bytes_accessed=0, transcendentals=0)


def out(shape, dtype=bf16):
    return jax.ShapeDtypeStruct(shape, dtype)


def attention_forward(proj, cosine, sine, seg_column, seg_row, gains):
    ranks, micro, rows, width = proj.shape
    length = ranks * rows
    width = width // 3
    heads = width // HD
    part = out((micro, length, width))
    by_rank = lambda n: pl.BlockSpec((ranks, 1, rows, n), lambda i: (0, i, 0, 0))
    lses = out((micro, heads, length, 1), f32)
    return pl.pallas_call(
        lambda *refs: forward_kernel(heads, *refs),
        grid=(micro,),
        in_specs=[by_rank(3 * width)]
        + [leading(v.shape) for v in (cosine, sine, seg_column, seg_row)]
        + [fixed(gains.shape)],
        out_specs=[by_rank(width)] + [leading(part.shape)] * 3 + [leading(lses.shape)],
        out_shape=[out((ranks, micro, rows, width)), part, part, part, lses],
        compiler_params=params(),
    )(proj, cosine, sine, seg_column, seg_row, gains)


def attention_backward(
    step, proj, cosine, sine, seg_column, seg_row, gains, query, keys, values, lses, grad_mixed
):
    ranks, micro, rows, width = proj.shape
    length = ranks * rows
    heads = width // 3 // HD

    def part(value):
        return pl.BlockSpec((1,) + value.shape[1:], lambda i: (step,) + (0,) * (value.ndim - 1))

    return pl.pallas_call(
        lambda *refs: backward_kernel(heads, *refs),
        grid=(1,),
        in_specs=[pl.BlockSpec((ranks, 1, rows, width), lambda i: (0, step, 0, 0))]
        + [part(v) for v in (cosine, sine, seg_column, seg_row)]
        + [fixed(gains.shape)]
        + [part(v) for v in (query, keys, values, lses)]
        + [fixed(grad_mixed.shape)],
        out_specs=[fixed((ranks, rows, width)), fixed((2, HD))],
        out_shape=[out((ranks, rows, width)), out((2, HD), f32)],
        scratch_shapes=[pltpu.VMEM((length, HD), f32)] * 3,
        compiler_params=params(),
    )(
        proj, cosine, sine, seg_column, seg_row, gains, query, keys, values, lses, grad_mixed
    )


def project(micro, tokens, gain, slab):
    ranks, count, _ = tokens.shape
    rows = count // micro
    width = slab.shape[1] - PAD

    def kernel(value, gain, weight, normed, proj):
        value = value[0].astype(f32)
        result = (value * inverse_rms(value) * gain[...]).astype(bf16)
        normed[...] = result.reshape(micro, 1, rows, D)
        proj[0] = dot(result, weight[:, :width])

    return pl.pallas_call(
        kernel,
        grid=(ranks,),
        in_specs=[leading((ranks, count, D)), fixed((1, D)), fixed(slab.shape)],
        out_specs=[
            pl.BlockSpec((micro, 1, rows, D), lambda i: (0, i, 0, 0)),
            leading((ranks, count, width)),
        ],
        out_shape=[out((micro, ranks, rows, D)), out((ranks, count, width), f32)],
        compiler_params=params(),
    )(tokens, gain, slab)


TILE = 512


def tiles(count):
    return pl.loop(0, count // TILE)


def tile(number):
    return pl.ds(pl.multiple_of(number * TILE, TILE), TILE)


HBM = pl.BlockSpec(memory_space=pl.ANY)


def copies(pairs, sems):
    started = [
        pltpu.make_async_copy(source, target, sems.at[place])
        for place, (source, target) in enumerate(pairs)
    ]
    for copy in started:
        copy.start()

    def wait():
        for copy in started:
            copy.wait()

    return wait


def plane_pairs(plane, pieces, target):
    planes = len(pieces)
    rows = target.shape[0] // planes
    return [
        (piece, target.at[pl.ds(lax.bitwise_xor(plane, jnp.int32(step)) * rows, rows)])
        for step, piece in enumerate(pieces)
    ]


def out_weight_pairs(plane, planes, gathered, target):
    ranks = gathered.shape[0]
    rows = D // (planes * ranks)
    return [
        (
            gathered.at[rank, pl.ds(step * rows, rows)],
            target.at[
                pl.ds((lax.bitwise_xor(plane, jnp.int32(step)) * ranks + rank) * rows, rows)
            ],
        )
        for rank in range(ranks)
        for step in range(planes)
    ]


def route(plane, planes, mixed, tokens, gathered, gain, router, routes, experts):
    count = tokens.shape[0]
    pieces = planes * gathered.shape[0]

    def kernel(
        plane, mixed, tokens, gathered, gain, router, routes, hidden, payload, gates,
        out_weight, sems,
    ):
        copies(out_weight_pairs(plane[0], planes, gathered, out_weight), sems)()

        @tiles(D)
        def _(number):
            at = tile(number)
            hidden[:, at] = tokens[:, at].astype(f32) + dot(mixed[...], out_weight[:, at])

        value = hidden[...]
        normed = (value * inverse_rms(value) * gain[...]).astype(bf16)
        payload[:, :D] = normed
        logits = dot(normed, router[...])
        column = lax.broadcasted_iota(jnp.int32, logits.shape, 1)
        routed = column == routes[:, 0:1]
        for choice in range(1, TOP):
            routed = routed | (column == routes[:, choice : choice + 1])
        logits = jnp.where(routed, logits, -1e30)
        weights = jnp.exp(logits - jnp.max(logits, axis=1, keepdims=True))
        weights = jnp.where(routed, weights, 0.0)
        weights = weights / jnp.sum(weights, axis=1, keepdims=True)
        gates[...] = weights
        high = weights.astype(bf16).astype(f32)
        payload[:, D:] = (high + pltpu.roll(weights - high, experts, 1)).astype(bf16)

    shapes = [out((count, D), f32), out((count, D + PAD)), out((count, PAD), f32)]
    return pl.pallas_call(
        kernel,
        grid_spec=pltpu.PrefetchScalarGridSpec(
            num_scalar_prefetch=1,
            grid=(1,),
            in_specs=[
                HBM if value is gathered else fixed(value.shape)
                for value in (mixed, tokens, gathered, gain, router, routes)
            ],
            out_specs=[fixed(shape.shape) for shape in shapes],
            scratch_shapes=[pltpu.VMEM((D, D), bf16), pltpu.SemaphoreType.DMA((pieces,))],
        ),
        out_shape=shapes,
        compiler_params=params(),
    )(plane, mixed, tokens, gathered, gain, router, routes)


def lane(value, number):
    column = lax.broadcasted_iota(jnp.int32, value.shape, 1)
    return jnp.sum(jnp.where(column == number, value.astype(f32), 0.0), axis=1, keepdims=True)


def one_hot(slot, slots):
    place = lax.broadcasted_iota(jnp.int32, (slots, slot.shape[1]), 0).astype(f32)
    return (place == slot).astype(bf16)


def expert_forward(where, payload, upstream, in_pieces, slots, experts):
    ranks, share, micro, rows, _ = payload.shape
    count = share * rows
    block = 2 * slots

    planes = len(in_pieces)

    def kernel(where, payload, upstream, *refs):
        (
            rows_in, tail, both, active, grad_produced, up_rows, places, in_weight, sems
        ) = refs[planes:]
        number = where[0]

        @pl.when((pl.program_id(0) == 0) & (pl.program_id(1) == 0))
        def _():
            copies(plane_pairs(where[1], refs[:planes], in_weight), sems)()

        for part in range(2):
            here = slice(part * slots, (part + 1) * slots)
            value = payload[part].reshape(count, D + PAD)
            marks = value[:, D:]
            first = lax.broadcasted_iota(jnp.int32, (8, PAD), 1) == number
            taken = dot(first.astype(bf16), marks, ((1,), (1,))) > 0.0
            before = lax.broadcasted_iota(jnp.int32, (count, count), 0)
            behind = lax.broadcasted_iota(jnp.int32, (count, count), 1)
            slot = dot(taken.astype(bf16), (before < behind).astype(bf16))
            select = one_hot(jnp.where(taken, slot, -1.0)[0:1], slots)
            wide = jnp.broadcast_to(lane(marks, number) > 0.0, (count, PAD))
            slot = dot((before > behind).astype(bf16), wide.astype(bf16))
            places[0, 0, part] = jnp.where(wide, slot, -1.0)
            rows_in[0, 0, here] = dot(select, value[:, :D]).astype(bf16)
            marks = dot(select, marks)
            tail[0, 0, here] = marks
            gate = lane(marks, number) + lane(marks, experts + number)
            picked = dot(select, upstream[part].reshape(count, D))
            up_rows[0, 0, here] = picked.astype(bf16)
            grad_produced[0, 0, here] = (gate * picked).astype(bf16)

        for number in range(FF // TILE):
            at = slice(number * TILE, (number + 1) * TILE)
            more = slice(FF + number * TILE, FF + (number + 1) * TILE)
            gate_part = dot(rows_in[0, 0], in_weight[:, at])
            up_part = dot(rows_in[0, 0], in_weight[:, more])
            both[0, 0, :, at] = gate_part
            both[0, 0, :, more] = up_part
            active[0, 0, :, at] = (
                gate_part / (1.0 + jnp.exp(-gate_part)) * up_part
            ).astype(bf16)

    def tokens_spec(width):
        return pl.BlockSpec((2, share, 1, rows, width), lambda m, b, _: (b, 0, m, 0, 0))

    pairs = ranks // 2
    shapes = [
        out((micro, pairs, block, D)),
        out((micro, pairs, block, PAD), f32),
        out((micro, pairs, block, 2 * FF), f32),
        out((micro, pairs, block, FF)),
        out((micro, pairs, block, D)),
        out((micro, pairs, block, D)),
        out((micro, pairs, 2, count, PAD), f32),
    ]
    return pl.pallas_call(
        kernel,
        grid_spec=pltpu.PrefetchScalarGridSpec(
            num_scalar_prefetch=1,
            grid=(micro, pairs),
            in_specs=[tokens_spec(D + PAD), tokens_spec(D)] + [HBM] * planes,
            out_specs=[
                pl.BlockSpec(
                    (1, 1) + s.shape[2:], lambda m, b, _, n=len(s.shape): (m, b) + (0,) * (n - 2)
                )
                for s in shapes
            ],
            scratch_shapes=[pltpu.VMEM((D, 2 * FF), bf16), pltpu.SemaphoreType.DMA((planes,))],
        ),
        out_shape=shapes,
        cost_estimate=cost(micro * pairs * block * D * (2 * FF + 2 * count)),
        compiler_params=params(),
    )(where, payload, upstream, *in_pieces)


def expert_backward(
    step, where, tail, both, active, grad_produced, up_rows, places, in_pieces, out_pieces,
    share, rows, experts,
):
    pairs, block = tail.shape[1:3]
    slots = block // 2
    count = places.shape[3]

    planes = len(in_pieces)

    def kernel(where, tail, both, active, grad_produced, up_rows, places, *refs):
        keep, give, grad_tokens, grad_both, in_weight, out_weight, sems = refs[2 * planes :]
        number = where[0]
        odd = where[2] == 1

        @pl.when(pl.program_id(0) == 0)
        def _():
            copies(
                plane_pairs(where[1], refs[:planes], in_weight)
                + plane_pairs(where[1], refs[planes : 2 * planes], out_weight),
                sems,
            )()

        gate = lane(tail[0, 0], number) + lane(tail[0, 0], experts + number)
        place = lax.broadcasted_iota(jnp.int32, (count, slots), 1).astype(f32)
        selects = [(places[0, 0, part][:, 0:1] == place).astype(bf16) for part in range(2)]

        def spread(value):
            return [
                dot(selects[part], value[part * slots : (part + 1) * slots])
                .astype(bf16)
                .reshape(share, rows, -1)
                for part in range(2)
            ]

        grad_gate = jnp.zeros((block, 1), f32)
        for tile in range(D // TILE):
            at = slice(tile * TILE, (tile + 1) * TILE)
            produced = dot(active[0, 0], out_weight[:, at]).astype(bf16).astype(f32)
            even_rank, odd_rank = spread((gate * produced).astype(bf16))
            keep[0, :, :, at] = jnp.where(odd, odd_rank, even_rank)
            give[0, :, :, at] = jnp.where(odd, even_rank, odd_rank)
            grad_gate = grad_gate + jnp.sum(
                up_rows[0, 0, :, at].astype(f32) * produced, axis=1, keepdims=True
            )

        for tile in range(FF // TILE):
            at = slice(tile * TILE, (tile + 1) * TILE)
            more = slice(FF + tile * TILE, FF + (tile + 1) * TILE)
            grad_active = dot(grad_produced[0, 0], out_weight[at, :], ((1,), (1,)))
            grad_active = grad_active.astype(bf16).astype(f32)
            gate_part = both[0, 0, :, at]
            up_part = both[0, 0, :, more]
            sigma = 1.0 / (1.0 + jnp.exp(-gate_part))
            grad_both[0, :, at] = (
                grad_active * up_part * (sigma * (1.0 + gate_part * (1.0 - sigma)))
            ).astype(bf16)
            grad_both[0, :, more] = (grad_active * (gate_part * sigma)).astype(bf16)

        for tile in range(D // TILE):
            at = slice(tile * TILE, (tile + 1) * TILE)
            grad_rows = dot(grad_both[0], in_weight[at, :], ((1,), (1,))).astype(bf16)
            grad_tokens[0, :, :, at], grad_tokens[1, :, :, at] = spread(grad_rows)

        high = grad_gate.astype(bf16).astype(f32)
        column = lax.broadcasted_iota(jnp.int32, (block, PAD), 1)
        extra = jnp.where(column == number, high, 0.0)
        extra = jnp.where(column == experts + number, grad_gate - high, extra)
        grad_tokens[0, :, :, D:], grad_tokens[1, :, :, D:] = spread(extra.astype(bf16))

    def part(value):
        return pl.BlockSpec(
            (1, 1) + value.shape[2:], lambda b, _: (step, b) + (0,) * (value.ndim - 2)
        )

    def tokens_spec(count, width):
        return pl.BlockSpec((count, share, rows, width), lambda b, _: (b, 0, 0, 0))

    return pl.pallas_call(
        kernel,
        grid_spec=pltpu.PrefetchScalarGridSpec(
            num_scalar_prefetch=1,
            grid=(pairs,),
            in_specs=[part(v) for v in (tail, both, active, grad_produced, up_rows, places)]
            + [HBM] * (2 * planes),
            out_specs=[
                tokens_spec(1, D),
                tokens_spec(1, D),
                tokens_spec(2, D + PAD),
                pl.BlockSpec((1, block, 2 * FF), lambda b, _: (b, 0, 0)),
            ],
            scratch_shapes=[
                pltpu.VMEM((D, 2 * FF), bf16),
                pltpu.VMEM((FF, D), bf16),
                pltpu.SemaphoreType.DMA((2 * planes,)),
            ],
        ),
        out_shape=[
            out((pairs, share, rows, D)),
            out((pairs, share, rows, D)),
            out((2 * pairs, share, rows, D + PAD)),
            out((pairs, block, 2 * FF)),
        ],
        cost_estimate=cost(pairs * block * D * (4 * FF + 2 * count)),
        compiler_params=params(),
    )(
        where, tail, both, active, grad_produced, up_rows, places, *in_pieces, *out_pieces
    )


def cut_ends(count, places):
    return [-(-count * place // 512) * 16 for place in (0, *places, 32)]


def weight_gradient(
    where, planes, left, rights, tail=None, first=0, steps=None, shift=False, cuts=None
):
    steps = planes if steps is None else steps
    count, width = left.shape
    parts = len(rights)
    part_rows = count // parts
    columns = rights[0].shape[1]
    width = width // planes
    step = min(TILE, columns & -columns)
    tails = [] if tail is None else [tail]
    whole = columns + sum(value.shape[1] for value in tails)

    ends = [cut_ends(width, (cuts or {}).get(number, ())) for number in range(steps)]
    shapes = [
        out((end - start, whole)) for one in ends for start, end in zip(one, one[1:])
    ]

    def of_plane(i, where):
        return (where[1] + first + i) % planes if shift else lax.bitwise_xor(where[1], first + i)

    def kernel(where, left, *refs):
        rights, tails, targets = refs[:parts], refs[parts : -len(shapes)], refs[-len(shapes) :]

        def fill(targets, ends):
            for value in tails:
                targets[0][:, columns:] = value[...]
            for number in range(columns // step):
                at = slice(number * step, (number + 1) * step)
                result = sum(
                    dot(left[part * part_rows : (part + 1) * part_rows], right[:, at], ((0,), (0,)))
                    for part, right in enumerate(rights)
                ).astype(bf16)
                for target, start, end in zip(targets, ends, ends[1:]):
                    target[:, at] = result[start:end]

        done = 0
        for number, one in enumerate(ends):
            mine = targets[done : done + len(one) - 1]
            done += len(one) - 1
            pl.when(pl.program_id(0) == number)(lambda mine=mine, one=one: fill(mine, one))

    return pl.pallas_call(
        kernel,
        grid_spec=pltpu.PrefetchScalarGridSpec(
            num_scalar_prefetch=1,
            grid=(steps,),
            in_specs=[pl.BlockSpec((count, width), lambda i, where: (0, of_plane(i, where)))]
            + [fixed(right.shape) for right in rights]
            + [
                pl.BlockSpec((width, value.shape[1]), lambda i, where: (of_plane(i, where), 0))
                for value in tails
            ],
            out_specs=[fixed(shape.shape) for shape in shapes],
        ),
        out_shape=shapes,
        cost_estimate=cost(0 if tails else count * steps * width * columns),
        compiler_params=params(),
    )(where, left, *rights, *tails)


def hidden_backward(
    step, plane, planes, parts, hidden, gates, upstream, gain, router, gathered, experts
):
    first = parts[0].shape
    count = first[1]
    terms = len(parts)

    def kernel(plane, *refs):
        parts = refs[:terms]
        hidden, gates, upstream, gain, router, gathered = refs[terms : terms + 6]
        (
            grad_hidden, grad_branch, grad_mixed, grad_logits, grad_gain, out_weight, sems
        ) = refs[terms + 6 :]
        wait = copies(out_weight_pairs(plane[0], planes, gathered, out_weight), sems)
        returned = sum(part[...].astype(f32) for part in parts[1:]) + parts[0][0].astype(f32)
        tail = returned[:, D:]
        grad_gates = gates[...] * (tail + pltpu.roll(tail, PAD - experts, 1))
        logits = grad_gates - gates[...] * jnp.sum(grad_gates, axis=1, keepdims=True)
        logits = logits.astype(bf16)
        grad_logits[...] = logits
        grad_normed = returned[:, :D] + dot(logits, router[...], ((1,), (1,)))
        value = hidden[...]
        inverse = inverse_rms(value)
        grad_gain[...] = jnp.sum(grad_normed * value * inverse, axis=0, keepdims=True)
        grad = upstream[...].astype(f32) + rms_backward(value, inverse, gain[...], grad_normed)
        grad_hidden[...] = grad
        grad_branch[...] = grad.astype(bf16)
        wait()

        @tiles(D)
        def _(number):
            at = tile(number)
            grad_mixed[:, at] = dot(grad_branch[...], out_weight[at, :], ((1,), (1,))).astype(bf16)

    shapes = [
        out((count, D), f32), out((count, D)), out((count, D)), out((count, PAD)),
        out((1, D), f32),
    ]
    args = (*parts, hidden, gates, upstream, gain, router, gathered)

    def spec(value):
        if value is gathered:
            return HBM
        if value is parts[0]:
            return pl.BlockSpec((1,) + first[1:], lambda *_: (0, 0, 0))
        if any(value is rows for rows in (hidden, gates, upstream)):
            return pl.BlockSpec((count, value.shape[1]), lambda *_: (step, 0))
        return fixed(value.shape)

    return pl.pallas_call(
        kernel,
        grid_spec=pltpu.PrefetchScalarGridSpec(
            num_scalar_prefetch=1,
            grid=(1,),
            in_specs=[spec(value) for value in args],
            out_specs=[fixed(shape.shape) for shape in shapes],
            scratch_shapes=[
                pltpu.VMEM((D, D), bf16),
                pltpu.SemaphoreType.DMA((planes * gathered.shape[0],)),
            ],
        ),
        out_shape=shapes,
        compiler_params=params(),
    )(plane, *args)


def project_backward(step, grad_proj, tokens, slab):
    ranks, rows, _ = grad_proj.shape
    width = slab.shape[1] - PAD

    def kernel(grad_proj, tokens, weight, grad_normed, grad_gain):
        value = tokens[...].reshape(2 * rows, D).astype(f32)
        inverse = inverse_rms(value)
        grad = dot(grad_proj[...].reshape(2 * rows, width), weight[:, :width], ((1,), (1,)))
        grad_normed[...] = grad.astype(bf16)

        @pl.when(pl.program_id(0) == 0)
        def _():
            grad_gain[...] = jnp.zeros_like(grad_gain)

        grad_gain[...] += jnp.sum(grad * value * inverse, axis=0, keepdims=True)

    return pl.pallas_call(
        kernel,
        grid=(ranks // 2,),
        in_specs=[
            pl.BlockSpec((2, rows, width), lambda i: (i, 0, 0)),
            pl.BlockSpec((2, rows, D), lambda i: (i, step, 0)),
            fixed(slab.shape),
        ],
        out_specs=[pl.BlockSpec((2 * rows, D), lambda i: (i, 0)), fixed((1, D))],
        out_shape=[out((ranks * rows, D)), out((1, D), f32)],
        compiler_params=params(),
    )(grad_proj, tokens, slab)


def cut_heads(weight, tail, ranks):
    rows = weight.shape[0]
    width = D // ranks

    def kernel(weight, tail, target):
        for rank in range(ranks):
            for part in range(3):
                at = part * D + rank * width
                target[rank, :, part * width : (part + 1) * width] = weight[:, at : at + width]
            target[rank, :, 3 * width :] = tail[...]

    return pl.pallas_call(
        kernel,
        out_shape=out((ranks, rows, 3 * width + PAD)),
        compiler_params=params(),
    )(weight, tail)


def unpack(packed, count):
    ranks, rows, columns = packed.shape
    width = (columns - PAD) // 3

    def kernel(packed, main, small):
        for rank in range(ranks):
            for part in range(3):
                at = part * D + rank * width
                main[:, at : at + width] = packed[rank, :, part * width : (part + 1) * width].astype(
                    f32
                )
        tails = sum(packed[rank, :, 3 * width :].astype(f32) for rank in range(ranks))
        small[...] = tails + pltpu.roll(tails, PAD - count, 1)

    return pl.pallas_call(
        kernel,
        out_shape=[out((rows, 3 * D), f32), out((rows, PAD), f32)],
        compiler_params=params(),
    )(packed)


def shift_rep(value, step):
    count = lax.axis_size("rep")
    return lax.ppermute(value, "rep", [(i, (i + step) % count) for i in range(count)])


def cross_rep(value, bits):
    return lax.ppermute(value, "rep", [(i, i ^ bits) for i in range(lax.axis_size("rep"))])


def after(value, *others):
    return lax.optimization_barrier((value,) + others)[0]


def two_parts(value):
    high = lax.reduce_precision(value, 8, 7)
    return high.astype(bf16), (value - high).astype(bf16)


def ring_rep(value, *work):
    count = lax.axis_size("rep")
    rank = lax.axis_index("rep")
    rows = value.shape[0]
    full = jnp.zeros((count * rows,) + value.shape[1:], value.dtype)
    full = lax.dynamic_update_slice_in_dim(full, value, rank * rows, 0)
    for step in range(1, count):
        value, work = lax.optimization_barrier((value, work)) if step == count - 1 else (value, work)
        value = shift_rep(value, 1)
        full = lax.dynamic_update_slice_in_dim(full, value, (rank - step) % count * rows, 0)
    return full, work


def on_device(
    tokens, cotangent, w_qkv, w_o, w_router, norm_gains, qk_gain, w_in, w_out, segments, routes
):
    planes = lax.axis_size("rep")
    ranks = lax.axis_size("ep")
    plane = lax.axis_index("rep")
    rank = lax.axis_index("ep")
    share = w_in.shape[0]
    own = plane % share
    experts = share * ranks
    where = jnp.stack([rank * share + own, plane, rank % 2]).astype(jnp.int32)
    micro = segments.shape[1]
    mine = tokens.shape[0]
    rows = mine // micro
    length = rows * ranks
    capacity = rows * TOP * 17 // (16 * experts)
    slots = -(-share * capacity // 16) * 16
    width = HEADS // ranks * HD
    qk_gains = qk_gain.astype(f32).reshape(2, HD)
    dense_rows = w_qkv.shape[0]

    def exchange(value, step):
        pairs = [(i, i // share * share + (i % share + step) % share) for i in range(planes)]
        return lax.ppermute(value, "rep", pairs)

    def with_group(value):
        return jnp.stack([value] + [exchange(value, step) for step in range(1, share)])

    def gather_ranks(value):
        return lax.all_gather(value, "ep", axis=0)

    assert planes & (planes - 1) == 0 and share & (share - 1) == 0
    last_step = planes - 1
    in_parts, out_parts = (
        {
            step: lax.dynamic_index_in_dim(weight, own ^ step % share, 0, keepdims=False)
            for step in range(planes)
        }
        for weight in (w_in, w_out)
    )

    def send(parts, steps):
        return {step: cross_rep(parts[step], step) for step in steps}

    stream = gather_ranks(tokens)
    out_rows = [w_o] + [cross_rep(w_o, step) for step in range(1, planes)]
    upstream_group = with_group(cotangent)
    slab = cut_heads(
        w_qkv,
        jnp.concatenate(
            [
                w_router,
                norm_gains.reshape(dense_rows, 2),
                jnp.zeros((dense_rows, PAD - experts - 2), bf16),
            ],
            axis=1,
        ),
        ranks,
    )
    slab = lax.all_to_all(slab, "ep", split_axis=0, concat_axis=0, tiled=True)
    slab = slab.reshape(ranks * dense_rows, 3 * width + PAD)
    out_rows, upstream_group, slab = lax.optimization_barrier((out_rows, upstream_group, slab))
    gathered = gather_ranks(jnp.concatenate(out_rows, axis=0))
    segment = segments[0]
    cosine, sine = jax.vmap(lambda one: rope_tables(doc_positions(one), HD))(segment)
    sine = jnp.where(jnp.arange(HD) < HD // 2, -sine, sine)
    tables = (cosine, sine, segment[:, :, None], segment[:, None, :], qk_gains)
    slab, (tables, in_parts, out_parts) = ring_rep(slab, tables, in_parts, out_parts)
    router = slab[:, 3 * width :]
    gain_pair = router[:, experts : experts + 2].reshape(-1).astype(f32)
    first_gain = gain_pair[None, :D]
    second_gain = gain_pair[None, D:]
    in_parts, out_parts, upstream_group, stream = after(
        (in_parts, out_parts, upstream_group, stream), slab
    )
    in_pieces = {0: in_parts[0], **send(in_parts, range(last_step - 1, 0, -1))}
    upstream_all = gather_ranks(upstream_group)

    normed, proj = project(micro, stream, first_gain, slab)
    proj = proj.reshape(ranks, micro, rows, 3 * width)
    mixed_h, query, keys, values, lses = attention_forward(proj, *tables)
    mixed = lax.all_to_all(mixed_h, "ep", split_axis=0, concat_axis=3, tiled=True)
    mixed = mixed.reshape(mine, D)
    hidden, payload, gates = route(
        where[1:2], planes, mixed, tokens, gathered, second_gain, router, routes, experts
    )
    normed_two = payload[:, :D]
    payload, in_pieces = lax.optimization_barrier((payload, in_pieces))
    payload = with_group(payload)
    payload, in_parts, out_parts = lax.optimization_barrier((payload, in_parts, out_parts))
    in_pieces.update(send(in_parts, [last_step]))
    in_pieces, out_parts = lax.optimization_barrier((in_pieces, out_parts))
    out_pieces = {0: out_parts[0], **send(out_parts, range(1, planes))}
    in_pieces = [in_pieces[step] for step in range(planes)]
    out_pieces = [out_pieces[step] for step in range(planes)]
    payload = gather_ranks(payload)

    shape = (ranks, share, micro, rows, -1)
    rows_in, tail, both, active, grad_produced, up_rows, places = expert_forward(
        where, payload.reshape(shape), upstream_all.reshape(shape), in_pieces, slots, experts
    )
    in_rows = micro * ranks * slots
    out_cut = weight_gradient(
        where, planes, active.reshape(in_rows, FF), [grad_produced.reshape(in_rows, D)]
    )

    def sum_rep(parts, shift=False):
        sums = [
            sum(parts[step].astype(f32) for step in range(first, planes, share))
            for first in range(share)
        ]
        return jnp.stack(
            [
                sum(
                    jnp.where(((own - step) % share if shift else own ^ step) == j, sums[step], 0.0)
                    for step in range(share)
                )
                for j in range(share)
            ]
        )

    tail, out_cut, out_pieces = lax.optimization_barrier((tail, out_cut, out_pieces))
    first = cross_rep(out_cut[1][:16], 1)
    tail, out_cut, first = lax.optimization_barrier((tail, out_cut, first))
    out_sent = send([out_cut[0], out_cut[1][16:], *out_cut[2:]], range(1, planes))
    back = []
    returned = []

    def scatter_ranks(value):
        return lax.psum_scatter(value, "ep", scatter_dimension=0)

    def exchange_back(value):
        return [value] + [exchange(value[step], share - step) for step in range(1, share)]

    for step in range(micro):
        back.append(
            expert_backward(
                step, where, tail, both, active, grad_produced, up_rows, places, in_pieces,
                out_pieces, share, rows, experts,
            )
        )
        returned.append(scatter_ranks(back[step][2]))
        if step == 0:
            tail, out_sent[last_step] = after((tail, out_sent[last_step]), back[step][2])
        else:
            tail = after(tail, back[step][2])
    rows_in = after(rows_in, tail)
    rows_flat = rows_in.reshape(in_rows, D)
    grads_flat = [back[step][3].reshape(in_rows // micro, 2 * FF) for step in range(micro)]
    (in_near,) = weight_gradient(
        where, planes, rows_flat, grads_flat, first=1, steps=1, shift=True
    )
    rows_flat, in_near = lax.optimization_barrier((rows_flat, in_near))
    cuts = {number: (20, 28) for number in range(planes - 3)}
    *in_rest, in_back, in_own = weight_gradient(
        where, planes, rows_flat, grads_flat, first=2, steps=last_step, shift=True, cuts=cuts
    )
    in_sent = {0: in_own, 1: shift_rep(in_near, 1)}

    def sum_rep(parts, shift=False):
        sums = [
            sum(parts[step].astype(f32) for step in range(first, planes, share))
            for first in range(share)
        ]
        return jnp.stack(
            [
                sum(
                    jnp.where(((own - step) % share if shift else own ^ step) == j, sums[step], 0.0)
                    for step in range(share)
                )
                for j in range(share)
            ]
        )

    tail, out_cut, out_pieces = lax.optimization_barrier((tail, out_cut, out_pieces))
    first = cross_rep(out_cut[1][:16], 1)
    tail, out_cut, first = lax.optimization_barrier((tail, out_cut, first))
    out_sent = send([out_cut[0], out_cut[1][16:], *out_cut[2:]], range(1, planes))
    back = []
    returned = []

    def scatter_ranks(value):
        return lax.psum_scatter(value, "ep", scatter_dimension=0)

    def exchange_back(value):
        return [value] + [exchange(value[step], share - step) for step in range(1, share)]

    for step in range(micro):
        back.append(
            expert_backward(
                step, where, tail, both, active, grad_produced, up_rows, places, in_pieces,
                out_pieces, share, rows, experts,
            )
        )
        returned.append(scatter_ranks(back[step][2]))
        if step == 0:
            tail, out_sent[last_step] = after((tail, out_sent[last_step]), back[step][2])
        else:
            tail = after(tail, back[step][2])
    rows_in = after(rows_in, tail)
    rows_flat = rows_in.reshape(in_rows, D)
    grads_flat = [back[step][3].reshape(in_rows // micro, 2 * FF) for step in range(micro)]
    (in_near,) = weight_gradient(
        where, planes, rows_flat, grads_flat, first=1, steps=1, shift=True
    )
    rows_flat, in_near = lax.optimization_barrier((rows_flat, in_near))
    cuts = {number: (20, 28) for number in range(planes - 3)}
    *in_rest, in_back, in_own = weight_gradient(
        where, planes, rows_flat, grads_flat, first=2, steps=last_step, shift=True, cuts=cuts
    )
    in_sent = {0: in_own, 1: shift_rep(in_near, 1)}

    def cuts(value, *places):
        ends = [-(-value.shape[0] * place // 512) * 16 for place in (0, *places, 32)]
        return [value[start:end] for start, end in zip(ends, ends[1:])]

    def swap(value, step):
        return lax.ppermute(value, "ep", [(i, i ^ step) for i in range(ranks)])

    bits = list(range((ranks // 2).bit_length() - 1))

    def cut_pairs(number, value, phase):
        way = bits if number % 2 == 0 else bits[::-1]
        bit = way[phase]
        low = 2 ** sum(other < bit for other in way[phase:])
        value = value.reshape((-1, 2, low) + value.shape[1:])
        side = rank // 2 // 2**bit % 2
        return [
            lax.dynamic_index_in_dim(value, which, 1, keepdims=False).reshape((-1,) + value.shape[3:])
            for which in (side, 1 - side)
        ]

    def pair_sum(number, keep, give):
        got = swap(give, 1)
        return [
            total(parts).astype(bf16)
            for parts in zip(cut_pairs(number, keep, 0), cut_pairs(number, got, 0))
        ]

    def halve(number, halves, phase):
        return halves[0], swap(halves[1], 2 * 2 ** (bits if number % 2 == 0 else bits[::-1])[phase])

    def total(parts):
        return sum(part.astype(f32) for part in parts)

    grad_inputs, branches, logit_grads, grad_projs, normed_sums = [], [], [], [], []
    gain_two_sum = gain_one_sum = qk_sum = 0.0
    in_rest, in_back, out_sent, in_sent = lax.optimization_barrier(
        (in_rest, in_back, out_sent, in_sent)
    )
    mixtures = [part[:2] for part in back]
    for step in range(micro):
        parts = after(returned[step], [one[1] for one in grad_inputs])
        parts, in_sent = lax.optimization_barrier((parts, in_sent))
        if step == micro - 1:
            mixtures = after(mixtures, parts)
            crossed = [halve(number, value, 0) for number, value in enumerate(mixtures)]
        parts = exchange_back(parts)
        parts, in_rest, in_back, mixtures = lax.optimization_barrier(
            (parts, in_rest, in_back, mixtures)
        )
        if step == 0:
            mixtures = [pair_sum(number, *part) for number, part in enumerate(mixtures)]
            in_sent[last_step] = shift_rep(in_back, last_step)
        if step == micro - 1:
            rest = [in_rest[3 * i : 3 * i + 3] for i in range(planes - 3)]
            rest_sent = [[shift_rep(part[0], i + 2) for i, part in enumerate(rest)]]
        grad_hidden, grad_branch, grad_mixed, grad_logits, gain_two = hidden_backward(
            step, where[1:2], planes, parts, hidden, gates, cotangent, second_gain, router, gathered,
            experts,
        )
        branches.append(grad_branch)
        logit_grads.append(grad_logits)
        gain_two_sum = gain_two_sum + gain_two
        if step == micro - 1:
            out_sum = dot(mixed, jnp.concatenate(branches, axis=0), ((0,), (0,))).astype(bf16)
            out_sum = out_sum.reshape(planes, ranks, dense_rows, D).transpose(1, 0, 2, 3)
        grad_mixed = lax.all_to_all(grad_mixed, "ep", split_axis=1, concat_axis=0, tiled=True)
        grad_mixed, mixtures = lax.optimization_barrier((grad_mixed, mixtures))
        if step == micro - 1:
            grad_mixed, crossed, rest_sent, rest, out_sum = lax.optimization_barrier(
                (grad_mixed, crossed, rest_sent, rest, out_sum)
            )
            out_sum = lax.psum_scatter(out_sum, "ep", scatter_dimension=0)
            rest_sent.append([shift_rep(part[1], i + 2) for i, part in enumerate(rest)])
        grad_proj, grad_qk = attention_backward(
            step, proj, *tables, query, keys, values, lses, grad_mixed
        )
        qk_sum = qk_sum + grad_qk.reshape(-1)
        if step < micro - 1:
            grad_proj, in_sent = lax.optimization_barrier((grad_proj, in_sent))
        else:
            grad_proj, normed_sums, rest_sent, rest = lax.optimization_barrier(
                (grad_proj, normed_sums, rest_sent, rest)
            )
        grad_projs.append(grad_proj)
        grad_normed, gain_one = project_backward(step, grad_proj, stream, slab)
        gain_one_sum = gain_one_sum + gain_one
        grad_inputs.append(
            (
                grad_hidden,
                grad_normed,
            )
        )
        if step < micro - 1:
            normed_sums.append(
                lax.psum_scatter(grad_normed, "ep", scatter_dimension=0, tiled=True)
            )

    router_sum = dot(normed_two, jnp.concatenate(logit_grads, axis=0), ((0,), (0,)))
    qk_columns = qk_sum.shape[0] // dense_rows
    small = jnp.concatenate(
        [
            router_sum[:, :experts],
            jnp.concatenate([gain_one_sum, gain_two_sum], axis=1).reshape(D, 2),
            jnp.tile(qk_sum.reshape(dense_rows, qk_columns), (planes * ranks, 1)),
        ],
        axis=1,
    )
    count = small.shape[1]

    def halves(value):
        high, low = two_parts(value)
        blank = jnp.zeros((value.shape[0], PAD - 2 * count), bf16)
        return jnp.concatenate([high, low, blank], axis=1)

    def joined(value):
        return value[..., :count].astype(f32) + value[..., count : 2 * count].astype(f32)

    grad_projs, rest, out_cut, out_sent, _ = lax.optimization_barrier(
        (grad_projs, rest, out_cut, out_sent, grad_inputs[-1][1])
    )
    rest_sent.append([shift_rep(part[2], i + 2) for i, part in enumerate(rest)])
    packed = weight_gradient(
        where,
        planes,
        normed.reshape(ranks * mine, D),
        [grad.reshape(length, 3 * width) for grad in grad_projs],
        halves(small),
    )
    packed, rest_sent, out_cut, out_sent, crossed = lax.optimization_barrier(
        (packed, rest_sent, out_cut, out_sent, crossed)
    )
    packed_sent = [packed[0]] + [cross_rep(packed[step], step) for step in range(1, planes)]
    normed_sums.append(
        lax.psum_scatter(
            after(grad_inputs[-1][1], packed), "ep", scatter_dimension=0, tiled=True
        )
    )
    packed_sent, out_sum = lax.optimization_barrier((packed_sent, out_sum))
    for phase in range(1, len(bits)):
        mixtures = [total(parts).astype(bf16) for parts in crossed]
        crossed = [
            halve(number, cut_pairs(number, value, phase), phase)
            for number, value in enumerate(mixtures)
        ]
    mixture = []
    for number in range(micro):
        parts = total(crossed[number])[0]
        mixture.append((parts[0], exchange_back(parts.astype(bf16))[1:]))
    own_sum = lax.dynamic_index_in_dim(out_sum, plane, 0, keepdims=False)
    out_sent_back = [
        cross_rep(lax.dynamic_index_in_dim(out_sum, plane ^ step, 0, keepdims=False), step)
        for step in range(1, planes)
    ]
    main = total([part[:, : 3 * width] for part in packed_sent]).astype(bf16)
    small = sum(joined(part[:, 3 * width :]) for part in packed_sent)
    packed = jnp.concatenate([main, halves(small)], axis=1).reshape(ranks, dense_rows, -1)
    packed = lax.all_to_all(packed, "ep", split_axis=0, concat_axis=0, tiled=True)
    packed, mixture, out_sent_back, normed_sums = lax.optimization_barrier(
        (packed, mixture, out_sent_back, normed_sums)
    )
    grad_tokens = []
    for step in range(micro):
        own_stream = tokens[step * rows : (step + 1) * rows].astype(f32)
        grad_tokens.append(
            grad_inputs[step][0]
            + rms_backward(
                own_stream, inverse_rms(own_stream), first_gain, normed_sums[step].astype(f32)
            )
        )
    grad_tokens = jnp.concatenate(grad_tokens, axis=0)
    output = jnp.concatenate([mine_part + total(others) for mine_part, others in mixture], axis=0)
    output = (hidden + output).astype(bf16)
    grad_w_o = total([own_sum, *out_sent_back])
    grad_w_qkv, small = unpack(packed, count)
    out_sent[1] = jnp.concatenate([first, out_sent[1]], axis=0)
    grad_w_out = sum_rep({0: out_cut[0], **out_sent})
    for i in range(planes - 3):
        in_sent[i + 2] = jnp.concatenate([parts[i] for parts in rest_sent], axis=0)
    grad_w_in = sum_rep(in_sent, shift=True)
    return (
        output,
        grad_tokens,
        grad_w_qkv,
        grad_w_o,
        small[:, :experts],
        small[:, experts : experts + 2].reshape(-1),
        small[:, experts + 2 : count].reshape(-1),
        grad_w_in,
        grad_w_out,
    )


def solution(mesh):
    placed = (
        P(("rep", "ep"), None),
        P(("rep", "ep"), None),
        P(("rep", "ep"), None),
        P(("rep", "ep"), None),
        P(("rep", "ep"), None),
        P(("rep", "ep")),
        P(),
        P("ep", "rep", None),
        P("ep", "rep", None),
        P("rep", None, None),
        P(("rep", "ep"), None),
    )
    return jax.shard_map(
        on_device,
        mesh=mesh,
        in_specs=placed,
        out_specs=(
            P(("rep", "ep"), None),
            P(("rep", "ep"), None),
            P(("rep", "ep"), None),
            P(("rep", "ep"), None),
            P(("rep", "ep"), None),
            P(("rep", "ep")),
            P(),
            P("ep", "rep", None),
            P("ep", "rep", None),
        ),
        check_vma=False,
    )
```

```python
import math

import jax
import jax.numpy as jnp
from jax import lax
from jax.experimental import pallas as pl
from jax.experimental.pallas import tpu as pltpu
from jax.sharding import PartitionSpec as P

D = 2048
HEADS = 16
HD = 128
FF = 1024
TOP = 8
HALF = 512
PAD = 128

epsilon = 1e-06
rope_base = 50000.0
bf16 = jnp.bfloat16
f32 = jnp.float32


def dot(a, b, dims=((1,), (0,))):
    return lax.dot_general(a, b, (dims, ((), ())), preferred_element_type=f32)


def inverse_rms(value):
    return lax.rsqrt(jnp.mean(value * value, axis=-1, keepdims=True) + epsilon)


def rms_backward(value, inverse, gain, grad):
    scaled = grad * gain
    inner = jnp.mean(scaled * value, axis=-1, keepdims=True)
    return inverse * (scaled - value * (inverse * inverse * inner))


def doc_positions(segment):
    index = jnp.arange(segment.shape[0], dtype=jnp.int32)
    change = jnp.concatenate([jnp.ones((1,), dtype=jnp.bool_), segment[1:] != segment[:-1]])
    start = lax.cummax(jnp.where(change, index, 0), axis=0)
    return index - start


def rope_tables(position, width):
    steps = jnp.arange(width // 2, dtype=f32) * (2.0 / width)
    rates = jnp.exp(-steps * math.log(rope_base))
    angle = position.astype(f32)[:, None] * rates[None, :]
    angle = jnp.concatenate([angle, angle], axis=-1)
    return (jnp.cos(angle), jnp.sin(angle))


def norm_rope(value, gain, cosine, sine):
    inverse = lax.rsqrt(jnp.mean(value * value, axis=1, keepdims=True) + epsilon)
    value = value * inverse * gain
    return value * cosine + pltpu.roll(value, HD // 2, 1) * sine


def norm_rope_back(value, gain, cosine, sine, grad):
    inverse = lax.rsqrt(jnp.mean(value * value, axis=1, keepdims=True) + epsilon)
    grad = grad * cosine + pltpu.roll(grad * sine, HD // 2, 1)
    normal = value * inverse
    scaled = grad * gain
    inner = jnp.mean(scaled * normal, axis=1, keepdims=True)
    return inverse * (scaled - normal * inner), jnp.sum(grad * normal, axis=0, keepdims=True)


def kept_scores(query, keys, q_seg, k_seg, start):
    scores = dot(query, keys, ((1,), (1,))) * (1.0 / math.sqrt(HD))
    q_index = start + lax.broadcasted_iota(jnp.int32, scores.shape, 0)
    k_index = lax.broadcasted_iota(jnp.int32, scores.shape, 1)
    keep = (jnp.abs(q_index - k_index) <= HALF) & (q_seg == k_seg)
    return jnp.where(keep, scores, -1e30)


BIG = 100 * 1024 * 1024 // 2


def forward_kernel(
    heads, proj, cosine, sine, seg_column, seg_row, gains, mixed, query, keys, values, lses
):
    ranks, _, rows, _ = proj.shape
    length = ranks * rows
    q_block = 2 * rows
    k_seg = seg_row[0]
    for head in range(heads):
        at = slice(head * HD, (head + 1) * HD)

        def raw(part):
            first = (part * heads + head) * HD
            return proj[:, 0, :, first : first + HD].reshape(length, HD)

        query[0, :, at] = norm_rope(raw(0), gains[0:1], cosine[0], sine[0]).astype(bf16)
        keys[0, :, at] = norm_rope(raw(1), gains[1:2], cosine[0], sine[0]).astype(bf16)
        values[0, :, at] = raw(2).astype(bf16)

        @pl.loop(0, length // q_block)
        def one_block(number, head=head, at=at):
            start = pl.multiple_of(number * q_block, q_block)
            here = pl.ds(start, q_block)
            scores = kept_scores(
                query[0, here, at], keys[0, :, at], seg_column[0, here], k_seg, start
            )
            top = jnp.max(scores, axis=1, keepdims=True)
            weights = jnp.exp(scores - top)
            total = jnp.sum(weights, axis=1, keepdims=True)
            lses[0, head, here] = top + jnp.log(total)
            weights = (weights * (1.0 / total)).astype(bf16)
            result = dot(weights, values[0, :, at]).astype(bf16)
            mixed[pl.ds(number * 2, 2), 0, :, at] = result.reshape(2, rows, HD)


def backward_kernel(
    heads, proj, cosine, sine, seg_column, seg_row, gains, query, keys, values, lses, grad_mixed,
    grad_proj, grad_gains, grad_q, grad_k, grad_v,
):
    ranks, _, rows, _ = proj.shape
    length = ranks * rows
    q_block = 2 * rows
    k_seg = seg_row[0]
    scale = 1.0 / math.sqrt(HD)
    sum_q = jnp.zeros((1, HD), f32)
    sum_k = jnp.zeros((1, HD), f32)
    for head in range(heads):
        at = slice(head * HD, (head + 1) * HD)
        grad_k[...] = jnp.zeros_like(grad_k)
        grad_v[...] = jnp.zeros_like(grad_v)

        @pl.loop(0, length // q_block)
        def one_block(number, head=head, at=at):
            start = pl.multiple_of(number * q_block, q_block)
            here = pl.ds(start, q_block)
            q_rows = query[0, here, at]
            g_rows = grad_mixed[here, at]
            k_all = keys[0, :, at]
            scores = kept_scores(q_rows, k_all, seg_column[0, here], k_seg, start)
            weights = jnp.exp(scores - lses[0, head, here])
            grad_weights = dot(g_rows, values[0, :, at], ((1,), (1,)))
            delta = jnp.sum(weights * grad_weights, axis=1, keepdims=True)
            grad_scores = (weights * (grad_weights - delta)).astype(bf16)
            grad_q[here] = dot(grad_scores, k_all) * scale
            grad_k[...] += dot(grad_scores, q_rows, ((0,), (0,)))
            grad_v[...] += dot(weights.astype(bf16), g_rows, ((0,), (0,)))

        def rounded(value):
            return value.astype(bf16).astype(f32)

        def raw(part):
            first = (part * heads + head) * HD
            return proj[:, 0, :, first : first + HD].reshape(length, HD)

        def put(part, value):
            first = (part * heads + head) * HD
            grad_proj[:, :, first : first + HD] = value.astype(bf16).reshape(ranks, rows, HD)

        back_q, gain_q = norm_rope_back(
            raw(0), gains[0:1], cosine[0], sine[0], rounded(grad_q[...])
        )
        back_k, gain_k = norm_rope_back(
            raw(1), gains[1:2], cosine[0], sine[0], rounded(grad_k[...] * scale)
        )
        sum_q, sum_k = sum_q + gain_q, sum_k + gain_k
        put(0, back_q)
        put(1, back_k)
        put(2, grad_v[...])
    grad_gains[0:1] = sum_q
    grad_gains[1:2] = sum_k


def fixed(shape):
    return pl.BlockSpec(shape, lambda *_: (0,) * len(shape), pipeline_mode=pl.Buffered(1))


def leading(shape):
    return pl.BlockSpec((1,) + shape[1:], lambda i: (i,) + (0,) * (len(shape) - 1))


def params():
    return pltpu.CompilerParams(vmem_limit_bytes=BIG)


def cost(products):
    return pl.CostEstimate(flops=20 * products, bytes_accessed=0, transcendentals=0)


def out(shape, dtype=bf16):
    return jax.ShapeDtypeStruct(shape, dtype)


def attention_forward(proj, cosine, sine, seg_column, seg_row, gains):
    ranks, micro, rows, width = proj.shape
    length = ranks * rows
    width = width // 3
    heads = width // HD
    part = out((micro, length, width))
    by_rank = lambda n: pl.BlockSpec((ranks, 1, rows, n), lambda i: (0, i, 0, 0))
    lses = out((micro, heads, length, 1), f32)
    return pl.pallas_call(
        lambda *refs: forward_kernel(heads, *refs),
        grid=(micro,),
        in_specs=[by_rank(3 * width)]
        + [leading(v.shape) for v in (cosine, sine, seg_column, seg_row)]
        + [fixed(gains.shape)],
        out_specs=[by_rank(width)] + [leading(part.shape)] * 3 + [leading(lses.shape)],
        out_shape=[out((ranks, micro, rows, width)), part, part, part, lses],
        compiler_params=params(),
    )(proj, cosine, sine, seg_column, seg_row, gains)


def attention_backward(
    step, proj, cosine, sine, seg_column, seg_row, gains, query, keys, values, lses, grad_mixed
):
    ranks, micro, rows, width = proj.shape
    length = ranks * rows
    heads = width // 3 // HD

    def part(value):
        return pl.BlockSpec((1,) + value.shape[1:], lambda i: (step,) + (0,) * (value.ndim - 1))

    return pl.pallas_call(
        lambda *refs: backward_kernel(heads, *refs),
        grid=(1,),
        in_specs=[pl.BlockSpec((ranks, 1, rows, width), lambda i: (0, step, 0, 0))]
        + [part(v) for v in (cosine, sine, seg_column, seg_row)]
        + [fixed(gains.shape)]
        + [part(v) for v in (query, keys, values, lses)]
        + [fixed(grad_mixed.shape)],
        out_specs=[fixed((ranks, rows, width)), fixed((2, HD))],
        out_shape=[out((ranks, rows, width)), out((2, HD), f32)],
        scratch_shapes=[pltpu.VMEM((length, HD), f32)] * 3,
        compiler_params=params(),
    )(
        proj, cosine, sine, seg_column, seg_row, gains, query, keys, values, lses, grad_mixed
    )


def project(micro, tokens, gain, slab):
    ranks, count, _ = tokens.shape
    rows = count // micro
    width = slab.shape[1] - PAD

    def kernel(value, gain, weight, normed, proj):
        value = value[0].astype(f32)
        result = (value * inverse_rms(value) * gain[...]).astype(bf16)
        normed[...] = result.reshape(micro, 1, rows, D)
        proj[0] = dot(result, weight[:, :width])

    return pl.pallas_call(
        kernel,
        grid=(ranks,),
        in_specs=[leading((ranks, count, D)), fixed((1, D)), fixed(slab.shape)],
        out_specs=[
            pl.BlockSpec((micro, 1, rows, D), lambda i: (0, i, 0, 0)),
            leading((ranks, count, width)),
        ],
        out_shape=[out((micro, ranks, rows, D)), out((ranks, count, width), f32)],
        compiler_params=params(),
    )(tokens, gain, slab)


TILE = 512


def tiles(count):
    return pl.loop(0, count // TILE)


def tile(number):
    return pl.ds(pl.multiple_of(number * TILE, TILE), TILE)


HBM = pl.BlockSpec(memory_space=pl.ANY)


def copies(pairs, sems):
    started = [
        pltpu.make_async_copy(source, target, sems.at[place])
        for place, (source, target) in enumerate(pairs)
    ]
    for copy in started:
        copy.start()

    def wait():
        for copy in started:
            copy.wait()

    return wait


def plane_pairs(plane, pieces, target):
    planes = len(pieces)
    rows = target.shape[0] // planes
    return [
        (piece, target.at[pl.ds(lax.bitwise_xor(plane, jnp.int32(step)) * rows, rows)])
        for step, piece in enumerate(pieces)
    ]


def out_weight_pairs(plane, planes, gathered, target):
    ranks = gathered.shape[0]
    rows = D // (planes * ranks)
    return [
        (
            gathered.at[rank, pl.ds(step * rows, rows)],
            target.at[
                pl.ds((lax.bitwise_xor(plane, jnp.int32(step)) * ranks + rank) * rows, rows)
            ],
        )
        for rank in range(ranks)
        for step in range(planes)
    ]


def route(plane, planes, mixed, tokens, gathered, gain, router, routes, experts):
    count = tokens.shape[0]
    pieces = planes * gathered.shape[0]

    def kernel(
        plane, mixed, tokens, gathered, gain, router, routes, hidden, payload, gates,
        out_weight, sems,
    ):
        copies(out_weight_pairs(plane[0], planes, gathered, out_weight), sems)()

        @tiles(D)
        def _(number):
            at = tile(number)
            hidden[:, at] = tokens[:, at].astype(f32) + dot(mixed[...], out_weight[:, at])

        value = hidden[...]
        normed = (value * inverse_rms(value) * gain[...]).astype(bf16)
        payload[:, :D] = normed
        logits = dot(normed, router[...])
        column = lax.broadcasted_iota(jnp.int32, logits.shape, 1)
        routed = column == routes[:, 0:1]
        for choice in range(1, TOP):
            routed = routed | (column == routes[:, choice : choice + 1])
        logits = jnp.where(routed, logits, -1e30)
        weights = jnp.exp(logits - jnp.max(logits, axis=1, keepdims=True))
        weights = jnp.where(routed, weights, 0.0)
        weights = weights / jnp.sum(weights, axis=1, keepdims=True)
        gates[...] = weights
        high = weights.astype(bf16).astype(f32)
        payload[:, D:] = (high + pltpu.roll(weights - high, experts, 1)).astype(bf16)

    shapes = [out((count, D), f32), out((count, D + PAD)), out((count, PAD), f32)]
    return pl.pallas_call(
        kernel,
        grid_spec=pltpu.PrefetchScalarGridSpec(
            num_scalar_prefetch=1,
            grid=(1,),
            in_specs=[
                HBM if value is gathered else fixed(value.shape)
                for value in (mixed, tokens, gathered, gain, router, routes)
            ],
            out_specs=[fixed(shape.shape) for shape in shapes],
            scratch_shapes=[pltpu.VMEM((D, D), bf16), pltpu.SemaphoreType.DMA((pieces,))],
        ),
        out_shape=shapes,
        compiler_params=params(),
    )(plane, mixed, tokens, gathered, gain, router, routes)


def lane(value, number):
    column = lax.broadcasted_iota(jnp.int32, value.shape, 1)
    return jnp.sum(jnp.where(column == number, value.astype(f32), 0.0), axis=1, keepdims=True)


def one_hot(slot, slots):
    place = lax.broadcasted_iota(jnp.int32, (slots, slot.shape[1]), 0).astype(f32)
    return (place == slot).astype(bf16)


def expert_forward(where, payload, upstream, in_pieces, slots, experts):
    ranks, share, micro, rows, _ = payload.shape
    count = share * rows
    block = 2 * slots

    planes = len(in_pieces)

    def kernel(where, payload, upstream, *refs):
        (
            rows_in, tail, both, active, grad_produced, up_rows, places, in_weight, sems
        ) = refs[planes:]
        number = where[0]

        @pl.when((pl.program_id(0) == 0) & (pl.program_id(1) == 0))
        def _():
            copies(plane_pairs(where[1], refs[:planes], in_weight), sems)()

        for part in range(2):
            here = slice(part * slots, (part + 1) * slots)
            value = payload[part].reshape(count, D + PAD)
            marks = value[:, D:]
            first = lax.broadcasted_iota(jnp.int32, (8, PAD), 1) == number
            taken = dot(first.astype(bf16), marks, ((1,), (1,))) > 0.0
            before = lax.broadcasted_iota(jnp.int32, (count, count), 0)
            behind = lax.broadcasted_iota(jnp.int32, (count, count), 1)
            slot = dot(taken.astype(bf16), (before < behind).astype(bf16))
            select = one_hot(jnp.where(taken, slot, -1.0)[0:1], slots)
            wide = jnp.broadcast_to(lane(marks, number) > 0.0, (count, PAD))
            slot = dot((before > behind).astype(bf16), wide.astype(bf16))
            places[0, 0, part] = jnp.where(wide, slot, -1.0)
            rows_in[0, 0, here] = dot(select, value[:, :D]).astype(bf16)
            marks = dot(select, marks)
            tail[0, 0, here] = marks
            gate = lane(marks, number) + lane(marks, experts + number)
            picked = dot(select, upstream[part].reshape(count, D))
            up_rows[0, 0, here] = picked.astype(bf16)
            grad_produced[0, 0, here] = (gate * picked).astype(bf16)

        for number in range(FF // TILE):
            at = slice(number * TILE, (number + 1) * TILE)
            more = slice(FF + number * TILE, FF + (number + 1) * TILE)
            gate_part = dot(rows_in[0, 0], in_weight[:, at])
            up_part = dot(rows_in[0, 0], in_weight[:, more])
            both[0, 0, :, at] = gate_part
            both[0, 0, :, more] = up_part
            active[0, 0, :, at] = (
                gate_part / (1.0 + jnp.exp(-gate_part)) * up_part
            ).astype(bf16)

    def tokens_spec(width):
        return pl.BlockSpec((2, share, 1, rows, width), lambda m, b, _: (b, 0, m, 0, 0))

    pairs = ranks // 2
    shapes = [
        out((micro, pairs, block, D)),
        out((micro, pairs, block, PAD), f32),
        out((micro, pairs, block, 2 * FF), f32),
        out((micro, pairs, block, FF)),
        out((micro, pairs, block, D)),
        out((micro, pairs, block, D)),
        out((micro, pairs, 2, count, PAD), f32),
    ]
    return pl.pallas_call(
        kernel,
        grid_spec=pltpu.PrefetchScalarGridSpec(
            num_scalar_prefetch=1,
            grid=(micro, pairs),
            in_specs=[tokens_spec(D + PAD), tokens_spec(D)] + [HBM] * planes,
            out_specs=[
                pl.BlockSpec(
                    (1, 1) + s.shape[2:], lambda m, b, _, n=len(s.shape): (m, b) + (0,) * (n - 2)
                )
                for s in shapes
            ],
            scratch_shapes=[pltpu.VMEM((D, 2 * FF), bf16), pltpu.SemaphoreType.DMA((planes,))],
        ),
        out_shape=shapes,
        cost_estimate=cost(micro * pairs * block * D * (2 * FF + 2 * count)),
        compiler_params=params(),
    )(where, payload, upstream, *in_pieces)


def expert_backward(
    step, where, tail, both, active, grad_produced, up_rows, places, in_pieces, out_pieces,
    share, rows, experts,
):
    pairs, block = tail.shape[1:3]
    slots = block // 2
    count = places.shape[3]

    planes = len(in_pieces)

    def kernel(where, tail, both, active, grad_produced, up_rows, places, *refs):
        keep, give, grad_tokens, grad_both, in_weight, out_weight, sems = refs[2 * planes :]
        number = where[0]
        odd = where[2] == 1

        @pl.when(pl.program_id(0) == 0)
        def _():
            copies(
                plane_pairs(where[1], refs[:planes], in_weight)
                + plane_pairs(where[1], refs[planes : 2 * planes], out_weight),
                sems,
            )()

        gate = lane(tail[0, 0], number) + lane(tail[0, 0], experts + number)
        place = lax.broadcasted_iota(jnp.int32, (count, slots), 1).astype(f32)
        selects = [(places[0, 0, part][:, 0:1] == place).astype(bf16) for part in range(2)]

        def spread(value):
            return [
                dot(selects[part], value[part * slots : (part + 1) * slots])
                .astype(bf16)
                .reshape(share, rows, -1)
                for part in range(2)
            ]

        grad_gate = jnp.zeros((block, 1), f32)
        for tile in range(D // TILE):
            at = slice(tile * TILE, (tile + 1) * TILE)
            produced = dot(active[0, 0], out_weight[:, at]).astype(bf16).astype(f32)
            even_rank, odd_rank = spread((gate * produced).astype(bf16))
            keep[0, :, :, at] = jnp.where(odd, odd_rank, even_rank)
            give[0, :, :, at] = jnp.where(odd, even_rank, odd_rank)
            grad_gate = grad_gate + jnp.sum(
                up_rows[0, 0, :, at].astype(f32) * produced, axis=1, keepdims=True
            )

        for tile in range(FF // TILE):
            at = slice(tile * TILE, (tile + 1) * TILE)
            more = slice(FF + tile * TILE, FF + (tile + 1) * TILE)
            grad_active = dot(grad_produced[0, 0], out_weight[at, :], ((1,), (1,)))
            grad_active = grad_active.astype(bf16).astype(f32)
            gate_part = both[0, 0, :, at]
            up_part = both[0, 0, :, more]
            sigma = 1.0 / (1.0 + jnp.exp(-gate_part))
            grad_both[0, :, at] = (
                grad_active * up_part * (sigma * (1.0 + gate_part * (1.0 - sigma)))
            ).astype(bf16)
            grad_both[0, :, more] = (grad_active * (gate_part * sigma)).astype(bf16)

        for tile in range(D // TILE):
            at = slice(tile * TILE, (tile + 1) * TILE)
            grad_rows = dot(grad_both[0], in_weight[at, :], ((1,), (1,))).astype(bf16)
            grad_tokens[0, :, :, at], grad_tokens[1, :, :, at] = spread(grad_rows)

        high = grad_gate.astype(bf16).astype(f32)
        column = lax.broadcasted_iota(jnp.int32, (block, PAD), 1)
        extra = jnp.where(column == number, high, 0.0)
        extra = jnp.where(column == experts + number, grad_gate - high, extra)
        grad_tokens[0, :, :, D:], grad_tokens[1, :, :, D:] = spread(extra.astype(bf16))

    def part(value):
        return pl.BlockSpec(
            (1, 1) + value.shape[2:], lambda b, _: (step, b) + (0,) * (value.ndim - 2)
        )

    def tokens_spec(count, width):
        return pl.BlockSpec((count, share, rows, width), lambda b, _: (b, 0, 0, 0))

    return pl.pallas_call(
        kernel,
        grid_spec=pltpu.PrefetchScalarGridSpec(
            num_scalar_prefetch=1,
            grid=(pairs,),
            in_specs=[part(v) for v in (tail, both, active, grad_produced, up_rows, places)]
            + [HBM] * (2 * planes),
            out_specs=[
                tokens_spec(1, D),
                tokens_spec(1, D),
                tokens_spec(2, D + PAD),
                pl.BlockSpec((1, block, 2 * FF), lambda b, _: (b, 0, 0)),
            ],
            scratch_shapes=[
                pltpu.VMEM((D, 2 * FF), bf16),
                pltpu.VMEM((FF, D), bf16),
                pltpu.SemaphoreType.DMA((2 * planes,)),
            ],
        ),
        out_shape=[
            out((pairs, share, rows, D)),
            out((pairs, share, rows, D)),
            out((2 * pairs, share, rows, D + PAD)),
            out((pairs, block, 2 * FF)),
        ],
        cost_estimate=cost(pairs * block * D * (4 * FF + 2 * count)),
        compiler_params=params(),
    )(
        where, tail, both, active, grad_produced, up_rows, places, *in_pieces, *out_pieces
    )


def cut_ends(count, places):
    return [-(-count * place // 512) * 16 for place in (0, *places, 32)]


def weight_gradient(
    where, planes, left, rights, tail=None, first=0, steps=None, shift=False, cuts=None
):
    steps = planes if steps is None else steps
    count, width = left.shape
    parts = len(rights)
    part_rows = count // parts
    columns = rights[0].shape[1]
    width = width // planes
    step = min(TILE, columns & -columns)
    tails = [] if tail is None else [tail]
    whole = columns + sum(value.shape[1] for value in tails)

    ends = [cut_ends(width, (cuts or {}).get(number, ())) for number in range(steps)]
    shapes = [
        out((end - start, whole)) for one in ends for start, end in zip(one, one[1:])
    ]

    def of_plane(i, where):
        return (where[1] + first + i) % planes if shift else lax.bitwise_xor(where[1], first + i)

    def kernel(where, left, *refs):
        rights, tails, targets = refs[:parts], refs[parts : -len(shapes)], refs[-len(shapes) :]

        def fill(targets, ends):
            for value in tails:
                targets[0][:, columns:] = value[...]
            for number in range(columns // step):
                at = slice(number * step, (number + 1) * step)
                result = sum(
                    dot(left[part * part_rows : (part + 1) * part_rows], right[:, at], ((0,), (0,)))
                    for part, right in enumerate(rights)
                ).astype(bf16)
                for target, start, end in zip(targets, ends, ends[1:]):
                    target[:, at] = result[start:end]

        done = 0
        for number, one in enumerate(ends):
            mine = targets[done : done + len(one) - 1]
            done += len(one) - 1
            pl.when(pl.program_id(0) == number)(lambda mine=mine, one=one: fill(mine, one))

    return pl.pallas_call(
        kernel,
        grid_spec=pltpu.PrefetchScalarGridSpec(
            num_scalar_prefetch=1,
            grid=(steps,),
            in_specs=[pl.BlockSpec((count, width), lambda i, where: (0, of_plane(i, where)))]
            + [fixed(right.shape) for right in rights]
            + [
                pl.BlockSpec((width, value.shape[1]), lambda i, where: (of_plane(i, where), 0))
                for value in tails
            ],
            out_specs=[fixed(shape.shape) for shape in shapes],
        ),
        out_shape=shapes,
        cost_estimate=cost(0 if tails else count * steps * width * columns),
        compiler_params=params(),
    )(where, left, *rights, *tails)


def hidden_backward(
    step, plane, planes, parts, hidden, gates, upstream, gain, router, gathered, experts
):
    first = parts[0].shape
    count = first[1]
    terms = len(parts)

    def kernel(plane, *refs):
        parts = refs[:terms]
        hidden, gates, upstream, gain, router, gathered = refs[terms : terms + 6]
        (
            grad_hidden, grad_branch, grad_mixed, grad_logits, grad_gain, out_weight, sems
        ) = refs[terms + 6 :]
        wait = copies(out_weight_pairs(plane[0], planes, gathered, out_weight), sems)
        returned = sum(part[...].astype(f32) for part in parts[1:]) + parts[0][0].astype(f32)
        tail = returned[:, D:]
        grad_gates = gates[...] * (tail + pltpu.roll(tail, PAD - experts, 1))
        logits = grad_gates - gates[...] * jnp.sum(grad_gates, axis=1, keepdims=True)
        logits = logits.astype(bf16)
        grad_logits[...] = logits
        grad_normed = returned[:, :D] + dot(logits, router[...], ((1,), (1,)))
        value = hidden[...]
        inverse = inverse_rms(value)
        grad_gain[...] = jnp.sum(grad_normed * value * inverse, axis=0, keepdims=True)
        grad = upstream[...].astype(f32) + rms_backward(value, inverse, gain[...], grad_normed)
        grad_hidden[...] = grad
        grad_branch[...] = grad.astype(bf16)
        wait()

        @tiles(D)
        def _(number):
            at = tile(number)
            grad_mixed[:, at] = dot(grad_branch[...], out_weight[at, :], ((1,), (1,))).astype(bf16)

    shapes = [
        out((count, D), f32), out((count, D)), out((count, D)), out((count, PAD)),
        out((1, D), f32),
    ]
    args = (*parts, hidden, gates, upstream, gain, router, gathered)

    def spec(value):
        if value is gathered:
            return HBM
        if value is parts[0]:
            return pl.BlockSpec((1,) + first[1:], lambda *_: (0, 0, 0))
        if any(value is rows for rows in (hidden, gates, upstream)):
            return pl.BlockSpec((count, value.shape[1]), lambda *_: (step, 0))
        return fixed(value.shape)

    return pl.pallas_call(
        kernel,
        grid_spec=pltpu.PrefetchScalarGridSpec(
            num_scalar_prefetch=1,
            grid=(1,),
            in_specs=[spec(value) for value in args],
            out_specs=[fixed(shape.shape) for shape in shapes],
            scratch_shapes=[
                pltpu.VMEM((D, D), bf16),
                pltpu.SemaphoreType.DMA((planes * gathered.shape[0],)),
            ],
        ),
        out_shape=shapes,
        compiler_params=params(),
    )(plane, *args)


def project_backward(step, grad_proj, tokens, slab):
    ranks, rows, _ = grad_proj.shape
    width = slab.shape[1] - PAD

    def kernel(grad_proj, tokens, weight, grad_normed, grad_gain):
        value = tokens[...].reshape(2 * rows, D).astype(f32)
        inverse = inverse_rms(value)
        grad = dot(grad_proj[...].reshape(2 * rows, width), weight[:, :width], ((1,), (1,)))
        grad_normed[...] = grad.astype(bf16)

        @pl.when(pl.program_id(0) == 0)
        def _():
            grad_gain[...] = jnp.zeros_like(grad_gain)

        grad_gain[...] += jnp.sum(grad * value * inverse, axis=0, keepdims=True)

    return pl.pallas_call(
        kernel,
        grid=(ranks // 2,),
        in_specs=[
            pl.BlockSpec((2, rows, width), lambda i: (i, 0, 0)),
            pl.BlockSpec((2, rows, D), lambda i: (i, step, 0)),
            fixed(slab.shape),
        ],
        out_specs=[pl.BlockSpec((2 * rows, D), lambda i: (i, 0)), fixed((1, D))],
        out_shape=[out((ranks * rows, D)), out((1, D), f32)],
        compiler_params=params(),
    )(grad_proj, tokens, slab)


def cut_heads(weight, tail, ranks):
    rows = weight.shape[0]
    width = D // ranks

    def kernel(weight, tail, target):
        for rank in range(ranks):
            for part in range(3):
                at = part * D + rank * width
                target[rank, :, part * width : (part + 1) * width] = weight[:, at : at + width]
            target[rank, :, 3 * width :] = tail[...]

    return pl.pallas_call(
        kernel,
        out_shape=out((ranks, rows, 3 * width + PAD)),
        compiler_params=params(),
    )(weight, tail)


def unpack(packed, count):
    ranks, rows, columns = packed.shape
    width = (columns - PAD) // 3

    def kernel(packed, main, small):
        for rank in range(ranks):
            for part in range(3):
                at = part * D + rank * width
                main[:, at : at + width] = packed[rank, :, part * width : (part + 1) * width].astype(
                    f32
                )
        tails = sum(packed[rank, :, 3 * width :].astype(f32) for rank in range(ranks))
        small[...] = tails + pltpu.roll(tails, PAD - count, 1)

    return pl.pallas_call(
        kernel,
        out_shape=[out((rows, 3 * D), f32), out((rows, PAD), f32)],
        compiler_params=params(),
    )(packed)


def shift_rep(value, step):
    count = lax.axis_size("rep")
    return lax.ppermute(value, "rep", [(i, (i + step) % count) for i in range(count)])


def cross_rep(value, bits):
    return lax.ppermute(value, "rep", [(i, i ^ bits) for i in range(lax.axis_size("rep"))])


def after(value, *others):
    return lax.optimization_barrier((value,) + others)[0]


def two_parts(value):
    high = lax.reduce_precision(value, 8, 7)
    return high.astype(bf16), (value - high).astype(bf16)


def ring_rep(value, *work):
    count = lax.axis_size("rep")
    rank = lax.axis_index("rep")
    rows = value.shape[0]
    full = jnp.zeros((count * rows,) + value.shape[1:], value.dtype)
    full = lax.dynamic_update_slice_in_dim(full, value, rank * rows, 0)
    for step in range(1, count):
        value, work = lax.optimization_barrier((value, work)) if step == count - 1 else (value, work)
        value = shift_rep(value, 1)
        full = lax.dynamic_update_slice_in_dim(full, value, (rank - step) % count * rows, 0)
    return full, work


def on_device(
    tokens, cotangent, w_qkv, w_o, w_router, norm_gains, qk_gain, w_in, w_out, segments, routes
):
    planes = lax.axis_size("rep")
    ranks = lax.axis_size("ep")
    plane = lax.axis_index("rep")
    rank = lax.axis_index("ep")
    share = w_in.shape[0]
    own = plane % share
    experts = share * ranks
    where = jnp.stack([rank * share + own, plane, rank % 2]).astype(jnp.int32)
    micro = segments.shape[1]
    mine = tokens.shape[0]
    rows = mine // micro
    length = rows * ranks
    capacity = rows * TOP * 17 // (16 * experts)
    slots = -(-share * capacity // 16) * 16
    width = HEADS // ranks * HD
    qk_gains = qk_gain.astype(f32).reshape(2, HD)
    dense_rows = w_qkv.shape[0]

    def exchange(value, step):
        pairs = [(i, i // share * share + (i % share + step) % share) for i in range(planes)]
        return lax.ppermute(value, "rep", pairs)

    def with_group(value):
        return jnp.stack([value] + [exchange(value, step) for step in range(1, share)])

    def gather_ranks(value):
        return lax.all_gather(value, "ep", axis=0)

    assert planes & (planes - 1) == 0 and share & (share - 1) == 0
    last_step = planes - 1
    in_parts, out_parts = (
        {
            step: lax.dynamic_index_in_dim(weight, own ^ step % share, 0, keepdims=False)
            for step in range(planes)
        }
        for weight in (w_in, w_out)
    )

    def send(parts, steps):
        return {step: cross_rep(parts[step], step) for step in steps}

    stream = gather_ranks(tokens)
    out_rows = [w_o] + [cross_rep(w_o, step) for step in range(1, planes)]
    upstream_group = with_group(cotangent)
    early_rows = cut_ends(out_parts[last_step].shape[0], (12,))[1]
    early = cross_rep(out_parts[last_step][:early_rows], last_step)
    slab = cut_heads(
        w_qkv,
        jnp.concatenate(
            [
                w_router,
                norm_gains.reshape(dense_rows, 2),
                jnp.zeros((dense_rows, PAD - experts - 2), bf16),
            ],
            axis=1,
        ),
        ranks,
    )
    slab = lax.all_to_all(slab, "ep", split_axis=0, concat_axis=0, tiled=True)
    slab = slab.reshape(ranks * dense_rows, 3 * width + PAD)
    out_rows, upstream_group, slab, early = lax.optimization_barrier(
        (out_rows, upstream_group, slab, early)
    )
    gathered = gather_ranks(jnp.concatenate(out_rows, axis=0))
    segment = segments[0]
    cosine, sine = jax.vmap(lambda one: rope_tables(doc_positions(one), HD))(segment)
    sine = jnp.where(jnp.arange(HD) < HD // 2, -sine, sine)
    tables = (cosine, sine, segment[:, :, None], segment[:, None, :], qk_gains)
    slab, (tables, in_parts, out_parts) = ring_rep(slab, tables, in_parts, out_parts)
    router = slab[:, 3 * width :]
    gain_pair = router[:, experts : experts + 2].reshape(-1).astype(f32)
    first_gain = gain_pair[None, :D]
    second_gain = gain_pair[None, D:]
    in_parts, out_parts, upstream_group, stream = after(
        (in_parts, out_parts, upstream_group, stream), slab
    )
    in_pieces = {0: in_parts[0], **send(in_parts, range(last_step - 1, 0, -1))}
    upstream_all = gather_ranks(upstream_group)

    normed, proj = project(micro, stream, first_gain, slab)
    proj = proj.reshape(ranks, micro, rows, 3 * width)
    mixed_h, query, keys, values, lses = attention_forward(proj, *tables)
    mixed = lax.all_to_all(mixed_h, "ep", split_axis=0, concat_axis=3, tiled=True)
    mixed = mixed.reshape(mine, D)
    hidden, payload, gates = route(
        where[1:2], planes, mixed, tokens, gathered, second_gain, router, routes, experts
    )
    normed_two = payload[:, :D]
    payload, in_pieces = lax.optimization_barrier((payload, in_pieces))
    payload = with_group(payload)
    payload, in_parts, out_parts = lax.optimization_barrier((payload, in_parts, out_parts))
    in_pieces.update(send(in_parts, [last_step]))
    in_pieces, out_parts = lax.optimization_barrier((in_pieces, out_parts))
    out_parts[last_step] = out_parts[last_step][early_rows:]
    out_pieces = {0: out_parts[0], **send(out_parts, range(1, planes))}
    in_pieces = [in_pieces[step] for step in range(planes)]
    out_pieces = [out_pieces[step] for step in range(planes)]
    payload = gather_ranks(payload)

    shape = (ranks, share, micro, rows, -1)
    rows_in, tail, both, active, grad_produced, up_rows, places = expert_forward(
        where, payload.reshape(shape), upstream_all.reshape(shape), in_pieces, slots, experts
    )
    in_rows = micro * ranks * slots
    out_cut = weight_gradient(
        where, planes, active.reshape(in_rows, FF), [grad_produced.reshape(in_rows, D)]
    )

    def sum_rep(parts, shift=False):
        sums = [
            sum(parts[step].astype(f32) for step in range(first, planes, share))
            for first in range(share)
        ]
        return jnp.stack(
            [
                sum(
                    jnp.where(((own - step) % share if shift else own ^ step) == j, sums[step], 0.0)
                    for step in range(share)
                )
                for j in range(share)
            ]
        )

    tail, out_cut, out_pieces = lax.optimization_barrier((tail, out_cut, out_pieces))
    out_pieces[last_step] = jnp.concatenate([early, out_pieces[last_step]], axis=0)
    first = cross_rep(out_cut[1][:16], 1)
    tail, out_cut, first = lax.optimization_barrier((tail, out_cut, first))
    out_sent = send([out_cut[0], out_cut[1][16:], *out_cut[2:]], range(1, planes))
    back = []
    returned = []

    def scatter_ranks(value):
        return lax.psum_scatter(value, "ep", scatter_dimension=0)

    def exchange_back(value):
        return [value] + [exchange(value[step], share - step) for step in range(1, share)]

    for step in range(micro):
        back.append(
            expert_backward(
                step, where, tail, both, active, grad_produced, up_rows, places, in_pieces,
                out_pieces, share, rows, experts,
            )
        )
        returned.append(scatter_ranks(back[step][2]))
        if step == 0:
            tail, out_sent[last_step] = after((tail, out_sent[last_step]), back[step][2])
        else:
            tail = after(tail, back[step][2])
    rows_in = after(rows_in, tail)
    rows_flat = rows_in.reshape(in_rows, D)
    grads_flat = [back[step][3].reshape(in_rows // micro, 2 * FF) for step in range(micro)]
    in_near = weight_gradient(
        where, planes, rows_flat, grads_flat, first=1, steps=1, shift=True, cuts={0: (24,)}
    )
    rows_flat, in_near = lax.optimization_barrier((rows_flat, in_near))
    cuts = {number: (20, 28) for number in range(planes - 3)}
    *in_rest, in_back, in_own = weight_gradient(
        where, planes, rows_flat, grads_flat, first=2, steps=last_step, shift=True, cuts=cuts
    )
    in_sent = {0: in_own}
    near_sent = [shift_rep(in_near[0], 1)]

    def swap(value, step):
        return lax.ppermute(value, "ep", [(i, i ^ step) for i in range(ranks)])

    bits = list(range((ranks // 2).bit_length() - 1))

    def cut_pairs(number, value, phase):
        way = bits if number % 2 == 0 else bits[::-1]
        bit = way[phase]
        low = 2 ** sum(other < bit for other in way[phase:])
        value = value.reshape((-1, 2, low) + value.shape[1:])
        side = rank // 2 // 2**bit % 2
        return [
            lax.dynamic_index_in_dim(value, which, 1, keepdims=False).reshape((-1,) + value.shape[3:])
            for which in (side, 1 - side)
        ]

    def pair_sum(number, keep, give):
        got = swap(give, 1)
        return [
            total(parts).astype(bf16)
            for parts in zip(cut_pairs(number, keep, 0), cut_pairs(number, got, 0))
        ]

    def halve(number, halves, phase):
        return halves[0], swap(halves[1], 2 * 2 ** (bits if number % 2 == 0 else bits[::-1])[phase])

    def total(parts):
        return sum(part.astype(f32) for part in parts)

    grad_inputs, branches, logit_grads, grad_projs, normed_sums = [], [], [], [], []
    gain_two_sum = gain_one_sum = qk_sum = 0.0
    in_rest, in_back, in_near, out_sent, near_sent = lax.optimization_barrier(
        (in_rest, in_back, in_near, out_sent, near_sent)
    )
    mixtures = [part[:2] for part in back]
    for step in range(micro):
        parts = after(returned[step], [one[1] for one in grad_inputs])
        parts, near_sent = lax.optimization_barrier((parts, near_sent))
        if step == micro - 1:
            mixtures = after(mixtures, parts)
            crossed = [halve(number, value, 0) for number, value in enumerate(mixtures)]
        parts = exchange_back(parts)
        parts, in_rest, in_back, in_near, mixtures = lax.optimization_barrier(
            (parts, in_rest, in_back, in_near, mixtures)
        )
        if step == 0:
            mixtures = [pair_sum(number, *part) for number, part in enumerate(mixtures)]
            in_sent[last_step] = shift_rep(in_back, last_step)
            near_sent.append(shift_rep(in_near[1], 1))
        if step == micro - 1:
            rest = [in_rest[3 * i : 3 * i + 3] for i in range(planes - 3)]
            rest_sent = [[shift_rep(part[0], i + 2) for i, part in enumerate(rest)]]
        grad_hidden, grad_branch, grad_mixed, grad_logits, gain_two = hidden_backward(
            step, where[1:2], planes, parts, hidden, gates, cotangent, second_gain, router, gathered,
            experts,
        )
        branches.append(grad_branch)
        logit_grads.append(grad_logits)
        gain_two_sum = gain_two_sum + gain_two
        if step == micro - 1:
            out_sum = dot(mixed, jnp.concatenate(branches, axis=0), ((0,), (0,))).astype(bf16)
            out_sum = out_sum.reshape(planes, ranks, dense_rows, D).transpose(1, 0, 2, 3)
        grad_mixed = lax.all_to_all(grad_mixed, "ep", split_axis=1, concat_axis=0, tiled=True)
        grad_mixed, mixtures = lax.optimization_barrier((grad_mixed, mixtures))
        if step == micro - 1:
            grad_mixed, crossed, rest_sent, rest, out_sum = lax.optimization_barrier(
                (grad_mixed, crossed, rest_sent, rest, out_sum)
            )
            out_sum = lax.psum_scatter(out_sum, "ep", scatter_dimension=0)
            rest_sent.append([shift_rep(part[1], i + 2) for i, part in enumerate(rest)])
        grad_proj, grad_qk = attention_backward(
            step, proj, *tables, query, keys, values, lses, grad_mixed
        )
        qk_sum = qk_sum + grad_qk.reshape(-1)
        if step < micro - 1:
            grad_proj, in_sent, near_sent = lax.optimization_barrier(
                (grad_proj, in_sent, near_sent)
            )
        else:
            grad_proj, normed_sums, rest_sent, rest = lax.optimization_barrier(
                (grad_proj, normed_sums, rest_sent, rest)
            )
        grad_projs.append(grad_proj)
        grad_normed, gain_one = project_backward(step, grad_proj, stream, slab)
        gain_one_sum = gain_one_sum + gain_one
        grad_inputs.append(
            (
                grad_hidden,
                grad_normed,
            )
        )
        if step < micro - 1:
            normed_sums.append(
                lax.psum_scatter(grad_normed, "ep", scatter_dimension=0, tiled=True)
            )

    router_sum = dot(normed_two, jnp.concatenate(logit_grads, axis=0), ((0,), (0,)))
    qk_columns = qk_sum.shape[0] // dense_rows
    small = jnp.concatenate(
        [
            router_sum[:, :experts],
            jnp.concatenate([gain_one_sum, gain_two_sum], axis=1).reshape(D, 2),
            jnp.tile(qk_sum.reshape(dense_rows, qk_columns), (planes * ranks, 1)),
        ],
        axis=1,
    )
    count = small.shape[1]

    def halves(value):
        high, low = two_parts(value)
        blank = jnp.zeros((value.shape[0], PAD - 2 * count), bf16)
        return jnp.concatenate([high, low, blank], axis=1)

    def joined(value):
        return value[..., :count].astype(f32) + value[..., count : 2 * count].astype(f32)

    grad_projs, rest, out_cut, out_sent, _ = lax.optimization_barrier(
        (grad_projs, rest, out_cut, out_sent, grad_inputs[-1][1])
    )
    rest_sent.append([shift_rep(part[2], i + 2) for i, part in enumerate(rest)])
    packed = weight_gradient(
        where,
        planes,
        normed.reshape(ranks * mine, D),
        [grad.reshape(length, 3 * width) for grad in grad_projs],
        halves(small),
    )
    packed, rest_sent, out_cut, out_sent, crossed = lax.optimization_barrier(
        (packed, rest_sent, out_cut, out_sent, crossed)
    )
    packed_sent = [packed[0]] + [cross_rep(packed[step], step) for step in range(1, planes)]
    normed_sums.append(
        lax.psum_scatter(
            after(grad_inputs[-1][1], packed), "ep", scatter_dimension=0, tiled=True
        )
    )
    packed_sent, out_sum = lax.optimization_barrier((packed_sent, out_sum))
    for phase in range(1, len(bits)):
        mixtures = [total(parts).astype(bf16) for parts in crossed]
        crossed = [
            halve(number, cut_pairs(number, value, phase), phase)
            for number, value in enumerate(mixtures)
        ]
    mixture = []
    for number in range(micro):
        parts = total(crossed[number])[0]
        mixture.append((parts[0], exchange_back(parts.astype(bf16))[1:]))
    own_sum = lax.dynamic_index_in_dim(out_sum, plane, 0, keepdims=False)
    out_sent_back = [
        cross_rep(lax.dynamic_index_in_dim(out_sum, plane ^ step, 0, keepdims=False), step)
        for step in range(1, planes)
    ]
    main = total([part[:, : 3 * width] for part in packed_sent]).astype(bf16)
    small = sum(joined(part[:, 3 * width :]) for part in packed_sent)
    packed = jnp.concatenate([main, halves(small)], axis=1).reshape(ranks, dense_rows, -1)
    packed = lax.all_to_all(packed, "ep", split_axis=0, concat_axis=0, tiled=True)
    packed, mixture, out_sent_back, normed_sums = lax.optimization_barrier(
        (packed, mixture, out_sent_back, normed_sums)
    )
    grad_tokens = []
    for step in range(micro):
        own_stream = tokens[step * rows : (step + 1) * rows].astype(f32)
        grad_tokens.append(
            grad_inputs[step][0]
            + rms_backward(
                own_stream, inverse_rms(own_stream), first_gain, normed_sums[step].astype(f32)
            )
        )
    grad_tokens = jnp.concatenate(grad_tokens, axis=0)
    output = jnp.concatenate([mine_part + total(others) for mine_part, others in mixture], axis=0)
    output = (hidden + output).astype(bf16)
    grad_w_o = total([own_sum, *out_sent_back])
    grad_w_qkv, small = unpack(packed, count)
    out_sent[1] = jnp.concatenate([first, out_sent[1]], axis=0)
    grad_w_out = sum_rep({0: out_cut[0], **out_sent})
    in_sent[1] = jnp.concatenate(near_sent, axis=0)
    for i in range(planes - 3):
        in_sent[i + 2] = jnp.concatenate([parts[i] for parts in rest_sent], axis=0)
    grad_w_in = sum_rep(in_sent, shift=True)
    return (
        output,
        grad_tokens,
        grad_w_qkv,
        grad_w_o,
        small[:, :experts],
        small[:, experts : experts + 2].reshape(-1),
        small[:, experts + 2 : count].reshape(-1),
        grad_w_in,
        grad_w_out,
    )


def solution(mesh):
    placed = (
        P(("rep", "ep"), None),
        P(("rep", "ep"), None),
        P(("rep", "ep"), None),
        P(("rep", "ep"), None),
        P(("rep", "ep"), None),
        P(("rep", "ep")),
        P(),
        P("ep", "rep", None),
        P("ep", "rep", None),
        P("rep", None, None),
        P(("rep", "ep"), None),
    )
    return jax.shard_map(
        on_device,
        mesh=mesh,
        in_specs=placed,
        out_specs=(
            P(("rep", "ep"), None),
            P(("rep", "ep"), None),
            P(("rep", "ep"), None),
            P(("rep", "ep"), None),
            P(("rep", "ep"), None),
            P(("rep", "ep")),
            P(),
            P("ep", "rep", None),
            P("ep", "rep", None),
        ),
        check_vma=False,
    )
```

```python
import math

import jax
import jax.numpy as jnp
from jax import lax
from jax.experimental import pallas as pl
from jax.experimental.pallas import tpu as pltpu
from jax.sharding import PartitionSpec as P

D = 2048
HEADS = 16
HD = 128
FF = 1024
TOP = 8
HALF = 512
PAD = 128

epsilon = 1e-06
rope_base = 50000.0
bf16 = jnp.bfloat16
f32 = jnp.float32


def dot(a, b, dims=((1,), (0,))):
    return lax.dot_general(a, b, (dims, ((), ())), preferred_element_type=f32)


def inverse_rms(value):
    return lax.rsqrt(jnp.mean(value * value, axis=-1, keepdims=True) + epsilon)


def rms_backward(value, inverse, gain, grad):
    scaled = grad * gain
    inner = jnp.mean(scaled * value, axis=-1, keepdims=True)
    return inverse * (scaled - value * (inverse * inverse * inner))


def doc_positions(segment):
    index = jnp.arange(segment.shape[0], dtype=jnp.int32)
    change = jnp.concatenate([jnp.ones((1,), dtype=jnp.bool_), segment[1:] != segment[:-1]])
    start = lax.cummax(jnp.where(change, index, 0), axis=0)
    return index - start


def rope_tables(position, width):
    steps = jnp.arange(width // 2, dtype=f32) * (2.0 / width)
    rates = jnp.exp(-steps * math.log(rope_base))
    angle = position.astype(f32)[:, None] * rates[None, :]
    angle = jnp.concatenate([angle, angle], axis=-1)
    return (jnp.cos(angle), jnp.sin(angle))


def norm_rope(value, gain, cosine, sine):
    inverse = lax.rsqrt(jnp.mean(value * value, axis=1, keepdims=True) + epsilon)
    value = value * inverse * gain
    return value * cosine + pltpu.roll(value, HD // 2, 1) * sine


def norm_rope_back(value, gain, cosine, sine, grad):
    inverse = lax.rsqrt(jnp.mean(value * value, axis=1, keepdims=True) + epsilon)
    grad = grad * cosine + pltpu.roll(grad * sine, HD // 2, 1)
    normal = value * inverse
    scaled = grad * gain
    inner = jnp.mean(scaled * normal, axis=1, keepdims=True)
    return inverse * (scaled - normal * inner), jnp.sum(grad * normal, axis=0, keepdims=True)


def kept_scores(query, keys, q_seg, k_seg, start):
    scores = dot(query, keys, ((1,), (1,))) * (1.0 / math.sqrt(HD))
    q_index = start + lax.broadcasted_iota(jnp.int32, scores.shape, 0)
    k_index = lax.broadcasted_iota(jnp.int32, scores.shape, 1)
    keep = (jnp.abs(q_index - k_index) <= HALF) & (q_seg == k_seg)
    return jnp.where(keep, scores, -1e30)


BIG = 100 * 1024 * 1024 // 2


def forward_kernel(
    heads, proj, cosine, sine, seg_column, seg_row, gains, mixed, query, keys, values, lses
):
    ranks, _, rows, _ = proj.shape
    length = ranks * rows
    q_block = 2 * rows
    k_seg = seg_row[0]
    for head in range(heads):
        at = slice(head * HD, (head + 1) * HD)

        def raw(part):
            first = (part * heads + head) * HD
            return proj[:, 0, :, first : first + HD].reshape(length, HD)

        query[0, :, at] = norm_rope(raw(0), gains[0:1], cosine[0], sine[0]).astype(bf16)
        keys[0, :, at] = norm_rope(raw(1), gains[1:2], cosine[0], sine[0]).astype(bf16)
        values[0, :, at] = raw(2).astype(bf16)

        @pl.loop(0, length // q_block)
        def one_block(number, head=head, at=at):
            start = pl.multiple_of(number * q_block, q_block)
            here = pl.ds(start, q_block)
            scores = kept_scores(
                query[0, here, at], keys[0, :, at], seg_column[0, here], k_seg, start
            )
            top = jnp.max(scores, axis=1, keepdims=True)
            weights = jnp.exp(scores - top)
            total = jnp.sum(weights, axis=1, keepdims=True)
            lses[0, head, here] = top + jnp.log(total)
            weights = (weights * (1.0 / total)).astype(bf16)
            result = dot(weights, values[0, :, at]).astype(bf16)
            mixed[pl.ds(number * 2, 2), 0, :, at] = result.reshape(2, rows, HD)


def backward_kernel(
    heads, proj, cosine, sine, seg_column, seg_row, gains, query, keys, values, lses, grad_mixed,
    grad_proj, grad_gains, grad_q, grad_k, grad_v,
):
    ranks, _, rows, _ = proj.shape
    length = ranks * rows
    q_block = 2 * rows
    k_seg = seg_row[0]
    scale = 1.0 / math.sqrt(HD)
    sum_q = jnp.zeros((1, HD), f32)
    sum_k = jnp.zeros((1, HD), f32)
    for head in range(heads):
        at = slice(head * HD, (head + 1) * HD)
        grad_k[...] = jnp.zeros_like(grad_k)
        grad_v[...] = jnp.zeros_like(grad_v)

        @pl.loop(0, length // q_block)
        def one_block(number, head=head, at=at):
            start = pl.multiple_of(number * q_block, q_block)
            here = pl.ds(start, q_block)
            q_rows = query[0, here, at]
            g_rows = grad_mixed[here, at]
            k_all = keys[0, :, at]
            scores = kept_scores(q_rows, k_all, seg_column[0, here], k_seg, start)
            weights = jnp.exp(scores - lses[0, head, here])
            grad_weights = dot(g_rows, values[0, :, at], ((1,), (1,)))
            delta = jnp.sum(weights * grad_weights, axis=1, keepdims=True)
            grad_scores = (weights * (grad_weights - delta)).astype(bf16)
            grad_q[here] = dot(grad_scores, k_all) * scale
            grad_k[...] += dot(grad_scores, q_rows, ((0,), (0,)))
            grad_v[...] += dot(weights.astype(bf16), g_rows, ((0,), (0,)))

        def rounded(value):
            return value.astype(bf16).astype(f32)

        def raw(part):
            first = (part * heads + head) * HD
            return proj[:, 0, :, first : first + HD].reshape(length, HD)

        def put(part, value):
            first = (part * heads + head) * HD
            grad_proj[:, :, first : first + HD] = value.astype(bf16).reshape(ranks, rows, HD)

        back_q, gain_q = norm_rope_back(
            raw(0), gains[0:1], cosine[0], sine[0], rounded(grad_q[...])
        )
        back_k, gain_k = norm_rope_back(
            raw(1), gains[1:2], cosine[0], sine[0], rounded(grad_k[...] * scale)
        )
        sum_q, sum_k = sum_q + gain_q, sum_k + gain_k
        put(0, back_q)
        put(1, back_k)
        put(2, grad_v[...])
    grad_gains[0:1] = sum_q
    grad_gains[1:2] = sum_k


def fixed(shape):
    return pl.BlockSpec(shape, lambda *_: (0,) * len(shape), pipeline_mode=pl.Buffered(1))


def leading(shape):
    return pl.BlockSpec((1,) + shape[1:], lambda i: (i,) + (0,) * (len(shape) - 1))


def params():
    return pltpu.CompilerParams(vmem_limit_bytes=BIG)


def cost(products):
    return pl.CostEstimate(flops=20 * products, bytes_accessed=0, transcendentals=0)


def out(shape, dtype=bf16):
    return jax.ShapeDtypeStruct(shape, dtype)


def attention_forward(proj, cosine, sine, seg_column, seg_row, gains):
    ranks, micro, rows, width = proj.shape
    length = ranks * rows
    width = width // 3
    heads = width // HD
    part = out((micro, length, width))
    by_rank = lambda n: pl.BlockSpec((ranks, 1, rows, n), lambda i: (0, i, 0, 0))
    lses = out((micro, heads, length, 1), f32)
    return pl.pallas_call(
        lambda *refs: forward_kernel(heads, *refs),
        grid=(micro,),
        in_specs=[by_rank(3 * width)]
        + [leading(v.shape) for v in (cosine, sine, seg_column, seg_row)]
        + [fixed(gains.shape)],
        out_specs=[by_rank(width)] + [leading(part.shape)] * 3 + [leading(lses.shape)],
        out_shape=[out((ranks, micro, rows, width)), part, part, part, lses],
        compiler_params=params(),
    )(proj, cosine, sine, seg_column, seg_row, gains)


def attention_backward(
    step, proj, cosine, sine, seg_column, seg_row, gains, query, keys, values, lses, grad_mixed
):
    ranks, micro, rows, width = proj.shape
    length = ranks * rows
    heads = width // 3 // HD

    def part(value):
        return pl.BlockSpec((1,) + value.shape[1:], lambda i: (step,) + (0,) * (value.ndim - 1))

    return pl.pallas_call(
        lambda *refs: backward_kernel(heads, *refs),
        grid=(1,),
        in_specs=[pl.BlockSpec((ranks, 1, rows, width), lambda i: (0, step, 0, 0))]
        + [part(v) for v in (cosine, sine, seg_column, seg_row)]
        + [fixed(gains.shape)]
        + [part(v) for v in (query, keys, values, lses)]
        + [fixed(grad_mixed.shape)],
        out_specs=[fixed((ranks, rows, width)), fixed((2, HD))],
        out_shape=[out((ranks, rows, width)), out((2, HD), f32)],
        scratch_shapes=[pltpu.VMEM((length, HD), f32)] * 3,
        compiler_params=params(),
    )(
        proj, cosine, sine, seg_column, seg_row, gains, query, keys, values, lses, grad_mixed
    )


def project(micro, tokens, gain, slab):
    ranks, count, _ = tokens.shape
    rows = count // micro
    width = slab.shape[1] - PAD

    def kernel(value, gain, weight, normed, proj):
        value = value[0].astype(f32)
        result = (value * inverse_rms(value) * gain[...]).astype(bf16)
        normed[...] = result.reshape(micro, 1, rows, D)
        proj[0] = dot(result, weight[:, :width])

    return pl.pallas_call(
        kernel,
        grid=(ranks,),
        in_specs=[leading((ranks, count, D)), fixed((1, D)), fixed(slab.shape)],
        out_specs=[
            pl.BlockSpec((micro, 1, rows, D), lambda i: (0, i, 0, 0)),
            leading((ranks, count, width)),
        ],
        out_shape=[out((micro, ranks, rows, D)), out((ranks, count, width), f32)],
        compiler_params=params(),
    )(tokens, gain, slab)


TILE = 512


def tiles(count):
    return pl.loop(0, count // TILE)


def tile(number):
    return pl.ds(pl.multiple_of(number * TILE, TILE), TILE)


HBM = pl.BlockSpec(memory_space=pl.ANY)


def copies(pairs, sems):
    started = [
        pltpu.make_async_copy(source, target, sems.at[place])
        for place, (source, target) in enumerate(pairs)
    ]
    for copy in started:
        copy.start()

    def wait():
        for copy in started:
            copy.wait()

    return wait


def plane_pairs(plane, pieces, target):
    planes = len(pieces)
    rows = target.shape[0] // planes
    return [
        (piece, target.at[pl.ds(lax.bitwise_xor(plane, jnp.int32(step)) * rows, rows)])
        for step, piece in enumerate(pieces)
    ]


def out_weight_pairs(plane, planes, gathered, target):
    ranks = gathered.shape[0]
    rows = D // (planes * ranks)
    return [
        (
            gathered.at[rank, pl.ds(step * rows, rows)],
            target.at[
                pl.ds((lax.bitwise_xor(plane, jnp.int32(step)) * ranks + rank) * rows, rows)
            ],
        )
        for rank in range(ranks)
        for step in range(planes)
    ]


def route(plane, planes, mixed, tokens, gathered, gain, router, routes, experts):
    count = tokens.shape[0]
    pieces = planes * gathered.shape[0]

    def kernel(
        plane, mixed, tokens, gathered, gain, router, routes, hidden, payload, gates,
        out_weight, sems,
    ):
        copies(out_weight_pairs(plane[0], planes, gathered, out_weight), sems)()

        @tiles(D)
        def _(number):
            at = tile(number)
            hidden[:, at] = tokens[:, at].astype(f32) + dot(mixed[...], out_weight[:, at])

        value = hidden[...]
        normed = (value * inverse_rms(value) * gain[...]).astype(bf16)
        payload[:, :D] = normed
        logits = dot(normed, router[...])
        column = lax.broadcasted_iota(jnp.int32, logits.shape, 1)
        routed = column == routes[:, 0:1]
        for choice in range(1, TOP):
            routed = routed | (column == routes[:, choice : choice + 1])
        logits = jnp.where(routed, logits, -1e30)
        weights = jnp.exp(logits - jnp.max(logits, axis=1, keepdims=True))
        weights = jnp.where(routed, weights, 0.0)
        weights = weights / jnp.sum(weights, axis=1, keepdims=True)
        gates[...] = weights
        high = weights.astype(bf16).astype(f32)
        payload[:, D:] = (high + pltpu.roll(weights - high, experts, 1)).astype(bf16)

    shapes = [out((count, D), f32), out((count, D + PAD)), out((count, PAD), f32)]
    return pl.pallas_call(
        kernel,
        grid_spec=pltpu.PrefetchScalarGridSpec(
            num_scalar_prefetch=1,
            grid=(1,),
            in_specs=[
                HBM if value is gathered else fixed(value.shape)
                for value in (mixed, tokens, gathered, gain, router, routes)
            ],
            out_specs=[fixed(shape.shape) for shape in shapes],
            scratch_shapes=[pltpu.VMEM((D, D), bf16), pltpu.SemaphoreType.DMA((pieces,))],
        ),
        out_shape=shapes,
        compiler_params=params(),
    )(plane, mixed, tokens, gathered, gain, router, routes)


def lane(value, number):
    column = lax.broadcasted_iota(jnp.int32, value.shape, 1)
    return jnp.sum(jnp.where(column == number, value.astype(f32), 0.0), axis=1, keepdims=True)


def one_hot(slot, slots):
    place = lax.broadcasted_iota(jnp.int32, (slots, slot.shape[1]), 0).astype(f32)
    return (place == slot).astype(bf16)


def expert_forward(where, payload, upstream, in_pieces, slots, experts):
    ranks, share, micro, rows, _ = payload.shape
    count = share * rows
    block = 2 * slots

    planes = len(in_pieces)

    def kernel(where, payload, upstream, *refs):
        (
            rows_in, tail, both, active, grad_produced, up_rows, places, in_weight, sems
        ) = refs[planes:]
        number = where[0]

        @pl.when((pl.program_id(0) == 0) & (pl.program_id(1) == 0))
        def _():
            copies(plane_pairs(where[1], refs[:planes], in_weight), sems)()

        for part in range(2):
            here = slice(part * slots, (part + 1) * slots)
            value = payload[part].reshape(count, D + PAD)
            marks = value[:, D:]
            first = lax.broadcasted_iota(jnp.int32, (8, PAD), 1) == number
            taken = dot(first.astype(bf16), marks, ((1,), (1,))) > 0.0
            before = lax.broadcasted_iota(jnp.int32, (count, count), 0)
            behind = lax.broadcasted_iota(jnp.int32, (count, count), 1)
            slot = dot(taken.astype(bf16), (before < behind).astype(bf16))
            select = one_hot(jnp.where(taken, slot, -1.0)[0:1], slots)
            wide = jnp.broadcast_to(lane(marks, number) > 0.0, (count, PAD))
            slot = dot((before > behind).astype(bf16), wide.astype(bf16))
            places[0, 0, part] = jnp.where(wide, slot, -1.0)
            rows_in[0, 0, here] = dot(select, value[:, :D]).astype(bf16)
            marks = dot(select, marks)
            tail[0, 0, here] = marks
            gate = lane(marks, number) + lane(marks, experts + number)
            picked = dot(select, upstream[part].reshape(count, D))
            up_rows[0, 0, here] = picked.astype(bf16)
            grad_produced[0, 0, here] = (gate * picked).astype(bf16)

        for number in range(FF // TILE):
            at = slice(number * TILE, (number + 1) * TILE)
            more = slice(FF + number * TILE, FF + (number + 1) * TILE)
            gate_part = dot(rows_in[0, 0], in_weight[:, at])
            up_part = dot(rows_in[0, 0], in_weight[:, more])
            both[0, 0, :, at] = gate_part
            both[0, 0, :, more] = up_part
            active[0, 0, :, at] = (
                gate_part / (1.0 + jnp.exp(-gate_part)) * up_part
            ).astype(bf16)

    def tokens_spec(width):
        return pl.BlockSpec((2, share, 1, rows, width), lambda m, b, _: (b, 0, m, 0, 0))

    pairs = ranks // 2
    shapes = [
        out((micro, pairs, block, D)),
        out((micro, pairs, block, PAD), f32),
        out((micro, pairs, block, 2 * FF), f32),
        out((micro, pairs, block, FF)),
        out((micro, pairs, block, D)),
        out((micro, pairs, block, D)),
        out((micro, pairs, 2, count, PAD), f32),
    ]
    return pl.pallas_call(
        kernel,
        grid_spec=pltpu.PrefetchScalarGridSpec(
            num_scalar_prefetch=1,
            grid=(micro, pairs),
            in_specs=[tokens_spec(D + PAD), tokens_spec(D)] + [HBM] * planes,
            out_specs=[
                pl.BlockSpec(
                    (1, 1) + s.shape[2:], lambda m, b, _, n=len(s.shape): (m, b) + (0,) * (n - 2)
                )
                for s in shapes
            ],
            scratch_shapes=[pltpu.VMEM((D, 2 * FF), bf16), pltpu.SemaphoreType.DMA((planes,))],
        ),
        out_shape=shapes,
        cost_estimate=cost(micro * pairs * block * D * (2 * FF + 2 * count)),
        compiler_params=params(),
    )(where, payload, upstream, *in_pieces)


def expert_backward(
    step, where, tail, both, active, grad_produced, up_rows, places, in_pieces, out_pieces,
    share, rows, experts,
):
    pairs, block = tail.shape[1:3]
    slots = block // 2
    count = places.shape[3]

    planes = len(in_pieces)

    def kernel(where, tail, both, active, grad_produced, up_rows, places, *refs):
        keep, give, grad_tokens, grad_both, in_weight, out_weight, sems = refs[2 * planes :]
        number = where[0]
        odd = where[2] == 1

        @pl.when(pl.program_id(0) == 0)
        def _():
            copies(
                plane_pairs(where[1], refs[:planes], in_weight)
                + plane_pairs(where[1], refs[planes : 2 * planes], out_weight),
                sems,
            )()

        gate = lane(tail[0, 0], number) + lane(tail[0, 0], experts + number)
        place = lax.broadcasted_iota(jnp.int32, (count, slots), 1).astype(f32)
        selects = [(places[0, 0, part][:, 0:1] == place).astype(bf16) for part in range(2)]

        def spread(value):
            return [
                dot(selects[part], value[part * slots : (part + 1) * slots])
                .astype(bf16)
                .reshape(share, rows, -1)
                for part in range(2)
            ]

        grad_gate = jnp.zeros((block, 1), f32)
        for tile in range(D // TILE):
            at = slice(tile * TILE, (tile + 1) * TILE)
            produced = dot(active[0, 0], out_weight[:, at]).astype(bf16).astype(f32)
            even_rank, odd_rank = spread((gate * produced).astype(bf16))
            keep[0, :, :, at] = jnp.where(odd, odd_rank, even_rank)
            give[0, :, :, at] = jnp.where(odd, even_rank, odd_rank)
            grad_gate = grad_gate + jnp.sum(
                up_rows[0, 0, :, at].astype(f32) * produced, axis=1, keepdims=True
            )

        for tile in range(FF // TILE):
            at = slice(tile * TILE, (tile + 1) * TILE)
            more = slice(FF + tile * TILE, FF + (tile + 1) * TILE)
            grad_active = dot(grad_produced[0, 0], out_weight[at, :], ((1,), (1,)))
            grad_active = grad_active.astype(bf16).astype(f32)
            gate_part = both[0, 0, :, at]
            up_part = both[0, 0, :, more]
            sigma = 1.0 / (1.0 + jnp.exp(-gate_part))
            grad_both[0, :, at] = (
                grad_active * up_part * (sigma * (1.0 + gate_part * (1.0 - sigma)))
            ).astype(bf16)
            grad_both[0, :, more] = (grad_active * (gate_part * sigma)).astype(bf16)

        for tile in range(D // TILE):
            at = slice(tile * TILE, (tile + 1) * TILE)
            grad_rows = dot(grad_both[0], in_weight[at, :], ((1,), (1,))).astype(bf16)
            grad_tokens[0, :, :, at], grad_tokens[1, :, :, at] = spread(grad_rows)

        high = grad_gate.astype(bf16).astype(f32)
        column = lax.broadcasted_iota(jnp.int32, (block, PAD), 1)
        extra = jnp.where(column == number, high, 0.0)
        extra = jnp.where(column == experts + number, grad_gate - high, extra)
        grad_tokens[0, :, :, D:], grad_tokens[1, :, :, D:] = spread(extra.astype(bf16))

    def part(value):
        return pl.BlockSpec(
            (1, 1) + value.shape[2:], lambda b, _: (step, b) + (0,) * (value.ndim - 2)
        )

    def tokens_spec(count, width):
        return pl.BlockSpec((count, share, rows, width), lambda b, _: (b, 0, 0, 0))

    return pl.pallas_call(
        kernel,
        grid_spec=pltpu.PrefetchScalarGridSpec(
            num_scalar_prefetch=1,
            grid=(pairs,),
            in_specs=[part(v) for v in (tail, both, active, grad_produced, up_rows, places)]
            + [HBM] * (2 * planes),
            out_specs=[
                tokens_spec(1, D),
                tokens_spec(1, D),
                tokens_spec(2, D + PAD),
                pl.BlockSpec((1, block, 2 * FF), lambda b, _: (b, 0, 0)),
            ],
            scratch_shapes=[
                pltpu.VMEM((D, 2 * FF), bf16),
                pltpu.VMEM((FF, D), bf16),
                pltpu.SemaphoreType.DMA((2 * planes,)),
            ],
        ),
        out_shape=[
            out((pairs, share, rows, D)),
            out((pairs, share, rows, D)),
            out((2 * pairs, share, rows, D + PAD)),
            out((pairs, block, 2 * FF)),
        ],
        cost_estimate=cost(pairs * block * D * (4 * FF + 2 * count)),
        compiler_params=params(),
    )(
        where, tail, both, active, grad_produced, up_rows, places, *in_pieces, *out_pieces
    )


def cut_ends(count, places):
    return [-(-count * place // 512) * 16 for place in (0, *places, 32)]


def weight_gradient(
    where, planes, left, rights, tail=None, first=0, steps=None, shift=False, cuts=None
):
    steps = planes if steps is None else steps
    count, width = left.shape
    parts = len(rights)
    part_rows = count // parts
    columns = rights[0].shape[1]
    width = width // planes
    step = min(TILE, columns & -columns)
    tails = [] if tail is None else [tail]
    split = columns // 3 * 2 if tails else columns
    wholes = [split, columns - split + tail.shape[1]] if tails else [split]

    ends = [cut_ends(width, (cuts or {}).get(number, ())) for number in range(steps)]
    shapes = [
        out((end - start, whole))
        for one in ends
        for start, end in zip(one, one[1:])
        for whole in wholes
    ]

    def of_plane(i, where):
        return (where[1] + first + i) % planes if shift else lax.bitwise_xor(where[1], first + i)

    def kernel(where, left, *refs):
        rights, tails, targets = refs[:parts], refs[parts : -len(shapes)], refs[-len(shapes) :]

        def fill(targets, ends):
            for value in tails:
                targets[1][:, columns - split :] = value[...]
            for number in range(columns // step):
                at = slice(number * step, (number + 1) * step)
                result = sum(
                    dot(left[part * part_rows : (part + 1) * part_rows], right[:, at], ((0,), (0,)))
                    for part, right in enumerate(rights)
                ).astype(bf16)
                if at.start >= split:
                    targets[1][:, at.start - split : at.stop - split] = result
                    continue
                for target, start, end in zip(targets[:: len(wholes)], ends, ends[1:]):
                    target[:, at] = result[start:end]

        done = 0
        for number, one in enumerate(ends):
            mine = targets[done : done + (len(one) - 1) * len(wholes)]
            done += len(mine)
            pl.when(pl.program_id(0) == number)(lambda mine=mine, one=one: fill(mine, one))

    return pl.pallas_call(
        kernel,
        grid_spec=pltpu.PrefetchScalarGridSpec(
            num_scalar_prefetch=1,
            grid=(steps,),
            in_specs=[pl.BlockSpec((count, width), lambda i, where: (0, of_plane(i, where)))]
            + [fixed(right.shape) for right in rights]
            + [
                pl.BlockSpec((width, value.shape[1]), lambda i, where: (of_plane(i, where), 0))
                for value in tails
            ],
            out_specs=[fixed(shape.shape) for shape in shapes],
        ),
        out_shape=shapes,
        cost_estimate=cost(0 if tails else count * steps * width * columns),
        compiler_params=params(),
    )(where, left, *rights, *tails)


def hidden_backward(
    step, plane, planes, parts, hidden, gates, upstream, gain, router, gathered, experts
):
    first = parts[0].shape
    count = first[1]
    terms = len(parts)

    def kernel(plane, *refs):
        parts = refs[:terms]
        hidden, gates, upstream, gain, router, gathered = refs[terms : terms + 6]
        (
            grad_hidden, grad_branch, grad_mixed, grad_logits, grad_gain, out_weight, sems
        ) = refs[terms + 6 :]
        wait = copies(out_weight_pairs(plane[0], planes, gathered, out_weight), sems)
        returned = sum(part[...].astype(f32) for part in parts[1:]) + parts[0][0].astype(f32)
        tail = returned[:, D:]
        grad_gates = gates[...] * (tail + pltpu.roll(tail, PAD - experts, 1))
        logits = grad_gates - gates[...] * jnp.sum(grad_gates, axis=1, keepdims=True)
        logits = logits.astype(bf16)
        grad_logits[...] = logits
        grad_normed = returned[:, :D] + dot(logits, router[...], ((1,), (1,)))
        value = hidden[...]
        inverse = inverse_rms(value)
        grad_gain[...] = jnp.sum(grad_normed * value * inverse, axis=0, keepdims=True)
        grad = upstream[...].astype(f32) + rms_backward(value, inverse, gain[...], grad_normed)
        grad_hidden[...] = grad
        grad_branch[...] = grad.astype(bf16)
        wait()

        @tiles(D)
        def _(number):
            at = tile(number)
            grad_mixed[:, at] = dot(grad_branch[...], out_weight[at, :], ((1,), (1,))).astype(bf16)

    shapes = [
        out((count, D), f32), out((count, D)), out((count, D)), out((count, PAD)),
        out((1, D), f32),
    ]
    args = (*parts, hidden, gates, upstream, gain, router, gathered)

    def spec(value):
        if value is gathered:
            return HBM
        if value is parts[0]:
            return pl.BlockSpec((1,) + first[1:], lambda *_: (0, 0, 0))
        if any(value is rows for rows in (hidden, gates, upstream)):
            return pl.BlockSpec((count, value.shape[1]), lambda *_: (step, 0))
        return fixed(value.shape)

    return pl.pallas_call(
        kernel,
        grid_spec=pltpu.PrefetchScalarGridSpec(
            num_scalar_prefetch=1,
            grid=(1,),
            in_specs=[spec(value) for value in args],
            out_specs=[fixed(shape.shape) for shape in shapes],
            scratch_shapes=[
                pltpu.VMEM((D, D), bf16),
                pltpu.SemaphoreType.DMA((planes * gathered.shape[0],)),
            ],
        ),
        out_shape=shapes,
        compiler_params=params(),
    )(plane, *args)


def project_backward(step, grad_proj, tokens, slab):
    ranks, rows, _ = grad_proj.shape
    width = slab.shape[1] - PAD

    def kernel(grad_proj, tokens, weight, grad_normed, grad_gain):
        value = tokens[...].reshape(2 * rows, D).astype(f32)
        inverse = inverse_rms(value)
        grad = dot(grad_proj[...].reshape(2 * rows, width), weight[:, :width], ((1,), (1,)))
        grad_normed[...] = grad.astype(bf16)

        @pl.when(pl.program_id(0) == 0)
        def _():
            grad_gain[...] = jnp.zeros_like(grad_gain)

        grad_gain[...] += jnp.sum(grad * value * inverse, axis=0, keepdims=True)

    return pl.pallas_call(
        kernel,
        grid=(ranks // 2,),
        in_specs=[
            pl.BlockSpec((2, rows, width), lambda i: (i, 0, 0)),
            pl.BlockSpec((2, rows, D), lambda i: (i, step, 0)),
            fixed(slab.shape),
        ],
        out_specs=[pl.BlockSpec((2 * rows, D), lambda i: (i, 0)), fixed((1, D))],
        out_shape=[out((ranks * rows, D)), out((1, D), f32)],
        compiler_params=params(),
    )(grad_proj, tokens, slab)


def cut_heads(weight, tail, ranks):
    rows = weight.shape[0]
    width = D // ranks

    def kernel(weight, tail, target):
        for rank in range(ranks):
            for part in range(3):
                at = part * D + rank * width
                target[rank, :, part * width : (part + 1) * width] = weight[:, at : at + width]
            target[rank, :, 3 * width :] = tail[...]

    return pl.pallas_call(
        kernel,
        out_shape=out((ranks, rows, 3 * width + PAD)),
        compiler_params=params(),
    )(weight, tail)


def unpack(heads, others, count):
    ranks, rows, columns = heads.shape
    width = columns // 2

    def kernel(heads, others, main, small):
        for rank in range(ranks):
            for part in range(3):
                at = part * D + rank * width
                value = heads[rank, :, part * width : (part + 1) * width] if part < 2 else others[
                    rank, :, :width
                ]
                main[:, at : at + width] = value.astype(f32)
        tails = sum(others[rank, :, width:].astype(f32) for rank in range(ranks))
        small[...] = tails + pltpu.roll(tails, PAD - count, 1)

    return pl.pallas_call(
        kernel,
        out_shape=[out((rows, 3 * D), f32), out((rows, PAD), f32)],
        compiler_params=params(),
    )(heads, others)


def shift_rep(value, step):
    count = lax.axis_size("rep")
    return lax.ppermute(value, "rep", [(i, (i + step) % count) for i in range(count)])


def cross_rep(value, bits):
    return lax.ppermute(value, "rep", [(i, i ^ bits) for i in range(lax.axis_size("rep"))])


def after(value, *others):
    return lax.optimization_barrier((value,) + others)[0]


def two_parts(value):
    high = lax.reduce_precision(value, 8, 7)
    return high.astype(bf16), (value - high).astype(bf16)


def ring_rep(value, *work):
    count = lax.axis_size("rep")
    rank = lax.axis_index("rep")
    rows = value.shape[0]
    full = jnp.zeros((count * rows,) + value.shape[1:], value.dtype)
    full = lax.dynamic_update_slice_in_dim(full, value, rank * rows, 0)
    for step in range(1, count):
        value, work = lax.optimization_barrier((value, work)) if step == count - 1 else (value, work)
        value = shift_rep(value, 1)
        full = lax.dynamic_update_slice_in_dim(full, value, (rank - step) % count * rows, 0)
    return full, work


def on_device(
    tokens, cotangent, w_qkv, w_o, w_router, norm_gains, qk_gain, w_in, w_out, segments, routes
):
    planes = lax.axis_size("rep")
    ranks = lax.axis_size("ep")
    plane = lax.axis_index("rep")
    rank = lax.axis_index("ep")
    share = w_in.shape[0]
    own = plane % share
    experts = share * ranks
    where = jnp.stack([rank * share + own, plane, rank % 2]).astype(jnp.int32)
    micro = segments.shape[1]
    mine = tokens.shape[0]
    rows = mine // micro
    length = rows * ranks
    capacity = rows * TOP * 17 // (16 * experts)
    slots = -(-share * capacity // 16) * 16
    width = HEADS // ranks * HD
    qk_gains = qk_gain.astype(f32).reshape(2, HD)
    dense_rows = w_qkv.shape[0]

    def exchange(value, step):
        pairs = [(i, i // share * share + (i % share + step) % share) for i in range(planes)]
        return lax.ppermute(value, "rep", pairs)

    def with_group(value):
        return jnp.stack([value] + [exchange(value, step) for step in range(1, share)])

    def gather_ranks(value):
        return lax.all_gather(value, "ep", axis=0)

    assert planes & (planes - 1) == 0 and share & (share - 1) == 0
    last_step = planes - 1
    in_parts, out_parts = (
        {
            step: lax.dynamic_index_in_dim(weight, own ^ step % share, 0, keepdims=False)
            for step in range(planes)
        }
        for weight in (w_in, w_out)
    )

    def send(parts, steps):
        return {step: cross_rep(parts[step], step) for step in steps}

    stream = gather_ranks(tokens)
    out_rows = [w_o] + [cross_rep(w_o, step) for step in range(1, planes)]
    upstream_group = with_group(cotangent)
    early_rows = cut_ends(out_parts[last_step].shape[0], (12,))[1]
    early = cross_rep(out_parts[last_step][:early_rows], last_step)
    slab = cut_heads(
        w_qkv,
        jnp.concatenate(
            [
                w_router,
                norm_gains.reshape(dense_rows, 2),
                jnp.zeros((dense_rows, PAD - experts - 2), bf16),
            ],
            axis=1,
        ),
        ranks,
    )
    slab = lax.all_to_all(slab, "ep", split_axis=0, concat_axis=0, tiled=True)
    slab = slab.reshape(ranks * dense_rows, 3 * width + PAD)
    out_rows, upstream_group, slab, early = lax.optimization_barrier(
        (out_rows, upstream_group, slab, early)
    )
    gathered = gather_ranks(jnp.concatenate(out_rows, axis=0))
    segment = segments[0]
    cosine, sine = jax.vmap(lambda one: rope_tables(doc_positions(one), HD))(segment)
    sine = jnp.where(jnp.arange(HD) < HD // 2, -sine, sine)
    tables = (cosine, sine, segment[:, :, None], segment[:, None, :], qk_gains)
    slab, (tables, in_parts, out_parts) = ring_rep(slab, tables, in_parts, out_parts)
    router = slab[:, 3 * width :]
    gain_pair = router[:, experts : experts + 2].reshape(-1).astype(f32)
    first_gain = gain_pair[None, :D]
    second_gain = gain_pair[None, D:]
    in_parts, out_parts, upstream_group, stream = after(
        (in_parts, out_parts, upstream_group, stream), slab
    )
    in_pieces = {0: in_parts[0], **send(in_parts, range(last_step - 1, 0, -1))}
    upstream_all = gather_ranks(upstream_group)

    normed, proj = project(micro, stream, first_gain, slab)
    proj = proj.reshape(ranks, micro, rows, 3 * width)
    mixed_h, query, keys, values, lses = attention_forward(proj, *tables)
    mixed = lax.all_to_all(mixed_h, "ep", split_axis=0, concat_axis=3, tiled=True)
    mixed = mixed.reshape(mine, D)
    hidden, payload, gates = route(
        where[1:2], planes, mixed, tokens, gathered, second_gain, router, routes, experts
    )
    normed_two = payload[:, :D]
    payload, in_pieces = lax.optimization_barrier((payload, in_pieces))
    payload = with_group(payload)
    payload, in_parts, out_parts = lax.optimization_barrier((payload, in_parts, out_parts))
    in_pieces.update(send(in_parts, [last_step]))
    in_pieces, out_parts = lax.optimization_barrier((in_pieces, out_parts))
    out_parts[last_step] = out_parts[last_step][early_rows:]
    out_pieces = {0: out_parts[0], **send(out_parts, range(1, planes))}
    in_pieces = [in_pieces[step] for step in range(planes)]
    out_pieces = [out_pieces[step] for step in range(planes)]
    payload = gather_ranks(payload)

    shape = (ranks, share, micro, rows, -1)
    rows_in, tail, both, active, grad_produced, up_rows, places = expert_forward(
        where, payload.reshape(shape), upstream_all.reshape(shape), in_pieces, slots, experts
    )
    in_rows = micro * ranks * slots
    out_cut = weight_gradient(
        where, planes, active.reshape(in_rows, FF), [grad_produced.reshape(in_rows, D)]
    )

    def sum_rep(parts, shift=False):
        sums = [
            sum(parts[step].astype(f32) for step in range(first, planes, share))
            for first in range(share)
        ]
        return jnp.stack(
            [
                sum(
                    jnp.where(((own - step) % share if shift else own ^ step) == j, sums[step], 0.0)
                    for step in range(share)
                )
                for j in range(share)
            ]
        )

    tail, out_cut, out_pieces = lax.optimization_barrier((tail, out_cut, out_pieces))
    out_pieces[last_step] = jnp.concatenate([early, out_pieces[last_step]], axis=0)
    first = cross_rep(out_cut[1][:16], 1)
    tail, out_cut, first = lax.optimization_barrier((tail, out_cut, first))
    out_sent = send([out_cut[0], out_cut[1][16:], *out_cut[2:]], range(1, planes))
    back = []
    returned = []

    def scatter_ranks(value):
        return lax.psum_scatter(value, "ep", scatter_dimension=0)

    def exchange_back(value):
        return [value] + [exchange(value[step], share - step) for step in range(1, share)]

    for step in range(micro):
        back.append(
            expert_backward(
                step, where, tail, both, active, grad_produced, up_rows, places, in_pieces,
                out_pieces, share, rows, experts,
            )
        )
        returned.append(scatter_ranks(back[step][2]))
        if step == 0:
            tail, out_sent[last_step] = after((tail, out_sent[last_step]), back[step][2])
        else:
            tail = after(tail, back[step][2])
    rows_in = after(rows_in, tail)
    rows_flat = rows_in.reshape(in_rows, D)
    grads_flat = [back[step][3].reshape(in_rows // micro, 2 * FF) for step in range(micro)]
    in_near = weight_gradient(
        where, planes, rows_flat, grads_flat, first=1, steps=1, shift=True, cuts={0: (24,)}
    )
    rows_flat, in_near = lax.optimization_barrier((rows_flat, in_near))
    cuts = {number: (19, 28) for number in range(planes - 3)}
    *in_rest, in_back, in_own = weight_gradient(
        where, planes, rows_flat, grads_flat, first=2, steps=last_step, shift=True, cuts=cuts
    )
    in_sent = {0: in_own}
    near_sent = [shift_rep(in_near[0], 1)]

    def swap(value, step):
        return lax.ppermute(value, "ep", [(i, i ^ step) for i in range(ranks)])

    bits = list(range((ranks // 2).bit_length() - 1))

    def cut_pairs(number, value, phase):
        way = bits if number % 2 == 0 else bits[::-1]
        bit = way[phase]
        low = 2 ** sum(other < bit for other in way[phase:])
        value = value.reshape((-1, 2, low) + value.shape[1:])
        side = rank // 2 // 2**bit % 2
        return [
            lax.dynamic_index_in_dim(value, which, 1, keepdims=False).reshape((-1,) + value.shape[3:])
            for which in (side, 1 - side)
        ]

    def pair_sum(number, keep, give):
        got = swap(give, 1)
        return [
            total(parts).astype(bf16)
            for parts in zip(cut_pairs(number, keep, 0), cut_pairs(number, got, 0))
        ]

    def halve(number, halves, phase):
        return halves[0], swap(halves[1], 2 * 2 ** (bits if number % 2 == 0 else bits[::-1])[phase])

    def total(parts):
        return sum(part.astype(f32) for part in parts)

    grad_inputs, branches, logit_grads, grad_projs, normed_sums = [], [], [], [], []
    gain_two_sum = gain_one_sum = qk_sum = 0.0
    in_rest, in_back, in_near, out_sent, near_sent = lax.optimization_barrier(
        (in_rest, in_back, in_near, out_sent, near_sent)
    )
    mixtures = [part[:2] for part in back]
    for step in range(micro):
        parts = after(returned[step], [one[1] for one in grad_inputs])
        parts, near_sent = lax.optimization_barrier((parts, near_sent))
        if step == micro - 1:
            mixtures = after(mixtures, parts)
            crossed = [halve(number, value, 0) for number, value in enumerate(mixtures)]
        parts = exchange_back(parts)
        parts, in_rest, in_back, in_near, mixtures = lax.optimization_barrier(
            (parts, in_rest, in_back, in_near, mixtures)
        )
        if step == 0:
            mixtures = [pair_sum(number, *part) for number, part in enumerate(mixtures)]
            in_sent[last_step] = shift_rep(in_back, last_step)
            near_sent.append(shift_rep(in_near[1], 1))
        if step == micro - 1:
            rest = [in_rest[3 * i : 3 * i + 3] for i in range(planes - 3)]
            rest_sent = [[shift_rep(part[0], i + 2) for i, part in enumerate(rest)]]
        grad_hidden, grad_branch, grad_mixed, grad_logits, gain_two = hidden_backward(
            step, where[1:2], planes, parts, hidden, gates, cotangent, second_gain, router, gathered,
            experts,
        )
        branches.append(grad_branch)
        logit_grads.append(grad_logits)
        gain_two_sum = gain_two_sum + gain_two
        if step == micro - 1:
            out_sum = dot(mixed, jnp.concatenate(branches, axis=0), ((0,), (0,))).astype(bf16)
            out_sum = out_sum.reshape(planes, ranks, dense_rows, D).transpose(1, 0, 2, 3)
        grad_mixed = lax.all_to_all(grad_mixed, "ep", split_axis=1, concat_axis=0, tiled=True)
        grad_mixed, mixtures = lax.optimization_barrier((grad_mixed, mixtures))
        if step == micro - 1:
            grad_mixed, crossed, rest_sent, rest, out_sum = lax.optimization_barrier(
                (grad_mixed, crossed, rest_sent, rest, out_sum)
            )
            out_sum = lax.psum_scatter(out_sum, "ep", scatter_dimension=0)
            rest_sent.append([shift_rep(part[1], i + 2) for i, part in enumerate(rest)])
        grad_proj, grad_qk = attention_backward(
            step, proj, *tables, query, keys, values, lses, grad_mixed
        )
        qk_sum = qk_sum + grad_qk.reshape(-1)
        if step < micro - 1:
            grad_proj, in_sent, near_sent = lax.optimization_barrier(
                (grad_proj, in_sent, near_sent)
            )
        else:
            grad_proj, normed_sums, rest_sent, rest = lax.optimization_barrier(
                (grad_proj, normed_sums, rest_sent, rest)
            )
        grad_projs.append(grad_proj)
        grad_normed, gain_one = project_backward(step, grad_proj, stream, slab)
        gain_one_sum = gain_one_sum + gain_one
        grad_inputs.append(
            (
                grad_hidden,
                grad_normed,
            )
        )
        if step < micro - 1:
            normed_sums.append(
                lax.psum_scatter(grad_normed, "ep", scatter_dimension=0, tiled=True)
            )

    router_sum = dot(normed_two, jnp.concatenate(logit_grads, axis=0), ((0,), (0,)))
    qk_columns = qk_sum.shape[0] // dense_rows
    small = jnp.concatenate(
        [
            router_sum[:, :experts],
            jnp.concatenate([gain_one_sum, gain_two_sum], axis=1).reshape(D, 2),
            jnp.tile(qk_sum.reshape(dense_rows, qk_columns), (planes * ranks, 1)),
        ],
        axis=1,
    )
    count = small.shape[1]

    def halves(value):
        high, low = two_parts(value)
        blank = jnp.zeros((value.shape[0], PAD - 2 * count), bf16)
        return jnp.concatenate([high, low, blank], axis=1)

    def joined(value):
        return value[..., :count].astype(f32) + value[..., count : 2 * count].astype(f32)

    grad_projs, rest, out_cut, out_sent, _ = lax.optimization_barrier(
        (grad_projs, rest, out_cut, out_sent, grad_inputs[-1][1])
    )
    rest_sent.append([shift_rep(part[2], i + 2) for i, part in enumerate(rest)])
    packed = weight_gradient(
        where,
        planes,
        normed.reshape(ranks * mine, D),
        [grad.reshape(length, 3 * width) for grad in grad_projs],
        halves(small),
    )
    packed, rest_sent, out_cut, out_sent, crossed = lax.optimization_barrier(
        (packed, rest_sent, out_cut, out_sent, crossed)
    )
    heads, others = packed[::2], packed[1::2]
    heads_sent = [heads[0]] + [cross_rep(heads[step], step) for step in range(1, planes)]
    heads_sent, others = lax.optimization_barrier((heads_sent, others))
    others_sent = [others[0]] + [cross_rep(others[step], step) for step in range(1, planes)]
    normed_sums.append(
        lax.psum_scatter(
            after(grad_inputs[-1][1], packed), "ep", scatter_dimension=0, tiled=True
        )
    )
    others_sent, out_sum = lax.optimization_barrier((others_sent, out_sum))
    for phase in range(1, len(bits)):
        mixtures = [total(parts).astype(bf16) for parts in crossed]
        crossed = [
            halve(number, cut_pairs(number, value, phase), phase)
            for number, value in enumerate(mixtures)
        ]
    mixture = []
    for number in range(micro):
        parts = total(crossed[number])[0]
        mixture.append((parts[0], exchange_back(parts.astype(bf16))[1:]))
    own_sum = lax.dynamic_index_in_dim(out_sum, plane, 0, keepdims=False)
    out_sent_back = [
        cross_rep(lax.dynamic_index_in_dim(out_sum, plane ^ step, 0, keepdims=False), step)
        for step in range(1, planes)
    ]
    def to_ranks(value):
        value = value.reshape(ranks, dense_rows, -1)
        return lax.all_to_all(value, "ep", split_axis=0, concat_axis=0, tiled=True)

    heads = to_ranks(total(heads_sent).astype(bf16))
    main = total([part[:, :width] for part in others_sent]).astype(bf16)
    small = sum(joined(part[:, width:]) for part in others_sent)
    packed = (heads, to_ranks(jnp.concatenate([main, halves(small)], axis=1)))
    packed, mixture, out_sent_back, normed_sums = lax.optimization_barrier(
        (packed, mixture, out_sent_back, normed_sums)
    )
    grad_tokens = []
    for step in range(micro):
        own_stream = tokens[step * rows : (step + 1) * rows].astype(f32)
        grad_tokens.append(
            grad_inputs[step][0]
            + rms_backward(
                own_stream, inverse_rms(own_stream), first_gain, normed_sums[step].astype(f32)
            )
        )
    grad_tokens = jnp.concatenate(grad_tokens, axis=0)
    output = jnp.concatenate([mine_part + total(others) for mine_part, others in mixture], axis=0)
    output = (hidden + output).astype(bf16)
    grad_w_o = total([own_sum, *out_sent_back])
    grad_w_qkv, small = unpack(*packed, count)
    out_sent[1] = jnp.concatenate([first, out_sent[1]], axis=0)
    grad_w_out = sum_rep({0: out_cut[0], **out_sent})
    in_sent[1] = jnp.concatenate(near_sent, axis=0)
    for i in range(planes - 3):
        in_sent[i + 2] = jnp.concatenate([parts[i] for parts in rest_sent], axis=0)
    grad_w_in = sum_rep(in_sent, shift=True)
    return (
        output,
        grad_tokens,
        grad_w_qkv,
        grad_w_o,
        small[:, :experts],
        small[:, experts : experts + 2].reshape(-1),
        small[:, experts + 2 : count].reshape(-1),
        grad_w_in,
        grad_w_out,
    )


def solution(mesh):
    placed = (
        P(("rep", "ep"), None),
        P(("rep", "ep"), None),
        P(("rep", "ep"), None),
        P(("rep", "ep"), None),
        P(("rep", "ep"), None),
        P(("rep", "ep")),
        P(),
        P("ep", "rep", None),
        P("ep", "rep", None),
        P("rep", None, None),
        P(("rep", "ep"), None),
    )
    return jax.shard_map(
        on_device,
        mesh=mesh,
        in_specs=placed,
        out_specs=(
            P(("rep", "ep"), None),
            P(("rep", "ep"), None),
            P(("rep", "ep"), None),
            P(("rep", "ep"), None),
            P(("rep", "ep"), None),
            P(("rep", "ep")),
            P(),
            P("ep", "rep", None),
            P("ep", "rep", None),
        ),
        check_vma=False,
    )
```

```python
import math

import jax
import jax.numpy as jnp
from jax import lax
from jax.experimental import pallas as pl
from jax.experimental.pallas import tpu as pltpu
from jax.sharding import PartitionSpec as P

D = 2048
HEADS = 16
HD = 128
FF = 1024
TOP = 8
HALF = 512
PAD = 128

epsilon = 1e-06
rope_base = 50000.0
bf16 = jnp.bfloat16
f32 = jnp.float32


def dot(a, b, dims=((1,), (0,))):
    return lax.dot_general(a, b, (dims, ((), ())), preferred_element_type=f32)


def inverse_rms(value):
    return lax.rsqrt(jnp.mean(value * value, axis=-1, keepdims=True) + epsilon)


def rms_backward(value, inverse, gain, grad):
    scaled = grad * gain
    inner = jnp.mean(scaled * value, axis=-1, keepdims=True)
    return inverse * (scaled - value * (inverse * inverse * inner))


def doc_positions(segment):
    index = jnp.arange(segment.shape[0], dtype=jnp.int32)
    change = jnp.concatenate([jnp.ones((1,), dtype=jnp.bool_), segment[1:] != segment[:-1]])
    start = lax.cummax(jnp.where(change, index, 0), axis=0)
    return index - start


def rope_tables(position, width):
    steps = jnp.arange(width // 2, dtype=f32) * (2.0 / width)
    rates = jnp.exp(-steps * math.log(rope_base))
    angle = position.astype(f32)[:, None] * rates[None, :]
    angle = jnp.concatenate([angle, angle], axis=-1)
    return (jnp.cos(angle), jnp.sin(angle))


def norm_rope(value, gain, cosine, sine):
    inverse = lax.rsqrt(jnp.mean(value * value, axis=1, keepdims=True) + epsilon)
    value = value * inverse * gain
    return value * cosine + pltpu.roll(value, HD // 2, 1) * sine


def norm_rope_back(value, gain, cosine, sine, grad):
    inverse = lax.rsqrt(jnp.mean(value * value, axis=1, keepdims=True) + epsilon)
    grad = grad * cosine + pltpu.roll(grad * sine, HD // 2, 1)
    normal = value * inverse
    scaled = grad * gain
    inner = jnp.mean(scaled * normal, axis=1, keepdims=True)
    return inverse * (scaled - normal * inner), jnp.sum(grad * normal, axis=0, keepdims=True)


def kept_scores(query, keys, q_seg, k_seg, start):
    scores = dot(query, keys, ((1,), (1,))) * (1.0 / math.sqrt(HD))
    q_index = start + lax.broadcasted_iota(jnp.int32, scores.shape, 0)
    k_index = lax.broadcasted_iota(jnp.int32, scores.shape, 1)
    keep = (jnp.abs(q_index - k_index) <= HALF) & (q_seg == k_seg)
    return jnp.where(keep, scores, -1e30)


BIG = 100 * 1024 * 1024 // 2


def forward_kernel(
    heads, proj, cosine, sine, seg_column, seg_row, gains, mixed, query, keys, values, lses
):
    ranks, _, rows, _ = proj.shape
    length = ranks * rows
    q_block = 2 * rows
    k_seg = seg_row[0]
    for head in range(heads):
        at = slice(head * HD, (head + 1) * HD)

        def raw(part):
            first = (part * heads + head) * HD
            return proj[:, 0, :, first : first + HD].reshape(length, HD)

        query[0, :, at] = norm_rope(raw(0), gains[0:1], cosine[0], sine[0]).astype(bf16)
        keys[0, :, at] = norm_rope(raw(1), gains[1:2], cosine[0], sine[0]).astype(bf16)
        values[0, :, at] = raw(2).astype(bf16)

        @pl.loop(0, length // q_block)
        def one_block(number, head=head, at=at):
            start = pl.multiple_of(number * q_block, q_block)
            here = pl.ds(start, q_block)
            scores = kept_scores(
                query[0, here, at], keys[0, :, at], seg_column[0, here], k_seg, start
            )
            top = jnp.max(scores, axis=1, keepdims=True)
            weights = jnp.exp(scores - top)
            total = jnp.sum(weights, axis=1, keepdims=True)
            lses[0, head, here] = top + jnp.log(total)
            weights = (weights * (1.0 / total)).astype(bf16)
            result = dot(weights, values[0, :, at]).astype(bf16)
            mixed[pl.ds(number * 2, 2), 0, :, at] = result.reshape(2, rows, HD)


def backward_kernel(
    heads, proj, cosine, sine, seg_column, seg_row, gains, query, keys, values, lses, grad_mixed,
    grad_proj, grad_gains, grad_q, grad_k, grad_v,
):
    ranks, _, rows, _ = proj.shape
    length = ranks * rows
    q_block = 2 * rows
    k_seg = seg_row[0]
    scale = 1.0 / math.sqrt(HD)
    sum_q = jnp.zeros((1, HD), f32)
    sum_k = jnp.zeros((1, HD), f32)
    for head in range(heads):
        at = slice(head * HD, (head + 1) * HD)
        grad_k[...] = jnp.zeros_like(grad_k)
        grad_v[...] = jnp.zeros_like(grad_v)

        @pl.loop(0, length // q_block)
        def one_block(number, head=head, at=at):
            start = pl.multiple_of(number * q_block, q_block)
            here = pl.ds(start, q_block)
            q_rows = query[0, here, at]
            g_rows = grad_mixed[here, at]
            k_all = keys[0, :, at]
            scores = kept_scores(q_rows, k_all, seg_column[0, here], k_seg, start)
            weights = jnp.exp(scores - lses[0, head, here])
            grad_weights = dot(g_rows, values[0, :, at], ((1,), (1,)))
            delta = jnp.sum(weights * grad_weights, axis=1, keepdims=True)
            grad_scores = (weights * (grad_weights - delta)).astype(bf16)
            grad_q[here] = dot(grad_scores, k_all) * scale
            grad_k[...] += dot(grad_scores, q_rows, ((0,), (0,)))
            grad_v[...] += dot(weights.astype(bf16), g_rows, ((0,), (0,)))

        def rounded(value):
            return value.astype(bf16).astype(f32)

        def raw(part):
            first = (part * heads + head) * HD
            return proj[:, 0, :, first : first + HD].reshape(length, HD)

        def put(part, value):
            first = (part * heads + head) * HD
            grad_proj[:, :, first : first + HD] = value.astype(bf16).reshape(ranks, rows, HD)

        back_q, gain_q = norm_rope_back(
            raw(0), gains[0:1], cosine[0], sine[0], rounded(grad_q[...])
        )
        back_k, gain_k = norm_rope_back(
            raw(1), gains[1:2], cosine[0], sine[0], rounded(grad_k[...] * scale)
        )
        sum_q, sum_k = sum_q + gain_q, sum_k + gain_k
        put(0, back_q)
        put(1, back_k)
        put(2, grad_v[...])
    grad_gains[0:1] = sum_q
    grad_gains[1:2] = sum_k


def fixed(shape):
    return pl.BlockSpec(shape, lambda *_: (0,) * len(shape), pipeline_mode=pl.Buffered(1))


def leading(shape):
    return pl.BlockSpec((1,) + shape[1:], lambda i: (i,) + (0,) * (len(shape) - 1))


def params():
    return pltpu.CompilerParams(vmem_limit_bytes=BIG)


def cost(products):
    return pl.CostEstimate(flops=20 * products, bytes_accessed=0, transcendentals=0)


def out(shape, dtype=bf16):
    return jax.ShapeDtypeStruct(shape, dtype)


def attention_forward(proj, cosine, sine, seg_column, seg_row, gains):
    ranks, micro, rows, width = proj.shape
    length = ranks * rows
    width = width // 3
    heads = width // HD
    part = out((micro, length, width))
    by_rank = lambda n: pl.BlockSpec((ranks, 1, rows, n), lambda i: (0, i, 0, 0))
    lses = out((micro, heads, length, 1), f32)
    return pl.pallas_call(
        lambda *refs: forward_kernel(heads, *refs),
        grid=(micro,),
        in_specs=[by_rank(3 * width)]
        + [leading(v.shape) for v in (cosine, sine, seg_column, seg_row)]
        + [fixed(gains.shape)],
        out_specs=[by_rank(width)] + [leading(part.shape)] * 3 + [leading(lses.shape)],
        out_shape=[out((ranks, micro, rows, width)), part, part, part, lses],
        compiler_params=params(),
    )(proj, cosine, sine, seg_column, seg_row, gains)


def attention_backward(
    step, proj, cosine, sine, seg_column, seg_row, gains, query, keys, values, lses, grad_mixed
):
    ranks, micro, rows, width = proj.shape
    length = ranks * rows
    heads = width // 3 // HD

    def part(value):
        return pl.BlockSpec((1,) + value.shape[1:], lambda i: (step,) + (0,) * (value.ndim - 1))

    return pl.pallas_call(
        lambda *refs: backward_kernel(heads, *refs),
        grid=(1,),
        in_specs=[pl.BlockSpec((ranks, 1, rows, width), lambda i: (0, step, 0, 0))]
        + [part(v) for v in (cosine, sine, seg_column, seg_row)]
        + [fixed(gains.shape)]
        + [part(v) for v in (query, keys, values, lses)]
        + [fixed(grad_mixed.shape)],
        out_specs=[fixed((ranks, rows, width)), fixed((2, HD))],
        out_shape=[out((ranks, rows, width)), out((2, HD), f32)],
        scratch_shapes=[pltpu.VMEM((length, HD), f32)] * 3,
        compiler_params=params(),
    )(
        proj, cosine, sine, seg_column, seg_row, gains, query, keys, values, lses, grad_mixed
    )


def project(micro, tokens, gain, slab):
    ranks, count, _ = tokens.shape
    rows = count // micro
    width = slab.shape[1] - PAD

    def kernel(value, gain, weight, normed, proj):
        value = value[0].astype(f32)
        result = (value * inverse_rms(value) * gain[...]).astype(bf16)
        normed[...] = result.reshape(micro, 1, rows, D)
        proj[0] = dot(result, weight[:, :width])

    return pl.pallas_call(
        kernel,
        grid=(ranks,),
        in_specs=[leading((ranks, count, D)), fixed((1, D)), fixed(slab.shape)],
        out_specs=[
            pl.BlockSpec((micro, 1, rows, D), lambda i: (0, i, 0, 0)),
            leading((ranks, count, width)),
        ],
        out_shape=[out((micro, ranks, rows, D)), out((ranks, count, width), f32)],
        compiler_params=params(),
    )(tokens, gain, slab)


TILE = 512


def tiles(count):
    return pl.loop(0, count // TILE)


def tile(number):
    return pl.ds(pl.multiple_of(number * TILE, TILE), TILE)


HBM = pl.BlockSpec(memory_space=pl.ANY)


def copies(pairs, sems):
    started = [
        pltpu.make_async_copy(source, target, sems.at[place])
        for place, (source, target) in enumerate(pairs)
    ]
    for copy in started:
        copy.start()

    def wait():
        for copy in started:
            copy.wait()

    return wait


def plane_pairs(plane, pieces, target):
    planes = len(pieces)
    rows = target.shape[0] // planes
    return [
        (piece, target.at[pl.ds(lax.bitwise_xor(plane, jnp.int32(step)) * rows, rows)])
        for step, piece in enumerate(pieces)
    ]


def out_weight_pairs(plane, planes, gathered, target):
    ranks = gathered.shape[0]
    rows = D // (planes * ranks)
    return [
        (
            gathered.at[rank, pl.ds(step * rows, rows)],
            target.at[
                pl.ds((lax.bitwise_xor(plane, jnp.int32(step)) * ranks + rank) * rows, rows)
            ],
        )
        for rank in range(ranks)
        for step in range(planes)
    ]


def route(plane, planes, mixed, tokens, gathered, gain, router, routes, experts):
    count = tokens.shape[0]
    pieces = planes * gathered.shape[0]

    def kernel(
        plane, mixed, tokens, gathered, gain, router, routes, hidden, payload, gates,
        out_weight, sems,
    ):
        copies(out_weight_pairs(plane[0], planes, gathered, out_weight), sems)()

        @tiles(D)
        def _(number):
            at = tile(number)
            hidden[:, at] = tokens[:, at].astype(f32) + dot(mixed[...], out_weight[:, at])

        value = hidden[...]
        normed = (value * inverse_rms(value) * gain[...]).astype(bf16)
        payload[:, :D] = normed
        logits = dot(normed, router[...])
        column = lax.broadcasted_iota(jnp.int32, logits.shape, 1)
        routed = column == routes[:, 0:1]
        for choice in range(1, TOP):
            routed = routed | (column == routes[:, choice : choice + 1])
        logits = jnp.where(routed, logits, -1e30)
        weights = jnp.exp(logits - jnp.max(logits, axis=1, keepdims=True))
        weights = jnp.where(routed, weights, 0.0)
        weights = weights / jnp.sum(weights, axis=1, keepdims=True)
        gates[...] = weights
        high = weights.astype(bf16).astype(f32)
        payload[:, D:] = (high + pltpu.roll(weights - high, experts, 1)).astype(bf16)

    shapes = [out((count, D), f32), out((count, D + PAD)), out((count, PAD), f32)]
    return pl.pallas_call(
        kernel,
        grid_spec=pltpu.PrefetchScalarGridSpec(
            num_scalar_prefetch=1,
            grid=(1,),
            in_specs=[
                HBM if value is gathered else fixed(value.shape)
                for value in (mixed, tokens, gathered, gain, router, routes)
            ],
            out_specs=[fixed(shape.shape) for shape in shapes],
            scratch_shapes=[pltpu.VMEM((D, D), bf16), pltpu.SemaphoreType.DMA((pieces,))],
        ),
        out_shape=shapes,
        compiler_params=params(),
    )(plane, mixed, tokens, gathered, gain, router, routes)


def lane(value, number):
    column = lax.broadcasted_iota(jnp.int32, value.shape, 1)
    return jnp.sum(jnp.where(column == number, value.astype(f32), 0.0), axis=1, keepdims=True)


def one_hot(slot, slots):
    place = lax.broadcasted_iota(jnp.int32, (slots, slot.shape[1]), 0).astype(f32)
    return (place == slot).astype(bf16)


def expert_forward(where, payload, upstream, in_pieces, slots, experts):
    ranks, share, micro, rows, _ = payload.shape
    count = share * rows
    block = 2 * slots

    planes = len(in_pieces)

    def kernel(where, payload, upstream, *refs):
        (
            rows_in, tail, both, active, grad_produced, up_rows, places, in_weight, sems
        ) = refs[planes:]
        number = where[0]

        @pl.when((pl.program_id(0) == 0) & (pl.program_id(1) == 0))
        def _():
            copies(plane_pairs(where[1], refs[:planes], in_weight), sems)()

        for part in range(2):
            here = slice(part * slots, (part + 1) * slots)
            value = payload[part].reshape(count, D + PAD)
            marks = value[:, D:]
            first = lax.broadcasted_iota(jnp.int32, (8, PAD), 1) == number
            taken = dot(first.astype(bf16), marks, ((1,), (1,))) > 0.0
            before = lax.broadcasted_iota(jnp.int32, (count, count), 0)
            behind = lax.broadcasted_iota(jnp.int32, (count, count), 1)
            slot = dot(taken.astype(bf16), (before < behind).astype(bf16))
            select = one_hot(jnp.where(taken, slot, -1.0)[0:1], slots)
            wide = jnp.broadcast_to(lane(marks, number) > 0.0, (count, PAD))
            slot = dot((before > behind).astype(bf16), wide.astype(bf16))
            places[0, 0, part] = jnp.where(wide, slot, -1.0)
            rows_in[0, 0, here] = dot(select, value[:, :D]).astype(bf16)
            marks = dot(select, marks)
            tail[0, 0, here] = marks
            gate = lane(marks, number) + lane(marks, experts + number)
            picked = dot(select, upstream[part].reshape(count, D))
            up_rows[0, 0, here] = picked.astype(bf16)
            grad_produced[0, 0, here] = (gate * picked).astype(bf16)

        for number in range(FF // TILE):
            at = slice(number * TILE, (number + 1) * TILE)
            more = slice(FF + number * TILE, FF + (number + 1) * TILE)
            gate_part = dot(rows_in[0, 0], in_weight[:, at])
            up_part = dot(rows_in[0, 0], in_weight[:, more])
            both[0, 0, :, at] = gate_part
            both[0, 0, :, more] = up_part
            active[0, 0, :, at] = (
                gate_part / (1.0 + jnp.exp(-gate_part)) * up_part
            ).astype(bf16)

    def tokens_spec(width):
        return pl.BlockSpec((2, share, 1, rows, width), lambda m, b, _: (b, 0, m, 0, 0))

    pairs = ranks // 2
    shapes = [
        out((micro, pairs, block, D)),
        out((micro, pairs, block, PAD), f32),
        out((micro, pairs, block, 2 * FF), f32),
        out((micro, pairs, block, FF)),
        out((micro, pairs, block, D)),
        out((micro, pairs, block, D)),
        out((micro, pairs, 2, count, PAD), f32),
    ]
    return pl.pallas_call(
        kernel,
        grid_spec=pltpu.PrefetchScalarGridSpec(
            num_scalar_prefetch=1,
            grid=(micro, pairs),
            in_specs=[tokens_spec(D + PAD), tokens_spec(D)] + [HBM] * planes,
            out_specs=[
                pl.BlockSpec(
                    (1, 1) + s.shape[2:], lambda m, b, _, n=len(s.shape): (m, b) + (0,) * (n - 2)
                )
                for s in shapes
            ],
            scratch_shapes=[pltpu.VMEM((D, 2 * FF), bf16), pltpu.SemaphoreType.DMA((planes,))],
        ),
        out_shape=shapes,
        cost_estimate=cost(micro * pairs * block * D * (2 * FF + 2 * count)),
        compiler_params=params(),
    )(where, payload, upstream, *in_pieces)


def expert_backward(
    step, where, tail, both, active, grad_produced, up_rows, places, in_pieces, out_pieces,
    share, rows, experts,
):
    pairs, block = tail.shape[1:3]
    slots = block // 2
    count = places.shape[3]

    planes = len(in_pieces)

    def kernel(where, tail, both, active, grad_produced, up_rows, places, *refs):
        keep, give, grad_tokens, grad_both, in_weight, out_weight, sems = refs[2 * planes :]
        number = where[0]
        odd = where[2] == 1

        @pl.when(pl.program_id(0) == 0)
        def _():
            copies(
                plane_pairs(where[1], refs[:planes], in_weight)
                + plane_pairs(where[1], refs[planes : 2 * planes], out_weight),
                sems,
            )()

        gate = lane(tail[0, 0], number) + lane(tail[0, 0], experts + number)
        place = lax.broadcasted_iota(jnp.int32, (count, slots), 1).astype(f32)
        selects = [(places[0, 0, part][:, 0:1] == place).astype(bf16) for part in range(2)]

        def spread(value):
            return [
                dot(selects[part], value[part * slots : (part + 1) * slots])
                .astype(bf16)
                .reshape(share, rows, -1)
                for part in range(2)
            ]

        grad_gate = jnp.zeros((block, 1), f32)
        for tile in range(D // TILE):
            at = slice(tile * TILE, (tile + 1) * TILE)
            produced = dot(active[0, 0], out_weight[:, at]).astype(bf16).astype(f32)
            even_rank, odd_rank = spread((gate * produced).astype(bf16))
            keep[0, :, :, at] = jnp.where(odd, odd_rank, even_rank)
            give[0, :, :, at] = jnp.where(odd, even_rank, odd_rank)
            grad_gate = grad_gate + jnp.sum(
                up_rows[0, 0, :, at].astype(f32) * produced, axis=1, keepdims=True
            )

        for tile in range(FF // TILE):
            at = slice(tile * TILE, (tile + 1) * TILE)
            more = slice(FF + tile * TILE, FF + (tile + 1) * TILE)
            grad_active = dot(grad_produced[0, 0], out_weight[at, :], ((1,), (1,)))
            grad_active = grad_active.astype(bf16).astype(f32)
            gate_part = both[0, 0, :, at]
            up_part = both[0, 0, :, more]
            sigma = 1.0 / (1.0 + jnp.exp(-gate_part))
            grad_both[0, :, at] = (
                grad_active * up_part * (sigma * (1.0 + gate_part * (1.0 - sigma)))
            ).astype(bf16)
            grad_both[0, :, more] = (grad_active * (gate_part * sigma)).astype(bf16)

        for tile in range(D // TILE):
            at = slice(tile * TILE, (tile + 1) * TILE)
            grad_rows = dot(grad_both[0], in_weight[at, :], ((1,), (1,))).astype(bf16)
            grad_tokens[0, :, :, at], grad_tokens[1, :, :, at] = spread(grad_rows)

        high = grad_gate.astype(bf16).astype(f32)
        column = lax.broadcasted_iota(jnp.int32, (block, PAD), 1)
        extra = jnp.where(column == number, high, 0.0)
        extra = jnp.where(column == experts + number, grad_gate - high, extra)
        grad_tokens[0, :, :, D:], grad_tokens[1, :, :, D:] = spread(extra.astype(bf16))

    def part(value):
        return pl.BlockSpec(
            (1, 1) + value.shape[2:], lambda b, _: (step, b) + (0,) * (value.ndim - 2)
        )

    def tokens_spec(count, width):
        return pl.BlockSpec((count, share, rows, width), lambda b, _: (b, 0, 0, 0))

    return pl.pallas_call(
        kernel,
        grid_spec=pltpu.PrefetchScalarGridSpec(
            num_scalar_prefetch=1,
            grid=(pairs,),
            in_specs=[part(v) for v in (tail, both, active, grad_produced, up_rows, places)]
            + [HBM] * (2 * planes),
            out_specs=[
                tokens_spec(1, D),
                tokens_spec(1, D),
                tokens_spec(2, D + PAD),
                pl.BlockSpec((1, block, 2 * FF), lambda b, _: (b, 0, 0)),
            ],
            scratch_shapes=[
                pltpu.VMEM((D, 2 * FF), bf16),
                pltpu.VMEM((FF, D), bf16),
                pltpu.SemaphoreType.DMA((2 * planes,)),
            ],
        ),
        out_shape=[
            out((pairs, share, rows, D)),
            out((pairs, share, rows, D)),
            out((2 * pairs, share, rows, D + PAD)),
            out((pairs, block, 2 * FF)),
        ],
        cost_estimate=cost(pairs * block * D * (4 * FF + 2 * count)),
        compiler_params=params(),
    )(
        where, tail, both, active, grad_produced, up_rows, places, *in_pieces, *out_pieces
    )


def cut_ends(count, places):
    return [-(-count * place // 512) * 16 for place in (0, *places, 32)]


def weight_gradient(
    where, planes, left, rights, tail=None, first=0, steps=None, shift=False, cuts=None
):
    steps = planes if steps is None else steps
    count, width = left.shape
    parts = len(rights)
    part_rows = count // parts
    columns = rights[0].shape[1]
    width = width // planes
    step = min(TILE, columns & -columns)
    tails = [] if tail is None else [tail]
    split = columns // 3 * 2 if tails else columns
    wholes = [split, columns - split + tail.shape[1]] if tails else [split]

    ends = [cut_ends(width, (cuts or {}).get(number, ())) for number in range(steps)]
    shapes = [
        out((end - start, whole))
        for one in ends
        for start, end in zip(one, one[1:])
        for whole in wholes
    ]

    def of_plane(i, where):
        return (where[1] + first + i) % planes if shift else lax.bitwise_xor(where[1], first + i)

    def kernel(where, left, *refs):
        rights, tails, targets = refs[:parts], refs[parts : -len(shapes)], refs[-len(shapes) :]

        def fill(targets, ends):
            for value in tails:
                targets[1][:, columns - split :] = value[...]
            for number in range(columns // step):
                at = slice(number * step, (number + 1) * step)
                result = sum(
                    dot(left[part * part_rows : (part + 1) * part_rows], right[:, at], ((0,), (0,)))
                    for part, right in enumerate(rights)
                ).astype(bf16)
                if at.start >= split:
                    targets[1][:, at.start - split : at.stop - split] = result
                    continue
                for target, start, end in zip(targets[:: len(wholes)], ends, ends[1:]):
                    target[:, at] = result[start:end]

        done = 0
        for number, one in enumerate(ends):
            mine = targets[done : done + (len(one) - 1) * len(wholes)]
            done += len(mine)
            pl.when(pl.program_id(0) == number)(lambda mine=mine, one=one: fill(mine, one))

    return pl.pallas_call(
        kernel,
        grid_spec=pltpu.PrefetchScalarGridSpec(
            num_scalar_prefetch=1,
            grid=(steps,),
            in_specs=[pl.BlockSpec((count, width), lambda i, where: (0, of_plane(i, where)))]
            + [fixed(right.shape) for right in rights]
            + [
                pl.BlockSpec((width, value.shape[1]), lambda i, where: (of_plane(i, where), 0))
                for value in tails
            ],
            out_specs=[fixed(shape.shape) for shape in shapes],
        ),
        out_shape=shapes,
        cost_estimate=cost(0 if tails else count * steps * width * columns),
        compiler_params=params(),
    )(where, left, *rights, *tails)


def hidden_backward(
    step, plane, planes, parts, hidden, gates, upstream, gain, router, gathered, experts
):
    first = parts[0].shape
    count = first[1]
    terms = len(parts)

    def kernel(plane, *refs):
        parts = refs[:terms]
        hidden, gates, upstream, gain, router, gathered = refs[terms : terms + 6]
        (
            grad_hidden, grad_branch, grad_mixed, grad_logits, grad_gain, out_weight, sems
        ) = refs[terms + 6 :]
        wait = copies(out_weight_pairs(plane[0], planes, gathered, out_weight), sems)
        returned = sum(part[...].astype(f32) for part in parts[1:]) + parts[0][0].astype(f32)
        tail = returned[:, D:]
        grad_gates = gates[...] * (tail + pltpu.roll(tail, PAD - experts, 1))
        logits = grad_gates - gates[...] * jnp.sum(grad_gates, axis=1, keepdims=True)
        logits = logits.astype(bf16)
        grad_logits[...] = logits
        grad_normed = returned[:, :D] + dot(logits, router[...], ((1,), (1,)))
        value = hidden[...]
        inverse = inverse_rms(value)
        grad_gain[...] = jnp.sum(grad_normed * value * inverse, axis=0, keepdims=True)
        grad = upstream[...].astype(f32) + rms_backward(value, inverse, gain[...], grad_normed)
        grad_hidden[...] = grad
        grad_branch[...] = grad.astype(bf16)
        wait()

        @tiles(D)
        def _(number):
            at = tile(number)
            grad_mixed[:, at] = dot(grad_branch[...], out_weight[at, :], ((1,), (1,))).astype(bf16)

    shapes = [
        out((count, D), f32), out((count, D)), out((count, D)), out((count, PAD)),
        out((1, D), f32),
    ]
    args = (*parts, hidden, gates, upstream, gain, router, gathered)

    def spec(value):
        if value is gathered:
            return HBM
        if value is parts[0]:
            return pl.BlockSpec((1,) + first[1:], lambda *_: (0, 0, 0))
        if any(value is rows for rows in (hidden, gates, upstream)):
            return pl.BlockSpec((count, value.shape[1]), lambda *_: (step, 0))
        return fixed(value.shape)

    return pl.pallas_call(
        kernel,
        grid_spec=pltpu.PrefetchScalarGridSpec(
            num_scalar_prefetch=1,
            grid=(1,),
            in_specs=[spec(value) for value in args],
            out_specs=[fixed(shape.shape) for shape in shapes],
            scratch_shapes=[
                pltpu.VMEM((D, D), bf16),
                pltpu.SemaphoreType.DMA((planes * gathered.shape[0],)),
            ],
        ),
        out_shape=shapes,
        compiler_params=params(),
    )(plane, *args)


def project_backward(step, grad_proj, tokens, slab):
    ranks, rows, _ = grad_proj.shape
    width = slab.shape[1] - PAD

    def kernel(grad_proj, tokens, weight, grad_normed, grad_gain):
        value = tokens[...].reshape(2 * rows, D).astype(f32)
        inverse = inverse_rms(value)
        grad = dot(grad_proj[...].reshape(2 * rows, width), weight[:, :width], ((1,), (1,)))
        grad_normed[...] = grad.astype(bf16)

        @pl.when(pl.program_id(0) == 0)
        def _():
            grad_gain[...] = jnp.zeros_like(grad_gain)

        grad_gain[...] += jnp.sum(grad * value * inverse, axis=0, keepdims=True)

    return pl.pallas_call(
        kernel,
        grid=(ranks // 2,),
        in_specs=[
            pl.BlockSpec((2, rows, width), lambda i: (i, 0, 0)),
            pl.BlockSpec((2, rows, D), lambda i: (i, step, 0)),
            fixed(slab.shape),
        ],
        out_specs=[pl.BlockSpec((2 * rows, D), lambda i: (i, 0)), fixed((1, D))],
        out_shape=[out((ranks * rows, D)), out((1, D), f32)],
        compiler_params=params(),
    )(grad_proj, tokens, slab)


def cut_heads(weight, tail, ranks):
    rows = weight.shape[0]
    width = D // ranks

    def kernel(weight, tail, target):
        for rank in range(ranks):
            for part in range(3):
                at = part * D + rank * width
                target[rank, :, part * width : (part + 1) * width] = weight[:, at : at + width]
            target[rank, :, 3 * width :] = tail[...]

    return pl.pallas_call(
        kernel,
        out_shape=out((ranks, rows, 3 * width + PAD)),
        compiler_params=params(),
    )(weight, tail)


def unpack(heads, others, count):
    ranks, rows, columns = heads.shape
    width = columns // 2

    def kernel(heads, others, main, small):
        for rank in range(ranks):
            for part in range(3):
                at = part * D + rank * width
                value = heads[rank, :, part * width : (part + 1) * width] if part < 2 else others[
                    rank, :, :width
                ]
                main[:, at : at + width] = value.astype(f32)
        tails = sum(others[rank, :, width:].astype(f32) for rank in range(ranks))
        small[...] = tails + pltpu.roll(tails, PAD - count, 1)

    return pl.pallas_call(
        kernel,
        out_shape=[out((rows, 3 * D), f32), out((rows, PAD), f32)],
        compiler_params=params(),
    )(heads, others)


def shift_rep(value, step):
    count = lax.axis_size("rep")
    return lax.ppermute(value, "rep", [(i, (i + step) % count) for i in range(count)])


def cross_rep(value, bits):
    return lax.ppermute(value, "rep", [(i, i ^ bits) for i in range(lax.axis_size("rep"))])


def after(value, *others):
    return lax.optimization_barrier((value,) + others)[0]


def two_parts(value):
    high = lax.reduce_precision(value, 8, 7)
    return high.astype(bf16), (value - high).astype(bf16)


def ring_rep(value, *work):
    count = lax.axis_size("rep")
    rank = lax.axis_index("rep")
    rows = value.shape[0]
    full = jnp.zeros((count * rows,) + value.shape[1:], value.dtype)
    full = lax.dynamic_update_slice_in_dim(full, value, rank * rows, 0)
    for step in range(1, count):
        value, work = lax.optimization_barrier((value, work)) if step == count - 1 else (value, work)
        value = shift_rep(value, 1)
        full = lax.dynamic_update_slice_in_dim(full, value, (rank - step) % count * rows, 0)
    return full, work


def on_device(
    tokens, cotangent, w_qkv, w_o, w_router, norm_gains, qk_gain, w_in, w_out, segments, routes
):
    planes = lax.axis_size("rep")
    ranks = lax.axis_size("ep")
    plane = lax.axis_index("rep")
    rank = lax.axis_index("ep")
    share = w_in.shape[0]
    own = plane % share
    experts = share * ranks
    where = jnp.stack([rank * share + own, plane, rank % 2]).astype(jnp.int32)
    micro = segments.shape[1]
    mine = tokens.shape[0]
    rows = mine // micro
    length = rows * ranks
    capacity = rows * TOP * 17 // (16 * experts)
    slots = -(-share * capacity // 16) * 16
    width = HEADS // ranks * HD
    qk_gains = qk_gain.astype(f32).reshape(2, HD)
    dense_rows = w_qkv.shape[0]

    def exchange(value, step):
        pairs = [(i, i // share * share + (i % share + step) % share) for i in range(planes)]
        return lax.ppermute(value, "rep", pairs)

    def with_group(value):
        return jnp.stack([value] + [exchange(value, step) for step in range(1, share)])

    def gather_ranks(value):
        return lax.all_gather(value, "ep", axis=0)

    assert planes & (planes - 1) == 0 and share & (share - 1) == 0
    last_step = planes - 1
    in_parts, out_parts = (
        {
            step: lax.dynamic_index_in_dim(weight, own ^ step % share, 0, keepdims=False)
            for step in range(planes)
        }
        for weight in (w_in, w_out)
    )

    def send(parts, steps):
        return {step: cross_rep(parts[step], step) for step in steps}

    stream = gather_ranks(tokens)
    out_rows = [w_o] + [cross_rep(w_o, step) for step in range(1, planes)]
    upstream_group = with_group(cotangent)
    early_rows = cut_ends(out_parts[last_step].shape[0], (12,))[1]
    early = cross_rep(out_parts[last_step][:early_rows], last_step)
    out_parts[last_step] = out_parts[last_step][early_rows:]
    slab = cut_heads(
        w_qkv,
        jnp.concatenate(
            [
                w_router,
                norm_gains.reshape(dense_rows, 2),
                jnp.zeros((dense_rows, PAD - experts - 2), bf16),
            ],
            axis=1,
        ),
        ranks,
    )
    slab = lax.all_to_all(slab, "ep", split_axis=0, concat_axis=0, tiled=True)
    slab = slab.reshape(ranks * dense_rows, 3 * width + PAD)
    out_rows, upstream_group, slab, early = lax.optimization_barrier(
        (out_rows, upstream_group, slab, early)
    )
    gathered = gather_ranks(jnp.concatenate(out_rows, axis=0))
    segment = segments[0]
    cosine, sine = jax.vmap(lambda one: rope_tables(doc_positions(one), HD))(segment)
    sine = jnp.where(jnp.arange(HD) < HD // 2, -sine, sine)
    tables = (cosine, sine, segment[:, :, None], segment[:, None, :], qk_gains)
    slab, (tables, in_parts, out_parts) = ring_rep(slab, tables, in_parts, out_parts)
    router = slab[:, 3 * width :]
    gain_pair = router[:, experts : experts + 2].reshape(-1).astype(f32)
    first_gain = gain_pair[None, :D]
    second_gain = gain_pair[None, D:]
    in_parts, out_parts, upstream_group, stream = after(
        (in_parts, out_parts, upstream_group, stream), slab
    )
    in_pieces = {0: in_parts[0], **send(in_parts, range(last_step - 1, 0, -1))}
    upstream_all = gather_ranks(upstream_group)

    normed, proj = project(micro, stream, first_gain, slab)
    proj = proj.reshape(ranks, micro, rows, 3 * width)
    mixed_h, query, keys, values, lses = attention_forward(proj, *tables)
    mixed = lax.all_to_all(mixed_h, "ep", split_axis=0, concat_axis=3, tiled=True)
    mixed = mixed.reshape(mine, D)
    hidden, payload, gates = route(
        where[1:2], planes, mixed, tokens, gathered, second_gain, router, routes, experts
    )
    normed_two = payload[:, :D]
    payload, in_pieces = lax.optimization_barrier((payload, in_pieces))
    payload = with_group(payload)
    payload, in_parts, out_parts = lax.optimization_barrier((payload, in_parts, out_parts))
    in_pieces.update(send(in_parts, [last_step]))
    in_pieces, out_parts = lax.optimization_barrier((in_pieces, out_parts))
    out_pieces = {0: out_parts[0], **send(out_parts, range(1, planes))}
    in_pieces = [in_pieces[step] for step in range(planes)]
    out_pieces = [out_pieces[step] for step in range(planes)]
    payload = gather_ranks(payload)

    shape = (ranks, share, micro, rows, -1)
    rows_in, tail, both, active, grad_produced, up_rows, places = expert_forward(
        where, payload.reshape(shape), upstream_all.reshape(shape), in_pieces, slots, experts
    )
    in_rows = micro * ranks * slots
    out_cut = weight_gradient(
        where,
        planes,
        active.reshape(in_rows, FF),
        [grad_produced.reshape(in_rows, D)],
        cuts={1: (2,)},
    )

    def sum_rep(parts, shift=False):
        sums = [
            sum(parts[step].astype(f32) for step in range(first, planes, share))
            for first in range(share)
        ]
        return jnp.stack(
            [
                sum(
                    jnp.where(((own - step) % share if shift else own ^ step) == j, sums[step], 0.0)
                    for step in range(share)
                )
                for j in range(share)
            ]
        )

    tail, out_cut, out_pieces = lax.optimization_barrier((tail, out_cut, out_pieces))
    out_pieces[last_step] = jnp.concatenate([early, out_pieces[last_step]], axis=0)
    first, *out_cut = out_cut[1], out_cut[0], *out_cut[2:]
    first = cross_rep(first, 1)
    tail, out_cut, first = lax.optimization_barrier((tail, out_cut, first))
    out_sent = send(out_cut, range(1, planes))
    back = []
    returned = []

    def scatter_ranks(value):
        return lax.psum_scatter(value, "ep", scatter_dimension=0)

    def exchange_back(value):
        return [value] + [exchange(value[step], share - step) for step in range(1, share)]

    for step in range(micro):
        back.append(
            expert_backward(
                step, where, tail, both, active, grad_produced, up_rows, places, in_pieces,
                out_pieces, share, rows, experts,
            )
        )
        returned.append(scatter_ranks(back[step][2]))
        if step == 0:
            tail, out_sent[last_step] = after((tail, out_sent[last_step]), back[step][2])
        else:
            tail = after(tail, back[step][2])
    rows_in = after(rows_in, tail)
    rows_flat = rows_in.reshape(in_rows, D)
    grads_flat = [back[step][3].reshape(in_rows // micro, 2 * FF) for step in range(micro)]
    in_near = weight_gradient(
        where, planes, rows_flat, grads_flat, first=1, steps=1, shift=True, cuts={0: (24,)}
    )
    rows_flat, in_near = lax.optimization_barrier((rows_flat, in_near))
    cuts = {number: (19, 28) for number in range(planes - 3)}
    *in_rest, in_back, in_own = weight_gradient(
        where, planes, rows_flat, grads_flat, first=2, steps=last_step, shift=True, cuts=cuts
    )
    in_sent = {0: in_own}
    near_sent = [shift_rep(in_near[0], 1)]

    def swap(value, step):
        return lax.ppermute(value, "ep", [(i, i ^ step) for i in range(ranks)])

    bits = list(range((ranks // 2).bit_length() - 1))

    def cut_pairs(number, value, phase):
        way = bits if number % 2 == 0 else bits[::-1]
        bit = way[phase]
        low = 2 ** sum(other < bit for other in way[phase:])
        value = value.reshape((-1, 2, low) + value.shape[1:])
        side = rank // 2 // 2**bit % 2
        return [
            lax.dynamic_index_in_dim(value, which, 1, keepdims=False).reshape((-1,) + value.shape[3:])
            for which in (side, 1 - side)
        ]

    def pair_sum(number, keep, give):
        got = swap(give, 1)
        return [
            total(parts).astype(bf16)
            for parts in zip(cut_pairs(number, keep, 0), cut_pairs(number, got, 0))
        ]

    def halve(number, halves, phase):
        return halves[0], swap(halves[1], 2 * 2 ** (bits if number % 2 == 0 else bits[::-1])[phase])

    def total(parts):
        return sum(part.astype(f32) for part in parts)

    grad_inputs, branches, logit_grads, grad_projs, normed_sums = [], [], [], [], []
    gain_two_sum = gain_one_sum = qk_sum = 0.0
    in_rest, in_back, in_near, out_sent, near_sent = lax.optimization_barrier(
        (in_rest, in_back, in_near, out_sent, near_sent)
    )
    mixtures = [part[:2] for part in back]
    for step in range(micro):
        parts = after(returned[step], [one[1] for one in grad_inputs])
        parts, near_sent = lax.optimization_barrier((parts, near_sent))
        if step == micro - 1:
            mixtures = after(mixtures, parts)
            crossed = [halve(number, value, 0) for number, value in enumerate(mixtures)]
        parts = exchange_back(parts)
        parts, in_rest, in_back, in_near, mixtures = lax.optimization_barrier(
            (parts, in_rest, in_back, in_near, mixtures)
        )
        if step == 0:
            mixtures = [pair_sum(number, *part) for number, part in enumerate(mixtures)]
            in_sent[last_step] = shift_rep(in_back, last_step)
            near_sent.append(shift_rep(in_near[1], 1))
        if step == micro - 1:
            rest = [in_rest[3 * i : 3 * i + 3] for i in range(planes - 3)]
            rest_sent = [[shift_rep(part[0], i + 2) for i, part in enumerate(rest)]]
        grad_hidden, grad_branch, grad_mixed, grad_logits, gain_two = hidden_backward(
            step, where[1:2], planes, parts, hidden, gates, cotangent, second_gain, router, gathered,
            experts,
        )
        branches.append(grad_branch)
        logit_grads.append(grad_logits)
        gain_two_sum = gain_two_sum + gain_two
        if step == micro - 1:
            out_sum = dot(mixed, jnp.concatenate(branches, axis=0), ((0,), (0,))).astype(bf16)
            out_sum = out_sum.reshape(planes, ranks, dense_rows, D).transpose(1, 0, 2, 3)
        grad_mixed = lax.all_to_all(grad_mixed, "ep", split_axis=1, concat_axis=0, tiled=True)
        grad_mixed, mixtures = lax.optimization_barrier((grad_mixed, mixtures))
        if step == micro - 1:
            grad_mixed, crossed, rest_sent, rest, out_sum = lax.optimization_barrier(
                (grad_mixed, crossed, rest_sent, rest, out_sum)
            )
            out_sum = lax.psum_scatter(out_sum, "ep", scatter_dimension=0)
            rest_sent.append([shift_rep(part[1], i + 2) for i, part in enumerate(rest)])
        grad_proj, grad_qk = attention_backward(
            step, proj, *tables, query, keys, values, lses, grad_mixed
        )
        qk_sum = qk_sum + grad_qk.reshape(-1)
        if step < micro - 1:
            grad_proj, in_sent, near_sent = lax.optimization_barrier(
                (grad_proj, in_sent, near_sent)
            )
        else:
            grad_proj, normed_sums, rest_sent, rest = lax.optimization_barrier(
                (grad_proj, normed_sums, rest_sent, rest)
            )
        grad_projs.append(grad_proj)
        grad_normed, gain_one = project_backward(step, grad_proj, stream, slab)
        gain_one_sum = gain_one_sum + gain_one
        grad_inputs.append(
            (
                grad_hidden,
                grad_normed,
            )
        )
        if step < micro - 1:
            normed_sums.append(
                lax.psum_scatter(grad_normed, "ep", scatter_dimension=0, tiled=True)
            )

    router_sum = dot(normed_two, jnp.concatenate(logit_grads, axis=0), ((0,), (0,)))
    qk_columns = qk_sum.shape[0] // dense_rows
    small = jnp.concatenate(
        [
            router_sum[:, :experts],
            jnp.concatenate([gain_one_sum, gain_two_sum], axis=1).reshape(D, 2),
            jnp.tile(qk_sum.reshape(dense_rows, qk_columns), (planes * ranks, 1)),
        ],
        axis=1,
    )
    count = small.shape[1]

    def halves(value):
        high, low = two_parts(value)
        blank = jnp.zeros((value.shape[0], PAD - 2 * count), bf16)
        return jnp.concatenate([high, low, blank], axis=1)

    def joined(value):
        return value[..., :count].astype(f32) + value[..., count : 2 * count].astype(f32)

    grad_projs, rest, out_cut, out_sent, _ = lax.optimization_barrier(
        (grad_projs, rest, out_cut, out_sent, grad_inputs[-1][1])
    )
    rest_sent.append([shift_rep(part[2], i + 2) for i, part in enumerate(rest)])
    packed = weight_gradient(
        where,
        planes,
        normed.reshape(ranks * mine, D),
        [grad.reshape(length, 3 * width) for grad in grad_projs],
        halves(small),
    )
    packed, rest_sent, out_cut, out_sent, crossed = lax.optimization_barrier(
        (packed, rest_sent, out_cut, out_sent, crossed)
    )
    heads, others = packed[::2], packed[1::2]
    heads_sent = [heads[0]] + [cross_rep(heads[step], step) for step in range(1, planes)]
    heads_sent, others = lax.optimization_barrier((heads_sent, others))
    others_sent = [others[0]] + [cross_rep(others[step], step) for step in range(1, planes)]
    normed_sums.append(
        lax.psum_scatter(
            after(grad_inputs[-1][1], packed), "ep", scatter_dimension=0, tiled=True
        )
    )
    others_sent, out_sum = lax.optimization_barrier((others_sent, out_sum))
    for phase in range(1, len(bits)):
        mixtures = [total(parts).astype(bf16) for parts in crossed]
        crossed = [
            halve(number, cut_pairs(number, value, phase), phase)
            for number, value in enumerate(mixtures)
        ]
    mixture = []
    for number in range(micro):
        parts = total(crossed[number])[0]
        mixture.append((parts[0], exchange_back(parts.astype(bf16))[1:]))
    own_sum = lax.dynamic_index_in_dim(out_sum, plane, 0, keepdims=False)
    out_sent_back = [
        cross_rep(lax.dynamic_index_in_dim(out_sum, plane ^ step, 0, keepdims=False), step)
        for step in range(1, planes)
    ]
    def to_ranks(value):
        value = value.reshape(ranks, dense_rows, -1)
        return lax.all_to_all(value, "ep", split_axis=0, concat_axis=0, tiled=True)

    heads = to_ranks(total(heads_sent).astype(bf16))
    main = total([part[:, :width] for part in others_sent]).astype(bf16)
    small = sum(joined(part[:, width:]) for part in others_sent)
    packed = (heads, to_ranks(jnp.concatenate([main, halves(small)], axis=1)))
    packed, mixture, out_sent_back, normed_sums = lax.optimization_barrier(
        (packed, mixture, out_sent_back, normed_sums)
    )
    grad_tokens = []
    for step in range(micro):
        own_stream = tokens[step * rows : (step + 1) * rows].astype(f32)
        grad_tokens.append(
            grad_inputs[step][0]
            + rms_backward(
                own_stream, inverse_rms(own_stream), first_gain, normed_sums[step].astype(f32)
            )
        )
    grad_tokens = jnp.concatenate(grad_tokens, axis=0)
    output = jnp.concatenate([mine_part + total(others) for mine_part, others in mixture], axis=0)
    output = (hidden + output).astype(bf16)
    grad_w_o = total([own_sum, *out_sent_back])
    grad_w_qkv, small = unpack(*packed, count)
    out_sent[1] = jnp.concatenate([first, out_sent[1]], axis=0)
    grad_w_out = sum_rep({0: out_cut[0], **out_sent})
    in_sent[1] = jnp.concatenate(near_sent, axis=0)
    for i in range(planes - 3):
        in_sent[i + 2] = jnp.concatenate([parts[i] for parts in rest_sent], axis=0)
    grad_w_in = sum_rep(in_sent, shift=True)
    return (
        output,
        grad_tokens,
        grad_w_qkv,
        grad_w_o,
        small[:, :experts],
        small[:, experts : experts + 2].reshape(-1),
        small[:, experts + 2 : count].reshape(-1),
        grad_w_in,
        grad_w_out,
    )


def solution(mesh):
    placed = (
        P(("rep", "ep"), None),
        P(("rep", "ep"), None),
        P(("rep", "ep"), None),
        P(("rep", "ep"), None),
        P(("rep", "ep"), None),
        P(("rep", "ep")),
        P(),
        P("ep", "rep", None),
        P("ep", "rep", None),
        P("rep", None, None),
        P(("rep", "ep"), None),
    )
    return jax.shard_map(
        on_device,
        mesh=mesh,
        in_specs=placed,
        out_specs=(
            P(("rep", "ep"), None),
            P(("rep", "ep"), None),
            P(("rep", "ep"), None),
            P(("rep", "ep"), None),
            P(("rep", "ep"), None),
            P(("rep", "ep")),
            P(),
            P("ep", "rep", None),
            P("ep", "rep", None),
        ),
        check_vma=False,
    )
```
